32 devices in a mesh: shard: 32 (over z, y, x, core).
Axes of the slice: x: 2, y: 2, z: 4, core: 2. Of those that a mesh axis runs over, the one named last changes fastest.
Arguments:
- features: bfloat16 [32768, 128], P('shard'), may hold values from -6 to 6
- conv_weight: bfloat16 [27, 128, 128], replicated, may hold values from -0.125 to 0.125
- down_weight: bfloat16 [8, 128, 256], replicated, may hold values from -0.25 to 0.25
- neighbour_map: int32 [27, 32768], P(None, 'shard'), may hold values from 0 to 1280, as said below
- halo_rows: int32 [4, 2048], P(None, 'shard'), may hold values from 0 to 1024, as said below
- child_map: int32 [8, 8192], P(None, 'shard'), may hold values from 0 to 1152, as said below
- child_rows: int32 [4, 1024], P(None, 'shard'), may hold values from 0 to 1024, as said below
- out_grad: bfloat16 [8192, 256], P('shard'), may hold values from -6 to 6
Outputs:
- coarse: bfloat16 [8192, 256], P('shard')
- input_grad: float32 [32768, 128], P('shard')
- conv_grad: float32 [27, 128, 128], replicated
- down_grad: float32 [8, 128, 256], replicated
The draws below stay inside these ranges and needn't reach their ends.
Inputs may be any that keep to these rules, and one draw needn't show every extreme that they name: `neighbour_map`: indices into the device's extended fine table: below 1024 a local voxel, 1024 + s*64 + c row c received in slot s, the largest value a missing neighbour. Offset 13 maps every voxel to itself. Rows received in slot s that a map reads are live entries of the sender's list. `halo_rows`: live entries come first in a slot, the rest are 1024; every slot toward a missing device is empty; the slot of offset +1 is full on every device that has a next device. `child_map`: as neighbour_map, for the extended hidden table with 32 rows per slot. `child_rows`: as halo_rows, with 32 rows per slot.
All inputs are finite; a program needn't handle non-finite values.
Results may differ from the reference program's by a relative error of at most 0.006.
Values may be sent and summed in bfloat16 or wider, within the bound.
No kernel may reach another device: no remote copies, remote signals or barrier semaphores. Data moves between devices by JAX's collectives and lax.ppermute only.
A program may use at most 64 MiB of HBM per device.

```python
import math
import jax
import jax.numpy as jnp
from jax import lax

C1 = 128
C2 = 256
V_DEV = 1024
REACH = 2
P_DEV = 256
SLOTS = 4
CAP = 64
CAP2 = 32
VOXELS = 32768
PARENTS = 8192
N_SHARD = 32


def slot_offsets():
    return jnp.concatenate([jnp.arange(-REACH, 0, dtype=jnp.int32), jnp.arange(1, REACH + 1, dtype=jnp.int32)])


def slot_counts(key, capacity):
    counts = jax.random.randint(key, (N_SHARD, SLOTS), capacity // 2, capacity + 1)
    counts = counts.at[:, REACH].set(capacity)
    target = jnp.arange(N_SHARD, dtype=jnp.int32)[:, None] + slot_offsets()[None, :]
    return jnp.where((target >= 0) & (target < N_SHARD), counts, 0)


def send_lists(key, capacity):
    counts = slot_counts(key, capacity)
    picked = jax.random.randint(jax.random.fold_in(key, 7), (N_SHARD, SLOTS, capacity), 0, V_DEV)
    places = jnp.arange(capacity, dtype=jnp.int32)[None, None, :]
    sent_rows = jnp.where(places < counts[:, :, None], picked, V_DEV)
    return sent_rows.transpose(1, 0, 2).reshape(SLOTS, N_SHARD * capacity)


def index_map(key, counts, capacity, kernel_count, row_count):
    subkeys = jax.random.split(key, 4)
    shape_all = (N_SHARD, kernel_count, row_count)
    category = jax.random.randint(subkeys[0], shape_all, 0, 4)
    local_row = jax.random.randint(subkeys[1], shape_all, 0, V_DEV)
    slot_pick = jax.random.randint(subkeys[2], shape_all, 0, SLOTS)
    source = jnp.arange(N_SHARD, dtype=jnp.int32)[:, None, None] - slot_offsets()[slot_pick]
    in_range = (source >= 0) & (source < N_SHARD)
    available = jnp.where(in_range, counts[jnp.clip(source, 0, N_SHARD - 1), slot_pick], 0)
    position = jax.random.randint(subkeys[3], shape_all, 0, jnp.maximum(available, 1))
    absent = V_DEV + SLOTS * capacity
    halo_index = jnp.where(available > 0, V_DEV + slot_pick * capacity + position, absent)
    return jnp.where(category < 2, local_row, jnp.where(category == 2, halo_index, absent))


def draw_halo_rows(key, part):
    common = jax.random.fold_in(key, 11)
    return send_lists(common, CAP)


def draw_neighbour_map(key, part):
    common = jax.random.fold_in(key, 11)
    counts = slot_counts(common, CAP)
    own_key = jax.random.fold_in(key, 21)
    chosen = index_map(own_key, counts, CAP, 27, V_DEV)
    chosen = chosen.at[:, 13, :].set(jnp.arange(V_DEV, dtype=jnp.int32)[None, :])
    return chosen.transpose(1, 0, 2).reshape(27, N_SHARD * V_DEV)


def draw_child_rows(key, part):
    common = jax.random.fold_in(key, 31)
    return send_lists(common, CAP2)


def draw_child_map(key, part):
    common = jax.random.fold_in(key, 31)
    counts = slot_counts(common, CAP2)
    own_key = jax.random.fold_in(key, 41)
    chosen = index_map(own_key, counts, CAP2, 8, P_DEV)
    return chosen.transpose(1, 0, 2).reshape(8, N_SHARD * P_DEV)


def level_of(key, shape, cuts, low, high):
    gain = 1.0
    for axis_at, shards_of in cuts:
        heights = jax.random.uniform(jax.random.fold_in(jax.random.fold_in(key, 6), axis_at), (shards_of,), jnp.float32, low / len(cuts), high / len(cuts))
        gain = gain * jnp.repeat(jnp.exp(heights), shape[axis_at] // shards_of).reshape((-1,) + (1,) * (len(shape) - 1 - axis_at))
    return gain


def scatter_about(key, extent, scale, bound, cuts=(), kind=jnp.bfloat16):
    entries = scale * jax.random.normal(key, extent, jnp.float32)
    if cuts:
        entries = entries * level_of(key, extent, cuts, -0.22, 0.18)
    return jnp.clip(entries, -bound, bound).astype(kind)


def setup_inputs(seed: int = 0) -> dict:
    key_of = jax.random.split(jax.random.key(seed), 9)
    return {
        "features": scatter_about(key_of[0], (VOXELS, C1), 1.0, 6.0, ((0, 32),)),
        "conv_weight": scatter_about(key_of[1], (27, C1, C1), (14 * C1) ** -0.5, 0.125),
        "down_weight": scatter_about(key_of[2], (8, C1, C2), (4 * C1) ** -0.5, 0.25),
        "neighbour_map": draw_neighbour_map(jax.random.fold_in(key_of[8], 71), 0),
        "halo_rows": draw_halo_rows(jax.random.fold_in(key_of[8], 71), 0),
        "child_map": draw_child_map(jax.random.fold_in(key_of[8], 71), 0),
        "child_rows": draw_child_rows(jax.random.fold_in(key_of[8], 71), 0),
        "out_grad": scatter_about(key_of[7], (PARENTS, C2), 1.0, 6.0, ((0, 32),)),
    }


def offsets_list(slot_count):
    half_count = slot_count // 2
    return [number - half_count for number in range(half_count)] + [number + 1 for number in range(half_count)]

def conv_forward(extended, neighbours, weights):

    def accumulate(running, inputs):
        index_row, kernel = inputs
        picked = jnp.take(extended, index_row, axis=0)
        return (running + jnp.dot(picked, kernel, preferred_element_type=jnp.float32), None)
    start_sum = jnp.zeros((neighbours.shape[1], weights.shape[2]), jnp.float32)
    result, unused = lax.scan(accumulate, start_sum, (neighbours, weights))
    return result

def conv_backward(extended, neighbours, weights, upstream):

    def accumulate(carried, inputs):
        index_row, kernel = inputs
        picked = jnp.take(extended, index_row, axis=0)
        weight_grad = lax.dot_general(picked, upstream, (((0,), (0,)), ((), ())), preferred_element_type=jnp.float32)
        back_rows = lax.dot_general(upstream, kernel, (((1,), (1,)), ((), ())), preferred_element_type=jnp.float32)
        return (carried.at[index_row].add(back_rows), weight_grad)
    start_sum = jnp.zeros((extended.shape[0], extended.shape[1]), jnp.float32)
    return lax.scan(accumulate, start_sum, (neighbours, weights))

def silu_slope(values):
    sigmoid_value = jax.nn.sigmoid(values)
    return sigmoid_value * (1.0 + values * (1.0 - sigmoid_value))

def incoming_rows(padded_all, rows_all, device, offsets):
    pieces = []
    for number in range(len(offsets)):
        source = device - offsets[number]
        in_range = (source >= 0) & (source < N_SHARD)
        clipped = jnp.clip(source, 0, N_SHARD - 1).astype(jnp.int32)
        source_table = lax.dynamic_index_in_dim(padded_all, clipped, 0, keepdims=False)
        wanted = lax.dynamic_index_in_dim(rows_all, clipped, 0, keepdims=False)[number]
        taken_rows = jnp.take(source_table, wanted, axis=0)
        pieces.append(jnp.where(in_range, taken_rows, jnp.zeros_like(taken_rows)))
    return jnp.concatenate(pieces)

def returned_rows(back_all, rows_all, device, offsets):
    gathered_sum = jnp.zeros((V_DEV + 1, back_all.shape[-1]), jnp.float32)
    own_rows = lax.dynamic_index_in_dim(rows_all, device, 0, keepdims=False)
    for number in range(len(offsets)):
        target = device + offsets[number]
        in_range = (target >= 0) & (target < N_SHARD)
        clipped = jnp.clip(target, 0, N_SHARD - 1).astype(jnp.int32)
        returned = lax.dynamic_index_in_dim(back_all, clipped, 0, keepdims=False)[number]
        returned = jnp.where(in_range, returned, jnp.zeros_like(returned))
        gathered_sum = gathered_sum.at[own_rows[number]].add(returned)
    return gathered_sum[:V_DEV]

def reference(features, conv_weight, down_weight, neighbour_map, halo_rows, child_map, child_rows, out_grad):
    offsets = offsets_list(SLOTS)
    device_ids = jnp.arange(N_SHARD, dtype=jnp.int32)
    feats_all = features.reshape(N_SHARD, V_DEV, C1)
    padded_x = jnp.concatenate([feats_all, jnp.zeros((N_SHARD, 1, C1), features.dtype)], axis=1)
    maps_x = neighbour_map.reshape(27, N_SHARD, V_DEV).transpose(1, 0, 2)
    lists_x = halo_rows.reshape(SLOTS, N_SHARD, CAP).transpose(1, 0, 2)
    maps_h = child_map.reshape(8, N_SHARD, P_DEV).transpose(1, 0, 2)
    lists_h = child_rows.reshape(SLOTS, N_SHARD, CAP2).transpose(1, 0, 2)
    grads_all = out_grad.reshape(N_SHARD, P_DEV, C2)
    zero_row = jnp.zeros((1, C1), features.dtype)

    def extended_x(device):
        return jnp.concatenate([feats_all[device], incoming_rows(padded_x, lists_x, device, offsets), zero_row])

    def forward_one(device):
        pre_act = conv_forward(extended_x(device), maps_x[device], conv_weight)
        hidden = (feats_all[device].astype(jnp.float32) + jax.nn.silu(pre_act)).astype(jnp.bfloat16)
        return (pre_act, hidden)
    pre_all, hidden_all = lax.map(forward_one, device_ids)
    padded_h = jnp.concatenate([hidden_all, jnp.zeros((N_SHARD, 1, C1), jnp.bfloat16)], axis=1)

    def down_one(device):
        extended = jnp.concatenate([hidden_all[device], incoming_rows(padded_h, lists_h, device, offsets), zero_row])
        lowered = conv_forward(extended, maps_h[device], down_weight).astype(jnp.bfloat16)
        back_ext, weight_terms = conv_backward(extended, maps_h[device], down_weight, grads_all[device])
        return (lowered, back_ext, weight_terms)
    lowered_all, back_h_all, down_terms = lax.map(down_one, device_ids)
    back_h_slots = back_h_all[:, V_DEV:V_DEV + SLOTS * CAP2].reshape(N_SHARD, SLOTS, CAP2, C1)

    def middle_one(device):
        hidden_grad = back_h_all[device, :V_DEV] + returned_rows(back_h_slots, lists_h, device, offsets)
        pre_grad = (hidden_grad * silu_slope(pre_all[device])).astype(jnp.bfloat16)
        back_ext, weight_terms = conv_backward(extended_x(device), maps_x[device], conv_weight, pre_grad)
        return (hidden_grad, back_ext, weight_terms)
    hidden_grads, back_x_all, conv_terms = lax.map(middle_one, device_ids)
    back_x_slots = back_x_all[:, V_DEV:V_DEV + SLOTS * CAP].reshape(N_SHARD, SLOTS, CAP, C1)

    def final_one(device):
        return hidden_grads[device] + back_x_all[device, :V_DEV] + returned_rows(back_x_slots, lists_x, device, offsets)
    input_grad = lax.map(final_one, device_ids).reshape(VOXELS, C1)
    grad_scale = 1.0 / math.sqrt(VOXELS)
    return (lowered_all.reshape(PARENTS, C2), input_grad, lax.optimization_barrier(jnp.sum(conv_terms, axis=0)) * grad_scale, lax.optimization_barrier(jnp.sum(down_terms, axis=0)) * grad_scale)
```

```python
import functools
import math

import jax
import jax.numpy as jnp
from jax import lax
from jax.experimental import pallas as pl
from jax.experimental.pallas import tpu as pltpu
from jax.sharding import PartitionSpec as P

BF16 = jnp.bfloat16
F32 = jnp.float32
LANES = 128
RIGHT = 4096


def offsets_list(slot_count):
    half_count = slot_count // 2
    return [number - half_count for number in range(half_count)] + [
        number + 1 for number in range(half_count)
    ]


def shift(value, axis, by):
    count = lax.axis_size(axis)
    pairs = [(i, i + by) for i in range(count) if 0 <= i + by < count]
    return lax.ppermute(value, axis, pairs)


def matmul(left, right):
    return jnp.dot(left, right, preferred_element_type=F32)


def matmul_rt(left, right):
    return lax.dot_general(left, right, (((1,), (1,)), ((), ())), preferred_element_type=F32)


def column(row):
    pieces = []
    for start in range(0, row.shape[1], LANES):
        piece = jnp.broadcast_to(row[:, start : start + LANES], (LANES, LANES))
        pieces.append(jnp.transpose(piece))
    return pieces[0] if len(pieces) == 1 else jnp.concatenate(pieces, axis=0)


def one_hot_rows(col, width):
    blocks = []
    lane = lax.broadcasted_iota(jnp.int32, col.shape, 1)
    for start in range(0, width, LANES):
        blocks.append(jnp.where(col == lane + start, 1.0, 0.0).astype(BF16))
    return jnp.concatenate(blocks, axis=1)


def one_hot_columns(row, height):
    place = lax.broadcasted_iota(jnp.int32, (height, row.shape[1]), 0)
    return jnp.where(place == row, 1.0, 0.0).astype(BF16)


def list_row(lists, first, per_row):
    pieces = [lists[first + n : first + n + 1, :] for n in range(per_row)]
    return pieces[0] if per_row == 1 else jnp.concatenate(pieces, axis=1)


def gather_lists(lists_ref, table):
    slots, cap = lists_ref.shape
    lists = lists_ref[...]
    per_row = max(1, min(slots, LANES // cap))
    parts = []
    for first in range(0, slots, per_row):
        chooser = one_hot_rows(column(list_row(lists, first, per_row)), table.shape[0])
        parts.append(matmul(chooser, table))
    return parts[0] if len(parts) == 1 else jnp.concatenate(parts, axis=0)


def head_kernel(features_ref, halo_ref, child_map_ref, out_grad_ref, down_ref, *outs):
    sends, back_ref = outs[:-1], outs[-1]
    slots, cap = halo_ref.shape
    voxels = features_ref.shape[0]
    octants = child_map_ref.shape[0]
    table_rows = back_ref.shape[0]
    cap2 = (table_rows - voxels) // slots
    listed = gather_lists(halo_ref, features_ref[...]).astype(BF16)
    for s in range(slots):
        sends[s][0:cap, :] = listed[s * cap : (s + 1) * cap, :]
    upstream = out_grad_ref[...]
    total = jnp.zeros((table_rows, LANES), F32)
    child_map = child_map_ref[...]
    for o in range(octants):
        part = matmul_rt(upstream, down_ref[o]).astype(BF16)
        total = total + matmul(one_hot_columns(child_map[o : o + 1, :], table_rows), part)
    back_ref[...] = total
    for s in range(slots):
        slot = slots - 1 - s
        first = voxels + slot * cap2
        sends[s][cap : cap + cap2, :] = total[first : first + cap2, :].astype(BF16)


def forward_kernel(slots, *refs):
    received = refs[:slots]
    (features_ref, map_ref, weight_ref, back_ref, child_ref) = refs[slots : slots + 5]
    (hidden_ref, leaving_ref, hgrad_ref, pgrad_ref, cgrad_ref) = refs[slots + 5 : slots + 10]
    (table_ref, stacked_ref, acc_ref) = refs[slots + 10 :]
    voxels = features_ref.shape[0]
    kernel_count = map_ref.shape[0]
    middle = kernel_count // 2
    cap2 = child_ref.shape[1]
    cap = received[0].shape[0] - cap2
    half, half_halo = voxels // 2, slots * cap // 2
    features = features_ref[...]
    table_ref[0:half, 0:LANES] = features[0:half]
    table_ref[0:half, LANES : 2 * LANES] = features[half:voxels]
    for s in range(slots):
        place = half + (s % (slots // 2)) * cap
        side = (s // (slots // 2)) * LANES
        table_ref[place : place + cap, side : side + LANES] = received[s][0:cap, :]
    table_rows = half + half_halo

    def gather(k):
        row = map_ref[pl.ds(k, 1), :]
        outside = row >= voxels
        beyond = row - voxels
        near_code = row + jnp.where(row >= half, RIGHT - half, 0)
        far_code = half + beyond + jnp.where(beyond >= half_halo, RIGHT - half_halo, 0)
        code = jnp.where(outside, far_code, near_code)
        col = column(code)
        chooser = one_hot_rows(col & (RIGHT - 1), table_rows)
        both = matmul(chooser, table_ref[...])
        picked = jnp.where(col >= RIGHT, both[:, LANES:], both[:, :LANES]).astype(BF16)
        stacked_ref[k] = picked
        return picked

    acc_ref[...] = matmul(features, weight_ref[middle])

    def step(j, carry):
        near, far = gather(j), gather(j + middle + 1)
        pair = jnp.concatenate([near, far], axis=1)
        kernel = jnp.concatenate([weight_ref[j], weight_ref[j + middle + 1]], axis=0)
        acc_ref[...] += matmul(pair, kernel)
        return carry

    lax.fori_loop(0, middle, step, 0)
    pre = acc_ref[...]
    sig = jax.nn.sigmoid(pre)
    hidden = (features.astype(F32) + pre * sig).astype(BF16)
    hidden_ref[...] = hidden
    leaving_ref[...] = gather_lists(child_ref, hidden).astype(BF16)
    hgrad = back_ref[...]
    lists = child_ref[...]
    for s in range(slots):
        returned = received[slots - 1 - s][cap : cap + cap2, :]
        hgrad = hgrad + matmul(one_hot_columns(lists[s : s + 1, :], voxels), returned)
    hgrad_ref[...] = hgrad
    pgrad = hgrad * (sig * (1.0 + pre * (1.0 - sig)))
    pgrad_ref[...] = pgrad.astype(BF16)
    pgrad_t = jnp.transpose(pgrad).astype(BF16)
    rows = kernel_count * LANES
    cgrad_ref[rows:, :] = jnp.zeros((cgrad_ref.shape[0] - rows, LANES), BF16)

    def put(k, value):
        cgrad_ref[pl.ds(pl.multiple_of(k * LANES, LANES), LANES), :] = jnp.transpose(value).astype(BF16)

    put(middle, matmul(pgrad_t, features))

    def weight_step(j, carry):
        pair = jnp.concatenate([stacked_ref[j], stacked_ref[j + middle + 1]], axis=1)
        both = matmul(pgrad_t, pair)
        put(j, both[:, :LANES])
        put(j + middle + 1, both[:, LANES:])
        return carry

    lax.fori_loop(0, middle, weight_step, 0)


def spread_kernel(slots, pgrad_ref, map_ref, weight_ref, back_ref, *sends):
    acc_ref = sends[-1]
    sends = sends[:-1]
    voxels = pgrad_ref.shape[0]
    kernel_count = map_ref.shape[0]
    middle = kernel_count // 2
    cap = sends[0].shape[0]
    table_rows = voxels + slots * cap
    pgrad = pgrad_ref[...]
    acc_ref[0:voxels, :] = matmul_rt(pgrad, weight_ref[middle])
    acc_ref[voxels:, :] = jnp.zeros((table_rows - voxels, LANES), F32)

    def step(j, carry):
        for k in (j, j + middle + 1):
            part = matmul_rt(pgrad, weight_ref[k]).astype(BF16)
            acc_ref[...] += matmul(one_hot_columns(map_ref[pl.ds(k, 1), :], table_rows), part)
        return carry

    lax.fori_loop(0, middle, step, 0)
    back_ref[...] = acc_ref[0:voxels, :]
    for s in range(slots):
        slot = slots - 1 - s
        first = voxels + slot * cap
        sends[s][...] = acc_ref[first : first + cap, :].astype(BF16)


def down_kernel(slots, *refs):
    received = refs[:slots]
    hidden_ref, map_ref, down_ref, out_grad_ref, coarse_ref, dgrad_ref = refs[slots:]
    table = jnp.concatenate([hidden_ref[...]] + [r[...] for r in received], axis=0)
    upstream = out_grad_ref[...]
    parents = upstream.shape[0]
    channels = down_ref.shape[1]
    upstream_t = jnp.transpose(upstream.astype(F32)).astype(BF16)
    total = jnp.zeros((parents, down_ref.shape[2]), F32)
    child_map = map_ref[...]
    for o in range(map_ref.shape[0]):
        chooser = one_hot_rows(column(child_map[o : o + 1, :]), table.shape[0])
        picked = matmul(chooser, table).astype(BF16)
        total = total + matmul(picked, down_ref[o])
        terms = matmul(upstream_t, picked)
        dgrad_ref[o * channels : (o + 1) * channels, :] = jnp.transpose(terms).astype(BF16)
    coarse_ref[...] = total.astype(BF16)


def tail_kernel(slots, *refs):
    received = refs[:slots]
    hgrad_ref, back_ref, halo_ref, out_ref = refs[slots:]
    voxels = hgrad_ref.shape[0]
    total = hgrad_ref[...] + back_ref[...]
    lists = halo_ref[...]
    for s in range(slots):
        chooser = one_hot_columns(lists[s : s + 1, :], voxels)
        total = total + matmul(chooser, received[slots - 1 - s][...])
    out_ref[...] = total


def vmem():
    return pl.BlockSpec(memory_space=pltpu.VMEM)


def call(kernel, operands, outs, scratch=(), limit=32, flops=0):
    return pl.pallas_call(
        kernel,
        out_shape=[jax.ShapeDtypeStruct(s, d) for s, d in outs],
        in_specs=[vmem() for _ in operands],
        out_specs=[vmem() for _ in outs],
        scratch_shapes=list(scratch),
        compiler_params=pltpu.CompilerParams(vmem_limit_bytes=limit * 2**20),
        cost_estimate=pl.CostEstimate(flops=flops, bytes_accessed=4 * 2**20, transcendentals=0),
    )(*operands)


def reduce_all(terms, scale, devices):
    rows, width = terms.shape
    parts = lax.all_to_all(terms, "shard", 0, 0, tiled=True)
    mine = jnp.sum(parts.reshape(devices, rows // devices, width).astype(F32), axis=0) * scale
    return lax.all_gather(mine.astype(BF16), "shard", axis=0, tiled=True)


def local(
    features, conv_weight, down_weight, neighbour_map, halo_rows, child_map, child_rows, out_grad
):
    voxels, channels = features.shape
    parents, coarse_channels = out_grad.shape
    kernel_count = conv_weight.shape[0]
    octants = down_weight.shape[0]
    slots, cap = halo_rows.shape
    cap2 = child_rows.shape[1]
    offsets = offsets_list(slots)
    devices = lax.axis_size("shard")
    scale = 1.0 / math.sqrt(voxels * devices)
    giga = 10**9

    first = call(
        head_kernel,
        (features, halo_rows, child_map, out_grad, down_weight),
        [((cap + cap2, channels), BF16)] * slots + [((voxels + slots * cap2, channels), F32)],
        flops=giga,
    )
    back_h = first[-1][:voxels]
    received = [shift(first[s], "shard", offsets[s]) for s in range(slots)]
    grain = 16 * devices
    grad_rows = -(-kernel_count * channels // grain) * grain
    hidden, leaving, hidden_grad, pre_grad, conv_terms = call(
        functools.partial(forward_kernel, slots),
        (*received, features, neighbour_map, conv_weight, back_h, child_rows),
        [
            ((voxels, channels), BF16),
            ((slots * cap2, channels), BF16),
            ((voxels, channels), F32),
            ((voxels, channels), BF16),
            ((grad_rows, channels), BF16),
        ],
        scratch=[
            pltpu.VMEM((voxels // 2 + slots * cap // 2, 2 * channels), BF16),
            pltpu.VMEM((kernel_count, voxels, channels), BF16),
            pltpu.VMEM((voxels, channels), F32),
        ],
        limit=48,
        flops=12 * giga,
    )
    received_h = [
        shift(leaving[s * cap2 : (s + 1) * cap2], "shard", offsets[s]) for s in range(slots)
    ]
    coarse, down_terms = call(
        functools.partial(down_kernel, slots),
        (*received_h, hidden, child_map, down_weight, out_grad),
        [
            ((parents, coarse_channels), BF16),
            ((octants * channels, coarse_channels), BF16),
        ],
        flops=2 * giga,
    )
    spread = call(
        functools.partial(spread_kernel, slots),
        (pre_grad, neighbour_map, conv_weight),
        [((voxels, channels), F32)] + [((cap, channels), BF16)] * slots,
        scratch=[pltpu.VMEM((voxels + slots * cap, channels), F32)],
        flops=20 * giga,
    )
    returned = [shift(spread[1 + s], "shard", offsets[s]) for s in range(slots)]
    (input_grad,) = call(
        functools.partial(tail_kernel, slots),
        (*returned, hidden_grad, spread[0], halo_rows),
        [((voxels, channels), F32)],
        flops=giga,
    )
    conv_sum = reduce_all(conv_terms, scale, devices)
    down_sum = reduce_all(down_terms, scale, devices)
    conv_grad = conv_sum[: kernel_count * channels].astype(F32).reshape(conv_weight.shape)
    down_grad = down_sum.astype(F32).reshape(down_weight.shape)
    return (coarse, input_grad, conv_grad, down_grad)


def solution(mesh):
    return jax.shard_map(
        local,
        mesh=mesh,
        in_specs=(
            P("shard", None),
            P(),
            P(),
            P(None, "shard"),
            P(None, "shard"),
            P(None, "shard"),
            P(None, "shard"),
            P("shard", None),
        ),
        out_specs=(P("shard", None), P("shard", None), P(), P()),
        check_vma=False,
    )
```

```python
import functools
import math

import jax
import jax.numpy as jnp
from jax import lax
from jax.experimental import pallas as pl
from jax.experimental.pallas import tpu as pltpu
from jax.sharding import PartitionSpec as P

BF16 = jnp.bfloat16
F32 = jnp.float32
LANES = 128


def offsets_list(slot_count):
    half_count = slot_count // 2
    return [number - half_count for number in range(half_count)] + [
        number + 1 for number in range(half_count)
    ]


def shift(value, axis, by):
    count = lax.axis_size(axis)
    pairs = [(i, i + by) for i in range(count) if 0 <= i + by < count]
    return lax.ppermute(value, axis, pairs)


def matmul(left, right):
    return jnp.dot(left, right, preferred_element_type=F32)


def matmul_rt(left, right):
    return lax.dot_general(left, right, (((1,), (1,)), ((), ())), preferred_element_type=F32)


def pick_one(mask):
    return jnp.where(mask, jnp.ones(mask.shape, BF16), jnp.zeros(mask.shape, BF16))


def encode(row):
    return jnp.left_shift((row & (LANES - 1)) + LANES, row >> 7).astype(F32)


def column(codes):
    pieces = []
    for start in range(0, codes.shape[1], LANES):
        piece = jnp.broadcast_to(codes[:, start : start + LANES], (LANES, LANES))
        pieces.append(jnp.transpose(piece))
    return pieces[0] if len(pieces) == 1 else jnp.concatenate(pieces, axis=0)


def one_hot_rows(col, width):
    lane = lax.broadcasted_iota(jnp.int32, (16, LANES), 1)
    blocks = []
    for start in range(0, width, LANES):
        pattern = jnp.broadcast_to(encode(lane + start).astype(BF16)[0:1], col.shape)
        blocks.append(pick_one(col == pattern))
    return jnp.concatenate(blocks, axis=1)


def one_hot_columns(codes, height):
    place = lax.broadcasted_iota(jnp.int32, (height, codes.shape[1]), 0)
    pattern = encode(place).astype(BF16)
    return pick_one(jnp.broadcast_to(codes, pattern.shape) == pattern)


def list_row(lists, first, per_row):
    pieces = [lists[first + n : first + n + 1, :] for n in range(per_row)]
    return pieces[0] if per_row == 1 else jnp.concatenate(pieces, axis=1)


def gather_lists(lists_ref, table):
    slots, cap = lists_ref.shape
    lists = lists_ref[...]
    per_row = max(1, min(slots, LANES // cap))
    parts = []
    for first in range(0, slots, per_row):
        codes = encode(list_row(lists, first, per_row))
        chooser = one_hot_rows(column(codes).astype(BF16), table.shape[0])
        parts.append(matmul(chooser, table))
    return parts[0] if len(parts) == 1 else jnp.concatenate(parts, axis=0)


def head_kernel(features_ref, halo_ref, child_map_ref, out_grad_ref, down_ref, *outs):
    sends, back_ref = outs[:-1], outs[-1]
    slots, cap = halo_ref.shape
    voxels = features_ref.shape[0]
    octants = child_map_ref.shape[0]
    table_rows = back_ref.shape[0]
    cap2 = (table_rows - voxels) // slots
    listed = gather_lists(halo_ref, features_ref[...]).astype(BF16)
    for s in range(slots):
        sends[s][0:cap, :] = listed[s * cap : (s + 1) * cap, :]
    upstream = out_grad_ref[...]
    total = jnp.zeros((table_rows, LANES), F32)
    codes = encode(child_map_ref[...]).astype(BF16)
    for o in range(octants):
        part = matmul_rt(upstream, down_ref[o]).astype(BF16)
        total = total + matmul(one_hot_columns(codes[o : o + 1, :], table_rows), part)
    back_ref[...] = total
    for s in range(slots):
        slot = slots - 1 - s
        first = voxels + slot * cap2
        sends[s][cap : cap + cap2, :] = total[first : first + cap2, :].astype(BF16)


def half_codes(row, voxels, received):
    half, half_received = voxels // 2, received // 2
    beyond = row - voxels
    outside = beyond >= 0
    near = row - jnp.where(row >= half, half, 0)
    far = half + beyond - jnp.where(beyond >= half_received, half_received, 0)
    code = encode(jnp.where(outside, far, near))
    near_sign = jnp.where(row >= half, -1.0, 1.0)
    far_sign = jnp.where(beyond >= half_received, -1.0, 1.0)
    return code * jnp.where(outside, far_sign, near_sign)


def forward_kernel(slots, *refs):
    received = refs[:slots]
    (features_ref, map_ref, weight_ref, back_ref, child_ref) = refs[slots : slots + 5]
    (hidden_ref, leaving_ref, hgrad_ref, pgrad_ref, cgrad_ref) = refs[slots + 5 : slots + 10]
    (table_ref, stacked_ref, acc_ref) = refs[slots + 10 :]
    voxels = features_ref.shape[0]
    kernel_count = map_ref.shape[0]
    middle = kernel_count // 2
    cap2 = child_ref.shape[1]
    cap = received[0].shape[0] - cap2
    half, half_halo = voxels // 2, slots * cap // 2
    features = features_ref[...]
    table_ref[0:half, 0:LANES] = features[0:half]
    table_ref[0:half, LANES : 2 * LANES] = features[half:voxels]
    for s in range(slots):
        place = half + (s % (slots // 2)) * cap
        side = (s // (slots // 2)) * LANES
        table_ref[place : place + cap, side : side + LANES] = received[s][0:cap, :]
    table_rows = half + half_halo

    def gather(k):
        col = column(half_codes(map_ref[pl.ds(k, 1), :], voxels, slots * cap))
        chooser = one_hot_rows(jnp.abs(col).astype(BF16), table_rows)
        both = matmul(chooser, table_ref[...])
        picked = jnp.where(col < 0.0, both[:, LANES:], both[:, :LANES]).astype(BF16)
        stacked_ref[k] = picked
        return picked

    acc_ref[...] = matmul(features, weight_ref[middle])

    def step(j, carry):
        near, far = gather(j), gather(j + middle + 1)
        pair = jnp.concatenate([near, far], axis=1)
        kernel = jnp.concatenate([weight_ref[j], weight_ref[j + middle + 1]], axis=0)
        acc_ref[...] += matmul(pair, kernel)
        return carry

    lax.fori_loop(0, middle, step, 0)
    pre = acc_ref[...]
    sig = jax.nn.sigmoid(pre)
    hidden = (features.astype(F32) + pre * sig).astype(BF16)
    hidden_ref[...] = hidden
    leaving_ref[...] = gather_lists(child_ref, hidden).astype(BF16)
    hgrad = back_ref[...]
    lists = encode(child_ref[...]).astype(BF16)
    for s in range(slots):
        returned = received[slots - 1 - s][cap : cap + cap2, :]
        hgrad = hgrad + matmul(one_hot_columns(lists[s : s + 1, :], voxels), returned)
    hgrad_ref[...] = hgrad
    pgrad = hgrad * (sig * (1.0 + pre * (1.0 - sig)))
    pgrad_ref[...] = pgrad.astype(BF16)
    pgrad_t = jnp.transpose(pgrad).astype(BF16)
    rows = kernel_count * LANES
    cgrad_ref[rows:, :] = jnp.zeros((cgrad_ref.shape[0] - rows, LANES), BF16)

    def put(k, value):
        cgrad_ref[pl.ds(pl.multiple_of(k * LANES, LANES), LANES), :] = jnp.transpose(value).astype(BF16)

    put(middle, matmul(pgrad_t, features))

    def weight_step(j, carry):
        pair = jnp.concatenate([stacked_ref[j], stacked_ref[j + middle + 1]], axis=1)
        both = matmul(pgrad_t, pair)
        put(j, both[:, :LANES])
        put(j + middle + 1, both[:, LANES:])
        return carry

    lax.fori_loop(0, middle, weight_step, 0)


def spread_kernel(slots, pgrad_ref, map_ref, weight_ref, back_ref, *sends):
    acc_ref = sends[-1]
    sends = sends[:-1]
    voxels = pgrad_ref.shape[0]
    kernel_count = map_ref.shape[0]
    middle = kernel_count // 2
    cap = sends[0].shape[0]
    half = voxels // 2
    table_rows = half + slots * cap // 2
    pgrad = pgrad_ref[...]
    own = matmul_rt(pgrad, weight_ref[middle])
    acc_ref[0:half, 0:LANES] = own[0:half]
    acc_ref[0:half, LANES:] = own[half:]
    acc_ref[half:, :] = jnp.zeros((table_rows - half, 2 * LANES), F32)

    def parts(k):
        codes = half_codes(map_ref[pl.ds(k, 1), :], voxels, slots * cap)
        terms = matmul_rt(pgrad, weight_ref[k])
        right = column(codes) < 0.0
        sides = [jnp.where(right, 0.0, terms), jnp.where(right, terms, 0.0)]
        chooser = one_hot_columns(jnp.abs(codes).astype(BF16), table_rows)
        return chooser, jnp.concatenate(sides, axis=1).astype(BF16)

    def step(j, carry):
        near_chooser, near_terms = parts(j)
        far_chooser, far_terms = parts(j + middle + 1)
        acc_ref[...] += matmul(near_chooser, near_terms) + matmul(far_chooser, far_terms)
        return carry

    lax.fori_loop(0, middle, step, 0)
    back_ref[0:half, :] = acc_ref[0:half, 0:LANES]
    back_ref[half:, :] = acc_ref[0:half, LANES:]
    for s in range(slots):
        slot = slots - 1 - s
        first = half + (slot % (slots // 2)) * cap
        side = (slot // (slots // 2)) * LANES
        sends[s][...] = acc_ref[first : first + cap, side : side + LANES].astype(BF16)


def down_kernel(slots, *refs):
    received = refs[:slots]
    hidden_ref, map_ref, down_ref, out_grad_ref, coarse_ref, dgrad_ref = refs[slots:]
    table = jnp.concatenate([hidden_ref[...]] + [r[...] for r in received], axis=0)
    upstream = out_grad_ref[...]
    parents = upstream.shape[0]
    channels = down_ref.shape[1]
    upstream_t = jnp.transpose(upstream.astype(F32)).astype(BF16)
    total = jnp.zeros((parents, down_ref.shape[2]), F32)
    codes = encode(map_ref[...])
    for o in range(map_ref.shape[0]):
        chooser = one_hot_rows(column(codes[o : o + 1, :]).astype(BF16), table.shape[0])
        picked = matmul(chooser, table).astype(BF16)
        total = total + matmul(picked, down_ref[o])
        terms = matmul(upstream_t, picked)
        dgrad_ref[o * channels : (o + 1) * channels, :] = jnp.transpose(terms).astype(BF16)
    coarse_ref[...] = total.astype(BF16)


def tail_kernel(slots, *refs):
    received = refs[:slots]
    hgrad_ref, back_ref, halo_ref, out_ref = refs[slots:]
    voxels = hgrad_ref.shape[0]
    total = hgrad_ref[...] + back_ref[...]
    lists = encode(halo_ref[...]).astype(BF16)
    for s in range(slots):
        chooser = one_hot_columns(lists[s : s + 1, :], voxels)
        total = total + matmul(chooser, received[slots - 1 - s][...])
    out_ref[...] = total


def vmem():
    return pl.BlockSpec(memory_space=pltpu.VMEM)


def call(kernel, operands, outs, scratch=(), limit=32, flops=0):
    return pl.pallas_call(
        kernel,
        out_shape=[jax.ShapeDtypeStruct(s, d) for s, d in outs],
        in_specs=[vmem() for _ in operands],
        out_specs=[vmem() for _ in outs],
        scratch_shapes=list(scratch),
        compiler_params=pltpu.CompilerParams(vmem_limit_bytes=limit * 2**20),
        cost_estimate=pl.CostEstimate(flops=flops, bytes_accessed=4 * 2**20, transcendentals=0),
    )(*operands)


def sum_kernel(devices, scale, parts_ref, out_ref):
    rows = parts_ref.shape[0] // devices
    total = parts_ref[0:rows, :].astype(F32)
    for d in range(1, devices):
        total = total + parts_ref[d * rows : (d + 1) * rows, :].astype(F32)
    total = (total * scale).astype(BF16)
    for d in range(devices):
        out_ref[d * rows : (d + 1) * rows, :] = total


def reduce_all(terms, scale, devices):
    parts = lax.all_to_all(terms, "shard", 0, 0, tiled=True)
    (mine,) = call(
        functools.partial(sum_kernel, devices, scale), (parts,), [(terms.shape, BF16)], flops=10**6
    )
    return lax.all_to_all(mine, "shard", 0, 0, tiled=True)


def local(
    features, conv_weight, down_weight, neighbour_map, halo_rows, child_map, child_rows, out_grad
):
    voxels, channels = features.shape
    parents, coarse_channels = out_grad.shape
    kernel_count = conv_weight.shape[0]
    octants = down_weight.shape[0]
    slots, cap = halo_rows.shape
    cap2 = child_rows.shape[1]
    offsets = offsets_list(slots)
    devices = lax.axis_size("shard")
    scale = 1.0 / math.sqrt(voxels * devices)
    giga = 10**9

    first = call(
        head_kernel,
        (features, halo_rows, child_map, out_grad, down_weight),
        [((cap + cap2, channels), BF16)] * slots + [((voxels + slots * cap2, channels), F32)],
        flops=giga,
    )
    back_h = first[-1][:voxels]
    received = [shift(first[s], "shard", offsets[s]) for s in range(slots)]
    grain = 16 * devices
    grad_rows = -(-kernel_count * channels // grain) * grain
    hidden, leaving, hidden_grad, pre_grad, conv_terms = call(
        functools.partial(forward_kernel, slots),
        (*received, features, neighbour_map, conv_weight, back_h, child_rows),
        [
            ((voxels, channels), BF16),
            ((slots * cap2, channels), BF16),
            ((voxels, channels), F32),
            ((voxels, channels), BF16),
            ((grad_rows, channels), BF16),
        ],
        scratch=[
            pltpu.VMEM((voxels // 2 + slots * cap // 2, 2 * channels), BF16),
            pltpu.VMEM((kernel_count, voxels, channels), BF16),
            pltpu.VMEM((voxels, channels), F32),
        ],
        limit=48,
        flops=12 * giga,
    )
    received_h = [
        shift(leaving[s * cap2 : (s + 1) * cap2], "shard", offsets[s]) for s in range(slots)
    ]
    coarse, down_terms = call(
        functools.partial(down_kernel, slots),
        (*received_h, hidden, child_map, down_weight, out_grad),
        [
            ((parents, coarse_channels), BF16),
            ((octants * channels, coarse_channels), BF16),
        ],
        flops=2 * giga,
    )
    spread = call(
        functools.partial(spread_kernel, slots),
        (pre_grad, neighbour_map, conv_weight),
        [((voxels, channels), F32)] + [((cap, channels), BF16)] * slots,
        scratch=[pltpu.VMEM((voxels // 2 + slots * cap // 2, 2 * channels), F32)],
        flops=20 * giga,
    )
    returned = [shift(spread[1 + s], "shard", offsets[s]) for s in range(slots)]
    (input_grad,) = call(
        functools.partial(tail_kernel, slots),
        (*returned, hidden_grad, spread[0], halo_rows),
        [((voxels, channels), F32)],
        flops=giga,
    )
    conv_sum = reduce_all(conv_terms, scale, devices)
    down_sum = reduce_all(down_terms, scale, devices)
    conv_grad = conv_sum[: kernel_count * channels].astype(F32).reshape(conv_weight.shape)
    down_grad = down_sum.astype(F32).reshape(down_weight.shape)
    return (coarse, input_grad, conv_grad, down_grad)


def solution(mesh):
    return jax.shard_map(
        local,
        mesh=mesh,
        in_specs=(
            P("shard", None),
            P(),
            P(),
            P(None, "shard"),
            P(None, "shard"),
            P(None, "shard"),
            P(None, "shard"),
            P("shard", None),
        ),
        out_specs=(P("shard", None), P("shard", None), P(), P()),
        check_vma=False,
    )
```

```python
import functools
import math

import jax
import jax.numpy as jnp
from jax import lax
from jax.experimental import pallas as pl
from jax.experimental.pallas import tpu as pltpu
from jax.sharding import PartitionSpec as P

BF16 = jnp.bfloat16
F32 = jnp.float32
LANES = 128


def offsets_list(slot_count):
    half_count = slot_count // 2
    return [number - half_count for number in range(half_count)] + [
        number + 1 for number in range(half_count)
    ]


def shift(value, axis, by):
    count = lax.axis_size(axis)
    pairs = [(i, i + by) for i in range(count) if 0 <= i + by < count]
    return lax.ppermute(value, axis, pairs)


def matmul(left, right):
    return jnp.dot(left, right, preferred_element_type=F32)


def matmul_rt(left, right):
    return lax.dot_general(left, right, (((1,), (1,)), ((), ())), preferred_element_type=F32)


def pick_one(mask):
    return jnp.where(mask, jnp.ones(mask.shape, BF16), jnp.zeros(mask.shape, BF16))


def encode(row):
    return jnp.left_shift((row & (LANES - 1)) + LANES, row >> 7).astype(F32)


def column(codes):
    pieces = []
    for start in range(0, codes.shape[1], LANES):
        piece = jnp.broadcast_to(codes[:, start : start + LANES], (LANES, LANES))
        pieces.append(jnp.transpose(piece))
    return pieces[0] if len(pieces) == 1 else jnp.concatenate(pieces, axis=0)


def one_hot_rows(col, width):
    lane = lax.broadcasted_iota(jnp.int32, (16, LANES), 1)
    blocks = []
    for start in range(0, width, LANES):
        pattern = jnp.broadcast_to(encode(lane + start).astype(BF16)[0:1], col.shape)
        blocks.append(pick_one(col == pattern))
    return jnp.concatenate(blocks, axis=1)


def one_hot_columns(codes, height):
    place = lax.broadcasted_iota(jnp.int32, (height, codes.shape[1]), 0)
    pattern = encode(place).astype(BF16)
    return pick_one(jnp.broadcast_to(codes, pattern.shape) == pattern)


def list_row(lists, first, per_row):
    pieces = [lists[first + n : first + n + 1, :] for n in range(per_row)]
    return pieces[0] if per_row == 1 else jnp.concatenate(pieces, axis=1)


def gather_lists(lists_ref, table):
    slots, cap = lists_ref.shape
    lists = lists_ref[...]
    per_row = max(1, min(slots, LANES // cap))
    parts = []
    for first in range(0, slots, per_row):
        codes = encode(list_row(lists, first, per_row))
        chooser = one_hot_rows(column(codes).astype(BF16), table.shape[0])
        parts.append(matmul(chooser, table))
    return parts[0] if len(parts) == 1 else jnp.concatenate(parts, axis=0)


def head_kernel(features_hbm, halo_hbm, child_map_hbm, out_grad_hbm, down_hbm, *refs):
    sources = (features_hbm, halo_hbm, child_map_hbm, out_grad_hbm, down_hbm)
    buffers, sems = refs[-len(sources) - 1 : -1], refs[-1]
    features_ref, halo_ref, child_map_ref, out_grad_ref, down_ref = buffers
    copies = [
        pltpu.make_async_copy(source, buffer, sems.at[n])
        for n, (source, buffer) in enumerate(zip(sources, buffers))
    ]
    for copy in copies:
        copy.start()
    outs = refs[: -len(sources) - 1]
    sends, back_ref = outs[:-1], outs[-1]
    slots, cap = halo_ref.shape
    voxels = features_ref.shape[0]
    octants = child_map_ref.shape[0]
    table_rows = voxels + slots * (sends[0].shape[0] - cap)
    cap2 = (table_rows - voxels) // slots
    copies[0].wait()
    copies[1].wait()
    listed = gather_lists(halo_ref, features_ref[...]).astype(BF16)
    for s in range(slots):
        sends[s][0:cap, :] = listed[s * cap : (s + 1) * cap, :]
    for copy in copies[2:]:
        copy.wait()
    upstream = out_grad_ref[...]
    both = jnp.zeros((table_rows, 2 * LANES), F32)
    codes = encode(child_map_ref[...]).astype(BF16)
    for o in range(octants):
        part = matmul_rt(upstream, down_ref[o])
        high = part.astype(BF16)
        low = (part - high.astype(F32)).astype(BF16)
        chooser = one_hot_columns(codes[o : o + 1, :], table_rows)
        both = both + matmul(chooser, jnp.concatenate([high, low], axis=1))
    total = both[:, :LANES] + both[:, LANES:]
    back_ref[...] = total[:voxels]
    for s in range(slots):
        slot = slots - 1 - s
        first = voxels + slot * cap2
        sends[s][cap : cap + cap2, :] = total[first : first + cap2, :].astype(BF16)


def half_codes(row, voxels, received):
    half, half_received = voxels // 2, received // 2
    beyond = row - voxels
    outside = beyond >= 0
    near = row - jnp.where(row >= half, half, 0)
    far = half + beyond - jnp.where(beyond >= half_received, half_received, 0)
    code = encode(jnp.where(outside, far, near))
    near_sign = jnp.where(row >= half, -1.0, 1.0)
    far_sign = jnp.where(beyond >= half_received, -1.0, 1.0)
    return code * jnp.where(outside, far_sign, near_sign)


def forward_kernel(slots, *refs):
    received = refs[:slots]
    (features_ref, map_ref, weight_ref, back_ref, child_ref) = refs[slots : slots + 5]
    (hidden_ref, leaving_ref, hgrad_ref, pgrad_ref, cgrad_ref) = refs[slots + 5 : slots + 10]
    (table_ref, stacked_ref, acc_ref) = refs[slots + 10 :]
    voxels = features_ref.shape[0]
    kernel_count = map_ref.shape[0]
    middle = kernel_count // 2
    cap2 = child_ref.shape[1]
    cap = received[0].shape[0] - cap2
    half, half_halo = voxels // 2, slots * cap // 2
    features = features_ref[...]
    table_ref[0:half, 0:LANES] = features[0:half]
    table_ref[0:half, LANES : 2 * LANES] = features[half:voxels]
    for s in range(slots):
        place = half + (s % (slots // 2)) * cap
        side = (s // (slots // 2)) * LANES
        table_ref[place : place + cap, side : side + LANES] = received[s][0:cap, :]
    table_rows = half + half_halo

    def gather(k):
        col = column(half_codes(map_ref[pl.ds(k, 1), :], voxels, slots * cap))
        chooser = one_hot_rows(jnp.abs(col).astype(BF16), table_rows)
        both = matmul(chooser, table_ref[...])
        picked = jnp.where(col < 0.0, both[:, LANES:], both[:, :LANES]).astype(BF16)
        stacked_ref[k] = picked
        return picked

    acc_ref[...] = matmul(features, weight_ref[middle])

    def step(j, carry):
        near, far = gather(j), gather(j + middle + 1)
        pair = jnp.concatenate([near, far], axis=1)
        kernel = jnp.concatenate([weight_ref[j], weight_ref[j + middle + 1]], axis=0)
        acc_ref[...] += matmul(pair, kernel)
        return carry

    lax.fori_loop(0, middle, step, 0)
    pre = acc_ref[...]
    sig = jax.nn.sigmoid(pre)
    hidden = (features.astype(F32) + pre * sig).astype(BF16)
    hidden_ref[...] = hidden
    leaving_ref[...] = gather_lists(child_ref, hidden).astype(BF16)
    hgrad = back_ref[...]
    lists = encode(child_ref[...]).astype(BF16)
    for s in range(slots):
        returned = received[slots - 1 - s][cap : cap + cap2, :]
        hgrad = hgrad + matmul(one_hot_columns(lists[s : s + 1, :], voxels), returned)
    hgrad_ref[...] = hgrad
    pgrad = hgrad * (sig * (1.0 + pre * (1.0 - sig)))
    pgrad_ref[...] = pgrad.astype(BF16)
    pgrad_t = jnp.transpose(pgrad).astype(BF16)

    def put(k, value):
        cgrad_ref[pl.ds(pl.multiple_of(k * LANES, LANES), LANES), :] = jnp.transpose(value).astype(BF16)

    put(middle, matmul(pgrad_t, features))

    def weight_step(j, carry):
        pair = jnp.concatenate([stacked_ref[j], stacked_ref[j + middle + 1]], axis=1)
        both = matmul(pgrad_t, pair)
        put(j, both[:, :LANES])
        put(j + middle + 1, both[:, LANES:])
        return carry

    lax.fori_loop(0, middle, weight_step, 0)


def spread_kernel(slots, pgrad_ref, map_ref, weight_ref, back_ref, *sends):
    acc_ref = sends[-1]
    sends = sends[:-1]
    voxels = pgrad_ref.shape[0]
    kernel_count = map_ref.shape[0]
    middle = kernel_count // 2
    cap = sends[0].shape[0]
    half = voxels // 2
    table_rows = half + slots * cap // 2
    pgrad = pgrad_ref[...]
    own = matmul_rt(pgrad, weight_ref[middle])
    acc_ref[0:half, 0:LANES] = own[0:half]
    acc_ref[0:half, LANES:] = own[half:]
    acc_ref[half:, :] = jnp.zeros((table_rows - half, 2 * LANES), F32)

    def parts(k):
        codes = half_codes(map_ref[pl.ds(k, 1), :], voxels, slots * cap)
        terms = matmul_rt(pgrad, weight_ref[k])
        right = column(codes) < 0.0
        sides = [jnp.where(right, 0.0, terms), jnp.where(right, terms, 0.0)]
        chooser = one_hot_columns(jnp.abs(codes).astype(BF16), table_rows)
        return chooser, jnp.concatenate(sides, axis=1).astype(BF16)

    def step(j, carry):
        near_chooser, near_terms = parts(j)
        far_chooser, far_terms = parts(j + middle + 1)
        acc_ref[...] += matmul(near_chooser, near_terms) + matmul(far_chooser, far_terms)
        return carry

    lax.fori_loop(0, middle, step, 0)
    back_ref[0:half, :] = acc_ref[0:half, 0:LANES]
    back_ref[half:, :] = acc_ref[0:half, LANES:]
    for s in range(slots):
        slot = slots - 1 - s
        first = half + (slot % (slots // 2)) * cap
        side = (slot // (slots // 2)) * LANES
        sends[s][...] = acc_ref[first : first + cap, side : side + LANES].astype(BF16)


def my_half(rows):
    core = lax.rem(lax.axis_index("shard"), 2)
    return pl.multiple_of(core * rows, 16), pl.multiple_of((1 - core) * rows, 16)


def down_kernel(slots, *refs):
    received = refs[:slots]
    (hidden_ref, map_ref, down_ref, out_grad_ref, cgrad_ref) = refs[slots : slots + 5]
    coarse_ref, terms_ref, send_ref = refs[slots + 5 :]
    table = jnp.concatenate([hidden_ref[...]] + [r[...] for r in received], axis=0)
    upstream = out_grad_ref[...]
    parents = upstream.shape[0]
    upstream_t = jnp.transpose(upstream.astype(F32)).astype(BF16)
    total = jnp.zeros((parents, down_ref.shape[2]), F32)
    codes = encode(map_ref[...])
    row = cgrad_ref.shape[0]
    terms_ref[0:row, :] = cgrad_ref[...]
    for o in range(map_ref.shape[0]):
        chooser = one_hot_rows(column(codes[o : o + 1, :]).astype(BF16), table.shape[0])
        picked = matmul(chooser, table).astype(BF16)
        total = total + matmul(picked, down_ref[o])
        terms = matmul(upstream_t, picked)
        for start in range(0, terms.shape[0], LANES):
            block = jnp.transpose(terms[start : start + LANES, :]).astype(BF16)
            terms_ref[row : row + LANES, :] = block
            row += LANES
    terms_ref[row:, :] = jnp.zeros((terms_ref.shape[0] - row, LANES), BF16)
    coarse_ref[...] = total.astype(BF16)
    send_ref[...] = terms_ref[pl.ds(my_half(send_ref.shape[0])[1], send_ref.shape[0]), :]


def pair_kernel(terms_ref, other_ref, out_ref):
    rows = other_ref.shape[0]
    mine = terms_ref[pl.ds(my_half(rows)[0], rows), :].astype(F32)
    out_ref[...] = (mine + other_ref[...].astype(F32)).astype(BF16)


def sum_kernel(groups, scale, parts_ref, after_ref, out_ref):
    rows = parts_ref.shape[0] // groups
    total = parts_ref[0:rows, :].astype(F32)
    for d in range(1, groups):
        total = total + parts_ref[d * rows : (d + 1) * rows, :].astype(F32)
    total = (total * scale).astype(BF16)
    for d in range(groups):
        out_ref[d * rows : (d + 1) * rows, :] = total


def final_kernel(mine_ref, other_ref, conv_ref, down_ref, whole_ref):
    rows = mine_ref.shape[0]
    mine, other = my_half(rows)
    whole_ref[pl.ds(mine, rows), :] = mine_ref[...]
    whole_ref[pl.ds(other, rows), :] = other_ref[...]
    row = conv_ref.shape[0]
    conv_ref[...] = whole_ref[0:row, :].astype(F32)
    for first in range(0, down_ref.shape[0], LANES):
        for start in range(0, down_ref.shape[1], LANES):
            block = whole_ref[row : row + LANES, :].astype(F32)
            down_ref[first : first + LANES, start : start + LANES] = block
            row += LANES


def tail_kernel(slots, *refs):
    received = refs[:slots]
    hgrad_ref, back_ref, halo_ref, out_ref = refs[slots:]
    voxels = hgrad_ref.shape[0]
    total = hgrad_ref[...] + back_ref[...]
    lists = encode(halo_ref[...]).astype(BF16)
    for s in range(slots):
        chooser = one_hot_columns(lists[s : s + 1, :], voxels)
        total = total + matmul(chooser, received[slots - 1 - s][...])
    out_ref[...] = total


def call(kernel, operands, outs, scratch=(), limit=32, flops=0, in_hbm=()):
    spaces = [pl.ANY if n in in_hbm else pltpu.VMEM for n in range(len(operands))]
    return pl.pallas_call(
        kernel,
        out_shape=[jax.ShapeDtypeStruct(s, d) for s, d in outs],
        in_specs=[pl.BlockSpec(memory_space=space) for space in spaces],
        out_specs=[pl.BlockSpec(memory_space=pltpu.VMEM) for _ in outs],
        scratch_shapes=list(scratch),
        compiler_params=pltpu.CompilerParams(vmem_limit_bytes=limit * 2**20),
        cost_estimate=pl.CostEstimate(flops=flops, bytes_accessed=4 * 2**20, transcendentals=0),
    )(*operands)


def swap_cores(value, devices):
    return lax.ppermute(value, "shard", [(i, i + 1 - 2 * (i % 2)) for i in range(devices)])


def exchange(value, devices):
    groups = [list(range(core, devices, 2)) for core in range(2)]
    return lax.all_to_all(value, "shard", 0, 0, axis_index_groups=groups, tiled=True)


def local(
    features, conv_weight, down_weight, neighbour_map, halo_rows, child_map, child_rows, out_grad
):
    voxels, channels = features.shape
    parents, coarse_channels = out_grad.shape
    kernel_count = conv_weight.shape[0]
    octants = down_weight.shape[0]
    slots, cap = halo_rows.shape
    cap2 = child_rows.shape[1]
    offsets = offsets_list(slots)
    devices = lax.axis_size("shard")
    scale = 1.0 / math.sqrt(voxels * devices)
    giga = 10**9

    first = call(
        head_kernel,
        (features, halo_rows, child_map, out_grad, down_weight),
        [((cap + cap2, channels), BF16)] * slots + [((voxels, channels), F32)],
        scratch=[
            pltpu.VMEM(value.shape, value.dtype)
            for value in (features, halo_rows, child_map, out_grad, down_weight)
        ]
        + [pltpu.SemaphoreType.DMA((5,))],
        limit=60,
        flops=giga,
        in_hbm=range(5),
    )
    back_h = first[-1]
    received = [shift(first[s], "shard", offsets[s]) for s in range(slots)]
    conv_rows = kernel_count * channels
    down_rows = octants * channels * coarse_channels // LANES
    grain = 16 * devices
    half_rows = -(-(conv_rows + down_rows) // grain) * grain // 2
    hidden, leaving, hidden_grad, pre_grad, conv_terms = call(
        functools.partial(forward_kernel, slots),
        (*received, features, neighbour_map, conv_weight, back_h, child_rows),
        [
            ((voxels, channels), BF16),
            ((slots * cap2, channels), BF16),
            ((voxels, channels), F32),
            ((voxels, channels), BF16),
            ((conv_rows, channels), BF16),
        ],
        scratch=[
            pltpu.VMEM((voxels // 2 + slots * cap // 2, 2 * channels), BF16),
            pltpu.VMEM((kernel_count, voxels, channels), BF16),
            pltpu.VMEM((voxels, channels), F32),
        ],
        limit=48,
        flops=12 * giga,
    )
    received_h = [
        shift(leaving[s * cap2 : (s + 1) * cap2], "shard", offsets[s]) for s in range(slots)
    ]
    coarse, terms, leaving_terms = call(
        functools.partial(down_kernel, slots),
        (*received_h, hidden, child_map, down_weight, out_grad, conv_terms),
        [
            ((parents, coarse_channels), BF16),
            ((2 * half_rows, LANES), BF16),
            ((half_rows, LANES), BF16),
        ],
        flops=2 * giga,
    )
    (pair_terms,) = call(
        pair_kernel,
        (terms, swap_cores(leaving_terms, devices)),
        [((half_rows, LANES), BF16)],
        flops=10**6,
    )
    parts = exchange(pair_terms, devices)
    spread = call(
        functools.partial(spread_kernel, slots),
        (pre_grad, neighbour_map, conv_weight),
        [((voxels, channels), F32)] + [((cap, channels), BF16)] * slots,
        scratch=[pltpu.VMEM((voxels // 2 + slots * cap // 2, 2 * channels), F32)],
        flops=20 * giga,
    )
    returned = [shift(spread[1 + s], "shard", offsets[s]) for s in range(slots)]
    (input_grad,) = call(
        functools.partial(tail_kernel, slots),
        (*returned, hidden_grad, spread[0], halo_rows),
        [((voxels, channels), F32)],
        flops=giga,
    )
    (summed,) = call(
        functools.partial(sum_kernel, devices // 2, scale),
        (parts, spread[1]),
        [((half_rows, LANES), BF16)],
        flops=10**6,
        in_hbm=(1,),
    )
    mine = exchange(summed, devices)
    conv_grad, down_grad = call(
        final_kernel,
        (mine, swap_cores(mine, devices)),
        [((conv_rows, LANES), F32), ((octants * channels, coarse_channels), F32)],
        scratch=[pltpu.VMEM((2 * half_rows, LANES), BF16)],
        flops=10**6,
    )
    conv_grad = conv_grad.reshape(conv_weight.shape)
    return (coarse, input_grad, conv_grad, down_grad.reshape(down_weight.shape))


def solution(mesh):
    return jax.shard_map(
        local,
        mesh=mesh,
        in_specs=(
            P("shard", None),
            P(),
            P(),
            P(None, "shard"),
            P(None, "shard"),
            P(None, "shard"),
            P(None, "shard"),
            P("shard", None),
        ),
        out_specs=(P("shard", None), P("shard", None), P(), P()),
        check_vma=False,
    )
```

```python
import functools
import math

import jax
import jax.numpy as jnp
from jax import lax
from jax.experimental import pallas as pl
from jax.experimental.pallas import tpu as pltpu
from jax.sharding import PartitionSpec as P

BF16 = jnp.bfloat16
F32 = jnp.float32
LANES = 128


def swaps(by_step, reach):
    devices = lax.axis_size("shard")
    moved = []
    for m in range(1, reach + 1):
        for phase in range(2):
            sign = [1 if (i // m) % 2 == phase else -1 for i in range(devices)]
            pairs = [(i, i + m * sign[i]) for i in range(devices) if 0 <= i + m * sign[i] < devices]
            moved.append(lax.ppermute(by_step[len(moved)], "shard", pairs))
    return moved


def is_even(m):
    return lax.rem(lax.div(lax.axis_index("shard"), m), 2) == 0


def to_steps(slots, back):
    reach = len(slots) // 2
    steps = []
    for m in range(1, reach + 1):
        first, second = slots[reach + m - 1], slots[reach - m]
        if back:
            first, second = second, first
        steps.append(lax.select(is_even(m), first, second))
        steps.append(lax.select(is_even(m), second, first))
    return steps


def to_slots(steps, back):
    reach = len(steps) // 2
    slots = [None] * len(steps)
    for m in range(1, reach + 1):
        first = lax.select(is_even(m), steps[2 * m - 2], steps[2 * m - 1])
        second = lax.select(is_even(m), steps[2 * m - 1], steps[2 * m - 2])
        if back:
            first, second = second, first
        slots[reach - m], slots[reach + m - 1] = first, second
    return slots


def matmul(left, right):
    return jnp.dot(left, right, preferred_element_type=F32)


def matmul_rt(left, right):
    return lax.dot_general(left, right, (((1,), (1,)), ((), ())), preferred_element_type=F32)


def pick_one(mask):
    return jnp.where(mask, jnp.ones(mask.shape, BF16), jnp.zeros(mask.shape, BF16))


def encode(row):
    return jnp.left_shift((row & (LANES - 1)) + LANES, row >> 7).astype(F32)


def column(codes):
    pieces = []
    for start in range(0, codes.shape[1], LANES):
        piece = jnp.broadcast_to(codes[:, start : start + LANES], (LANES, LANES))
        pieces.append(jnp.transpose(piece))
    return pieces[0] if len(pieces) == 1 else jnp.concatenate(pieces, axis=0)


def one_hot_rows(col, width):
    lane = lax.broadcasted_iota(jnp.int32, (16, LANES), 1)
    blocks = []
    for start in range(0, width, LANES):
        pattern = jnp.broadcast_to(encode(lane + start).astype(BF16)[0:1], col.shape)
        blocks.append(pick_one(col == pattern))
    return jnp.concatenate(blocks, axis=1)


def one_hot_columns(codes, height):
    place = lax.broadcasted_iota(jnp.int32, (height, codes.shape[1]), 0)
    pattern = encode(place).astype(BF16)
    return pick_one(jnp.broadcast_to(codes, pattern.shape) == pattern)


def list_row(lists, first, per_row):
    pieces = [lists[first + n : first + n + 1, :] for n in range(per_row)]
    return pieces[0] if per_row == 1 else jnp.concatenate(pieces, axis=1)


def gather_lists(lists_ref, table):
    slots, cap = lists_ref.shape
    lists = lists_ref[...]
    per_row = max(1, min(slots, LANES // cap))
    parts = []
    for first in range(0, slots, per_row):
        codes = encode(list_row(lists, first, per_row))
        chooser = one_hot_rows(column(codes).astype(BF16), table.shape[0])
        parts.append(matmul(chooser, table))
    return parts[0] if len(parts) == 1 else jnp.concatenate(parts, axis=0)


def head_kernel(features_hbm, halo_hbm, child_map_hbm, out_grad_hbm, down_hbm, *refs):
    sources = (features_hbm, halo_hbm, child_map_hbm, out_grad_hbm, down_hbm)
    buffers, sems = refs[-len(sources) - 1 : -1], refs[-1]
    features_ref, halo_ref, child_map_ref, out_grad_ref, down_ref = buffers
    copies = [
        pltpu.make_async_copy(source, buffer, sems.at[n])
        for n, (source, buffer) in enumerate(zip(sources, buffers))
    ]
    for copy in copies:
        copy.start()
    outs = refs[: -len(sources) - 1]
    sends, back_ref = outs[:-1], outs[-1]
    slots, cap = halo_ref.shape
    voxels = features_ref.shape[0]
    octants = child_map_ref.shape[0]
    table_rows = voxels + slots * (sends[0].shape[0] - cap)
    cap2 = (table_rows - voxels) // slots
    copies[0].wait()
    copies[1].wait()
    listed = gather_lists(halo_ref, features_ref[...]).astype(BF16)
    for send, block in zip(sends, to_steps(jnp.split(listed, slots), False)):
        send[0:cap, :] = block
    for copy in copies[2:]:
        copy.wait()
    upstream = out_grad_ref[...]
    both = jnp.zeros((table_rows, 2 * LANES), F32)
    codes = encode(child_map_ref[...]).astype(BF16)
    for o in range(octants):
        part = matmul_rt(upstream, down_ref[o])
        high = part.astype(BF16)
        low = (part - high.astype(F32)).astype(BF16)
        chooser = one_hot_columns(codes[o : o + 1, :], table_rows)
        both = both + matmul(chooser, jnp.concatenate([high, low], axis=1))
    total = both[:, :LANES] + both[:, LANES:]
    back_ref[...] = total[:voxels]
    for send, block in zip(sends, to_steps(jnp.split(total[voxels:].astype(BF16), slots), True)):
        send[cap : cap + cap2, :] = block


def half_codes(row, voxels, received):
    half, half_received = voxels // 2, received // 2
    beyond = row - voxels
    outside = beyond >= 0
    near = row - jnp.where(row >= half, half, 0)
    far = half + beyond - jnp.where(beyond >= half_received, half_received, 0)
    code = encode(jnp.where(outside, far, near))
    near_sign = jnp.where(row >= half, -1.0, 1.0)
    far_sign = jnp.where(beyond >= half_received, -1.0, 1.0)
    return code * jnp.where(outside, far_sign, near_sign)


def forward_kernel(slots, *refs):
    received = refs[:slots]
    (features_ref, map_ref, weight_ref, child_ref, back_hbm) = refs[slots : slots + 5]
    (hidden_ref, hgrad_ref, pgrad_ref, cgrad_ref) = refs[slots + 5 : slots + 9]
    sends = refs[slots + 9 : 2 * slots + 9]
    (table_ref, stacked_ref, acc_ref, back_ref, sem) = refs[2 * slots + 9 :]
    back_copy = pltpu.make_async_copy(back_hbm, back_ref, sem)
    back_copy.start()
    voxels = features_ref.shape[0]
    kernel_count = map_ref.shape[0]
    middle = kernel_count // 2
    cap2 = child_ref.shape[1]
    cap = received[0].shape[0] - cap2
    half, half_halo = voxels // 2, slots * cap // 2
    features = features_ref[...]
    table_ref[0:half, 0:LANES] = features[0:half]
    table_ref[0:half, LANES : 2 * LANES] = features[half:voxels]
    for s, block in enumerate(to_slots([r[0:cap, :] for r in received], False)):
        place = half + (s % (slots // 2)) * cap
        side = (s // (slots // 2)) * LANES
        table_ref[place : place + cap, side : side + LANES] = block
    table_rows = half + half_halo

    def gather(k):
        col = column(half_codes(map_ref[pl.ds(k, 1), :], voxels, slots * cap))
        chooser = one_hot_rows(jnp.abs(col).astype(BF16), table_rows)
        both = matmul(chooser, table_ref[...])
        picked = jnp.where(col < 0.0, both[:, LANES:], both[:, :LANES]).astype(BF16)
        stacked_ref[k] = picked
        return picked

    acc_ref[...] = matmul(features, weight_ref[middle])

    def step(j, carry):
        near, far = gather(j), gather(j + middle + 1)
        pair = jnp.concatenate([near, far], axis=1)
        kernel = jnp.concatenate([weight_ref[j], weight_ref[j + middle + 1]], axis=0)
        acc_ref[...] += matmul(pair, kernel)
        return carry

    lax.fori_loop(0, middle, step, 0)
    pre = acc_ref[...]
    sig = jax.nn.sigmoid(pre)
    hidden = (features.astype(F32) + pre * sig).astype(BF16)
    hidden_ref[...] = hidden
    leaving = gather_lists(child_ref, hidden).astype(BF16)
    for send, block in zip(sends, to_steps(jnp.split(leaving, slots), False)):
        send[...] = block
    back_copy.wait()
    hgrad = back_ref[...]
    lists = encode(child_ref[...]).astype(BF16)
    for s, block in enumerate(to_slots([r[cap : cap + cap2, :] for r in received], True)):
        hgrad = hgrad + matmul(one_hot_columns(lists[s : s + 1, :], voxels), block)
    hgrad_ref[...] = hgrad
    pgrad = hgrad * (sig * (1.0 + pre * (1.0 - sig)))
    pgrad_ref[...] = pgrad.astype(BF16)
    pgrad_t = jnp.transpose(pgrad).astype(BF16)

    def put(k, value):
        cgrad_ref[pl.ds(pl.multiple_of(k * LANES, LANES), LANES), :] = jnp.transpose(value).astype(BF16)

    put(middle, matmul(pgrad_t, features))

    def weight_step(j, carry):
        pair = jnp.concatenate([stacked_ref[j], stacked_ref[j + middle + 1]], axis=1)
        both = matmul(pgrad_t, pair)
        put(j, both[:, :LANES])
        put(j + middle + 1, both[:, LANES:])
        return carry

    lax.fori_loop(0, middle, weight_step, 0)


def spread_kernel(slots, pgrad_ref, map_ref, weight_ref, after_ref, back_ref, *sends):
    acc_ref = sends[-1]
    sends = sends[:-1]
    voxels = pgrad_ref.shape[0]
    kernel_count = map_ref.shape[0]
    middle = kernel_count // 2
    cap = sends[0].shape[0]
    half = voxels // 2
    table_rows = half + slots * cap // 2
    pgrad = pgrad_ref[...]
    own = matmul_rt(pgrad, weight_ref[middle])
    acc_ref[0:half, 0:LANES] = own[0:half]
    acc_ref[0:half, LANES:] = own[half:]
    acc_ref[half:, :] = jnp.zeros((table_rows - half, 2 * LANES), F32)

    def parts(k):
        codes = half_codes(map_ref[pl.ds(k, 1), :], voxels, slots * cap)
        terms = matmul_rt(pgrad, weight_ref[k])
        right = column(codes) < 0.0
        sides = [jnp.where(right, 0.0, terms), jnp.where(right, terms, 0.0)]
        chooser = one_hot_columns(jnp.abs(codes).astype(BF16), table_rows)
        return chooser, jnp.concatenate(sides, axis=1).astype(BF16)

    def step(j, carry):
        near_chooser, near_terms = parts(j)
        far_chooser, far_terms = parts(j + middle + 1)
        acc_ref[...] += matmul(near_chooser, near_terms) + matmul(far_chooser, far_terms)
        return carry

    lax.fori_loop(0, middle, step, 0)
    back_ref[0:half, :] = acc_ref[0:half, 0:LANES]
    back_ref[half:, :] = acc_ref[0:half, LANES:]
    blocks = []
    for s in range(slots):
        first = half + (s % (slots // 2)) * cap
        side = (s // (slots // 2)) * LANES
        blocks.append(acc_ref[first : first + cap, side : side + LANES].astype(BF16))
    for send, block in zip(sends, to_steps(blocks, True)):
        send[...] = block


def my_half(rows):
    core = lax.rem(lax.axis_index("shard"), 2)
    return pl.multiple_of(core * rows, 16), pl.multiple_of((1 - core) * rows, 16)


def down_kernel(slots, *refs):
    received = refs[:slots]
    (hidden_ref, map_ref, down_ref, out_grad_ref, cgrad_ref) = refs[slots : slots + 5]
    coarse_ref, terms_ref, send_ref = refs[slots + 5 :]
    table = jnp.concatenate([hidden_ref[...]] + to_slots([r[...] for r in received], False), axis=0)
    upstream = out_grad_ref[...]
    parents = upstream.shape[0]
    upstream_t = jnp.transpose(upstream.astype(F32)).astype(BF16)
    total = jnp.zeros((parents, down_ref.shape[2]), F32)
    codes = encode(map_ref[...])
    row = cgrad_ref.shape[0]
    terms_ref[0:row, :] = cgrad_ref[...]
    for o in range(map_ref.shape[0]):
        chooser = one_hot_rows(column(codes[o : o + 1, :]).astype(BF16), table.shape[0])
        picked = matmul(chooser, table).astype(BF16)
        total = total + matmul(picked, down_ref[o])
        terms = matmul(upstream_t, picked)
        for start in range(0, terms.shape[0], LANES):
            block = jnp.transpose(terms[start : start + LANES, :]).astype(BF16)
            terms_ref[row : row + LANES, :] = block
            row += LANES
    terms_ref[row:, :] = jnp.zeros((terms_ref.shape[0] - row, LANES), BF16)
    coarse_ref[...] = total.astype(BF16)
    send_ref[...] = terms_ref[pl.ds(my_half(send_ref.shape[0])[1], send_ref.shape[0]), :]


def pair_kernel(terms_ref, other_ref, out_ref):
    rows = other_ref.shape[0]
    mine = terms_ref[pl.ds(my_half(rows)[0], rows), :].astype(F32)
    out_ref[...] = (mine + other_ref[...].astype(F32)).astype(BF16)


def sum_kernel(devices, scale, parts_ref, after_ref, out_ref):
    rows = parts_ref.shape[0] // devices
    for core in range(2):
        mine = range(core, devices, 2)
        total = jnp.zeros((rows, LANES), F32)
        for d in mine:
            total = total + parts_ref[d * rows : (d + 1) * rows, :].astype(F32)
        total = (total * scale).astype(BF16)
        for d in mine:
            out_ref[d * rows : (d + 1) * rows, :] = total


def final_kernel(mine_ref, other_ref, conv_ref, down_ref, whole_ref):
    rows = mine_ref.shape[0]
    mine, other = my_half(rows)
    whole_ref[pl.ds(mine, rows), :] = mine_ref[...]
    whole_ref[pl.ds(other, rows), :] = other_ref[...]
    row = conv_ref.shape[0]
    conv_ref[...] = whole_ref[0:row, :].astype(F32)
    for first in range(0, down_ref.shape[0], LANES):
        for start in range(0, down_ref.shape[1], LANES):
            block = whole_ref[row : row + LANES, :].astype(F32)
            down_ref[first : first + LANES, start : start + LANES] = block
            row += LANES


def tail_kernel(slots, *refs):
    received = refs[:slots]
    hgrad_ref, back_ref, halo_ref, out_ref = refs[slots:]
    voxels = hgrad_ref.shape[0]
    total = hgrad_ref[...] + back_ref[...]
    lists = encode(halo_ref[...]).astype(BF16)
    for s, block in enumerate(to_slots([r[...] for r in received], True)):
        total = total + matmul(one_hot_columns(lists[s : s + 1, :], voxels), block)
    out_ref[...] = total


def call(kernel, operands, outs, scratch=(), limit=32, flops=0, in_hbm=()):
    spaces = [pl.ANY if n in in_hbm else pltpu.VMEM for n in range(len(operands))]
    return pl.pallas_call(
        kernel,
        out_shape=[jax.ShapeDtypeStruct(s, d) for s, d in outs],
        in_specs=[pl.BlockSpec(memory_space=space) for space in spaces],
        out_specs=[pl.BlockSpec(memory_space=pltpu.VMEM) for _ in outs],
        scratch_shapes=list(scratch),
        compiler_params=pltpu.CompilerParams(vmem_limit_bytes=limit * 2**20),
        cost_estimate=pl.CostEstimate(flops=flops, bytes_accessed=4 * 2**20, transcendentals=0),
    )(*operands)


def swap_cores(value, devices):
    return lax.ppermute(value, "shard", [(i, i + 1 - 2 * (i % 2)) for i in range(devices)])


def exchange(value):
    return lax.all_to_all(value, "shard", 0, 0, tiled=True)


def local(
    features, conv_weight, down_weight, neighbour_map, halo_rows, child_map, child_rows, out_grad
):
    voxels, channels = features.shape
    parents, coarse_channels = out_grad.shape
    kernel_count = conv_weight.shape[0]
    octants = down_weight.shape[0]
    slots, cap = halo_rows.shape
    cap2 = child_rows.shape[1]
    reach = slots // 2
    devices = lax.axis_size("shard")
    scale = 1.0 / math.sqrt(voxels * devices)
    giga = 10**9

    first = call(
        head_kernel,
        (features, halo_rows, child_map, out_grad, down_weight),
        [((cap + cap2, channels), BF16)] * slots + [((voxels, channels), F32)],
        scratch=[
            pltpu.VMEM(value.shape, value.dtype)
            for value in (features, halo_rows, child_map, out_grad, down_weight)
        ]
        + [pltpu.SemaphoreType.DMA((5,))],
        limit=60,
        flops=giga,
        in_hbm=range(5),
    )
    back_h = first[-1]
    received = swaps(first[:-1], reach)
    conv_rows = kernel_count * channels
    down_rows = octants * channels * coarse_channels // LANES
    grain = 8 * devices
    half_rows = -(-(conv_rows + down_rows) // (2 * grain)) * grain
    hidden, hidden_grad, pre_grad, conv_terms, *leaving = call(
        functools.partial(forward_kernel, slots),
        (*received, features, neighbour_map, conv_weight, child_rows, back_h),
        [
            ((voxels, channels), BF16),
            ((voxels, channels), F32),
            ((voxels, channels), BF16),
            ((conv_rows, channels), BF16),
        ]
        + [((cap2, channels), BF16)] * slots,
        scratch=[
            pltpu.VMEM((voxels // 2 + slots * cap // 2, 2 * channels), BF16),
            pltpu.VMEM((kernel_count, voxels, channels), BF16),
            pltpu.VMEM((voxels, channels), F32),
            pltpu.VMEM((voxels, channels), F32),
            pltpu.SemaphoreType.DMA(()),
        ],
        limit=48,
        flops=12 * giga,
        in_hbm=(slots + 4,),
    )
    received_h = swaps(leaving, reach)
    coarse, terms, leaving_terms = call(
        functools.partial(down_kernel, slots),
        (*received_h, hidden, child_map, down_weight, out_grad, conv_terms),
        [
            ((parents, coarse_channels), BF16),
            ((2 * half_rows, LANES), BF16),
            ((half_rows, LANES), BF16),
        ],
        flops=2 * giga,
    )
    (pair_terms,) = call(
        pair_kernel,
        (terms, swap_cores(leaving_terms, devices)),
        [((half_rows, LANES), BF16)],
        flops=10**6,
    )
    parts = exchange(pair_terms)
    spread = call(
        functools.partial(spread_kernel, slots),
        (pre_grad, neighbour_map, conv_weight, pair_terms),
        [((voxels, channels), F32)] + [((cap, channels), BF16)] * slots,
        scratch=[pltpu.VMEM((voxels // 2 + slots * cap // 2, 2 * channels), F32)],
        flops=20 * giga,
        in_hbm=(3,),
    )
    (summed,) = call(
        functools.partial(sum_kernel, devices, scale),
        (parts, spread[1]),
        [((half_rows, LANES), BF16)],
        flops=10**6,
        in_hbm=(1,),
    )
    summed, *returning = lax.optimization_barrier((summed, *spread[1:]))
    mine, *returned = lax.optimization_barrier((exchange(summed), *swaps(returning, reach)))
    (input_grad,) = call(
        functools.partial(tail_kernel, slots),
        (*returned, hidden_grad, spread[0], halo_rows),
        [((voxels, channels), F32)],
        flops=giga,
    )
    conv_grad, down_grad = call(
        final_kernel,
        (mine, swap_cores(mine, devices)),
        [((conv_rows, LANES), F32), ((octants * channels, coarse_channels), F32)],
        scratch=[pltpu.VMEM((2 * half_rows, LANES), BF16)],
        flops=10**6,
    )
    conv_grad = conv_grad.reshape(conv_weight.shape)
    return (coarse, input_grad, conv_grad, down_grad.reshape(down_weight.shape))


def solution(mesh):
    return jax.shard_map(
        local,
        mesh=mesh,
        in_specs=(
            P("shard", None),
            P(),
            P(),
            P(None, "shard"),
            P(None, "shard"),
            P(None, "shard"),
            P(None, "shard"),
            P("shard", None),
        ),
        out_specs=(P("shard", None), P("shard", None), P(), P()),
        check_vma=False,
    )
```

```python
import functools
import math

import jax
import jax.numpy as jnp
from jax import lax
from jax.experimental import pallas as pl
from jax.experimental.pallas import tpu as pltpu
from jax.sharding import PartitionSpec as P

BF16 = jnp.bfloat16
F32 = jnp.float32
LANES = 128


def swaps(by_step, reach):
    devices = lax.axis_size("shard")
    moved = []
    for m in range(1, reach + 1):
        for phase in range(2):
            sign = [1 if (i // m) % 2 == phase else -1 for i in range(devices)]
            pairs = [(i, i + m * sign[i]) for i in range(devices) if 0 <= i + m * sign[i] < devices]
            moved.append(lax.ppermute(by_step[len(moved)], "shard", pairs))
    return moved


def is_even(m):
    return lax.rem(lax.div(lax.axis_index("shard"), m), 2) == 0


def to_steps(slots, back):
    reach = len(slots) // 2
    steps = []
    for m in range(1, reach + 1):
        first, second = slots[reach + m - 1], slots[reach - m]
        if back:
            first, second = second, first
        steps.append(lax.select(is_even(m), first, second))
        steps.append(lax.select(is_even(m), second, first))
    return steps


def to_slots(steps, back):
    reach = len(steps) // 2
    slots = [None] * len(steps)
    for m in range(1, reach + 1):
        first = lax.select(is_even(m), steps[2 * m - 2], steps[2 * m - 1])
        second = lax.select(is_even(m), steps[2 * m - 1], steps[2 * m - 2])
        if back:
            first, second = second, first
        slots[reach - m], slots[reach + m - 1] = first, second
    return slots


def matmul(left, right):
    return jnp.dot(left, right, preferred_element_type=F32)


def matmul_rt(left, right):
    return lax.dot_general(left, right, (((1,), (1,)), ((), ())), preferred_element_type=F32)


def pick_one(mask):
    return jnp.where(mask, jnp.ones(mask.shape, BF16), jnp.zeros(mask.shape, BF16))


def encode(row):
    return jnp.left_shift((row & (LANES - 1)) + LANES, row >> 7).astype(F32)


def column(codes):
    pieces = []
    for start in range(0, codes.shape[1], LANES):
        piece = jnp.broadcast_to(codes[:, start : start + LANES], (LANES, LANES))
        pieces.append(jnp.transpose(piece))
    return pieces[0] if len(pieces) == 1 else jnp.concatenate(pieces, axis=0)


def one_hot_rows(col, width):
    lane = lax.broadcasted_iota(jnp.int32, (16, LANES), 1)
    blocks = []
    for start in range(0, width, LANES):
        pattern = jnp.broadcast_to(encode(lane + start).astype(BF16)[0:1], col.shape)
        blocks.append(pick_one(col == pattern))
    return jnp.concatenate(blocks, axis=1)


def one_hot_columns(codes, height):
    place = lax.broadcasted_iota(jnp.int32, (height, codes.shape[1]), 0)
    pattern = encode(place).astype(BF16)
    return pick_one(jnp.broadcast_to(codes, pattern.shape) == pattern)


def pick_rows(col, table):
    both = matmul(one_hot_rows(jnp.abs(col), table.shape[0]), table).astype(BF16)
    return jnp.where(col < jnp.zeros(col.shape, BF16), both[:, LANES:], both[:, :LANES])


def list_row(lists, first, per_row):
    pieces = [lists[first + n : first + n + 1, :] for n in range(per_row)]
    return pieces[0] if per_row == 1 else jnp.concatenate(pieces, axis=1)


def gather_lists(lists_ref, table):
    slots, cap = lists_ref.shape
    lists = lists_ref[...]
    per_row = max(1, min(slots, LANES // cap))
    parts = []
    for first in range(0, slots, per_row):
        codes = encode(list_row(lists, first, per_row))
        chooser = one_hot_rows(column(codes).astype(BF16), table.shape[0])
        parts.append(matmul(chooser, table))
    return parts[0] if len(parts) == 1 else jnp.concatenate(parts, axis=0)


def head_kernel(features_hbm, halo_hbm, child_map_hbm, out_grad_hbm, down_hbm, *refs):
    sources = (features_hbm, halo_hbm, child_map_hbm, out_grad_hbm, down_hbm)
    buffers, sems = refs[-len(sources) - 1 : -1], refs[-1]
    features_ref, halo_ref, child_map_ref, out_grad_ref, down_ref = buffers
    copies = [
        pltpu.make_async_copy(source, buffer, sems.at[n])
        for n, (source, buffer) in enumerate(zip(sources, buffers))
    ]
    for copy in copies:
        copy.start()
    outs = refs[: -len(sources) - 1]
    sends, back_ref = outs[:-1], outs[-1]
    slots, cap = halo_ref.shape
    voxels = features_ref.shape[0]
    octants = child_map_ref.shape[0]
    table_rows = voxels + slots * (sends[0].shape[0] - cap)
    cap2 = (table_rows - voxels) // slots
    copies[0].wait()
    copies[1].wait()
    listed = gather_lists(halo_ref, features_ref[...]).astype(BF16)
    for send, block in zip(sends, to_steps(jnp.split(listed, slots), False)):
        send[0:cap, :] = block
    for copy in copies[2:]:
        copy.wait()
    upstream = out_grad_ref[...]
    both = jnp.zeros((table_rows, 2 * LANES), F32)
    codes = encode(child_map_ref[...]).astype(BF16)
    for o in range(octants):
        part = matmul_rt(upstream, down_ref[o])
        high = part.astype(BF16)
        low = (part - high.astype(F32)).astype(BF16)
        chooser = one_hot_columns(codes[o : o + 1, :], table_rows)
        both = both + matmul(chooser, jnp.concatenate([high, low], axis=1))
    total = both[:, :LANES] + both[:, LANES:]
    back_ref[...] = total[:voxels]
    for send, block in zip(sends, to_steps(jnp.split(total[voxels:].astype(BF16), slots), True)):
        send[cap : cap + cap2, :] = block


def half_codes(row, voxels, received):
    half, half_received = voxels // 2, received // 2
    beyond = row - voxels
    outside = beyond >= 0
    near = row - jnp.where(row >= half, half, 0)
    far = half + beyond - jnp.where(beyond >= half_received, half_received, 0)
    code = encode(jnp.where(outside, far, near))
    near_sign = jnp.where(row >= half, -1.0, 1.0)
    far_sign = jnp.where(beyond >= half_received, -1.0, 1.0)
    return code * jnp.where(outside, far_sign, near_sign)


def forward_kernel(slots, *refs):
    received = refs[:slots]
    (features_ref, map_ref, weight_ref, child_ref, back_hbm) = refs[slots : slots + 5]
    (hidden_ref, hgrad_ref, pgrad_ref, cgrad_ref) = refs[slots + 5 : slots + 9]
    sends = refs[slots + 9 : 2 * slots + 9]
    (table_ref, stacked_ref, acc_ref, back_ref, sem) = refs[2 * slots + 9 :]
    back_copy = pltpu.make_async_copy(back_hbm, back_ref, sem)
    back_copy.start()
    voxels = features_ref.shape[0]
    kernel_count = map_ref.shape[0]
    middle = kernel_count // 2
    cap2 = child_ref.shape[1]
    cap = received[0].shape[0] - cap2
    half, half_halo = voxels // 2, slots * cap // 2
    features = features_ref[...]
    table_ref[0:half, 0:LANES] = features[0:half]
    table_ref[0:half, LANES : 2 * LANES] = features[half:voxels]
    for s, block in enumerate(to_slots([r[0:cap, :] for r in received], False)):
        place = half + (s % (slots // 2)) * cap
        side = (s // (slots // 2)) * LANES
        table_ref[place : place + cap, side : side + LANES] = block
    table_rows = half + half_halo

    def gather(k):
        codes = half_codes(map_ref[pl.ds(k, 1), :], voxels, slots * cap).astype(BF16)
        picked = pick_rows(column(codes), table_ref[...])
        stacked_ref[k] = picked
        return picked

    acc_ref[...] = matmul(features, weight_ref[middle])

    def step(j, carry):
        near, far = gather(j), gather(j + middle + 1)
        pair = jnp.concatenate([near, far], axis=1)
        kernel = jnp.concatenate([weight_ref[j], weight_ref[j + middle + 1]], axis=0)
        acc_ref[...] += matmul(pair, kernel)
        return carry

    lax.fori_loop(0, middle, step, 0)
    pre = acc_ref[...]
    sig = jax.nn.sigmoid(pre)
    hidden = (features.astype(F32) + pre * sig).astype(BF16)
    hidden_ref[...] = hidden
    leaving = gather_lists(child_ref, hidden).astype(BF16)
    for send, block in zip(sends, to_steps(jnp.split(leaving, slots), False)):
        send[...] = block
    back_copy.wait()
    hgrad = back_ref[...]
    lists = encode(child_ref[...]).astype(BF16)
    for s, block in enumerate(to_slots([r[cap : cap + cap2, :] for r in received], True)):
        hgrad = hgrad + matmul(one_hot_columns(lists[s : s + 1, :], voxels), block)
    hgrad_ref[...] = hgrad
    pgrad = hgrad * (sig * (1.0 + pre * (1.0 - sig)))
    pgrad_ref[...] = pgrad.astype(BF16)
    pgrad_t = jnp.transpose(pgrad).astype(BF16)

    def put(k, value):
        cgrad_ref[pl.ds(pl.multiple_of(k * LANES, LANES), LANES), :] = jnp.transpose(value).astype(BF16)

    put(middle, matmul(pgrad_t, features))

    def weight_step(j, carry):
        pair = jnp.concatenate([stacked_ref[j], stacked_ref[j + middle + 1]], axis=1)
        both = matmul(pgrad_t, pair)
        put(j, both[:, :LANES])
        put(j + middle + 1, both[:, LANES:])
        return carry

    lax.fori_loop(0, middle, weight_step, 0)


def spread_kernel(slots, pgrad_ref, map_ref, weight_ref, after_ref, back_ref, *sends):
    acc_ref, codes_ref = sends[-2:]
    sends = sends[:-2]
    voxels = pgrad_ref.shape[0]
    kernel_count = map_ref.shape[0]
    middle = kernel_count // 2
    cap = sends[0].shape[0]
    half = voxels // 2
    table_rows = half + slots * cap // 2
    pgrad = pgrad_ref[...]
    own = matmul_rt(pgrad, weight_ref[middle])
    acc_ref[0:half, 0:LANES] = own[0:half]
    acc_ref[0:half, LANES:] = own[half:]
    acc_ref[half:, :] = jnp.zeros((table_rows - half, 2 * LANES), F32)

    codes_ref[...] = jnp.zeros(codes_ref.shape, F32)
    codes_ref[0:kernel_count, :] = half_codes(map_ref[...], voxels, slots * cap)
    turned = jnp.concatenate(
        [
            jnp.transpose(codes_ref[:, first : first + LANES]).astype(BF16)
            for first in range(0, voxels, LANES)
        ],
        axis=0,
    )
    number = lax.broadcasted_iota(jnp.int32, (LANES, LANES), 0)

    def parts(k, spread_codes):
        terms = matmul_rt(pgrad, weight_ref[k])
        right = spread_codes < 0.0
        sides = [jnp.where(right, 0.0, terms), jnp.where(right, terms, 0.0)]
        codes = jnp.abs(codes_ref[pl.ds(k, 1), :]).astype(BF16)
        return one_hot_columns(codes, table_rows), jnp.concatenate(sides, axis=1).astype(BF16)

    def step(j, carry):
        chosen = [pick_one(number == k) for k in (j, j + middle + 1)]
        both = matmul(turned, jnp.concatenate(chosen, axis=1))
        near_chooser, near_terms = parts(j, both[:, :LANES])
        far_chooser, far_terms = parts(j + middle + 1, both[:, LANES:])
        acc_ref[...] += matmul(near_chooser, near_terms) + matmul(far_chooser, far_terms)
        return carry

    lax.fori_loop(0, middle, step, 0)
    back_ref[0:half, :] = acc_ref[0:half, 0:LANES]
    back_ref[half:, :] = acc_ref[0:half, LANES:]
    blocks = []
    for s in range(slots):
        first = half + (s % (slots // 2)) * cap
        side = (s // (slots // 2)) * LANES
        blocks.append(acc_ref[first : first + cap, side : side + LANES].astype(BF16))
    for send, block in zip(sends, to_steps(blocks, True)):
        send[...] = block


def my_half(rows):
    core = lax.rem(lax.axis_index("shard"), 2)
    return pl.multiple_of(core * rows, 16), pl.multiple_of((1 - core) * rows, 16)


def down_kernel(slots, *refs):
    received = refs[:slots]
    (hidden_ref, map_ref, down_ref, out_grad_ref, cgrad_ref) = refs[slots : slots + 5]
    coarse_ref, terms_ref, send_ref, table_ref = refs[slots + 5 :]
    voxels = hidden_ref.shape[0]
    cap2 = received[0].shape[0]
    half, half_halo = voxels // 2, slots * cap2 // 2
    blocks = to_slots([r[...] for r in received], False)
    table_ref[0:half, 0:LANES] = hidden_ref[0:half, :]
    table_ref[0:half, LANES:] = hidden_ref[half:, :]
    for s, block in enumerate(blocks):
        place = half + (s % (slots // 2)) * cap2
        side = (s // (slots // 2)) * LANES
        table_ref[place : place + cap2, side : side + LANES] = block
    padding = table_ref.shape[0] - half - half_halo
    table_ref[half + half_halo :, :] = jnp.zeros((padding, 2 * LANES), BF16)
    upstream = out_grad_ref[...]
    parents = upstream.shape[0]
    octants = map_ref.shape[0]
    upstream_t = jnp.transpose(upstream.astype(F32)).astype(BF16)
    codes = half_codes(map_ref[...], voxels, slots * cap2)
    col = jnp.concatenate([column(codes[o : o + 1, :]) for o in range(octants)], axis=0)
    picked = pick_rows(col.astype(BF16), table_ref[...])
    picked = jnp.concatenate(jnp.split(picked, octants), axis=1)
    row = cgrad_ref.shape[0]
    terms_ref[0:row, :] = cgrad_ref[...]
    terms = matmul(upstream_t, picked)
    for o in range(octants):
        for start in range(0, terms.shape[0], LANES):
            block = terms[start : start + LANES, o * LANES : (o + 1) * LANES]
            terms_ref[row : row + LANES, :] = jnp.transpose(block).astype(BF16)
            row += LANES
    total = matmul(picked, down_ref[...].reshape(octants * LANES, down_ref.shape[2]))
    terms_ref[row:, :] = jnp.zeros((terms_ref.shape[0] - row, LANES), BF16)
    coarse_ref[...] = total.astype(BF16)
    send_ref[...] = terms_ref[pl.ds(my_half(send_ref.shape[0])[1], send_ref.shape[0]), :]


def pair_kernel(terms_ref, other_ref, out_ref):
    rows = other_ref.shape[0]
    mine = terms_ref[pl.ds(my_half(rows)[0], rows), :].astype(F32)
    out_ref[...] = (mine + other_ref[...].astype(F32)).astype(BF16)


def sum_kernel(devices, scale, parts_ref, after_ref, out_ref):
    rows = parts_ref.shape[0] // devices
    for core in range(2):
        mine = range(core, devices, 2)
        total = jnp.zeros((rows, LANES), F32)
        for d in mine:
            total = total + parts_ref[d * rows : (d + 1) * rows, :].astype(F32)
        total = (total * scale).astype(BF16)
        for d in mine:
            out_ref[d * rows : (d + 1) * rows, :] = total


def final_kernel(mine_ref, other_ref, conv_ref, down_ref, whole_ref):
    rows = mine_ref.shape[0]
    mine, other = my_half(rows)
    whole_ref[pl.ds(mine, rows), :] = mine_ref[...]
    whole_ref[pl.ds(other, rows), :] = other_ref[...]
    row = conv_ref.shape[0]
    conv_ref[...] = whole_ref[0:row, :].astype(F32)
    for first in range(0, down_ref.shape[0], LANES):
        for start in range(0, down_ref.shape[1], LANES):
            block = whole_ref[row : row + LANES, :].astype(F32)
            down_ref[first : first + LANES, start : start + LANES] = block
            row += LANES


def tail_kernel(slots, *refs):
    received = refs[:slots]
    hgrad_ref, back_ref, halo_ref, out_ref = refs[slots:]
    voxels = hgrad_ref.shape[0]
    total = hgrad_ref[...] + back_ref[...]
    lists = encode(halo_ref[...]).astype(BF16)
    for s, block in enumerate(to_slots([r[...] for r in received], True)):
        total = total + matmul(one_hot_columns(lists[s : s + 1, :], voxels), block)
    out_ref[...] = total


def call(kernel, operands, outs, scratch=(), limit=32, flops=0, in_hbm=()):
    spaces = [pl.ANY if n in in_hbm else pltpu.VMEM for n in range(len(operands))]
    return pl.pallas_call(
        kernel,
        out_shape=[jax.ShapeDtypeStruct(s, d) for s, d in outs],
        in_specs=[pl.BlockSpec(memory_space=space) for space in spaces],
        out_specs=[pl.BlockSpec(memory_space=pltpu.VMEM) for _ in outs],
        scratch_shapes=list(scratch),
        compiler_params=pltpu.CompilerParams(vmem_limit_bytes=limit * 2**20),
        cost_estimate=pl.CostEstimate(flops=flops, bytes_accessed=4 * 2**20, transcendentals=0),
    )(*operands)


def swap_cores(value, devices):
    return lax.ppermute(value, "shard", [(i, i + 1 - 2 * (i % 2)) for i in range(devices)])


def exchange(value):
    return lax.all_to_all(value, "shard", 0, 0, tiled=True)


def local(
    features, conv_weight, down_weight, neighbour_map, halo_rows, child_map, child_rows, out_grad
):
    voxels, channels = features.shape
    parents, coarse_channels = out_grad.shape
    kernel_count = conv_weight.shape[0]
    octants = down_weight.shape[0]
    slots, cap = halo_rows.shape
    cap2 = child_rows.shape[1]
    reach = slots // 2
    devices = lax.axis_size("shard")
    scale = 1.0 / math.sqrt(voxels * devices)
    giga = 10**9

    first = call(
        head_kernel,
        (features, halo_rows, child_map, out_grad, down_weight),
        [((cap + cap2, channels), BF16)] * slots + [((voxels, channels), F32)],
        scratch=[
            pltpu.VMEM(value.shape, value.dtype)
            for value in (features, halo_rows, child_map, out_grad, down_weight)
        ]
        + [pltpu.SemaphoreType.DMA((5,))],
        limit=60,
        flops=giga,
        in_hbm=range(5),
    )
    back_h = first[-1]
    received = swaps(first[:-1], reach)
    conv_rows = kernel_count * channels
    down_rows = octants * channels * coarse_channels // LANES
    grain = 8 * devices
    half_rows = -(-(conv_rows + down_rows) // (2 * grain)) * grain
    hidden, hidden_grad, pre_grad, conv_terms, *leaving = call(
        functools.partial(forward_kernel, slots),
        (*received, features, neighbour_map, conv_weight, child_rows, back_h),
        [
            ((voxels, channels), BF16),
            ((voxels, channels), F32),
            ((voxels, channels), BF16),
            ((conv_rows, channels), BF16),
        ]
        + [((cap2, channels), BF16)] * slots,
        scratch=[
            pltpu.VMEM((voxels // 2 + slots * cap // 2, 2 * channels), BF16),
            pltpu.VMEM((kernel_count, voxels, channels), BF16),
            pltpu.VMEM((voxels, channels), F32),
            pltpu.VMEM((voxels, channels), F32),
            pltpu.SemaphoreType.DMA(()),
        ],
        limit=48,
        flops=12 * giga,
        in_hbm=(slots + 4,),
    )
    received_h = swaps(leaving, reach)
    coarse, terms, leaving_terms = call(
        functools.partial(down_kernel, slots),
        (*received_h, hidden, child_map, down_weight, out_grad, conv_terms),
        [
            ((parents, coarse_channels), BF16),
            ((2 * half_rows, LANES), BF16),
            ((half_rows, LANES), BF16),
        ],
        scratch=[pltpu.VMEM((-(-(voxels + slots * cap2) // 256) * 128, 2 * channels), BF16)],
        flops=2 * giga,
    )
    (pair_terms,) = call(
        pair_kernel,
        (terms, swap_cores(leaving_terms, devices)),
        [((half_rows, LANES), BF16)],
        flops=10**6,
    )
    parts = exchange(pair_terms)
    spread = call(
        functools.partial(spread_kernel, slots),
        (pre_grad, neighbour_map, conv_weight, pair_terms),
        [((voxels, channels), F32)] + [((cap, channels), BF16)] * slots,
        scratch=[
            pltpu.VMEM((voxels // 2 + slots * cap // 2, 2 * channels), F32),
            pltpu.VMEM((LANES, voxels), F32),
        ],
        flops=20 * giga,
        in_hbm=(3,),
    )
    (summed,) = call(
        functools.partial(sum_kernel, devices, scale),
        (parts, spread[1]),
        [((half_rows, LANES), BF16)],
        flops=10**6,
        in_hbm=(1,),
    )
    summed, *returning = lax.optimization_barrier((summed, *spread[1:]))
    returned = swaps(returning, reach)
    (input_grad,) = call(
        functools.partial(tail_kernel, slots),
        (*returned, hidden_grad, spread[0], halo_rows),
        [((voxels, channels), F32)],
        flops=giga,
    )
    mine, input_grad = lax.optimization_barrier((exchange(summed), input_grad))
    conv_grad, down_grad = call(
        final_kernel,
        (mine, swap_cores(mine, devices)),
        [((conv_rows, LANES), F32), ((octants * channels, coarse_channels), F32)],
        scratch=[pltpu.VMEM((2 * half_rows, LANES), BF16)],
        flops=10**6,
    )
    conv_grad = conv_grad.reshape(conv_weight.shape)
    return (coarse, input_grad, conv_grad, down_grad.reshape(down_weight.shape))


def solution(mesh):
    return jax.shard_map(
        local,
        mesh=mesh,
        in_specs=(
            P("shard", None),
            P(),
            P(),
            P(None, "shard"),
            P(None, "shard"),
            P(None, "shard"),
            P(None, "shard"),
            P("shard", None),
        ),
        out_specs=(P("shard", None), P("shard", None), P(), P()),
        check_vma=False,
    )
```

```python
import functools
import math

import jax
import jax.numpy as jnp
from jax import lax
from jax.experimental import pallas as pl
from jax.experimental.pallas import tpu as pltpu
from jax.sharding import PartitionSpec as P

BF16 = jnp.bfloat16
F32 = jnp.float32
LANES = 128


def swaps(by_step, reach):
    devices = lax.axis_size("shard")
    moved = []
    for m in range(1, reach + 1):
        for phase in range(2):
            sign = [1 if (i // m) % 2 == phase else -1 for i in range(devices)]
            pairs = [(i, i + m * sign[i]) for i in range(devices) if 0 <= i + m * sign[i] < devices]
            moved.append(lax.ppermute(by_step[len(moved)], "shard", pairs))
    return moved


def is_even(m):
    return lax.rem(lax.div(lax.axis_index("shard"), m), 2) == 0


def to_steps(slots, back):
    reach = len(slots) // 2
    steps = []
    for m in range(1, reach + 1):
        first, second = slots[reach + m - 1], slots[reach - m]
        if back:
            first, second = second, first
        steps.append(lax.select(is_even(m), first, second))
        steps.append(lax.select(is_even(m), second, first))
    return steps


def to_slots(steps, back):
    reach = len(steps) // 2
    slots = [None] * len(steps)
    for m in range(1, reach + 1):
        first = lax.select(is_even(m), steps[2 * m - 2], steps[2 * m - 1])
        second = lax.select(is_even(m), steps[2 * m - 1], steps[2 * m - 2])
        if back:
            first, second = second, first
        slots[reach - m], slots[reach + m - 1] = first, second
    return slots


def matmul(left, right):
    return jnp.dot(left, right, preferred_element_type=F32)


def matmul_rt(left, right):
    return lax.dot_general(left, right, (((1,), (1,)), ((), ())), preferred_element_type=F32)


def pick_one(mask):
    return jnp.where(mask, jnp.ones(mask.shape, BF16), jnp.zeros(mask.shape, BF16))


def encode(row):
    return jnp.left_shift((row & (LANES - 1)) + LANES, row >> 7).astype(F32)


def column(codes):
    pieces = []
    for start in range(0, codes.shape[1], LANES):
        piece = jnp.broadcast_to(codes[:, start : start + LANES], (LANES, LANES))
        pieces.append(jnp.transpose(piece))
    return pieces[0] if len(pieces) == 1 else jnp.concatenate(pieces, axis=0)


def one_hot_rows(col, width):
    lane = lax.broadcasted_iota(jnp.int32, (16, LANES), 1)
    blocks = []
    for start in range(0, width, LANES):
        pattern = jnp.broadcast_to(encode(lane + start).astype(BF16)[0:1], col.shape)
        blocks.append(pick_one(col == pattern))
    return jnp.concatenate(blocks, axis=1)


def one_hot_columns(codes, height):
    place = lax.broadcasted_iota(jnp.int32, (height, codes.shape[1]), 0)
    pattern = encode(place).astype(BF16)
    return pick_one(jnp.broadcast_to(codes, pattern.shape) == pattern)


def pick_rows(col, table):
    both = matmul(one_hot_rows(jnp.abs(col), table.shape[0]), table).astype(BF16)
    return jnp.where(col < jnp.zeros(col.shape, BF16), both[:, LANES:], both[:, :LANES])


def list_row(lists, first, per_row):
    pieces = [lists[first + n : first + n + 1, :] for n in range(per_row)]
    return pieces[0] if per_row == 1 else jnp.concatenate(pieces, axis=1)


def gather_lists(lists_ref, table):
    slots, cap = lists_ref.shape
    lists = lists_ref[...]
    per_row = max(1, min(slots, LANES // cap))
    parts = []
    for first in range(0, slots, per_row):
        codes = encode(list_row(lists, first, per_row))
        chooser = one_hot_rows(column(codes).astype(BF16), table.shape[0])
        parts.append(matmul(chooser, table))
    return parts[0] if len(parts) == 1 else jnp.concatenate(parts, axis=0)


def head_kernel(features_hbm, halo_hbm, child_map_hbm, out_grad_hbm, down_hbm, *refs):
    sources = (features_hbm, halo_hbm, child_map_hbm, out_grad_hbm, down_hbm)
    buffers, sems = refs[-len(sources) - 1 : -1], refs[-1]
    features_ref, halo_ref, child_map_ref, out_grad_ref, down_ref = buffers
    copies = [
        pltpu.make_async_copy(source, buffer, sems.at[n])
        for n, (source, buffer) in enumerate(zip(sources, buffers))
    ]
    for copy in copies:
        copy.start()
    outs = refs[: -len(sources) - 1]
    sends, back_ref = outs[:-1], outs[-1]
    slots, cap = halo_ref.shape
    voxels = features_ref.shape[0]
    octants = child_map_ref.shape[0]
    table_rows = voxels + slots * (sends[0].shape[0] - cap)
    cap2 = (table_rows - voxels) // slots
    copies[0].wait()
    copies[1].wait()
    listed = gather_lists(halo_ref, features_ref[...]).astype(BF16)
    for send, block in zip(sends, to_steps(jnp.split(listed, slots), False)):
        send[0:cap, :] = block
    for copy in copies[2:]:
        copy.wait()
    upstream = out_grad_ref[...]
    codes = encode(child_map_ref[...]).astype(BF16)
    choosers, parts = [], []
    for o in range(octants):
        part = matmul_rt(upstream, down_ref[o])
        high = part.astype(BF16)
        low = (part - high.astype(F32)).astype(BF16)
        choosers.append(one_hot_columns(codes[o : o + 1, :], table_rows))
        parts.append(jnp.concatenate([high, low], axis=1))
    both = matmul(jnp.concatenate(choosers, axis=1), jnp.concatenate(parts, axis=0))
    total = both[:, :LANES] + both[:, LANES:]
    back_ref[...] = total[:voxels]
    for send, block in zip(sends, to_steps(jnp.split(total[voxels:].astype(BF16), slots), True)):
        send[cap : cap + cap2, :] = block


def half_codes(row, voxels, received):
    half, half_received = voxels // 2, received // 2
    beyond = row - voxels
    outside = beyond >= 0
    near = row - jnp.where(row >= half, half, 0)
    far = half + beyond - jnp.where(beyond >= half_received, half_received, 0)
    code = encode(jnp.where(outside, far, near))
    near_sign = jnp.where(row >= half, -1.0, 1.0)
    far_sign = jnp.where(beyond >= half_received, -1.0, 1.0)
    return code * jnp.where(outside, far_sign, near_sign)


def forward_kernel(slots, *refs):
    received = refs[:slots]
    (features_ref, map_ref, weight_ref, child_ref, back_hbm) = refs[slots : slots + 5]
    (hidden_ref, hgrad_ref, pgrad_ref, cgrad_ref) = refs[slots + 5 : slots + 9]
    sends = refs[slots + 9 : 2 * slots + 9]
    (table_ref, stacked_ref, acc_ref, back_ref, sem) = refs[2 * slots + 9 : 2 * slots + 14]
    chooser_refs, col_refs = refs[2 * slots + 14 : 2 * slots + 16], refs[2 * slots + 16 :]
    back_copy = pltpu.make_async_copy(back_hbm, back_ref, sem)
    back_copy.start()
    voxels = features_ref.shape[0]
    kernel_count = map_ref.shape[0]
    middle = kernel_count // 2
    cap2 = child_ref.shape[1]
    cap = received[0].shape[0] - cap2
    half, half_halo = voxels // 2, slots * cap // 2
    features = features_ref[...]
    table_ref[0:half, 0:LANES] = features[0:half]
    table_ref[0:half, LANES : 2 * LANES] = features[half:voxels]
    for s, block in enumerate(to_slots([r[0:cap, :] for r in received], False)):
        place = half + (s % (slots // 2)) * cap
        side = (s // (slots // 2)) * LANES
        table_ref[place : place + cap, side : side + LANES] = block
    table_rows = half + half_halo

    def build(j, side):
        for n, k in enumerate((j, j + middle + 1)):
            codes = half_codes(map_ref[pl.ds(k, 1), :], voxels, slots * cap).astype(BF16)
            col = column(codes)
            col_refs[side][n] = col
            chooser_refs[side][n] = one_hot_rows(jnp.abs(col), table_rows)

    def use(j, side):
        pair = []
        for n, k in enumerate((j, j + middle + 1)):
            both = matmul(chooser_refs[side][n], table_ref[...]).astype(BF16)
            right = col_refs[side][n] < jnp.zeros((voxels, LANES), BF16)
            pair.append(jnp.where(right, both[:, LANES:], both[:, :LANES]))
            stacked_ref[k] = pair[n]
        return pair

    def convolve(j, pair):
        kernel = jnp.concatenate([weight_ref[j], weight_ref[j + middle + 1]], axis=0)
        acc_ref[...] += matmul(jnp.concatenate(pair, axis=1), kernel)

    acc_ref[...] = matmul(features, weight_ref[middle])
    build(0, 0)

    def step(i, carry):
        for side in range(2):
            j = 2 * i + side
            pair = use(j, side)
            build(j + 1, 1 - side)
            convolve(j, pair)
        return carry

    lax.fori_loop(0, middle // 2, step, 0)
    convolve(middle - 1, use(middle - 1, 0))
    pre = acc_ref[...]
    sig = jax.nn.sigmoid(pre)
    hidden = (features.astype(F32) + pre * sig).astype(BF16)
    hidden_ref[...] = hidden
    leaving = gather_lists(child_ref, hidden).astype(BF16)
    for send, block in zip(sends, to_steps(jnp.split(leaving, slots), False)):
        send[...] = block
    back_copy.wait()
    hgrad = back_ref[...]
    lists = encode(child_ref[...]).astype(BF16)
    for s, block in enumerate(to_slots([r[cap : cap + cap2, :] for r in received], True)):
        hgrad = hgrad + matmul(one_hot_columns(lists[s : s + 1, :], voxels), block)
    hgrad_ref[...] = hgrad
    pgrad = hgrad * (sig * (1.0 + pre * (1.0 - sig)))
    pgrad_ref[...] = pgrad.astype(BF16)
    pgrad_t = jnp.transpose(pgrad).astype(BF16)

    def put(k, value):
        cgrad_ref[pl.ds(pl.multiple_of(k * LANES, LANES), LANES), :] = jnp.transpose(value).astype(BF16)

    put(middle, matmul(pgrad_t, features))

    def weight_step(j, carry):
        pair = jnp.concatenate([stacked_ref[j], stacked_ref[j + middle + 1]], axis=1)
        both = matmul(pgrad_t, pair)
        put(j, both[:, :LANES])
        put(j + middle + 1, both[:, LANES:])
        return carry

    for j in range(middle):
        weight_step(j, 0)


def spread_kernel(slots, pgrad_ref, map_ref, weight_ref, after_ref, back_ref, *sends):
    acc_ref = sends[-1]
    sends = sends[:-1]
    voxels = pgrad_ref.shape[0]
    kernel_count = map_ref.shape[0]
    middle = kernel_count // 2
    cap = sends[0].shape[0]
    half = voxels // 2
    table_rows = half + slots * cap // 2
    pgrad = pgrad_ref[...]
    own = matmul_rt(pgrad, weight_ref[middle])
    acc_ref[0:half, 0:LANES] = own[0:half]
    acc_ref[0:half, LANES:] = own[half:]
    acc_ref[half:, :] = jnp.zeros((table_rows - half, 2 * LANES), F32)

    def parts(k):
        codes = half_codes(map_ref[pl.ds(k, 1), :], voxels, slots * cap)
        terms = matmul_rt(pgrad, weight_ref[k])
        right = column(codes) < 0.0
        sides = [jnp.where(right, 0.0, terms), jnp.where(right, terms, 0.0)]
        chooser = one_hot_columns(jnp.abs(codes).astype(BF16), table_rows)
        return chooser, jnp.concatenate(sides, axis=1).astype(BF16)

    def step(j, carry):
        near_chooser, near_terms = parts(j)
        far_chooser, far_terms = parts(j + middle + 1)
        acc_ref[...] += matmul(near_chooser, near_terms) + matmul(far_chooser, far_terms)
        return carry

    lax.fori_loop(0, middle, step, 0)
    back_ref[0:half, :] = acc_ref[0:half, 0:LANES]
    back_ref[half:, :] = acc_ref[0:half, LANES:]
    blocks = []
    for s in range(slots):
        first = half + (s % (slots // 2)) * cap
        side = (s // (slots // 2)) * LANES
        blocks.append(acc_ref[first : first + cap, side : side + LANES].astype(BF16))
    for send, block in zip(sends, to_steps(blocks, True)):
        send[...] = block


def my_half(rows):
    core = lax.rem(lax.axis_index("shard"), 2)
    return pl.multiple_of(core * rows, 16), pl.multiple_of((1 - core) * rows, 16)


def down_kernel(slots, *refs):
    received = refs[:slots]
    (hidden_ref, map_ref, down_ref, out_grad_ref, cgrad_ref) = refs[slots : slots + 5]
    coarse_ref, terms_ref, send_ref, table_ref = refs[slots + 5 :]
    voxels = hidden_ref.shape[0]
    cap2 = received[0].shape[0]
    half, half_halo = voxels // 2, slots * cap2 // 2
    blocks = to_slots([r[...] for r in received], False)
    table_ref[0:half, 0:LANES] = hidden_ref[0:half, :]
    table_ref[0:half, LANES:] = hidden_ref[half:, :]
    for s, block in enumerate(blocks):
        place = half + (s % (slots // 2)) * cap2
        side = (s // (slots // 2)) * LANES
        table_ref[place : place + cap2, side : side + LANES] = block
    padding = table_ref.shape[0] - half - half_halo
    table_ref[half + half_halo :, :] = jnp.zeros((padding, 2 * LANES), BF16)
    upstream = out_grad_ref[...]
    parents = upstream.shape[0]
    octants = map_ref.shape[0]
    upstream_t = jnp.transpose(upstream.astype(F32)).astype(BF16)
    codes = half_codes(map_ref[...], voxels, slots * cap2)
    col = jnp.concatenate([column(codes[o : o + 1, :]) for o in range(octants)], axis=0)
    picked = pick_rows(col.astype(BF16), table_ref[...])
    picked = jnp.concatenate(jnp.split(picked, octants), axis=1)
    row = cgrad_ref.shape[0]
    terms_ref[0:row, :] = cgrad_ref[...]
    terms = matmul(upstream_t, picked)
    for o in range(octants):
        for start in range(0, terms.shape[0], LANES):
            block = terms[start : start + LANES, o * LANES : (o + 1) * LANES]
            terms_ref[row : row + LANES, :] = jnp.transpose(block).astype(BF16)
            row += LANES
    total = matmul(picked, down_ref[...].reshape(octants * LANES, down_ref.shape[2]))
    terms_ref[row:, :] = jnp.zeros((terms_ref.shape[0] - row, LANES), BF16)
    coarse_ref[...] = total.astype(BF16)
    send_ref[...] = terms_ref[pl.ds(my_half(send_ref.shape[0])[1], send_ref.shape[0]), :]


def pair_kernel(terms_ref, other_ref, out_ref):
    rows = other_ref.shape[0]
    mine = terms_ref[pl.ds(my_half(rows)[0], rows), :].astype(F32)
    out_ref[...] = (mine + other_ref[...].astype(F32)).astype(BF16)


def sum_kernel(devices, scale, parts_ref, after_ref, out_ref):
    rows = parts_ref.shape[0] // devices
    for core in range(2):
        mine = range(core, devices, 2)
        total = jnp.zeros((rows, LANES), F32)
        for d in mine:
            total = total + parts_ref[d * rows : (d + 1) * rows, :].astype(F32)
        total = (total * scale).astype(BF16)
        for d in mine:
            out_ref[d * rows : (d + 1) * rows, :] = total


def final_kernel(mine_ref, other_ref, conv_ref, down_ref, whole_ref):
    rows = mine_ref.shape[0]
    mine, other = my_half(rows)
    whole_ref[pl.ds(mine, rows), :] = mine_ref[...]
    whole_ref[pl.ds(other, rows), :] = other_ref[...]
    row = conv_ref.shape[0]
    conv_ref[...] = whole_ref[0:row, :].astype(F32)
    for first in range(0, down_ref.shape[0], LANES):
        for start in range(0, down_ref.shape[1], LANES):
            block = whole_ref[row : row + LANES, :].astype(F32)
            down_ref[first : first + LANES, start : start + LANES] = block
            row += LANES


def tail_kernel(slots, *refs):
    received = refs[:slots]
    hgrad_ref, back_ref, halo_ref, out_ref = refs[slots:]
    voxels = hgrad_ref.shape[0]
    total = hgrad_ref[...] + back_ref[...]
    lists = encode(halo_ref[...]).astype(BF16)
    for s, block in enumerate(to_slots([r[...] for r in received], True)):
        total = total + matmul(one_hot_columns(lists[s : s + 1, :], voxels), block)
    out_ref[...] = total


def call(kernel, operands, outs, scratch=(), limit=32, flops=0, in_hbm=()):
    spaces = [pl.ANY if n in in_hbm else pltpu.VMEM for n in range(len(operands))]
    return pl.pallas_call(
        kernel,
        out_shape=[jax.ShapeDtypeStruct(s, d) for s, d in outs],
        in_specs=[pl.BlockSpec(memory_space=space) for space in spaces],
        out_specs=[pl.BlockSpec(memory_space=pltpu.VMEM) for _ in outs],
        scratch_shapes=list(scratch),
        compiler_params=pltpu.CompilerParams(vmem_limit_bytes=limit * 2**20),
        cost_estimate=pl.CostEstimate(flops=flops, bytes_accessed=4 * 2**20, transcendentals=0),
    )(*operands)


def swap_cores(value, devices):
    return lax.ppermute(value, "shard", [(i, i + 1 - 2 * (i % 2)) for i in range(devices)])


def exchange(value):
    return lax.all_to_all(value, "shard", 0, 0, tiled=True)


def local(
    features, conv_weight, down_weight, neighbour_map, halo_rows, child_map, child_rows, out_grad
):
    voxels, channels = features.shape
    parents, coarse_channels = out_grad.shape
    kernel_count = conv_weight.shape[0]
    octants = down_weight.shape[0]
    slots, cap = halo_rows.shape
    cap2 = child_rows.shape[1]
    reach = slots // 2
    devices = lax.axis_size("shard")
    scale = 1.0 / math.sqrt(voxels * devices)
    giga = 10**9

    first = call(
        head_kernel,
        (features, halo_rows, child_map, out_grad, down_weight),
        [((cap + cap2, channels), BF16)] * slots + [((voxels, channels), F32)],
        scratch=[
            pltpu.VMEM(value.shape, value.dtype)
            for value in (features, halo_rows, child_map, out_grad, down_weight)
        ]
        + [pltpu.SemaphoreType.DMA((5,))],
        limit=60,
        flops=giga,
        in_hbm=range(5),
    )
    back_h = first[-1]
    received = swaps(first[:-1], reach)
    conv_rows = kernel_count * channels
    down_rows = octants * channels * coarse_channels // LANES
    grain = 8 * devices
    half_rows = -(-(conv_rows + down_rows) // (2 * grain)) * grain
    hidden, hidden_grad, pre_grad, conv_terms, *leaving = call(
        functools.partial(forward_kernel, slots),
        (*received, features, neighbour_map, conv_weight, child_rows, back_h),
        [
            ((voxels, channels), BF16),
            ((voxels, channels), F32),
            ((voxels, channels), BF16),
            ((conv_rows, channels), BF16),
        ]
        + [((cap2, channels), BF16)] * slots,
        scratch=[
            pltpu.VMEM((voxels // 2 + slots * cap // 2, 2 * channels), BF16),
            pltpu.VMEM((kernel_count, voxels, channels), BF16),
            pltpu.VMEM((voxels, channels), F32),
            pltpu.VMEM((voxels, channels), F32),
            pltpu.SemaphoreType.DMA(()),
        ]
        + [pltpu.VMEM((2, voxels, (voxels + slots * cap) // 2), BF16)] * 2
        + [pltpu.VMEM((2, voxels, LANES), BF16)] * 2,
        limit=48,
        flops=12 * giga,
        in_hbm=(slots + 4,),
    )
    received_h = swaps(leaving, reach)
    coarse, terms, leaving_terms = call(
        functools.partial(down_kernel, slots),
        (*received_h, hidden, child_map, down_weight, out_grad, conv_terms),
        [
            ((parents, coarse_channels), BF16),
            ((2 * half_rows, LANES), BF16),
            ((half_rows, LANES), BF16),
        ],
        scratch=[pltpu.VMEM((-(-(voxels + slots * cap2) // 256) * 128, 2 * channels), BF16)],
        flops=2 * giga,
    )
    (pair_terms,) = call(
        pair_kernel,
        (terms, swap_cores(leaving_terms, devices)),
        [((half_rows, LANES), BF16)],
        flops=10**6,
    )
    parts = exchange(pair_terms)
    spread = call(
        functools.partial(spread_kernel, slots),
        (pre_grad, neighbour_map, conv_weight, pair_terms),
        [((voxels, channels), F32)] + [((cap, channels), BF16)] * slots,
        scratch=[pltpu.VMEM((voxels // 2 + slots * cap // 2, 2 * channels), F32)],
        flops=20 * giga,
        in_hbm=(3,),
    )
    (summed,) = call(
        functools.partial(sum_kernel, devices, scale),
        (parts, spread[1]),
        [((half_rows, LANES), BF16)],
        flops=10**6,
        in_hbm=(1,),
    )
    summed, *returning = lax.optimization_barrier((summed, *spread[1:]))
    mine, *returned = lax.optimization_barrier((exchange(summed), *swaps(returning, reach)))
    (input_grad,) = call(
        functools.partial(tail_kernel, slots),
        (*returned, hidden_grad, spread[0], halo_rows),
        [((voxels, channels), F32)],
        flops=giga,
    )
    conv_grad, down_grad = call(
        final_kernel,
        (mine, swap_cores(mine, devices)),
        [((conv_rows, LANES), F32), ((octants * channels, coarse_channels), F32)],
        scratch=[pltpu.VMEM((2 * half_rows, LANES), BF16)],
        flops=10**6,
    )
    conv_grad = conv_grad.reshape(conv_weight.shape)
    return (coarse, input_grad, conv_grad, down_grad.reshape(down_weight.shape))


def solution(mesh):
    return jax.shard_map(
        local,
        mesh=mesh,
        in_specs=(
            P("shard", None),
            P(),
            P(),
            P(None, "shard"),
            P(None, "shard"),
            P(None, "shard"),
            P(None, "shard"),
            P("shard", None),
        ),
        out_specs=(P("shard", None), P("shard", None), P(), P()),
        check_vma=False,
    )
```

```python
import functools
import math

import jax
import jax.numpy as jnp
from jax import lax
from jax.experimental import pallas as pl
from jax.experimental.pallas import tpu as pltpu
from jax.sharding import PartitionSpec as P

BF16 = jnp.bfloat16
F32 = jnp.float32
LANES = 128


def swaps(by_step, order):
    devices = lax.axis_size("shard")
    moved = {}
    for step in order:
        m, phase = step // 2 + 1, step % 2
        sign = [1 if (i // m) % 2 == phase else -1 for i in range(devices)]
        pairs = [(i, i + m * sign[i]) for i in range(devices) if 0 <= i + m * sign[i] < devices]
        moved[step] = lax.ppermute(by_step[step], "shard", pairs)
    return [moved[step] for step in range(len(by_step))]


def is_even(m):
    return lax.rem(lax.div(lax.axis_index("shard"), m), 2) == 0


def to_steps(slots, back):
    reach = len(slots) // 2
    steps = []
    for m in range(1, reach + 1):
        first, second = slots[reach + m - 1], slots[reach - m]
        if back:
            first, second = second, first
        steps.append(lax.select(is_even(m), first, second))
        steps.append(lax.select(is_even(m), second, first))
    return steps


def to_slots(steps, back):
    reach = len(steps) // 2
    slots = [None] * len(steps)
    for m in range(1, reach + 1):
        first = lax.select(is_even(m), steps[2 * m - 2], steps[2 * m - 1])
        second = lax.select(is_even(m), steps[2 * m - 1], steps[2 * m - 2])
        if back:
            first, second = second, first
        slots[reach - m], slots[reach + m - 1] = first, second
    return slots


def matmul(left, right):
    return jnp.dot(left, right, preferred_element_type=F32)


def matmul_rt(left, right):
    return lax.dot_general(left, right, (((1,), (1,)), ((), ())), preferred_element_type=F32)


def pick_one(mask):
    return jnp.where(mask, jnp.ones(mask.shape, BF16), jnp.zeros(mask.shape, BF16))


def encode(row):
    return jnp.left_shift((row & (LANES - 1)) + LANES, row >> 7).astype(F32)


def column(codes):
    pieces = []
    for start in range(0, codes.shape[1], LANES):
        piece = jnp.broadcast_to(codes[:, start : start + LANES], (LANES, LANES))
        pieces.append(jnp.transpose(piece))
    return pieces[0] if len(pieces) == 1 else jnp.concatenate(pieces, axis=0)


def one_hot_rows(col, width):
    lane = lax.broadcasted_iota(jnp.int32, (16, LANES), 1)
    blocks = []
    for start in range(0, width, LANES):
        pattern = jnp.broadcast_to(encode(lane + start).astype(BF16)[0:1], col.shape)
        blocks.append(pick_one(col == pattern))
    return jnp.concatenate(blocks, axis=1)


def one_hot_columns(codes, height):
    place = lax.broadcasted_iota(jnp.int32, (height, codes.shape[1]), 0)
    pattern = encode(place).astype(BF16)
    return pick_one(jnp.broadcast_to(codes, pattern.shape) == pattern)


def pick_rows(col, table):
    both = matmul(one_hot_rows(jnp.abs(col), table.shape[0]), table).astype(BF16)
    return jnp.where(col < jnp.zeros(col.shape, BF16), both[:, LANES:], both[:, :LANES])


def list_row(lists, first, per_row):
    pieces = [lists[first + n : first + n + 1, :] for n in range(per_row)]
    return pieces[0] if per_row == 1 else jnp.concatenate(pieces, axis=1)


def add_lists(total, lists_ref, blocks):
    slots, cap = lists_ref.shape
    codes = encode(lists_ref[...]).astype(F32)
    per_row = max(1, min(slots, LANES // cap))
    for first in range(0, slots, per_row):
        row = list_row(codes, first, per_row).astype(BF16)
        rows = jnp.concatenate(blocks[first : first + per_row], axis=0)
        total = total + matmul(one_hot_columns(row, total.shape[0]), rows)
    return total


def gather_lists(lists_ref, table):
    slots, cap = lists_ref.shape
    lists = lists_ref[...]
    per_row = max(1, min(slots, LANES // cap))
    parts = []
    for first in range(0, slots, per_row):
        codes = encode(list_row(lists, first, per_row))
        chooser = one_hot_rows(column(codes).astype(BF16), table.shape[0])
        parts.append(matmul(chooser, table))
    return parts[0] if len(parts) == 1 else jnp.concatenate(parts, axis=0)


def head_kernel(features_hbm, halo_hbm, child_map_hbm, out_grad_hbm, down_hbm, *refs):
    sources = (features_hbm, halo_hbm, child_map_hbm, out_grad_hbm, down_hbm)
    buffers, sems = refs[-len(sources) - 1 : -1], refs[-1]
    features_ref, halo_ref, child_map_ref, out_grad_ref, down_ref = buffers
    copies = [
        pltpu.make_async_copy(source, buffer, sems.at[n])
        for n, (source, buffer) in enumerate(zip(sources, buffers))
    ]
    for copy in copies:
        copy.start()
    outs = refs[: -len(sources) - 1]
    sends, back_ref = outs[:-1], outs[-1]
    slots, cap = halo_ref.shape
    voxels = features_ref.shape[0]
    octants = child_map_ref.shape[0]
    table_rows = voxels + slots * (sends[0].shape[0] - cap)
    cap2 = (table_rows - voxels) // slots
    copies[0].wait()
    copies[1].wait()
    listed = gather_lists(halo_ref, features_ref[...]).astype(BF16)
    for send, block in zip(sends, to_steps(jnp.split(listed, slots), False)):
        send[0:cap, :] = block
    for copy in copies[2:]:
        copy.wait()
    upstream = out_grad_ref[...]
    codes = encode(child_map_ref[...]).astype(BF16)
    choosers, parts = [], []
    for o in range(octants):
        part = matmul_rt(upstream, down_ref[o])
        high = part.astype(BF16)
        low = (part - high.astype(F32)).astype(BF16)
        choosers.append(one_hot_columns(codes[o : o + 1, :], table_rows))
        parts.append(jnp.concatenate([high, low], axis=1))
    both = matmul(jnp.concatenate(choosers, axis=1), jnp.concatenate(parts, axis=0))
    total = both[:, :LANES] + both[:, LANES:]
    back_ref[...] = total[:voxels]
    for send, block in zip(sends, to_steps(jnp.split(total[voxels:].astype(BF16), slots), True)):
        send[cap : cap + cap2, :] = block


def half_codes(row, voxels, received):
    half, half_received = voxels // 2, received // 2
    beyond = row - voxels
    outside = beyond >= 0
    near = row - jnp.where(row >= half, half, 0)
    far = half + beyond - jnp.where(beyond >= half_received, half_received, 0)
    code = encode(jnp.where(outside, far, near))
    near_sign = jnp.where(row >= half, -1.0, 1.0)
    far_sign = jnp.where(beyond >= half_received, -1.0, 1.0)
    return code * jnp.where(outside, far_sign, near_sign)


def forward_kernel(slots, *refs):
    received = refs[:slots]
    features_ref, map_ref, weight_ref, child_ref = refs[slots : slots + 4]
    hidden_ref, pre_ref, stacked_ref = refs[slots + 4 : slots + 7]
    sends = refs[slots + 7 : 2 * slots + 7]
    table_ref, acc_ref = refs[2 * slots + 7 : 2 * slots + 9]
    chooser_refs, col_refs = refs[2 * slots + 9 : 2 * slots + 11], refs[2 * slots + 11 :]
    voxels = features_ref.shape[0]
    kernel_count = map_ref.shape[0]
    middle = kernel_count // 2
    cap2 = child_ref.shape[1]
    cap = received[0].shape[0] - cap2
    half, half_halo = voxels // 2, slots * cap // 2
    features = features_ref[...]
    table_ref[0:half, 0:LANES] = features[0:half]
    table_ref[0:half, LANES : 2 * LANES] = features[half:voxels]
    for s, block in enumerate(to_slots([r[0:cap, :] for r in received], False)):
        place = half + (s % (slots // 2)) * cap
        side = (s // (slots // 2)) * LANES
        table_ref[place : place + cap, side : side + LANES] = block
    table_rows = half + half_halo

    def build(j, side):
        for n, k in enumerate((j, j + middle + 1)):
            codes = half_codes(map_ref[pl.ds(k, 1), :], voxels, slots * cap).astype(BF16)
            col = column(codes)
            col_refs[side][n] = col
            chooser_refs[side][n] = one_hot_rows(jnp.abs(col), table_rows)

    def use(j, side):
        pair = []
        for n, k in enumerate((j, j + middle + 1)):
            both = matmul(chooser_refs[side][n], table_ref[...]).astype(BF16)
            right = col_refs[side][n] < jnp.zeros((voxels, LANES), BF16)
            pair.append(jnp.where(right, both[:, LANES:], both[:, :LANES]))
            stacked_ref[k] = pair[n]
        return pair

    def convolve(j, pair):
        kernel = jnp.concatenate([weight_ref[j], weight_ref[j + middle + 1]], axis=0)
        acc_ref[...] += matmul(jnp.concatenate(pair, axis=1), kernel)

    acc_ref[...] = matmul(features, weight_ref[middle])
    build(0, 0)

    def step(i, carry):
        for side in range(2):
            j = 2 * i + side
            pair = use(j, side)
            build(j + 1, 1 - side)
            convolve(j, pair)
        return carry

    lax.fori_loop(0, middle // 2, step, 0)
    convolve(middle - 1, use(middle - 1, 0))
    pre = acc_ref[...]
    pre_ref[...] = pre
    hidden = (features.astype(F32) + pre * jax.nn.sigmoid(pre)).astype(BF16)
    hidden_ref[...] = hidden
    leaving = gather_lists(child_ref, hidden).astype(BF16)
    for send, block in zip(sends, to_steps(jnp.split(leaving, slots), False)):
        send[...] = block


def gradient_kernel(slots, *refs):
    received = refs[:slots]
    stacked_ref, pre_ref, features_ref, child_ref, back_ref = refs[slots : slots + 5]
    hgrad_ref, pgrad_ref, cgrad_ref = refs[slots + 5 :]
    cap2 = child_ref.shape[1]
    cap = received[0].shape[0] - cap2
    middle = stacked_ref.shape[0] // 2
    blocks = to_slots([r[cap : cap + cap2, :] for r in received], True)
    hgrad = add_lists(back_ref[...], child_ref, blocks)
    hgrad_ref[...] = hgrad
    pre = pre_ref[...]
    sig = jax.nn.sigmoid(pre)
    pgrad = hgrad * (sig * (1.0 + pre * (1.0 - sig)))
    pgrad_ref[...] = pgrad.astype(BF16)
    pgrad_t = jnp.transpose(pgrad).astype(BF16)

    def put(k, value):
        cgrad_ref[k * LANES : (k + 1) * LANES, :] = jnp.transpose(value).astype(BF16)

    put(middle, matmul(pgrad_t, features_ref[...]))
    for j in range(middle):
        pair = jnp.concatenate([stacked_ref[j], stacked_ref[j + middle + 1]], axis=1)
        both = matmul(pgrad_t, pair)
        put(j, both[:, :LANES])
        put(j + middle + 1, both[:, LANES:])


def spread_kernel(slots, pgrad_ref, map_ref, weight_ref, after_ref, back_ref, *sends):
    acc_ref = sends[-1]
    sends = sends[:-1]
    voxels = pgrad_ref.shape[0]
    kernel_count = map_ref.shape[0]
    middle = kernel_count // 2
    cap = sends[0].shape[0]
    half = voxels // 2
    table_rows = half + slots * cap // 2
    pgrad = pgrad_ref[...]
    own = matmul_rt(pgrad, weight_ref[middle])
    acc_ref[0:half, 0:LANES] = own[0:half]
    acc_ref[0:half, LANES:] = own[half:]
    acc_ref[half:, :] = jnp.zeros((table_rows - half, 2 * LANES), F32)

    def parts(k):
        codes = half_codes(map_ref[pl.ds(k, 1), :], voxels, slots * cap)
        terms = matmul_rt(pgrad, weight_ref[k])
        right = column(codes) < 0.0
        sides = [jnp.where(right, 0.0, terms), jnp.where(right, terms, 0.0)]
        chooser = one_hot_columns(jnp.abs(codes).astype(BF16), table_rows)
        return chooser, jnp.concatenate(sides, axis=1).astype(BF16)

    def step(j, carry):
        near_chooser, near_terms = parts(j)
        far_chooser, far_terms = parts(j + middle + 1)
        acc_ref[...] += matmul(near_chooser, near_terms) + matmul(far_chooser, far_terms)
        return carry

    lax.fori_loop(0, middle, step, 0)
    back_ref[0:half, :] = acc_ref[0:half, 0:LANES]
    back_ref[half:, :] = acc_ref[0:half, LANES:]
    blocks = []
    for s in range(slots):
        first = half + (s % (slots // 2)) * cap
        side = (s // (slots // 2)) * LANES
        blocks.append(acc_ref[first : first + cap, side : side + LANES].astype(BF16))
    for send, block in zip(sends, to_steps(blocks, True)):
        send[...] = block


def my_half(rows):
    core = lax.rem(lax.axis_index("shard"), 2)
    return pl.multiple_of(core * rows, 16), pl.multiple_of((1 - core) * rows, 16)


def down_kernel(slots, *refs):
    received = refs[:slots]
    (hidden_ref, map_ref, down_ref, out_grad_ref, cgrad_ref) = refs[slots : slots + 5]
    coarse_ref, terms_ref, send_ref, table_ref = refs[slots + 5 :]
    voxels = hidden_ref.shape[0]
    cap2 = received[0].shape[0]
    half, half_halo = voxels // 2, slots * cap2 // 2
    blocks = to_slots([r[...] for r in received], False)
    table_ref[0:half, 0:LANES] = hidden_ref[0:half, :]
    table_ref[0:half, LANES:] = hidden_ref[half:, :]
    for s, block in enumerate(blocks):
        place = half + (s % (slots // 2)) * cap2
        side = (s // (slots // 2)) * LANES
        table_ref[place : place + cap2, side : side + LANES] = block
    padding = table_ref.shape[0] - half - half_halo
    table_ref[half + half_halo :, :] = jnp.zeros((padding, 2 * LANES), BF16)
    upstream = out_grad_ref[...]
    parents = upstream.shape[0]
    octants = map_ref.shape[0]
    upstream_t = jnp.transpose(upstream.astype(F32)).astype(BF16)
    codes = half_codes(map_ref[...], voxels, slots * cap2)
    col = jnp.concatenate([column(codes[o : o + 1, :]) for o in range(octants)], axis=0)
    picked = pick_rows(col.astype(BF16), table_ref[...])
    picked = jnp.concatenate(jnp.split(picked, octants), axis=1)
    row = cgrad_ref.shape[0]
    terms_ref[0:row, :] = cgrad_ref[...]
    terms = matmul(upstream_t, picked)
    for o in range(octants):
        for start in range(0, terms.shape[0], LANES):
            block = terms[start : start + LANES, o * LANES : (o + 1) * LANES]
            terms_ref[row : row + LANES, :] = jnp.transpose(block).astype(BF16)
            row += LANES
    total = matmul(picked, down_ref[...].reshape(octants * LANES, down_ref.shape[2]))
    terms_ref[row:, :] = jnp.zeros((terms_ref.shape[0] - row, LANES), BF16)
    coarse_ref[...] = total.astype(BF16)
    send_ref[...] = terms_ref[pl.ds(my_half(send_ref.shape[0])[1], send_ref.shape[0]), :]


def pair_kernel(terms_ref, other_ref, out_ref):
    rows = other_ref.shape[0]
    mine = terms_ref[pl.ds(my_half(rows)[0], rows), :].astype(F32)
    out_ref[...] = (mine + other_ref[...].astype(F32)).astype(BF16)


def sum_kernel(devices, scale, parts_ref, after_ref, out_ref):
    rows = parts_ref.shape[0] // devices
    for core in range(2):
        mine = range(core, devices, 2)
        total = jnp.zeros((rows, LANES), F32)
        for d in mine:
            total = total + parts_ref[d * rows : (d + 1) * rows, :].astype(F32)
        total = (total * scale).astype(BF16)
        for d in mine:
            out_ref[d * rows : (d + 1) * rows, :] = total


def final_kernel(mine_ref, other_ref, conv_ref, down_ref, whole_ref):
    rows = mine_ref.shape[0]
    mine, other = my_half(rows)
    whole_ref[pl.ds(mine, rows), :] = mine_ref[...]
    whole_ref[pl.ds(other, rows), :] = other_ref[...]
    row = conv_ref.shape[0]
    conv_ref[...] = whole_ref[0:row, :].astype(F32)
    for first in range(0, down_ref.shape[0], LANES):
        for start in range(0, down_ref.shape[1], LANES):
            block = whole_ref[row : row + LANES, :].astype(F32)
            down_ref[first : first + LANES, start : start + LANES] = block
            row += LANES


def tail_kernel(slots, *refs):
    received = refs[:slots]
    hgrad_ref, back_ref, halo_ref, out_ref = refs[slots:]
    blocks = to_slots([r[...] for r in received], True)
    out_ref[...] = add_lists(hgrad_ref[...] + back_ref[...], halo_ref, blocks)


def call(kernel, operands, outs, scratch=(), limit=32, flops=0, in_hbm=()):
    spaces = [pl.ANY if n in in_hbm else pltpu.VMEM for n in range(len(operands))]
    return pl.pallas_call(
        kernel,
        out_shape=[jax.ShapeDtypeStruct(s, d) for s, d in outs],
        in_specs=[pl.BlockSpec(memory_space=space) for space in spaces],
        out_specs=[pl.BlockSpec(memory_space=pltpu.VMEM) for _ in outs],
        scratch_shapes=list(scratch),
        compiler_params=pltpu.CompilerParams(vmem_limit_bytes=limit * 2**20),
        cost_estimate=pl.CostEstimate(flops=flops, bytes_accessed=4 * 2**20, transcendentals=0),
    )(*operands)


def swap_cores(value, devices):
    return lax.ppermute(value, "shard", [(i, i + 1 - 2 * (i % 2)) for i in range(devices)])


def exchange(value):
    return lax.all_to_all(value, "shard", 0, 0, tiled=True)


def local(
    features, conv_weight, down_weight, neighbour_map, halo_rows, child_map, child_rows, out_grad
):
    voxels, channels = features.shape
    parents, coarse_channels = out_grad.shape
    kernel_count = conv_weight.shape[0]
    octants = down_weight.shape[0]
    slots, cap = halo_rows.shape
    cap2 = child_rows.shape[1]
    devices = lax.axis_size("shard")
    scale = 1.0 / math.sqrt(voxels * devices)
    giga = 10**9

    first = call(
        head_kernel,
        (features, halo_rows, child_map, out_grad, down_weight),
        [((cap + cap2, channels), BF16)] * slots + [((voxels, channels), F32)],
        scratch=[
            pltpu.VMEM(value.shape, value.dtype)
            for value in (features, halo_rows, child_map, out_grad, down_weight)
        ]
        + [pltpu.SemaphoreType.DMA((5,))],
        limit=60,
        flops=giga,
        in_hbm=range(5),
    )
    back_h = first[-1]
    received = swaps(first[:-1], (2, 3, 1, 0))
    conv_rows = kernel_count * channels
    down_rows = octants * channels * coarse_channels // LANES
    grain = 8 * devices
    half_rows = -(-(conv_rows + down_rows) // (2 * grain)) * grain
    hidden, pre_act, stacked, *leaving = call(
        functools.partial(forward_kernel, slots),
        (*received, features, neighbour_map, conv_weight, child_rows),
        [
            ((voxels, channels), BF16),
            ((voxels, channels), F32),
            ((kernel_count, voxels, channels), BF16),
        ]
        + [((cap2, channels), BF16)] * slots,
        scratch=[
            pltpu.VMEM((voxels // 2 + slots * cap // 2, 2 * channels), BF16),
            pltpu.VMEM((voxels, channels), F32),
        ]
        + [pltpu.VMEM((2, voxels, (voxels + slots * cap) // 2), BF16)] * 2
        + [pltpu.VMEM((2, voxels, LANES), BF16)] * 2,
        limit=32,
        flops=12 * giga,
    )
    hidden_grad, pre_grad, conv_terms = call(
        functools.partial(gradient_kernel, slots),
        (*received, stacked, pre_act, features, child_rows, back_h),
        [
            ((voxels, channels), F32),
            ((voxels, channels), BF16),
            ((conv_rows, channels), BF16),
        ],
        flops=3 * giga,
    )
    received_h = swaps(leaving, (1, 3, 2, 0))
    coarse, terms, leaving_terms = call(
        functools.partial(down_kernel, slots),
        (*received_h, hidden, child_map, down_weight, out_grad, conv_terms),
        [
            ((parents, coarse_channels), BF16),
            ((2 * half_rows, LANES), BF16),
            ((half_rows, LANES), BF16),
        ],
        scratch=[pltpu.VMEM((-(-(voxels + slots * cap2) // 256) * 128, 2 * channels), BF16)],
        flops=2 * giga,
    )
    (pair_terms,) = call(
        pair_kernel,
        (terms, swap_cores(leaving_terms, devices)),
        [((half_rows, LANES), BF16)],
        flops=10**6,
    )
    parts = exchange(pair_terms)
    spread = call(
        functools.partial(spread_kernel, slots),
        (pre_grad, neighbour_map, conv_weight, pair_terms),
        [((voxels, channels), F32)] + [((cap, channels), BF16)] * slots,
        scratch=[pltpu.VMEM((voxels // 2 + slots * cap // 2, 2 * channels), F32)],
        flops=20 * giga,
        in_hbm=(3,),
    )
    (summed,) = call(
        functools.partial(sum_kernel, devices, scale),
        (parts, spread[1]),
        [((half_rows, LANES), BF16)],
        flops=10**6,
        in_hbm=(1,),
    )
    summed, *returning = lax.optimization_barrier((summed, *spread[1:]))
    mine, *returned = lax.optimization_barrier((exchange(summed), *swaps(returning, (3, 1, 0, 2))))
    (input_grad,) = call(
        functools.partial(tail_kernel, slots),
        (*returned, hidden_grad, spread[0], halo_rows),
        [((voxels, channels), F32)],
        flops=giga,
    )
    conv_grad, down_grad = call(
        final_kernel,
        (mine, swap_cores(mine, devices)),
        [((conv_rows, LANES), F32), ((octants * channels, coarse_channels), F32)],
        scratch=[pltpu.VMEM((2 * half_rows, LANES), BF16)],
        flops=10**6,
    )
    conv_grad = conv_grad.reshape(conv_weight.shape)
    return (coarse, input_grad, conv_grad, down_grad.reshape(down_weight.shape))


def solution(mesh):
    return jax.shard_map(
        local,
        mesh=mesh,
        in_specs=(
            P("shard", None),
            P(),
            P(),
            P(None, "shard"),
            P(None, "shard"),
            P(None, "shard"),
            P(None, "shard"),
            P("shard", None),
        ),
        out_specs=(P("shard", None), P("shard", None), P(), P()),
        check_vma=False,
    )
```

```python
import functools
import math

import jax
import jax.numpy as jnp
from jax import lax
from jax.experimental import pallas as pl
from jax.experimental.pallas import tpu as pltpu
from jax.sharding import PartitionSpec as P

BF16 = jnp.bfloat16
F32 = jnp.float32
LANES = 128


def swaps(by_step, order):
    devices = lax.axis_size("shard")
    moved = {}
    for step in order:
        m, phase = step // 2 + 1, step % 2
        sign = [1 if (i // m) % 2 == phase else -1 for i in range(devices)]
        pairs = [(i, i + m * sign[i]) for i in range(devices) if 0 <= i + m * sign[i] < devices]
        moved[step] = lax.ppermute(by_step[step], "shard", pairs)
    return [moved[step] for step in range(len(by_step))]


def is_even(m):
    return lax.rem(lax.div(lax.axis_index("shard"), m), 2) == 0


def to_steps(slots, back):
    reach = len(slots) // 2
    steps = []
    for m in range(1, reach + 1):
        first, second = slots[reach + m - 1], slots[reach - m]
        if back:
            first, second = second, first
        steps.append(lax.select(is_even(m), first, second))
        steps.append(lax.select(is_even(m), second, first))
    return steps


def to_slots(steps, back):
    reach = len(steps) // 2
    slots = [None] * len(steps)
    for m in range(1, reach + 1):
        first = lax.select(is_even(m), steps[2 * m - 2], steps[2 * m - 1])
        second = lax.select(is_even(m), steps[2 * m - 1], steps[2 * m - 2])
        if back:
            first, second = second, first
        slots[reach - m], slots[reach + m - 1] = first, second
    return slots


def matmul(left, right):
    return jnp.dot(left, right, preferred_element_type=F32)


def matmul_rt(left, right):
    return lax.dot_general(left, right, (((1,), (1,)), ((), ())), preferred_element_type=F32)


def pick_one(mask):
    return jnp.where(mask, jnp.ones(mask.shape, BF16), jnp.zeros(mask.shape, BF16))


def encode(row):
    return jnp.left_shift((row & (LANES - 1)) + LANES, row >> 7).astype(F32)


def column(codes):
    pieces = []
    for start in range(0, codes.shape[1], LANES):
        piece = jnp.broadcast_to(codes[:, start : start + LANES], (LANES, LANES))
        pieces.append(jnp.transpose(piece))
    return pieces[0] if len(pieces) == 1 else jnp.concatenate(pieces, axis=0)


def one_hot_rows(col, width):
    lane = lax.broadcasted_iota(jnp.int32, (16, LANES), 1)
    blocks = []
    for start in range(0, width, LANES):
        pattern = jnp.broadcast_to(encode(lane + start).astype(BF16)[0:1], col.shape)
        blocks.append(pick_one(col == pattern))
    return jnp.concatenate(blocks, axis=1)


def one_hot_columns(codes, height):
    place = lax.broadcasted_iota(jnp.int32, (height, codes.shape[1]), 0)
    pattern = encode(place).astype(BF16)
    return pick_one(jnp.broadcast_to(codes, pattern.shape) == pattern)


def pick_rows(col, table):
    both = matmul(one_hot_rows(jnp.abs(col), table.shape[0]), table).astype(BF16)
    return jnp.where(col < jnp.zeros(col.shape, BF16), both[:, LANES:], both[:, :LANES])


def list_row(lists, first, per_row):
    pieces = [lists[first + n : first + n + 1, :] for n in range(per_row)]
    return pieces[0] if per_row == 1 else jnp.concatenate(pieces, axis=1)


def add_lists(total, lists_ref, blocks):
    slots, cap = lists_ref.shape
    codes = encode(lists_ref[...]).astype(F32)
    per_row = max(1, min(slots, LANES // cap))
    for first in range(0, slots, per_row):
        row = list_row(codes, first, per_row).astype(BF16)
        rows = jnp.concatenate(blocks[first : first + per_row], axis=0)
        total = total + matmul(one_hot_columns(row, total.shape[0]), rows)
    return total


def gather_lists(lists_ref, table):
    slots, cap = lists_ref.shape
    lists = lists_ref[...]
    per_row = max(1, min(slots, LANES // cap))
    parts = []
    for first in range(0, slots, per_row):
        codes = encode(list_row(lists, first, per_row))
        chooser = one_hot_rows(column(codes).astype(BF16), table.shape[0])
        parts.append(matmul(chooser, table))
    return parts[0] if len(parts) == 1 else jnp.concatenate(parts, axis=0)


def head_kernel(features_hbm, halo_hbm, child_map_hbm, out_grad_hbm, down_hbm, *refs):
    sources = (features_hbm, halo_hbm, child_map_hbm, out_grad_hbm, down_hbm)
    buffers, sems = refs[-len(sources) - 1 : -1], refs[-1]
    features_ref, halo_ref, child_map_ref, out_grad_ref, down_ref = buffers
    copies = [
        pltpu.make_async_copy(source, buffer, sems.at[n])
        for n, (source, buffer) in enumerate(zip(sources, buffers))
    ]
    for copy in copies:
        copy.start()
    outs = refs[: -len(sources) - 1]
    sends, back_ref = outs[:-1], outs[-1]
    slots, cap = halo_ref.shape
    voxels = features_ref.shape[0]
    octants = child_map_ref.shape[0]
    table_rows = voxels + slots * (sends[0].shape[0] - cap)
    cap2 = (table_rows - voxels) // slots
    copies[0].wait()
    copies[1].wait()
    listed = gather_lists(halo_ref, features_ref[...]).astype(BF16)
    for send, block in zip(sends, to_steps(jnp.split(listed, slots), False)):
        send[0:cap, :] = block
    for copy in copies[2:]:
        copy.wait()
    upstream = out_grad_ref[...]
    codes = encode(child_map_ref[...]).astype(BF16)
    choosers, parts = [], []
    for o in range(octants):
        part = matmul_rt(upstream, down_ref[o])
        high = part.astype(BF16)
        low = (part - high.astype(F32)).astype(BF16)
        choosers.append(one_hot_columns(codes[o : o + 1, :], table_rows))
        parts.append(jnp.concatenate([high, low], axis=1))
    both = matmul(jnp.concatenate(choosers, axis=1), jnp.concatenate(parts, axis=0))
    total = both[:, :LANES] + both[:, LANES:]
    back_ref[...] = total[:voxels]
    for send, block in zip(sends, to_steps(jnp.split(total[voxels:].astype(BF16), slots), True)):
        send[cap : cap + cap2, :] = block


def half_codes(row, voxels, received):
    half, half_received = voxels // 2, received // 2
    beyond = row - voxels
    outside = beyond >= 0
    near = row - jnp.where(row >= half, half, 0)
    far = half + beyond - jnp.where(beyond >= half_received, half_received, 0)
    code = encode(jnp.where(outside, far, near))
    near_sign = jnp.where(row >= half, -1.0, 1.0)
    far_sign = jnp.where(beyond >= half_received, -1.0, 1.0)
    return code * jnp.where(outside, far_sign, near_sign)


def offset_of(n, middle):
    return n + jnp.where(n >= middle, 1, 0)


def turn_kernel(features_ref, weight_ref, features_t_ref, weight_t_ref):
    kernel_count = weight_ref.shape[0]
    middle = kernel_count // 2
    for first in range(0, features_ref.shape[0], LANES):
        block = jnp.transpose(features_ref[first : first + LANES, :].astype(F32))
        features_t_ref[:, first : first + LANES] = block.astype(BF16)
    order = [k for k in range(kernel_count) if k != middle] + [middle]
    for n, k in enumerate(order):
        block = jnp.transpose(weight_ref[k].astype(F32))
        weight_t_ref[:, n * LANES : (n + 1) * LANES] = block.astype(BF16)


def forward_kernel(slots, *refs):
    received = refs[:slots]
    features_ref, features_t_ref, map_ref, weight_t_ref, child_ref = refs[slots : slots + 5]
    hidden_ref, pre_ref, stacked_ref = refs[slots + 5 : slots + 8]
    sends = refs[slots + 8 : 2 * slots + 8]
    table_ref, pattern_ref, *chooser_refs = refs[2 * slots + 8 :]
    voxels = features_ref.shape[0]
    gathers = map_ref.shape[0] - 1
    middle = gathers // 2
    cap2 = child_ref.shape[1]
    cap = received[0].shape[0] - cap2
    table_ref[:, 0:voxels] = features_t_ref[...]
    halo = jnp.concatenate(to_slots([r[0:cap, :] for r in received], False), axis=0)
    table_ref[:, voxels:] = jnp.transpose(halo.astype(F32)).astype(BF16)
    place = lax.broadcasted_iota(jnp.int32, pattern_ref.shape, 0)
    pattern_ref[...] = encode(place).astype(BF16)

    def build(n, side):
        k = offset_of(n, middle)
        codes = encode(map_ref[pl.ds(k, 1), :]).astype(BF16)
        for start in range(0, voxels, LANES):
            block = jnp.broadcast_to(codes[:, start : start + LANES], pattern_ref.shape)
            chooser_refs[side][:, start : start + LANES] = pick_one(block == pattern_ref[...])

    def use(n, side):
        rows = pl.ds(pl.multiple_of(n * LANES, LANES), LANES)
        stacked_ref[rows, :] = matmul(table_ref[...], chooser_refs[side][...]).astype(BF16)

    def step(i, carry):
        for side in range(2):
            n = 2 * i + side
            use(n, side)
            build(n + 1, 1 - side)
        return carry

    build(0, 0)
    lax.fori_loop(0, gathers // 2 - 1, step, 0)
    use(gathers - 2, 0)
    build(gathers - 1, 1)
    use(gathers - 1, 1)
    stacked_ref[gathers * LANES :, :] = features_t_ref[...]
    pre = jnp.transpose(matmul(weight_t_ref[...], stacked_ref[...]))
    pre_ref[...] = pre
    hidden = (features_ref[...].astype(F32) + pre * jax.nn.sigmoid(pre)).astype(BF16)
    hidden_ref[...] = hidden
    leaving = gather_lists(child_ref, hidden).astype(BF16)
    for send, block in zip(sends, to_steps(jnp.split(leaving, slots), False)):
        send[...] = block


def gradient_kernel(slots, *refs):
    received = refs[:slots]
    stacked_ref, pre_ref, child_ref, back_ref = refs[slots : slots + 4]
    hgrad_ref, pgrad_ref, cgrad_ref = refs[slots + 4 :]
    cap2 = child_ref.shape[1]
    cap = received[0].shape[0] - cap2
    blocks = to_slots([r[cap : cap + cap2, :] for r in received], True)
    hgrad = add_lists(back_ref[...], child_ref, blocks)
    hgrad_ref[...] = hgrad
    pre = pre_ref[...]
    sig = jax.nn.sigmoid(pre)
    pgrad = (hgrad * (sig * (1.0 + pre * (1.0 - sig)))).astype(BF16)
    pgrad_ref[...] = pgrad
    terms = matmul(stacked_ref[...], pgrad).astype(BF16)
    last = terms.shape[0] - LANES
    cgrad_ref[0 : last // 2, :] = terms[0 : last // 2]
    cgrad_ref[last // 2 : last // 2 + LANES, :] = terms[last:]
    cgrad_ref[last // 2 + LANES :, :] = terms[last // 2 : last]


def spread_kernel(slots, pgrad_ref, map_ref, weight_ref, after_ref, back_ref, *sends):
    acc_ref = sends[-1]
    sends = sends[:-1]
    voxels = pgrad_ref.shape[0]
    kernel_count = map_ref.shape[0]
    middle = kernel_count // 2
    cap = sends[0].shape[0]
    half = voxels // 2
    table_rows = half + slots * cap // 2
    pgrad = pgrad_ref[...]
    own = matmul_rt(pgrad, weight_ref[middle])
    acc_ref[0:half, 0:LANES] = own[0:half]
    acc_ref[0:half, LANES:] = own[half:]
    acc_ref[half:, :] = jnp.zeros((table_rows - half, 2 * LANES), F32)

    def parts(k):
        codes = half_codes(map_ref[pl.ds(k, 1), :], voxels, slots * cap)
        terms = matmul_rt(pgrad, weight_ref[k])
        right = column(codes) < 0.0
        sides = [jnp.where(right, 0.0, terms), jnp.where(right, terms, 0.0)]
        chooser = one_hot_columns(jnp.abs(codes).astype(BF16), table_rows)
        return chooser, jnp.concatenate(sides, axis=1).astype(BF16)

    def step(j, carry):
        near_chooser, near_terms = parts(j)
        far_chooser, far_terms = parts(j + middle + 1)
        acc_ref[...] += matmul(near_chooser, near_terms) + matmul(far_chooser, far_terms)
        return carry

    lax.fori_loop(0, middle, step, 0)
    back_ref[0:half, :] = acc_ref[0:half, 0:LANES]
    back_ref[half:, :] = acc_ref[0:half, LANES:]
    blocks = []
    for s in range(slots):
        first = half + (s % (slots // 2)) * cap
        side = (s // (slots // 2)) * LANES
        blocks.append(acc_ref[first : first + cap, side : side + LANES].astype(BF16))
    for send, block in zip(sends, to_steps(blocks, True)):
        send[...] = block


def my_half(rows):
    core = lax.rem(lax.axis_index("shard"), 2)
    return pl.multiple_of(core * rows, 16), pl.multiple_of((1 - core) * rows, 16)


def down_kernel(slots, *refs):
    received = refs[:slots]
    (hidden_ref, map_ref, down_ref, out_grad_ref, cgrad_ref) = refs[slots : slots + 5]
    coarse_ref, terms_ref, send_ref, table_ref = refs[slots + 5 :]
    voxels = hidden_ref.shape[0]
    cap2 = received[0].shape[0]
    half, half_halo = voxels // 2, slots * cap2 // 2
    blocks = to_slots([r[...] for r in received], False)
    table_ref[0:half, 0:LANES] = hidden_ref[0:half, :]
    table_ref[0:half, LANES:] = hidden_ref[half:, :]
    for s, block in enumerate(blocks):
        place = half + (s % (slots // 2)) * cap2
        side = (s // (slots // 2)) * LANES
        table_ref[place : place + cap2, side : side + LANES] = block
    padding = table_ref.shape[0] - half - half_halo
    table_ref[half + half_halo :, :] = jnp.zeros((padding, 2 * LANES), BF16)
    upstream = out_grad_ref[...]
    parents = upstream.shape[0]
    octants = map_ref.shape[0]
    upstream_t = jnp.transpose(upstream.astype(F32)).astype(BF16)
    codes = half_codes(map_ref[...], voxels, slots * cap2)
    col = jnp.concatenate([column(codes[o : o + 1, :]) for o in range(octants)], axis=0)
    picked = pick_rows(col.astype(BF16), table_ref[...])
    picked = jnp.concatenate(jnp.split(picked, octants), axis=1)
    row = cgrad_ref.shape[0]
    terms_ref[0:row, :] = cgrad_ref[...]
    terms = matmul(upstream_t, picked)
    for o in range(octants):
        for start in range(0, terms.shape[0], LANES):
            block = terms[start : start + LANES, o * LANES : (o + 1) * LANES]
            terms_ref[row : row + LANES, :] = jnp.transpose(block).astype(BF16)
            row += LANES
    total = matmul(picked, down_ref[...].reshape(octants * LANES, down_ref.shape[2]))
    terms_ref[row:, :] = jnp.zeros((terms_ref.shape[0] - row, LANES), BF16)
    coarse_ref[...] = total.astype(BF16)
    send_ref[...] = terms_ref[pl.ds(my_half(send_ref.shape[0])[1], send_ref.shape[0]), :]


def pair_kernel(terms_ref, other_ref, out_ref):
    rows = other_ref.shape[0]
    mine = terms_ref[pl.ds(my_half(rows)[0], rows), :].astype(F32)
    out_ref[...] = (mine + other_ref[...].astype(F32)).astype(BF16)


def sum_kernel(devices, scale, parts_ref, after_ref, out_ref):
    rows = parts_ref.shape[0] // devices
    for core in range(2):
        mine = range(core, devices, 2)
        total = jnp.zeros((rows, LANES), F32)
        for d in mine:
            total = total + parts_ref[d * rows : (d + 1) * rows, :].astype(F32)
        total = (total * scale).astype(BF16)
        for d in mine:
            out_ref[d * rows : (d + 1) * rows, :] = total


def final_kernel(mine_ref, other_ref, conv_ref, down_ref, whole_ref):
    rows = mine_ref.shape[0]
    mine, other = my_half(rows)
    whole_ref[pl.ds(mine, rows), :] = mine_ref[...]
    whole_ref[pl.ds(other, rows), :] = other_ref[...]
    row = conv_ref.shape[0]
    conv_ref[...] = whole_ref[0:row, :].astype(F32)
    for first in range(0, down_ref.shape[0], LANES):
        for start in range(0, down_ref.shape[1], LANES):
            block = whole_ref[row : row + LANES, :].astype(F32)
            down_ref[first : first + LANES, start : start + LANES] = block
            row += LANES


def tail_kernel(slots, *refs):
    received = refs[:slots]
    hgrad_ref, back_ref, halo_ref, out_ref = refs[slots:]
    blocks = to_slots([r[...] for r in received], True)
    out_ref[...] = add_lists(hgrad_ref[...] + back_ref[...], halo_ref, blocks)


def call(kernel, operands, outs, scratch=(), limit=32, flops=0, in_hbm=()):
    spaces = [pl.ANY if n in in_hbm else pltpu.VMEM for n in range(len(operands))]
    return pl.pallas_call(
        kernel,
        out_shape=[jax.ShapeDtypeStruct(s, d) for s, d in outs],
        in_specs=[pl.BlockSpec(memory_space=space) for space in spaces],
        out_specs=[pl.BlockSpec(memory_space=pltpu.VMEM) for _ in outs],
        scratch_shapes=list(scratch),
        compiler_params=pltpu.CompilerParams(vmem_limit_bytes=limit * 2**20),
        cost_estimate=pl.CostEstimate(flops=flops, bytes_accessed=4 * 2**20, transcendentals=0),
    )(*operands)


def swap_cores(value, devices):
    return lax.ppermute(value, "shard", [(i, i + 1 - 2 * (i % 2)) for i in range(devices)])


def exchange(value):
    return lax.all_to_all(value, "shard", 0, 0, tiled=True)


def local(
    features, conv_weight, down_weight, neighbour_map, halo_rows, child_map, child_rows, out_grad
):
    voxels, channels = features.shape
    parents, coarse_channels = out_grad.shape
    kernel_count = conv_weight.shape[0]
    octants = down_weight.shape[0]
    slots, cap = halo_rows.shape
    cap2 = child_rows.shape[1]
    devices = lax.axis_size("shard")
    scale = 1.0 / math.sqrt(voxels * devices)
    giga = 10**9

    first = call(
        head_kernel,
        (features, halo_rows, child_map, out_grad, down_weight),
        [((cap + cap2, channels), BF16)] * slots + [((voxels, channels), F32)],
        scratch=[
            pltpu.VMEM(value.shape, value.dtype)
            for value in (features, halo_rows, child_map, out_grad, down_weight)
        ]
        + [pltpu.SemaphoreType.DMA((5,))],
        limit=60,
        flops=giga,
        in_hbm=range(5),
    )
    back_h = first[-1]
    received = swaps(first[:-1], (2, 3, 1, 0))
    conv_rows = kernel_count * channels
    down_rows = octants * channels * coarse_channels // LANES
    grain = 8 * devices
    half_rows = -(-(conv_rows + down_rows) // (2 * grain)) * grain
    features_t, weight_t = call(
        turn_kernel,
        (features, conv_weight),
        [((channels, voxels), BF16), ((channels, conv_rows), BF16)],
        flops=giga,
    )
    hidden, pre_act, stacked, *leaving = call(
        functools.partial(forward_kernel, slots),
        (*received, features, features_t, neighbour_map, weight_t, child_rows),
        [
            ((voxels, channels), BF16),
            ((voxels, channels), F32),
            ((conv_rows, voxels), BF16),
        ]
        + [((cap2, channels), BF16)] * slots,
        scratch=[
            pltpu.VMEM((channels, voxels + slots * cap), BF16),
            pltpu.VMEM((voxels + slots * cap, LANES), BF16),
        ]
        + [pltpu.VMEM((voxels + slots * cap, voxels), BF16)] * 2,
        limit=32,
        flops=12 * giga,
    )
    hidden_grad, pre_grad, conv_terms = call(
        functools.partial(gradient_kernel, slots),
        (*received, stacked, pre_act, child_rows, back_h),
        [
            ((voxels, channels), F32),
            ((voxels, channels), BF16),
            ((conv_rows, channels), BF16),
        ],
        flops=3 * giga,
    )
    received_h = swaps(leaving, (1, 3, 2, 0))
    coarse, terms, leaving_terms = call(
        functools.partial(down_kernel, slots),
        (*received_h, hidden, child_map, down_weight, out_grad, conv_terms),
        [
            ((parents, coarse_channels), BF16),
            ((2 * half_rows, LANES), BF16),
            ((half_rows, LANES), BF16),
        ],
        scratch=[pltpu.VMEM((-(-(voxels + slots * cap2) // 256) * 128, 2 * channels), BF16)],
        flops=2 * giga,
    )
    (pair_terms,) = call(
        pair_kernel,
        (terms, swap_cores(leaving_terms, devices)),
        [((half_rows, LANES), BF16)],
        flops=10**6,
    )
    parts = exchange(pair_terms)
    spread = call(
        functools.partial(spread_kernel, slots),
        (pre_grad, neighbour_map, conv_weight, pair_terms),
        [((voxels, channels), F32)] + [((cap, channels), BF16)] * slots,
        scratch=[pltpu.VMEM((voxels // 2 + slots * cap // 2, 2 * channels), F32)],
        flops=20 * giga,
        in_hbm=(3,),
    )
    (summed,) = call(
        functools.partial(sum_kernel, devices, scale),
        (parts, spread[1]),
        [((half_rows, LANES), BF16)],
        flops=10**6,
        in_hbm=(1,),
    )
    summed, *returning = lax.optimization_barrier((summed, *spread[1:]))
    mine, *returned = lax.optimization_barrier((exchange(summed), *swaps(returning, (3, 1, 0, 2))))
    (input_grad,) = call(
        functools.partial(tail_kernel, slots),
        (*returned, hidden_grad, spread[0], halo_rows),
        [((voxels, channels), F32)],
        flops=giga,
    )
    conv_grad, down_grad = call(
        final_kernel,
        (mine, swap_cores(mine, devices)),
        [((conv_rows, LANES), F32), ((octants * channels, coarse_channels), F32)],
        scratch=[pltpu.VMEM((2 * half_rows, LANES), BF16)],
        flops=10**6,
    )
    conv_grad = conv_grad.reshape(conv_weight.shape)
    return (coarse, input_grad, conv_grad, down_grad.reshape(down_weight.shape))


def solution(mesh):
    return jax.shard_map(
        local,
        mesh=mesh,
        in_specs=(
            P("shard", None),
            P(),
            P(),
            P(None, "shard"),
            P(None, "shard"),
            P(None, "shard"),
            P(None, "shard"),
            P("shard", None),
        ),
        out_specs=(P("shard", None), P("shard", None), P(), P()),
        check_vma=False,
    )
```

```python
import functools
import math

import jax
import jax.numpy as jnp
from jax import lax
from jax.experimental import pallas as pl
from jax.experimental.pallas import tpu as pltpu
from jax.sharding import PartitionSpec as P

BF16 = jnp.bfloat16
F32 = jnp.float32
LANES = 128


def swaps(by_step, order):
    devices = lax.axis_size("shard")
    moved = {}
    for step in order:
        m, phase = step // 2 + 1, step % 2
        sign = [1 if (i // m) % 2 == phase else -1 for i in range(devices)]
        pairs = [(i, i + m * sign[i]) for i in range(devices) if 0 <= i + m * sign[i] < devices]
        moved[step] = lax.ppermute(by_step[step], "shard", pairs)
    return [moved[step] for step in range(len(by_step))]


def is_even(m):
    return lax.rem(lax.div(lax.axis_index("shard"), m), 2) == 0


def to_steps(slots, back):
    reach = len(slots) // 2
    steps = []
    for m in range(1, reach + 1):
        first, second = slots[reach + m - 1], slots[reach - m]
        if back:
            first, second = second, first
        steps.append(lax.select(is_even(m), first, second))
        steps.append(lax.select(is_even(m), second, first))
    return steps


def to_slots(steps, back):
    reach = len(steps) // 2
    slots = [None] * len(steps)
    for m in range(1, reach + 1):
        first = lax.select(is_even(m), steps[2 * m - 2], steps[2 * m - 1])
        second = lax.select(is_even(m), steps[2 * m - 1], steps[2 * m - 2])
        if back:
            first, second = second, first
        slots[reach - m], slots[reach + m - 1] = first, second
    return slots


def matmul(left, right):
    return jnp.dot(left, right, preferred_element_type=F32)


def matmul_rt(left, right):
    return lax.dot_general(left, right, (((1,), (1,)), ((), ())), preferred_element_type=F32)


def pick_one(mask):
    return jnp.where(mask, jnp.ones(mask.shape, BF16), jnp.zeros(mask.shape, BF16))


def encode(row):
    return jnp.left_shift((row & (LANES - 1)) + LANES, row >> 7).astype(F32)


def column(codes):
    pieces = []
    for start in range(0, codes.shape[1], LANES):
        piece = jnp.broadcast_to(codes[:, start : start + LANES], (LANES, LANES))
        pieces.append(jnp.transpose(piece))
    return pieces[0] if len(pieces) == 1 else jnp.concatenate(pieces, axis=0)


def one_hot_rows(col, width, first=0):
    lane = lax.broadcasted_iota(jnp.int32, (16, LANES), 1)
    blocks = []
    for start in range(first, first + width, LANES):
        pattern = jnp.broadcast_to(encode(lane + start).astype(BF16)[0:1], col.shape)
        blocks.append(pick_one(col == pattern))
    return jnp.concatenate(blocks, axis=1)


def one_hot_columns(codes, height):
    place = lax.broadcasted_iota(jnp.int32, (height, codes.shape[1]), 0)
    pattern = encode(place).astype(BF16)
    return pick_one(jnp.broadcast_to(codes, pattern.shape) == pattern)


def pick_rows(col, table):
    both = matmul(one_hot_rows(jnp.abs(col), table.shape[0]), table).astype(BF16)
    return jnp.where(col < jnp.zeros(col.shape, BF16), both[:, LANES:], both[:, :LANES])


def list_row(lists, first, per_row):
    pieces = [lists[first + n : first + n + 1, :] for n in range(per_row)]
    return pieces[0] if per_row == 1 else jnp.concatenate(pieces, axis=1)


def add_lists(total, lists_ref, blocks):
    slots, cap = lists_ref.shape
    codes = encode(lists_ref[...]).astype(F32)
    per_row = max(1, min(slots, LANES // cap))
    for first in range(0, slots, per_row):
        row = list_row(codes, first, per_row).astype(BF16)
        rows = jnp.concatenate(blocks[first : first + per_row], axis=0)
        total = total + matmul(one_hot_columns(row, total.shape[0]), rows)
    return total


def gather_lists(lists_ref, table):
    slots, cap = lists_ref.shape
    lists = lists_ref[...]
    per_row = max(1, min(slots, LANES // cap))
    parts = []
    for first in range(0, slots, per_row):
        codes = encode(list_row(lists, first, per_row))
        chooser = one_hot_rows(column(codes).astype(BF16), table.shape[0])
        parts.append(matmul(chooser, table))
    return parts[0] if len(parts) == 1 else jnp.concatenate(parts, axis=0)


def head_kernel(features_hbm, halo_hbm, child_map_hbm, out_grad_hbm, down_hbm, *refs):
    sources = (features_hbm, halo_hbm, child_map_hbm, out_grad_hbm, down_hbm)
    buffers, sems = refs[-len(sources) - 1 : -1], refs[-1]
    features_ref, halo_ref, child_map_ref, out_grad_ref, down_ref = buffers
    copies = [
        pltpu.make_async_copy(source, buffer, sems.at[n])
        for n, (source, buffer) in enumerate(zip(sources, buffers))
    ]
    for copy in copies:
        copy.start()
    outs = refs[: -len(sources) - 1]
    sends, back_ref = outs[:-1], outs[-1]
    slots, cap = halo_ref.shape
    voxels = features_ref.shape[0]
    octants = child_map_ref.shape[0]
    table_rows = voxels + slots * (sends[0].shape[0] - cap)
    cap2 = (table_rows - voxels) // slots
    copies[0].wait()
    copies[1].wait()
    listed = gather_lists(halo_ref, features_ref[...]).astype(BF16)
    for send, block in zip(sends, to_steps(jnp.split(listed, slots), False)):
        send[0:cap, :] = block
    for copy in copies[2:]:
        copy.wait()
    upstream = out_grad_ref[...]
    codes = encode(child_map_ref[...]).astype(BF16)
    choosers, parts = [], []
    for o in range(octants):
        part = matmul_rt(upstream, down_ref[o])
        high = part.astype(BF16)
        low = (part - high.astype(F32)).astype(BF16)
        choosers.append(one_hot_columns(codes[o : o + 1, :], table_rows))
        parts.append(jnp.concatenate([high, low], axis=1))
    both = matmul(jnp.concatenate(choosers, axis=1), jnp.concatenate(parts, axis=0))
    total = both[:, :LANES] + both[:, LANES:]
    back_ref[...] = total[:voxels]
    for send, block in zip(sends, to_steps(jnp.split(total[voxels:].astype(BF16), slots), True)):
        send[cap : cap + cap2, :] = block


def half_codes(row, voxels, received):
    half, half_received = voxels // 2, received // 2
    beyond = row - voxels
    outside = beyond >= 0
    near = row - jnp.where(row >= half, half, 0)
    far = half + beyond - jnp.where(beyond >= half_received, half_received, 0)
    code = encode(jnp.where(outside, far, near))
    near_sign = jnp.where(row >= half, -1.0, 1.0)
    far_sign = jnp.where(beyond >= half_received, -1.0, 1.0)
    return code * jnp.where(outside, far_sign, near_sign)


def offset_of(n, middle):
    return n + jnp.where(n >= middle, 1, 0)


def forward_kernel(slots, *refs):
    received = refs[:slots]
    features_ref, map_ref, weight_ref, child_ref = refs[slots : slots + 4]
    hidden_ref, pre_ref, stacked_ref = refs[slots + 4 : slots + 7]
    sends = refs[slots + 7 : 2 * slots + 7]
    table_ref, halo_ref, kernel_ref = refs[2 * slots + 7 : 2 * slots + 10]
    own_refs, far_refs, col_refs = (
        refs[2 * slots + 10 + 2 * n : 2 * slots + 12 + 2 * n] for n in range(3)
    )
    voxels = features_ref.shape[0]
    gathers = map_ref.shape[0] - 1
    middle = gathers // 2
    cap2 = child_ref.shape[1]
    cap = received[0].shape[0] - cap2
    half, half_halo = voxels // 2, slots * cap // 2
    features = features_ref[...]
    table_ref[:, 0:LANES] = features[0:half]
    table_ref[:, LANES:] = features[half:voxels]
    halo_ref[...] = jnp.zeros(halo_ref.shape, BF16)
    for s, block in enumerate(to_slots([r[0:cap, :] for r in received], False)):
        place = (s % (slots // 2)) * cap
        side = (s // (slots // 2)) * LANES
        for n in range(2):
            row, lane = n * half_halo + place, 2 * n * LANES + side
            halo_ref[row : row + cap, lane : lane + LANES] = block
    kernel_ref[0:middle] = weight_ref[0:middle]
    kernel_ref[middle:gathers] = weight_ref[middle + 1 :]
    kernel_ref[gathers] = weight_ref[middle]

    def build(j, side):
        for n in range(2):
            k = offset_of(2 * j + n, middle)
            codes = half_codes(map_ref[pl.ds(k, 1), :], voxels, slots * cap).astype(BF16)
            col = column(codes)
            col_refs[side][n] = col
            col = jnp.abs(col)
            own_refs[side][n] = one_hot_rows(col, half)
            lanes = slice(n * half_halo, (n + 1) * half_halo)
            far_refs[side][:, lanes] = one_hot_rows(col, half_halo, half)

    def use(j, side):
        far = matmul(far_refs[side][...], halo_ref[...])
        pair = []
        for n in range(2):
            both = matmul(own_refs[side][n], table_ref[...])
            both = (both + far[:, 2 * n * LANES : 2 * (n + 1) * LANES]).astype(BF16)
            right = col_refs[side][n] < jnp.zeros((voxels, LANES), BF16)
            pair.append(jnp.where(right, both[:, LANES:], both[:, :LANES]))
        lanes = pl.ds(pl.multiple_of(2 * j * LANES, 2 * LANES), 2 * LANES)
        stacked_ref[:, lanes] = jnp.concatenate(pair, axis=1)

    def step(i, carry):
        for side in range(2):
            j = 2 * i + side
            use(j, side)
            build(j + 1, 1 - side)
        return carry

    build(0, 0)
    lax.fori_loop(0, middle // 2, step, 0)
    use(middle - 1, 0)
    stacked_ref[:, gathers * LANES :] = features
    pre = matmul(stacked_ref[...], kernel_ref[...].reshape(-1, LANES))
    pre_ref[...] = pre
    hidden = (features.astype(F32) + pre * jax.nn.sigmoid(pre)).astype(BF16)
    hidden_ref[...] = hidden
    leaving = gather_lists(child_ref, hidden).astype(BF16)
    for send, block in zip(sends, to_steps(jnp.split(leaving, slots), False)):
        send[...] = block


def gradient_kernel(slots, *refs):
    received = refs[:slots]
    stacked_ref, pre_ref, child_ref, back_ref = refs[slots : slots + 4]
    hgrad_ref, pgrad_ref, cgrad_ref = refs[slots + 4 :]
    cap2 = child_ref.shape[1]
    cap = received[0].shape[0] - cap2
    kernel_count = cgrad_ref.shape[0] // LANES
    middle = kernel_count // 2
    blocks = to_slots([r[cap : cap + cap2, :] for r in received], True)
    hgrad = add_lists(back_ref[...], child_ref, blocks)
    hgrad_ref[...] = hgrad
    pre = pre_ref[...]
    sig = jax.nn.sigmoid(pre)
    pgrad = hgrad * (sig * (1.0 + pre * (1.0 - sig)))
    pgrad_ref[...] = pgrad.astype(BF16)
    terms = matmul(jnp.transpose(pgrad).astype(BF16), stacked_ref[...])
    order = [k for k in range(kernel_count) if k != middle] + [middle]
    for n, k in enumerate(order):
        block = jnp.transpose(terms[:, n * LANES : (n + 1) * LANES])
        cgrad_ref[k * LANES : (k + 1) * LANES, :] = block.astype(BF16)


def spread_kernel(slots, pgrad_ref, map_ref, weight_ref, after_ref, back_ref, *sends):
    acc_ref = sends[-1]
    sends = sends[:-1]
    voxels = pgrad_ref.shape[0]
    kernel_count = map_ref.shape[0]
    middle = kernel_count // 2
    cap = sends[0].shape[0]
    half = voxels // 2
    table_rows = half + slots * cap // 2
    pgrad = pgrad_ref[...]
    own = matmul_rt(pgrad, weight_ref[middle])
    acc_ref[0:half, 0:LANES] = own[0:half]
    acc_ref[0:half, LANES:] = own[half:]
    acc_ref[half:, :] = jnp.zeros((table_rows - half, 2 * LANES), F32)

    def parts(k):
        codes = half_codes(map_ref[pl.ds(k, 1), :], voxels, slots * cap)
        terms = matmul_rt(pgrad, weight_ref[k])
        right = column(codes) < 0.0
        sides = [jnp.where(right, 0.0, terms), jnp.where(right, terms, 0.0)]
        chooser = one_hot_columns(jnp.abs(codes).astype(BF16), table_rows)
        return chooser, jnp.concatenate(sides, axis=1).astype(BF16)

    def step(j, carry):
        near_chooser, near_terms = parts(j)
        far_chooser, far_terms = parts(j + middle + 1)
        acc_ref[...] += matmul(near_chooser, near_terms) + matmul(far_chooser, far_terms)
        return carry

    lax.fori_loop(0, middle, step, 0)
    back_ref[0:half, :] = acc_ref[0:half, 0:LANES]
    back_ref[half:, :] = acc_ref[0:half, LANES:]
    blocks = []
    for s in range(slots):
        first = half + (s % (slots // 2)) * cap
        side = (s // (slots // 2)) * LANES
        blocks.append(acc_ref[first : first + cap, side : side + LANES].astype(BF16))
    for send, block in zip(sends, to_steps(blocks, True)):
        send[...] = block


def my_half(rows):
    core = lax.rem(lax.axis_index("shard"), 2)
    return pl.multiple_of(core * rows, 16), pl.multiple_of((1 - core) * rows, 16)


def down_kernel(slots, *refs):
    received = refs[:slots]
    (hidden_ref, map_ref, down_ref, out_grad_ref, cgrad_ref) = refs[slots : slots + 5]
    coarse_ref, terms_ref, send_ref, table_ref = refs[slots + 5 :]
    voxels = hidden_ref.shape[0]
    cap2 = received[0].shape[0]
    half, half_halo = voxels // 2, slots * cap2 // 2
    blocks = to_slots([r[...] for r in received], False)
    table_ref[0:half, 0:LANES] = hidden_ref[0:half, :]
    table_ref[0:half, LANES:] = hidden_ref[half:, :]
    for s, block in enumerate(blocks):
        place = half + (s % (slots // 2)) * cap2
        side = (s // (slots // 2)) * LANES
        table_ref[place : place + cap2, side : side + LANES] = block
    padding = table_ref.shape[0] - half - half_halo
    table_ref[half + half_halo :, :] = jnp.zeros((padding, 2 * LANES), BF16)
    upstream = out_grad_ref[...]
    parents = upstream.shape[0]
    octants = map_ref.shape[0]
    upstream_t = jnp.transpose(upstream.astype(F32)).astype(BF16)
    codes = half_codes(map_ref[...], voxels, slots * cap2)
    col = jnp.concatenate([column(codes[o : o + 1, :]) for o in range(octants)], axis=0)
    picked = pick_rows(col.astype(BF16), table_ref[...])
    picked = jnp.concatenate(jnp.split(picked, octants), axis=1)
    row = cgrad_ref.shape[0]
    terms_ref[0:row, :] = cgrad_ref[...]
    terms = matmul(upstream_t, picked)
    for o in range(octants):
        for start in range(0, terms.shape[0], LANES):
            block = terms[start : start + LANES, o * LANES : (o + 1) * LANES]
            terms_ref[row : row + LANES, :] = jnp.transpose(block).astype(BF16)
            row += LANES
    total = matmul(picked, down_ref[...].reshape(octants * LANES, down_ref.shape[2]))
    terms_ref[row:, :] = jnp.zeros((terms_ref.shape[0] - row, LANES), BF16)
    coarse_ref[...] = total.astype(BF16)
    send_ref[...] = terms_ref[pl.ds(my_half(send_ref.shape[0])[1], send_ref.shape[0]), :]


def pair_kernel(terms_ref, other_ref, out_ref):
    rows = other_ref.shape[0]
    mine = terms_ref[pl.ds(my_half(rows)[0], rows), :].astype(F32)
    out_ref[...] = (mine + other_ref[...].astype(F32)).astype(BF16)


def sum_kernel(devices, scale, parts_ref, after_ref, out_ref):
    rows = parts_ref.shape[0] // devices
    for core in range(2):
        mine = range(core, devices, 2)
        total = jnp.zeros((rows, LANES), F32)
        for d in mine:
            total = total + parts_ref[d * rows : (d + 1) * rows, :].astype(F32)
        total = (total * scale).astype(BF16)
        for d in mine:
            out_ref[d * rows : (d + 1) * rows, :] = total


def final_kernel(mine_ref, other_ref, conv_ref, down_ref, whole_ref):
    rows = mine_ref.shape[0]
    mine, other = my_half(rows)
    whole_ref[pl.ds(mine, rows), :] = mine_ref[...]
    whole_ref[pl.ds(other, rows), :] = other_ref[...]
    row = conv_ref.shape[0]
    conv_ref[...] = whole_ref[0:row, :].astype(F32)
    for first in range(0, down_ref.shape[0], LANES):
        for start in range(0, down_ref.shape[1], LANES):
            block = whole_ref[row : row + LANES, :].astype(F32)
            down_ref[first : first + LANES, start : start + LANES] = block
            row += LANES


def tail_kernel(slots, *refs):
    received = refs[:slots]
    hgrad_ref, back_ref, halo_ref, out_ref = refs[slots:]
    blocks = to_slots([r[...] for r in received], True)
    out_ref[...] = add_lists(hgrad_ref[...] + back_ref[...], halo_ref, blocks)


def call(kernel, operands, outs, scratch=(), limit=32, flops=0, in_hbm=()):
    spaces = [pl.ANY if n in in_hbm else pltpu.VMEM for n in range(len(operands))]
    return pl.pallas_call(
        kernel,
        out_shape=[jax.ShapeDtypeStruct(s, d) for s, d in outs],
        in_specs=[pl.BlockSpec(memory_space=space) for space in spaces],
        out_specs=[pl.BlockSpec(memory_space=pltpu.VMEM) for _ in outs],
        scratch_shapes=list(scratch),
        compiler_params=pltpu.CompilerParams(vmem_limit_bytes=limit * 2**20),
        cost_estimate=pl.CostEstimate(flops=flops, bytes_accessed=4 * 2**20, transcendentals=0),
    )(*operands)


def swap_cores(value, devices):
    return lax.ppermute(value, "shard", [(i, i + 1 - 2 * (i % 2)) for i in range(devices)])


def exchange(value):
    return lax.all_to_all(value, "shard", 0, 0, tiled=True)


def local(
    features, conv_weight, down_weight, neighbour_map, halo_rows, child_map, child_rows, out_grad
):
    voxels, channels = features.shape
    parents, coarse_channels = out_grad.shape
    kernel_count = conv_weight.shape[0]
    octants = down_weight.shape[0]
    slots, cap = halo_rows.shape
    cap2 = child_rows.shape[1]
    devices = lax.axis_size("shard")
    scale = 1.0 / math.sqrt(voxels * devices)
    giga = 10**9

    first = call(
        head_kernel,
        (features, halo_rows, child_map, out_grad, down_weight),
        [((cap + cap2, channels), BF16)] * slots + [((voxels, channels), F32)],
        scratch=[
            pltpu.VMEM(value.shape, value.dtype)
            for value in (features, halo_rows, child_map, out_grad, down_weight)
        ]
        + [pltpu.SemaphoreType.DMA((5,))],
        limit=60,
        flops=giga,
        in_hbm=range(5),
    )
    back_h = first[-1]
    received = swaps(first[:-1], (2, 3, 1, 0))
    conv_rows = kernel_count * channels
    down_rows = octants * channels * coarse_channels // LANES
    grain = 8 * devices
    half_rows = -(-(conv_rows + down_rows) // (2 * grain)) * grain
    hidden, pre_act, stacked, *leaving = call(
        functools.partial(forward_kernel, slots),
        (*received, features, neighbour_map, conv_weight, child_rows),
        [
            ((voxels, channels), BF16),
            ((voxels, channels), F32),
            ((voxels, conv_rows), BF16),
        ]
        + [((cap2, channels), BF16)] * slots,
        scratch=[
            pltpu.VMEM((voxels // 2, 2 * channels), BF16),
            pltpu.VMEM((slots * cap, 4 * channels), BF16),
            pltpu.VMEM(conv_weight.shape, BF16),
        ]
        + [pltpu.VMEM((2, voxels, voxels // 2), BF16)] * 2
        + [pltpu.VMEM((voxels, slots * cap), BF16)] * 2
        + [pltpu.VMEM((2, voxels, LANES), BF16)] * 2,
        limit=32,
        flops=12 * giga,
    )
    hidden_grad, pre_grad, conv_terms = call(
        functools.partial(gradient_kernel, slots),
        (*received, stacked, pre_act, child_rows, back_h),
        [
            ((voxels, channels), F32),
            ((voxels, channels), BF16),
            ((conv_rows, channels), BF16),
        ],
        flops=3 * giga,
    )
    received_h = swaps(leaving, (1, 3, 2, 0))
    coarse, terms, leaving_terms = call(
        functools.partial(down_kernel, slots),
        (*received_h, hidden, child_map, down_weight, out_grad, conv_terms),
        [
            ((parents, coarse_channels), BF16),
            ((2 * half_rows, LANES), BF16),
            ((half_rows, LANES), BF16),
        ],
        scratch=[pltpu.VMEM((-(-(voxels + slots * cap2) // 256) * 128, 2 * channels), BF16)],
        flops=2 * giga,
    )
    (pair_terms,) = call(
        pair_kernel,
        (terms, swap_cores(leaving_terms, devices)),
        [((half_rows, LANES), BF16)],
        flops=10**6,
    )
    parts = exchange(pair_terms)
    spread = call(
        functools.partial(spread_kernel, slots),
        (pre_grad, neighbour_map, conv_weight, pair_terms),
        [((voxels, channels), F32)] + [((cap, channels), BF16)] * slots,
        scratch=[pltpu.VMEM((voxels // 2 + slots * cap // 2, 2 * channels), F32)],
        flops=20 * giga,
        in_hbm=(3,),
    )
    (summed,) = call(
        functools.partial(sum_kernel, devices, scale),
        (parts, spread[1]),
        [((half_rows, LANES), BF16)],
        flops=10**6,
        in_hbm=(1,),
    )
    summed, *returning = lax.optimization_barrier((summed, *spread[1:]))
    mine, *returned = lax.optimization_barrier((exchange(summed), *swaps(returning, (3, 1, 0, 2))))
    (input_grad,) = call(
        functools.partial(tail_kernel, slots),
        (*returned, hidden_grad, spread[0], halo_rows),
        [((voxels, channels), F32)],
        flops=giga,
    )
    conv_grad, down_grad = call(
        final_kernel,
        (mine, swap_cores(mine, devices)),
        [((conv_rows, LANES), F32), ((octants * channels, coarse_channels), F32)],
        scratch=[pltpu.VMEM((2 * half_rows, LANES), BF16)],
        flops=10**6,
    )
    conv_grad = conv_grad.reshape(conv_weight.shape)
    return (coarse, input_grad, conv_grad, down_grad.reshape(down_weight.shape))


def solution(mesh):
    return jax.shard_map(
        local,
        mesh=mesh,
        in_specs=(
            P("shard", None),
            P(),
            P(),
            P(None, "shard"),
            P(None, "shard"),
            P(None, "shard"),
            P(None, "shard"),
            P("shard", None),
        ),
        out_specs=(P("shard", None), P("shard", None), P(), P()),
        check_vma=False,
    )
```

```python
import functools
import math

import jax
import jax.numpy as jnp
from jax import lax
from jax.experimental import pallas as pl
from jax.experimental.pallas import tpu as pltpu
from jax.sharding import PartitionSpec as P

BF16 = jnp.bfloat16
F32 = jnp.float32
LANES = 128


def swaps(by_step, order):
    devices = lax.axis_size("shard")
    moved = {}
    for step in order:
        m, phase = step // 2 + 1, step % 2
        sign = [1 if (i // m) % 2 == phase else -1 for i in range(devices)]
        pairs = [(i, i + m * sign[i]) for i in range(devices) if 0 <= i + m * sign[i] < devices]
        moved[step] = lax.ppermute(by_step[step], "shard", pairs)
    return [moved[step] for step in range(len(by_step))]


def is_even(m):
    return lax.rem(lax.div(lax.axis_index("shard"), m), 2) == 0


def to_steps(slots, back):
    reach = len(slots) // 2
    steps = []
    for m in range(1, reach + 1):
        first, second = slots[reach + m - 1], slots[reach - m]
        if back:
            first, second = second, first
        steps.append(lax.select(is_even(m), first, second))
        steps.append(lax.select(is_even(m), second, first))
    return steps


def to_slots(steps, back):
    reach = len(steps) // 2
    slots = [None] * len(steps)
    for m in range(1, reach + 1):
        first = lax.select(is_even(m), steps[2 * m - 2], steps[2 * m - 1])
        second = lax.select(is_even(m), steps[2 * m - 1], steps[2 * m - 2])
        if back:
            first, second = second, first
        slots[reach - m], slots[reach + m - 1] = first, second
    return slots


def matmul(left, right):
    return jnp.dot(left, right, preferred_element_type=F32)


def matmul_rt(left, right):
    return lax.dot_general(left, right, (((1,), (1,)), ((), ())), preferred_element_type=F32)


def pick_one(mask):
    return jnp.where(mask, jnp.ones(mask.shape, BF16), jnp.zeros(mask.shape, BF16))


def encode(row):
    return jnp.left_shift((row & (LANES - 1)) + LANES, row >> 7).astype(F32)


def column(codes):
    pieces = []
    for start in range(0, codes.shape[1], LANES):
        piece = jnp.broadcast_to(codes[:, start : start + LANES], (LANES, LANES))
        pieces.append(jnp.transpose(piece))
    return pieces[0] if len(pieces) == 1 else jnp.concatenate(pieces, axis=0)


def one_hot_rows(col, width, first=0):
    lane = lax.broadcasted_iota(jnp.int32, (16, LANES), 1)
    blocks = []
    for start in range(first, first + width, LANES):
        pattern = jnp.broadcast_to(encode(lane + start).astype(BF16)[0:1], col.shape)
        blocks.append(pick_one(col == pattern))
    return jnp.concatenate(blocks, axis=1)


def one_hot_columns(codes, height):
    place = lax.broadcasted_iota(jnp.int32, (height, codes.shape[1]), 0)
    pattern = encode(place).astype(BF16)
    return pick_one(jnp.broadcast_to(codes, pattern.shape) == pattern)


def pick_rows(col, table):
    both = matmul(one_hot_rows(jnp.abs(col), table.shape[0]), table).astype(BF16)
    return jnp.where(col < jnp.zeros(col.shape, BF16), both[:, LANES:], both[:, :LANES])


def list_row(lists, first, per_row):
    pieces = [lists[first + n : first + n + 1, :] for n in range(per_row)]
    return pieces[0] if per_row == 1 else jnp.concatenate(pieces, axis=1)


def add_lists(total, lists_ref, blocks):
    slots, cap = lists_ref.shape
    codes = encode(lists_ref[...]).astype(F32)
    per_row = max(1, min(slots, LANES // cap))
    for first in range(0, slots, per_row):
        row = list_row(codes, first, per_row).astype(BF16)
        rows = jnp.concatenate(blocks[first : first + per_row], axis=0)
        total = total + matmul(one_hot_columns(row, total.shape[0]), rows)
    return total


def gather_lists(lists_ref, table):
    slots, cap = lists_ref.shape
    lists = lists_ref[...]
    per_row = max(1, min(slots, LANES // cap))
    parts = []
    for first in range(0, slots, per_row):
        codes = encode(list_row(lists, first, per_row))
        chooser = one_hot_rows(column(codes).astype(BF16), table.shape[0])
        parts.append(matmul(chooser, table))
    return parts[0] if len(parts) == 1 else jnp.concatenate(parts, axis=0)


def head_kernel(features_hbm, halo_hbm, child_map_hbm, out_grad_hbm, down_hbm, *refs):
    sources = (features_hbm, halo_hbm, child_map_hbm, out_grad_hbm, down_hbm)
    buffers, sems = refs[-len(sources) - 1 : -1], refs[-1]
    features_ref, halo_ref, child_map_ref, out_grad_ref, down_ref = buffers
    copies = [
        pltpu.make_async_copy(source, buffer, sems.at[n])
        for n, (source, buffer) in enumerate(zip(sources, buffers))
    ]
    for copy in copies:
        copy.start()
    outs = refs[: -len(sources) - 1]
    sends, back_ref = outs[:-1], outs[-1]
    slots, cap = halo_ref.shape
    voxels = features_ref.shape[0]
    octants = child_map_ref.shape[0]
    table_rows = voxels + slots * (sends[0].shape[0] - cap)
    cap2 = (table_rows - voxels) // slots
    copies[0].wait()
    copies[1].wait()
    listed = gather_lists(halo_ref, features_ref[...]).astype(BF16)
    for send, block in zip(sends, to_steps(jnp.split(listed, slots), False)):
        send[0:cap, :] = block
    for copy in copies[2:]:
        copy.wait()
    upstream = out_grad_ref[...]
    codes = encode(child_map_ref[...]).astype(BF16)
    choosers, parts = [], []
    for o in range(octants):
        part = matmul_rt(upstream, down_ref[o])
        high = part.astype(BF16)
        low = (part - high.astype(F32)).astype(BF16)
        choosers.append(one_hot_columns(codes[o : o + 1, :], table_rows))
        parts.append(jnp.concatenate([high, low], axis=1))
    both = matmul(jnp.concatenate(choosers, axis=1), jnp.concatenate(parts, axis=0))
    total = both[:, :LANES] + both[:, LANES:]
    back_ref[...] = total[:voxels]
    for send, block in zip(sends, to_steps(jnp.split(total[voxels:].astype(BF16), slots), True)):
        send[cap : cap + cap2, :] = block


def half_codes(row, voxels, received):
    half, half_received = voxels // 2, received // 2
    beyond = row - voxels
    outside = beyond >= 0
    near = row - jnp.where(row >= half, half, 0)
    far = half + beyond - jnp.where(beyond >= half_received, half_received, 0)
    code = encode(jnp.where(outside, far, near))
    near_sign = jnp.where(row >= half, -1.0, 1.0)
    far_sign = jnp.where(beyond >= half_received, -1.0, 1.0)
    return code * jnp.where(outside, far_sign, near_sign)


def offset_of(n, middle):
    return n + jnp.where(n >= middle, 1, 0)


def code_column(map_ref, k, voxels, received):
    return column(half_codes(map_ref[pl.ds(k, 1), :], voxels, received).astype(BF16))


def pick_side(col, both):
    return jnp.where(col < jnp.zeros(col.shape, BF16), both[:, LANES:], both[:, :LANES])


def local_kernel(received, features_ref, map_ref, early_ref, table_ref):
    voxels = features_ref.shape[0]
    half = voxels // 2
    table_ref[:, 0:LANES] = features_ref[0:half, :]
    table_ref[:, LANES:] = features_ref[half:, :]
    middle = map_ref.shape[0] // 2
    for n in range(early_ref.shape[1] // LANES):
        col = code_column(map_ref, offset_of(n, middle), voxels, received)
        both = matmul(one_hot_rows(jnp.abs(col), half), table_ref[...]).astype(BF16)
        early_ref[:, n * LANES : (n + 1) * LANES] = pick_side(col, both)


def forward_kernel(slots, *refs):
    received = refs[:slots]
    features_ref, map_ref, weight_ref, child_ref, early_ref = refs[slots : slots + 5]
    hidden_ref, pre_ref, stacked_ref = refs[slots + 5 : slots + 8]
    sends = refs[slots + 8 : 2 * slots + 8]
    table_ref, halo_ref, kernel_ref = refs[2 * slots + 8 : 2 * slots + 11]
    own_refs, far_refs, col_refs = (
        refs[2 * slots + 11 + 2 * n : 2 * slots + 13 + 2 * n] for n in range(3)
    )
    voxels = features_ref.shape[0]
    gathers = map_ref.shape[0] - 1
    middle = gathers // 2
    cap2 = child_ref.shape[1]
    cap = received[0].shape[0] - cap2
    half, half_halo = voxels // 2, slots * cap // 2
    features = features_ref[...]
    table_ref[:, 0:LANES] = features[0:half]
    table_ref[:, LANES:] = features[half:voxels]
    halo_ref[...] = jnp.zeros(halo_ref.shape, BF16)
    for s, block in enumerate(to_slots([r[0:cap, :] for r in received], False)):
        place = (s % (slots // 2)) * cap
        side = (s // (slots // 2)) * LANES
        for n in range(2):
            row, lane = n * half_halo + place, 2 * n * LANES + side
            halo_ref[row : row + cap, lane : lane + LANES] = block
    kernel_ref[0:middle] = weight_ref[0:middle]
    kernel_ref[middle:gathers] = weight_ref[middle + 1 :]
    kernel_ref[gathers] = weight_ref[middle]

    def build(j, side):
        for n in range(2):
            col = code_column(map_ref, offset_of(2 * j + n, middle), voxels, slots * cap)
            col_refs[side][n] = col
            col = jnp.abs(col)
            own_refs[side][n] = one_hot_rows(col, half)
            lanes = slice(n * half_halo, (n + 1) * half_halo)
            far_refs[side][:, lanes] = one_hot_rows(col, half_halo, half)

    def use(j, side):
        far = matmul(far_refs[side][...], halo_ref[...])
        pair = []
        for n in range(2):
            both = matmul(own_refs[side][n], table_ref[...])
            both = (both + far[:, 2 * n * LANES : 2 * (n + 1) * LANES]).astype(BF16)
            pair.append(pick_side(col_refs[side][n], both))
        lanes = pl.ds(pl.multiple_of(2 * j * LANES, 2 * LANES), 2 * LANES)
        stacked_ref[:, lanes] = jnp.concatenate(pair, axis=1)

    begun = early_ref.shape[1] // (2 * LANES)
    for j in range(begun):
        cols = [
            code_column(map_ref, offset_of(2 * j + n, middle), voxels, slots * cap)
            for n in range(2)
        ]
        choosers = [one_hot_rows(jnp.abs(col), half_halo, half) for col in cols]
        far = matmul(jnp.concatenate(choosers, axis=1), halo_ref[...]).astype(BF16)
        for n in range(2):
            picked = pick_side(cols[n], far[:, 2 * n * LANES : 2 * (n + 1) * LANES])
            lanes = slice((2 * j + n) * LANES, (2 * j + n + 1) * LANES)
            stacked_ref[:, lanes] = early_ref[:, lanes] + picked

    def step(i, carry):
        for side in range(2):
            j = begun + 2 * i + side
            use(j, side)
            build(j + 1, 1 - side)
        return carry

    left = middle - begun
    build(begun, 0)
    lax.fori_loop(0, (left - 1) // 2, step, 0)
    if left % 2 == 0:
        use(middle - 2, 0)
        build(middle - 1, 1)
    use(middle - 1, 1 - left % 2)
    stacked_ref[:, gathers * LANES :] = features
    pre = matmul(stacked_ref[...], kernel_ref[...].reshape(-1, LANES))
    pre_ref[...] = pre
    hidden = (features.astype(F32) + pre * jax.nn.sigmoid(pre)).astype(BF16)
    hidden_ref[...] = hidden
    leaving = gather_lists(child_ref, hidden).astype(BF16)
    for send, block in zip(sends, to_steps(jnp.split(leaving, slots), False)):
        send[...] = block


def gradient_kernel(slots, *refs):
    received = refs[:slots]
    stacked_ref, pre_ref, child_ref, back_ref = refs[slots : slots + 4]
    hgrad_ref, pgrad_ref, cgrad_ref = refs[slots + 4 :]
    cap2 = child_ref.shape[1]
    cap = received[0].shape[0] - cap2
    kernel_count = cgrad_ref.shape[0] // LANES
    middle = kernel_count // 2
    blocks = to_slots([r[cap : cap + cap2, :] for r in received], True)
    hgrad = add_lists(back_ref[...], child_ref, blocks)
    hgrad_ref[...] = hgrad
    pre = pre_ref[...]
    sig = jax.nn.sigmoid(pre)
    pgrad = hgrad * (sig * (1.0 + pre * (1.0 - sig)))
    pgrad_ref[...] = pgrad.astype(BF16)
    terms = matmul(jnp.transpose(pgrad).astype(BF16), stacked_ref[...])
    order = [k for k in range(kernel_count) if k != middle] + [middle]
    for n, k in enumerate(order):
        block = jnp.transpose(terms[:, n * LANES : (n + 1) * LANES])
        cgrad_ref[k * LANES : (k + 1) * LANES, :] = block.astype(BF16)


def spread_kernel(slots, pgrad_ref, map_ref, weight_ref, after_ref, back_ref, *sends):
    acc_ref = sends[-1]
    sends = sends[:-1]
    voxels = pgrad_ref.shape[0]
    kernel_count = map_ref.shape[0]
    middle = kernel_count // 2
    cap = sends[0].shape[0]
    half = voxels // 2
    table_rows = half + slots * cap // 2
    pgrad = pgrad_ref[...]
    own = matmul_rt(pgrad, weight_ref[middle])
    acc_ref[0:half, 0:LANES] = own[0:half]
    acc_ref[0:half, LANES:] = own[half:]
    acc_ref[half:, :] = jnp.zeros((table_rows - half, 2 * LANES), F32)

    def parts(k):
        codes = half_codes(map_ref[pl.ds(k, 1), :], voxels, slots * cap)
        terms = matmul_rt(pgrad, weight_ref[k])
        right = column(codes) < 0.0
        sides = [jnp.where(right, 0.0, terms), jnp.where(right, terms, 0.0)]
        chooser = one_hot_columns(jnp.abs(codes).astype(BF16), table_rows)
        return chooser, jnp.concatenate(sides, axis=1).astype(BF16)

    def step(j, carry):
        near_chooser, near_terms = parts(j)
        far_chooser, far_terms = parts(j + middle + 1)
        acc_ref[...] += matmul(near_chooser, near_terms) + matmul(far_chooser, far_terms)
        return carry

    lax.fori_loop(0, middle, step, 0)
    back_ref[0:half, :] = acc_ref[0:half, 0:LANES]
    back_ref[half:, :] = acc_ref[0:half, LANES:]
    blocks = []
    for s in range(slots):
        first = half + (s % (slots // 2)) * cap
        side = (s // (slots // 2)) * LANES
        blocks.append(acc_ref[first : first + cap, side : side + LANES].astype(BF16))
    for send, block in zip(sends, to_steps(blocks, True)):
        send[...] = block


def my_half(rows):
    core = lax.rem(lax.axis_index("shard"), 2)
    return pl.multiple_of(core * rows, 16), pl.multiple_of((1 - core) * rows, 16)


def down_kernel(slots, *refs):
    received = refs[:slots]
    (hidden_ref, map_ref, down_ref, out_grad_ref, cgrad_ref) = refs[slots : slots + 5]
    coarse_ref, terms_ref, send_ref, table_ref = refs[slots + 5 :]
    voxels = hidden_ref.shape[0]
    cap2 = received[0].shape[0]
    half, half_halo = voxels // 2, slots * cap2 // 2
    blocks = to_slots([r[...] for r in received], False)
    table_ref[0:half, 0:LANES] = hidden_ref[0:half, :]
    table_ref[0:half, LANES:] = hidden_ref[half:, :]
    for s, block in enumerate(blocks):
        place = half + (s % (slots // 2)) * cap2
        side = (s // (slots // 2)) * LANES
        table_ref[place : place + cap2, side : side + LANES] = block
    padding = table_ref.shape[0] - half - half_halo
    table_ref[half + half_halo :, :] = jnp.zeros((padding, 2 * LANES), BF16)
    upstream = out_grad_ref[...]
    parents = upstream.shape[0]
    octants = map_ref.shape[0]
    upstream_t = jnp.transpose(upstream.astype(F32)).astype(BF16)
    codes = half_codes(map_ref[...], voxels, slots * cap2)
    col = jnp.concatenate([column(codes[o : o + 1, :]) for o in range(octants)], axis=0)
    picked = pick_rows(col.astype(BF16), table_ref[...])
    picked = jnp.concatenate(jnp.split(picked, octants), axis=1)
    row = cgrad_ref.shape[0]
    terms_ref[0:row, :] = cgrad_ref[...]
    terms = matmul(upstream_t, picked)
    for o in range(octants):
        for start in range(0, terms.shape[0], LANES):
            block = terms[start : start + LANES, o * LANES : (o + 1) * LANES]
            terms_ref[row : row + LANES, :] = jnp.transpose(block).astype(BF16)
            row += LANES
    total = matmul(picked, down_ref[...].reshape(octants * LANES, down_ref.shape[2]))
    terms_ref[row:, :] = jnp.zeros((terms_ref.shape[0] - row, LANES), BF16)
    coarse_ref[...] = total.astype(BF16)
    send_ref[...] = terms_ref[pl.ds(my_half(send_ref.shape[0])[1], send_ref.shape[0]), :]


def pair_kernel(terms_ref, other_ref, out_ref):
    rows = other_ref.shape[0]
    mine = terms_ref[pl.ds(my_half(rows)[0], rows), :].astype(F32)
    out_ref[...] = (mine + other_ref[...].astype(F32)).astype(BF16)


def sum_kernel(devices, scale, parts_ref, after_ref, out_ref):
    rows = parts_ref.shape[0] // devices
    for core in range(2):
        mine = range(core, devices, 2)
        total = jnp.zeros((rows, LANES), F32)
        for d in mine:
            total = total + parts_ref[d * rows : (d + 1) * rows, :].astype(F32)
        total = (total * scale).astype(BF16)
        for d in mine:
            out_ref[d * rows : (d + 1) * rows, :] = total


def final_kernel(own, *refs):
    block_ref, conv_hbm, down_hbm = refs[0], *refs[-5:-3]
    conv_ref, down_ref, sems = refs[-3:]
    rows = block_ref.shape[0]
    conv_rows = conv_hbm.shape[0]
    core = lax.rem(lax.axis_index("shard"), 2)
    piece = 4 * LANES
    assert rows <= conv_rows <= 2 * rows and rows % LANES == 0

    def write(half):
        first, last = half * rows, (half + 1) * rows
        copies = []
        for start in range(first, min(last, conv_rows), piece):
            size = min(piece, last - start, conv_rows - start)
            place = pl.ds(start, size)
            value = block_ref[start - first : start - first + size, :]
            conv_ref[place, :] = value.astype(F32)
            sem = sems.at[len(copies)]
            copies.append(pltpu.make_async_copy(conv_ref.at[place], conv_hbm.at[place], sem))
            copies[-1].start()
        across = down_hbm.shape[1] // LANES
        for down in range(0, down_hbm.shape[0], LANES):
            row = conv_rows + down * across
            for side in range(across):
                start = row + side * LANES
                if first <= start < last:
                    value = block_ref[start - first : start - first + LANES, :]
                    lanes = slice(side * LANES, (side + 1) * LANES)
                    down_ref[down : down + LANES, lanes] = value.astype(F32)
            if first <= row < last:
                place = pl.ds(down, LANES)
                sem = sems.at[len(copies)]
                copies.append(pltpu.make_async_copy(down_ref.at[place], down_hbm.at[place], sem))
                copies[-1].start()
        for copy in copies:
            copy.wait()

    for half in range(2):
        pl.when(core == (half if own else 1 - half))(functools.partial(write, half))


def tail_kernel(slots, *refs):
    received = refs[:slots]
    hgrad_ref, back_ref, halo_ref, out_ref = refs[slots:]
    blocks = to_slots([r[...] for r in received], True)
    out_ref[...] = add_lists(hgrad_ref[...] + back_ref[...], halo_ref, blocks)


def call(
    kernel, operands, outs, scratch=(), limit=32, flops=0, in_hbm=(), out_hbm=False, aliases={}
):
    spaces = [pl.ANY if n in in_hbm else pltpu.VMEM for n in range(len(operands))]
    return pl.pallas_call(
        kernel,
        out_shape=[jax.ShapeDtypeStruct(s, d) for s, d in outs],
        in_specs=[pl.BlockSpec(memory_space=space) for space in spaces],
        out_specs=[pl.BlockSpec(memory_space=pl.ANY if out_hbm else pltpu.VMEM) for _ in outs],
        input_output_aliases=aliases,
        scratch_shapes=list(scratch),
        compiler_params=pltpu.CompilerParams(vmem_limit_bytes=limit * 2**20),
        cost_estimate=pl.CostEstimate(flops=flops, bytes_accessed=4 * 2**20, transcendentals=0),
    )(*operands)


def swap_cores(value, devices):
    return lax.ppermute(value, "shard", [(i, i + 1 - 2 * (i % 2)) for i in range(devices)])


def exchange(value):
    return lax.all_to_all(value, "shard", 0, 0, tiled=True)


def local(
    features, conv_weight, down_weight, neighbour_map, halo_rows, child_map, child_rows, out_grad
):
    voxels, channels = features.shape
    parents, coarse_channels = out_grad.shape
    kernel_count = conv_weight.shape[0]
    octants = down_weight.shape[0]
    slots, cap = halo_rows.shape
    cap2 = child_rows.shape[1]
    devices = lax.axis_size("shard")
    scale = 1.0 / math.sqrt(voxels * devices)
    giga = 10**9

    first = call(
        head_kernel,
        (features, halo_rows, child_map, out_grad, down_weight),
        [((cap + cap2, channels), BF16)] * slots + [((voxels, channels), F32)],
        scratch=[
            pltpu.VMEM(value.shape, value.dtype)
            for value in (features, halo_rows, child_map, out_grad, down_weight)
        ]
        + [pltpu.SemaphoreType.DMA((5,))],
        limit=60,
        flops=giga,
        in_hbm=range(5),
    )
    back_h = first[-1]
    received = swaps(first[:-1], (2, 3, 1, 0))
    conv_rows = kernel_count * channels
    down_rows = octants * channels * coarse_channels // LANES
    grain = 8 * devices
    half_rows = -(-(conv_rows + down_rows) // (2 * grain)) * grain
    (early,) = call(
        functools.partial(local_kernel, slots * cap),
        (features, neighbour_map),
        [((voxels, 8 * channels), BF16)],
        scratch=[pltpu.VMEM((voxels // 2, 2 * channels), BF16)],
        flops=4 * giga,
    )
    hidden, pre_act, stacked, *leaving = call(
        functools.partial(forward_kernel, slots),
        (*received, features, neighbour_map, conv_weight, child_rows, early),
        [
            ((voxels, channels), BF16),
            ((voxels, channels), F32),
            ((voxels, conv_rows), BF16),
        ]
        + [((cap2, channels), BF16)] * slots,
        scratch=[
            pltpu.VMEM((voxels // 2, 2 * channels), BF16),
            pltpu.VMEM((slots * cap, 4 * channels), BF16),
            pltpu.VMEM(conv_weight.shape, BF16),
        ]
        + [pltpu.VMEM((2, voxels, voxels // 2), BF16)] * 2
        + [pltpu.VMEM((voxels, slots * cap), BF16)] * 2
        + [pltpu.VMEM((2, voxels, LANES), BF16)] * 2,
        limit=32,
        flops=12 * giga,
    )
    hidden_grad, pre_grad, conv_terms = call(
        functools.partial(gradient_kernel, slots),
        (*received, stacked, pre_act, child_rows, back_h),
        [
            ((voxels, channels), F32),
            ((voxels, channels), BF16),
            ((conv_rows, channels), BF16),
        ],
        flops=3 * giga,
    )
    received_h = swaps(leaving, (1, 3, 2, 0))
    coarse, terms, leaving_terms = call(
        functools.partial(down_kernel, slots),
        (*received_h, hidden, child_map, down_weight, out_grad, conv_terms),
        [
            ((parents, coarse_channels), BF16),
            ((2 * half_rows, LANES), BF16),
            ((half_rows, LANES), BF16),
        ],
        scratch=[pltpu.VMEM((-(-(voxels + slots * cap2) // 256) * 128, 2 * channels), BF16)],
        flops=2 * giga,
    )
    (pair_terms,) = call(
        pair_kernel,
        (terms, swap_cores(leaving_terms, devices)),
        [((half_rows, LANES), BF16)],
        flops=10**6,
    )
    parts = exchange(pair_terms)
    spread = call(
        functools.partial(spread_kernel, slots),
        (pre_grad, neighbour_map, conv_weight, pair_terms),
        [((voxels, channels), F32)] + [((cap, channels), BF16)] * slots,
        scratch=[pltpu.VMEM((voxels // 2 + slots * cap // 2, 2 * channels), F32)],
        flops=20 * giga,
        in_hbm=(3,),
    )
    (summed,) = call(
        functools.partial(sum_kernel, devices, scale),
        (parts, spread[1]),
        [((half_rows, LANES), BF16)],
        flops=10**6,
        in_hbm=(1,),
    )
    summed, *returning = lax.optimization_barrier((summed, *spread[1:]))
    mine, *returned = lax.optimization_barrier((exchange(summed), *swaps(returning, (3, 1, 0, 2))))
    (input_grad,) = call(
        functools.partial(tail_kernel, slots),
        (*returned, hidden_grad, spread[0], halo_rows),
        [((voxels, channels), F32)],
        flops=giga,
    )
    other = swap_cores(mine, devices)
    gradients = ()
    for own, block in ((True, mine), (False, other)):
        gradients = call(
            functools.partial(final_kernel, own),
            (block, *gradients),
            [((conv_rows, LANES), F32), ((octants * channels, coarse_channels), F32)],
            scratch=[
                pltpu.VMEM((conv_rows, LANES), F32),
                pltpu.VMEM((octants * channels, coarse_channels), F32),
                pltpu.SemaphoreType.DMA((32,)),
            ],
            flops=10**6,
            in_hbm=(1, 2),
            out_hbm=True,
            aliases={1: 0, 2: 1} if gradients else {},
        )
    conv_grad, down_grad = gradients
    conv_grad = conv_grad.reshape(conv_weight.shape)
    return (coarse, input_grad, conv_grad, down_grad.reshape(down_weight.shape))


def solution(mesh):
    return jax.shard_map(
        local,
        mesh=mesh,
        in_specs=(
            P("shard", None),
            P(),
            P(),
            P(None, "shard"),
            P(None, "shard"),
            P(None, "shard"),
            P(None, "shard"),
            P("shard", None),
        ),
        out_specs=(P("shard", None), P("shard", None), P(), P()),
        check_vma=False,
    )
```

```python
import functools
import math

import jax
import jax.numpy as jnp
from jax import lax
from jax.experimental import pallas as pl
from jax.experimental.pallas import tpu as pltpu
from jax.sharding import PartitionSpec as P

BF16 = jnp.bfloat16
F32 = jnp.float32
LANES = 128


def swaps(by_step, order):
    devices = lax.axis_size("shard")
    moved = {}
    for step in order:
        m, phase = step // 2 + 1, step % 2
        sign = [1 if (i // m) % 2 == phase else -1 for i in range(devices)]
        pairs = [(i, i + m * sign[i]) for i in range(devices) if 0 <= i + m * sign[i] < devices]
        moved[step] = lax.ppermute(by_step[step], "shard", pairs)
    return [moved[step] for step in range(len(by_step))]


def is_even(m):
    return lax.rem(lax.div(lax.axis_index("shard"), m), 2) == 0


def to_steps(slots, back):
    reach = len(slots) // 2
    steps = []
    for m in range(1, reach + 1):
        first, second = slots[reach + m - 1], slots[reach - m]
        if back:
            first, second = second, first
        steps.append(lax.select(is_even(m), first, second))
        steps.append(lax.select(is_even(m), second, first))
    return steps


def to_slots(steps, back):
    reach = len(steps) // 2
    slots = [None] * len(steps)
    for m in range(1, reach + 1):
        first = lax.select(is_even(m), steps[2 * m - 2], steps[2 * m - 1])
        second = lax.select(is_even(m), steps[2 * m - 1], steps[2 * m - 2])
        if back:
            first, second = second, first
        slots[reach - m], slots[reach + m - 1] = first, second
    return slots


def matmul(left, right):
    return jnp.dot(left, right, preferred_element_type=F32)


def matmul_rt(left, right):
    return lax.dot_general(left, right, (((1,), (1,)), ((), ())), preferred_element_type=F32)


def pick_one(mask):
    return jnp.where(mask, jnp.ones(mask.shape, BF16), jnp.zeros(mask.shape, BF16))


def encode(row):
    return jnp.left_shift((row & (LANES - 1)) + LANES, row >> 7).astype(F32)


def column(codes):
    pieces = []
    for start in range(0, codes.shape[1], LANES):
        piece = jnp.broadcast_to(codes[:, start : start + LANES], (LANES, LANES))
        pieces.append(jnp.transpose(piece))
    return pieces[0] if len(pieces) == 1 else jnp.concatenate(pieces, axis=0)


def one_hot_rows(col, width, first=0):
    lane = lax.broadcasted_iota(jnp.int32, (16, LANES), 1)
    blocks = []
    for start in range(first, first + width, LANES):
        pattern = jnp.broadcast_to(encode(lane + start).astype(BF16)[0:1], col.shape)
        blocks.append(pick_one(col == pattern))
    return jnp.concatenate(blocks, axis=1)


def one_hot_columns(codes, height):
    place = lax.broadcasted_iota(jnp.int32, (height, codes.shape[1]), 0)
    pattern = encode(place).astype(BF16)
    return pick_one(jnp.broadcast_to(codes, pattern.shape) == pattern)


def pick_rows(col, table):
    both = matmul(one_hot_rows(jnp.abs(col), table.shape[0]), table).astype(BF16)
    return jnp.where(col < jnp.zeros(col.shape, BF16), both[:, LANES:], both[:, :LANES])


def list_row(lists, first, per_row):
    pieces = [lists[first + n : first + n + 1, :] for n in range(per_row)]
    return pieces[0] if per_row == 1 else jnp.concatenate(pieces, axis=1)


def add_lists(total, lists_ref, blocks):
    slots, cap = lists_ref.shape
    codes = encode(lists_ref[...]).astype(F32)
    per_row = max(1, min(slots, LANES // cap))
    for first in range(0, slots, per_row):
        row = list_row(codes, first, per_row).astype(BF16)
        rows = jnp.concatenate(blocks[first : first + per_row], axis=0)
        total = total + matmul(one_hot_columns(row, total.shape[0]), rows)
    return total


def gather_lists(lists_ref, table):
    slots, cap = lists_ref.shape
    lists = lists_ref[...]
    per_row = max(1, min(slots, LANES // cap))
    parts = []
    for first in range(0, slots, per_row):
        codes = encode(list_row(lists, first, per_row))
        chooser = one_hot_rows(column(codes).astype(BF16), table.shape[0])
        parts.append(matmul(chooser, table))
    return parts[0] if len(parts) == 1 else jnp.concatenate(parts, axis=0)


def head_kernel(features_hbm, halo_hbm, child_map_hbm, out_grad_hbm, down_hbm, *refs):
    sources = (features_hbm, halo_hbm, child_map_hbm, out_grad_hbm, down_hbm)
    buffers, sems = refs[-len(sources) - 1 : -1], refs[-1]
    features_ref, halo_ref, child_map_ref, out_grad_ref, down_ref = buffers
    copies = [
        pltpu.make_async_copy(source, buffer, sems.at[n])
        for n, (source, buffer) in enumerate(zip(sources, buffers))
    ]
    for copy in copies:
        copy.start()
    outs = refs[: -len(sources) - 1]
    sends, back_ref = outs[:-1], outs[-1]
    slots, cap = halo_ref.shape
    voxels = features_ref.shape[0]
    octants = child_map_ref.shape[0]
    table_rows = voxels + slots * (sends[0].shape[0] - cap)
    cap2 = (table_rows - voxels) // slots
    copies[0].wait()
    copies[1].wait()
    listed = gather_lists(halo_ref, features_ref[...]).astype(BF16)
    for send, block in zip(sends, to_steps(jnp.split(listed, slots), False)):
        send[0:cap, :] = block
    for copy in copies[2:]:
        copy.wait()
    upstream = out_grad_ref[...]
    codes = encode(child_map_ref[...]).astype(BF16)
    choosers, parts = [], []
    for o in range(octants):
        part = matmul_rt(upstream, down_ref[o])
        high = part.astype(BF16)
        low = (part - high.astype(F32)).astype(BF16)
        choosers.append(one_hot_columns(codes[o : o + 1, :], table_rows))
        parts.append(jnp.concatenate([high, low], axis=1))
    both = matmul(jnp.concatenate(choosers, axis=1), jnp.concatenate(parts, axis=0))
    total = both[:, :LANES] + both[:, LANES:]
    back_ref[...] = total[:voxels]
    for send, block in zip(sends, to_steps(jnp.split(total[voxels:].astype(BF16), slots), True)):
        send[cap : cap + cap2, :] = block


def half_codes(row, voxels, received):
    half, half_received = voxels // 2, received // 2
    beyond = row - voxels
    outside = beyond >= 0
    near = row - jnp.where(row >= half, half, 0)
    far = half + beyond - jnp.where(beyond >= half_received, half_received, 0)
    code = encode(jnp.where(outside, far, near))
    near_sign = jnp.where(row >= half, -1.0, 1.0)
    far_sign = jnp.where(beyond >= half_received, -1.0, 1.0)
    return code * jnp.where(outside, far_sign, near_sign)


def offset_of(n, middle):
    return n + jnp.where(n >= middle, 1, 0)


def code_column(map_ref, k, voxels, received):
    return column(half_codes(map_ref[pl.ds(k, 1), :], voxels, received).astype(BF16))


def pick_side(col, both):
    return jnp.where(col < jnp.zeros(col.shape, BF16), both[:, LANES:], both[:, :LANES])


def local_kernel(received, features_ref, map_ref, early_ref, table_ref):
    voxels = features_ref.shape[0]
    half = voxels // 2
    table_ref[:, 0:LANES] = features_ref[0:half, :]
    table_ref[:, LANES:] = features_ref[half:, :]
    middle = map_ref.shape[0] // 2
    for n in range(early_ref.shape[1] // LANES):
        col = code_column(map_ref, offset_of(n, middle), voxels, received)
        both = matmul(one_hot_rows(jnp.abs(col), half), table_ref[...]).astype(BF16)
        early_ref[:, n * LANES : (n + 1) * LANES] = pick_side(col, both)


def forward_kernel(slots, *refs):
    received = refs[:slots]
    features_ref, map_ref, weight_ref, child_ref, early_ref = refs[slots : slots + 5]
    hidden_ref, pre_ref, stacked_ref = refs[slots + 5 : slots + 8]
    sends = refs[slots + 8 : 2 * slots + 8]
    table_ref, halo_ref, kernel_ref = refs[2 * slots + 8 :]
    voxels = features_ref.shape[0]
    gathers = map_ref.shape[0] - 1
    middle = gathers // 2
    cap2 = child_ref.shape[1]
    cap = received[0].shape[0] - cap2
    half, half_halo = voxels // 2, slots * cap // 2
    features = features_ref[...]
    table_ref[:, 0:LANES] = features[0:half]
    table_ref[:, LANES:] = features[half:voxels]
    halo_ref[...] = jnp.zeros(halo_ref.shape, BF16)
    for s, block in enumerate(to_slots([r[0:cap, :] for r in received], False)):
        place = (s % (slots // 2)) * cap
        side = (s // (slots // 2)) * LANES
        for n in range(2):
            row, lane = n * half_halo + place, 2 * n * LANES + side
            halo_ref[row : row + cap, lane : lane + LANES] = block
    kernel_ref[0:middle] = weight_ref[0:middle]
    kernel_ref[middle:gathers] = weight_ref[middle + 1 :]
    kernel_ref[gathers] = weight_ref[middle]

    begun = early_ref.shape[1] // (2 * LANES)
    for j in range(middle):
        numbers = (2 * j, 2 * j + 1)
        cols = [code_column(map_ref, offset_of(n, middle), voxels, slots * cap) for n in numbers]
        choosers = [one_hot_rows(jnp.abs(col), half_halo, half) for col in cols]
        far = matmul(jnp.concatenate(choosers, axis=1), halo_ref[...])
        for n in numbers:
            col = cols[n % 2]
            both = far[:, 2 * (n % 2) * LANES : 2 * (n % 2 + 1) * LANES]
            lanes = slice(n * LANES, (n + 1) * LANES)
            if j < begun:
                picked = pick_side(col, both.astype(BF16)) + early_ref[:, lanes]
            else:
                own = matmul(one_hot_rows(jnp.abs(col), half), table_ref[...])
                picked = pick_side(col, (both + own).astype(BF16))
            stacked_ref[:, lanes] = picked

    stacked_ref[:, gathers * LANES :] = features
    pre = matmul(stacked_ref[...], kernel_ref[...].reshape(-1, LANES))
    pre_ref[...] = pre
    hidden = (features.astype(F32) + pre * jax.nn.sigmoid(pre)).astype(BF16)
    hidden_ref[...] = hidden
    leaving = gather_lists(child_ref, hidden).astype(BF16)
    for send, block in zip(sends, to_steps(jnp.split(leaving, slots), False)):
        send[...] = block


def gradient_kernel(slots, *refs):
    received = refs[:slots]
    stacked_ref, pre_ref, child_ref, back_ref = refs[slots : slots + 4]
    hidden_ref, child_map_ref, out_grad_ref = refs[slots + 4 : slots + 7]
    hgrad_ref, pgrad_ref, cgrad_ref, early_ref, upstream_t_ref = refs[slots + 7 :]
    cap2 = child_ref.shape[1]
    cap = received[0].shape[0] - cap2
    kernel_count = cgrad_ref.shape[0] // LANES
    middle = kernel_count // 2
    blocks = to_slots([r[cap : cap + cap2, :] for r in received], True)
    hgrad = add_lists(back_ref[...], child_ref, blocks)
    hgrad_ref[...] = hgrad
    pre = pre_ref[...]
    sig = jax.nn.sigmoid(pre)
    pgrad = hgrad * (sig * (1.0 + pre * (1.0 - sig)))
    pgrad_ref[...] = pgrad.astype(BF16)
    terms = matmul(jnp.transpose(pgrad).astype(BF16), stacked_ref[...])
    order = [k for k in range(kernel_count) if k != middle] + [middle]
    for n, k in enumerate(order):
        block = jnp.transpose(terms[:, n * LANES : (n + 1) * LANES])
        cgrad_ref[k * LANES : (k + 1) * LANES, :] = block.astype(BF16)
    voxels, parents = hidden_ref.shape[0], out_grad_ref.shape[0]
    half = voxels // 2
    hidden = hidden_ref[...]
    table = jnp.concatenate([hidden[0:half], hidden[half:]], axis=1)
    for o in range(child_map_ref.shape[0]):
        col = code_column(child_map_ref, o, voxels, slots * cap2)
        both = matmul(one_hot_rows(jnp.abs(col), half), table).astype(BF16)
        early_ref[:, o * LANES : (o + 1) * LANES] = pick_side(col, both)
    upstream_t_ref[...] = jnp.transpose(out_grad_ref[...].astype(F32)).astype(BF16)


def spread_kernel(slots, pgrad_ref, map_ref, weight_ref, after_ref, back_ref, *sends):
    acc_ref = sends[-1]
    sends = sends[:-1]
    voxels = pgrad_ref.shape[0]
    kernel_count = map_ref.shape[0]
    middle = kernel_count // 2
    cap = sends[0].shape[0]
    half = voxels // 2
    table_rows = half + slots * cap // 2
    pgrad = pgrad_ref[...]
    own = matmul_rt(pgrad, weight_ref[middle])
    acc_ref[0:half, 0:LANES] = own[0:half]
    acc_ref[0:half, LANES:] = own[half:]
    acc_ref[half:, :] = jnp.zeros((table_rows - half, 2 * LANES), F32)

    def parts(k):
        codes = half_codes(map_ref[pl.ds(k, 1), :], voxels, slots * cap)
        terms = matmul_rt(pgrad, weight_ref[k])
        right = column(codes) < 0.0
        sides = [jnp.where(right, 0.0, terms), jnp.where(right, terms, 0.0)]
        chooser = one_hot_columns(jnp.abs(codes).astype(BF16), table_rows)
        return chooser, jnp.concatenate(sides, axis=1).astype(BF16)

    def step(j, carry):
        near_chooser, near_terms = parts(j)
        far_chooser, far_terms = parts(j + middle + 1)
        acc_ref[...] += matmul(near_chooser, near_terms) + matmul(far_chooser, far_terms)
        return carry

    lax.fori_loop(0, middle, step, 0)
    back_ref[0:half, :] = acc_ref[0:half, 0:LANES]
    back_ref[half:, :] = acc_ref[0:half, LANES:]
    blocks = []
    for s in range(slots):
        first = half + (s % (slots // 2)) * cap
        side = (s // (slots // 2)) * LANES
        blocks.append(acc_ref[first : first + cap, side : side + LANES].astype(BF16))
    for send, block in zip(sends, to_steps(blocks, True)):
        send[...] = block


def my_half(rows):
    core = lax.rem(lax.axis_index("shard"), 2)
    return pl.multiple_of(core * rows, 16), pl.multiple_of((1 - core) * rows, 16)


def down_kernel(slots, voxels, *refs):
    received = refs[:slots]
    (early_ref, map_ref, down_ref, upstream_t_ref, cgrad_ref) = refs[slots : slots + 5]
    coarse_ref, terms_ref, send_ref = refs[slots + 5 :]
    cap2 = received[0].shape[0]
    octants, parents = map_ref.shape
    blocks = to_slots([r[...] for r in received], False)
    halo = jnp.concatenate(blocks, axis=0)
    rows = map_ref[...]
    codes = encode(jnp.where(rows >= voxels, rows - voxels, slots * cap2))
    picked = []
    for o in range(octants):
        chooser = one_hot_rows(column(codes[o : o + 1, :]).astype(BF16), slots * cap2)
        far = matmul(chooser, halo).astype(BF16)
        picked.append(far + early_ref[:, o * LANES : (o + 1) * LANES])
    picked = jnp.concatenate(picked, axis=1)
    row = cgrad_ref.shape[0]
    terms_ref[0:row, :] = cgrad_ref[...]
    terms = matmul(upstream_t_ref[...], picked)
    for o in range(octants):
        for start in range(0, terms.shape[0], LANES):
            block = terms[start : start + LANES, o * LANES : (o + 1) * LANES]
            terms_ref[row : row + LANES, :] = jnp.transpose(block).astype(BF16)
            row += LANES
    total = matmul(picked, down_ref[...].reshape(octants * LANES, down_ref.shape[2]))
    terms_ref[row:, :] = jnp.zeros((terms_ref.shape[0] - row, LANES), BF16)
    coarse_ref[...] = total.astype(BF16)
    send_ref[...] = terms_ref[pl.ds(my_half(send_ref.shape[0])[1], send_ref.shape[0]), :]


def pair_kernel(terms_ref, other_ref, out_ref):
    rows = other_ref.shape[0]
    mine = terms_ref[pl.ds(my_half(rows)[0], rows), :].astype(F32)
    out_ref[...] = (mine + other_ref[...].astype(F32)).astype(BF16)


def sum_kernel(devices, scale, parts_ref, after_ref, out_ref):
    rows = parts_ref.shape[0] // devices
    for core in range(2):
        mine = range(core, devices, 2)
        total = jnp.zeros((rows, LANES), F32)
        for d in mine:
            total = total + parts_ref[d * rows : (d + 1) * rows, :].astype(F32)
        total = (total * scale).astype(BF16)
        for d in mine:
            out_ref[d * rows : (d + 1) * rows, :] = total


def final_kernel(own, *refs):
    block_ref, conv_hbm, down_hbm = refs[0], *refs[-5:-3]
    conv_ref, down_ref, sems = refs[-3:]
    rows = block_ref.shape[0]
    conv_rows = conv_hbm.shape[0]
    core = lax.rem(lax.axis_index("shard"), 2)
    piece = 4 * LANES
    assert rows <= conv_rows <= 2 * rows and rows % LANES == 0

    def write(half):
        first, last = half * rows, (half + 1) * rows
        copies = []
        for start in range(first, min(last, conv_rows), piece):
            size = min(piece, last - start, conv_rows - start)
            place = pl.ds(start, size)
            value = block_ref[start - first : start - first + size, :]
            conv_ref[place, :] = value.astype(F32)
            sem = sems.at[len(copies)]
            copies.append(pltpu.make_async_copy(conv_ref.at[place], conv_hbm.at[place], sem))
            copies[-1].start()
        across = down_hbm.shape[1] // LANES
        for down in range(0, down_hbm.shape[0], LANES):
            row = conv_rows + down * across
            for side in range(across):
                start = row + side * LANES
                if first <= start < last:
                    value = block_ref[start - first : start - first + LANES, :]
                    lanes = slice(side * LANES, (side + 1) * LANES)
                    down_ref[down : down + LANES, lanes] = value.astype(F32)
            if first <= row < last:
                place = pl.ds(down, LANES)
                sem = sems.at[len(copies)]
                copies.append(pltpu.make_async_copy(down_ref.at[place], down_hbm.at[place], sem))
                copies[-1].start()
        for copy in copies:
            copy.wait()

    for half in range(2):
        pl.when(core == (half if own else 1 - half))(functools.partial(write, half))


def tail_kernel(slots, *refs):
    received = refs[:slots]
    hgrad_ref, back_ref, halo_ref, out_ref = refs[slots:]
    blocks = to_slots([r[...] for r in received], True)
    out_ref[...] = add_lists(hgrad_ref[...] + back_ref[...], halo_ref, blocks)


def call(
    kernel, operands, outs, scratch=(), limit=32, flops=0, in_hbm=(), out_hbm=False, aliases={}
):
    spaces = [pl.ANY if n in in_hbm else pltpu.VMEM for n in range(len(operands))]
    return pl.pallas_call(
        kernel,
        out_shape=[jax.ShapeDtypeStruct(s, d) for s, d in outs],
        in_specs=[pl.BlockSpec(memory_space=space) for space in spaces],
        out_specs=[pl.BlockSpec(memory_space=pl.ANY if out_hbm else pltpu.VMEM) for _ in outs],
        input_output_aliases=aliases,
        scratch_shapes=list(scratch),
        compiler_params=pltpu.CompilerParams(vmem_limit_bytes=limit * 2**20),
        cost_estimate=pl.CostEstimate(flops=flops, bytes_accessed=4 * 2**20, transcendentals=0),
    )(*operands)


def swap_cores(value, devices):
    return lax.ppermute(value, "shard", [(i, i + 1 - 2 * (i % 2)) for i in range(devices)])


def exchange(value):
    return lax.all_to_all(value, "shard", 0, 0, tiled=True)


def local(
    features, conv_weight, down_weight, neighbour_map, halo_rows, child_map, child_rows, out_grad
):
    voxels, channels = features.shape
    parents, coarse_channels = out_grad.shape
    kernel_count = conv_weight.shape[0]
    octants = down_weight.shape[0]
    slots, cap = halo_rows.shape
    cap2 = child_rows.shape[1]
    devices = lax.axis_size("shard")
    scale = 1.0 / math.sqrt(voxels * devices)
    giga = 10**9

    first = call(
        head_kernel,
        (features, halo_rows, child_map, out_grad, down_weight),
        [((cap + cap2, channels), BF16)] * slots + [((voxels, channels), F32)],
        scratch=[
            pltpu.VMEM(value.shape, value.dtype)
            for value in (features, halo_rows, child_map, out_grad, down_weight)
        ]
        + [pltpu.SemaphoreType.DMA((5,))],
        limit=60,
        flops=giga,
        in_hbm=range(5),
    )
    back_h = first[-1]
    received = swaps(first[:-1], (2, 3, 1, 0))
    conv_rows = kernel_count * channels
    down_rows = octants * channels * coarse_channels // LANES
    grain = 8 * devices
    half_rows = -(-(conv_rows + down_rows) // (2 * grain)) * grain
    (early,) = call(
        functools.partial(local_kernel, slots * cap),
        (features, neighbour_map),
        [((voxels, 12 * channels), BF16)],
        scratch=[pltpu.VMEM((voxels // 2, 2 * channels), BF16)],
        flops=4 * giga,
    )
    hidden, pre_act, stacked, *leaving = call(
        functools.partial(forward_kernel, slots),
        (*received, features, neighbour_map, conv_weight, child_rows, early),
        [
            ((voxels, channels), BF16),
            ((voxels, channels), F32),
            ((voxels, conv_rows), BF16),
        ]
        + [((cap2, channels), BF16)] * slots,
        scratch=[
            pltpu.VMEM((voxels // 2, 2 * channels), BF16),
            pltpu.VMEM((slots * cap, 4 * channels), BF16),
            pltpu.VMEM(conv_weight.shape, BF16),
        ],
        limit=32,
        flops=12 * giga,
    )
    hidden_grad, pre_grad, conv_terms, early_h, out_grad_t = call(
        functools.partial(gradient_kernel, slots),
        (*received, stacked, pre_act, child_rows, back_h, hidden, child_map, out_grad),
        [
            ((voxels, channels), F32),
            ((voxels, channels), BF16),
            ((conv_rows, channels), BF16),
            ((parents, octants * channels), BF16),
            ((coarse_channels, parents), BF16),
        ],
        flops=3 * giga,
    )
    received_h = swaps(leaving, (1, 3, 2, 0))
    coarse, terms, leaving_terms = call(
        functools.partial(down_kernel, slots, voxels),
        (*received_h, early_h, child_map, down_weight, out_grad_t, conv_terms),
        [
            ((parents, coarse_channels), BF16),
            ((2 * half_rows, LANES), BF16),
            ((half_rows, LANES), BF16),
        ],
        flops=2 * giga,
    )
    (pair_terms,) = call(
        pair_kernel,
        (terms, swap_cores(leaving_terms, devices)),
        [((half_rows, LANES), BF16)],
        flops=10**6,
    )
    parts = exchange(pair_terms)
    spread = call(
        functools.partial(spread_kernel, slots),
        (pre_grad, neighbour_map, conv_weight, pair_terms),
        [((voxels, channels), F32)] + [((cap, channels), BF16)] * slots,
        scratch=[pltpu.VMEM((voxels // 2 + slots * cap // 2, 2 * channels), F32)],
        flops=20 * giga,
        in_hbm=(3,),
    )
    (summed,) = call(
        functools.partial(sum_kernel, devices, scale),
        (parts, spread[1]),
        [((half_rows, LANES), BF16)],
        flops=10**6,
        in_hbm=(1,),
    )
    summed, *returning = lax.optimization_barrier((summed, *spread[1:]))
    returned = swaps(returning, (0, 1, 2, 3))
    (input_grad,) = call(
        functools.partial(tail_kernel, slots),
        (*returned, hidden_grad, spread[0], halo_rows),
        [((voxels, channels), F32)],
        flops=giga,
    )
    mine, input_grad = lax.optimization_barrier((exchange(summed), input_grad))
    other = swap_cores(mine, devices)
    gradients = ()
    for own, block in ((True, mine), (False, other)):
        gradients = call(
            functools.partial(final_kernel, own),
            (block, *gradients),
            [((conv_rows, LANES), F32), ((octants * channels, coarse_channels), F32)],
            scratch=[
                pltpu.VMEM((conv_rows, LANES), F32),
                pltpu.VMEM((octants * channels, coarse_channels), F32),
                pltpu.SemaphoreType.DMA((32,)),
            ],
            flops=10**6,
            in_hbm=(1, 2),
            out_hbm=True,
            aliases={1: 0, 2: 1} if gradients else {},
        )
    conv_grad, down_grad = gradients
    conv_grad = conv_grad.reshape(conv_weight.shape)
    return (coarse, input_grad, conv_grad, down_grad.reshape(down_weight.shape))


def solution(mesh):
    return jax.shard_map(
        local,
        mesh=mesh,
        in_specs=(
            P("shard", None),
            P(),
            P(),
            P(None, "shard"),
            P(None, "shard"),
            P(None, "shard"),
            P(None, "shard"),
            P("shard", None),
        ),
        out_specs=(P("shard", None), P("shard", None), P(), P()),
        check_vma=False,
    )
```

```python
import functools
import math

import jax
import jax.numpy as jnp
from jax import lax
from jax.experimental import pallas as pl
from jax.experimental.pallas import tpu as pltpu
from jax.sharding import PartitionSpec as P

BF16 = jnp.bfloat16
F32 = jnp.float32
LANES = 128


def swaps(by_step, order):
    devices = lax.axis_size("shard")
    moved = {}
    for step in order:
        m, phase = step // 2 + 1, step % 2
        sign = [1 if (i // m) % 2 == phase else -1 for i in range(devices)]
        pairs = [(i, i + m * sign[i]) for i in range(devices) if 0 <= i + m * sign[i] < devices]
        moved[step] = lax.ppermute(by_step[step], "shard", pairs)
    return [moved[step] for step in range(len(by_step))]


def is_even(m):
    return lax.rem(lax.div(lax.axis_index("shard"), m), 2) == 0


def to_steps(slots, back):
    reach = len(slots) // 2
    steps = []
    for m in range(1, reach + 1):
        first, second = slots[reach + m - 1], slots[reach - m]
        if back:
            first, second = second, first
        steps.append(lax.select(is_even(m), first, second))
        steps.append(lax.select(is_even(m), second, first))
    return steps


def to_slots(steps, back):
    reach = len(steps) // 2
    slots = [None] * len(steps)
    for m in range(1, reach + 1):
        first = lax.select(is_even(m), steps[2 * m - 2], steps[2 * m - 1])
        second = lax.select(is_even(m), steps[2 * m - 1], steps[2 * m - 2])
        if back:
            first, second = second, first
        slots[reach - m], slots[reach + m - 1] = first, second
    return slots


def matmul(left, right):
    return jnp.dot(left, right, preferred_element_type=F32)


def matmul_rt(left, right):
    return lax.dot_general(left, right, (((1,), (1,)), ((), ())), preferred_element_type=F32)


def pick_one(mask):
    return jnp.where(mask, jnp.ones(mask.shape, BF16), jnp.zeros(mask.shape, BF16))


def encode(row):
    return jnp.left_shift((row & (LANES - 1)) + LANES, row >> 7).astype(F32)


def column(codes):
    pieces = []
    for start in range(0, codes.shape[1], LANES):
        piece = jnp.broadcast_to(codes[:, start : start + LANES], (LANES, LANES))
        pieces.append(jnp.transpose(piece))
    return pieces[0] if len(pieces) == 1 else jnp.concatenate(pieces, axis=0)


def one_hot_rows(col, width, first=0):
    lane = lax.broadcasted_iota(jnp.int32, (16, LANES), 1)
    blocks = []
    for start in range(first, first + width, LANES):
        pattern = jnp.broadcast_to(encode(lane + start).astype(BF16)[0:1], col.shape)
        blocks.append(pick_one(col == pattern))
    return jnp.concatenate(blocks, axis=1)


def one_hot_columns(codes, height):
    place = lax.broadcasted_iota(jnp.int32, (height, codes.shape[1]), 0)
    pattern = encode(place).astype(BF16)
    return pick_one(jnp.broadcast_to(codes, pattern.shape) == pattern)


def pick_rows(col, table):
    both = matmul(one_hot_rows(jnp.abs(col), table.shape[0]), table).astype(BF16)
    return jnp.where(col < jnp.zeros(col.shape, BF16), both[:, LANES:], both[:, :LANES])


def list_row(lists, first, per_row):
    pieces = [lists[first + n : first + n + 1, :] for n in range(per_row)]
    return pieces[0] if per_row == 1 else jnp.concatenate(pieces, axis=1)


def add_lists(total, lists_ref, blocks):
    slots, cap = lists_ref.shape
    codes = encode(lists_ref[...]).astype(F32)
    per_row = max(1, min(slots, LANES // cap))
    for first in range(0, slots, per_row):
        row = list_row(codes, first, per_row).astype(BF16)
        rows = jnp.concatenate(blocks[first : first + per_row], axis=0)
        total = total + matmul(one_hot_columns(row, total.shape[0]), rows)
    return total


def gather_lists(lists_ref, table):
    slots, cap = lists_ref.shape
    lists = lists_ref[...]
    per_row = max(1, min(slots, LANES // cap))
    parts = []
    for first in range(0, slots, per_row):
        codes = encode(list_row(lists, first, per_row))
        chooser = one_hot_rows(column(codes).astype(BF16), table.shape[0])
        parts.append(matmul(chooser, table))
    return parts[0] if len(parts) == 1 else jnp.concatenate(parts, axis=0)


def head_kernel(features_hbm, halo_hbm, child_map_hbm, out_grad_hbm, down_hbm, *refs):
    sources = (features_hbm, halo_hbm, child_map_hbm, out_grad_hbm, down_hbm)
    buffers, sems = refs[-len(sources) - 1 : -1], refs[-1]
    features_ref, halo_ref, child_map_ref, out_grad_ref, down_ref = buffers
    copies = [
        pltpu.make_async_copy(source, buffer, sems.at[n])
        for n, (source, buffer) in enumerate(zip(sources, buffers))
    ]
    for copy in copies:
        copy.start()
    outs = refs[: -len(sources) - 1]
    sends, back_ref = outs[:-1], outs[-1]
    slots, cap = halo_ref.shape
    voxels = features_ref.shape[0]
    octants = child_map_ref.shape[0]
    table_rows = voxels + slots * (sends[0].shape[0] - cap)
    cap2 = (table_rows - voxels) // slots
    copies[0].wait()
    copies[1].wait()
    listed = gather_lists(halo_ref, features_ref[...]).astype(BF16)
    for send, block in zip(sends, to_steps(jnp.split(listed, slots), False)):
        send[0:cap, :] = block
    for copy in copies[2:]:
        copy.wait()
    upstream = out_grad_ref[...]
    codes = encode(child_map_ref[...]).astype(BF16)
    choosers, parts = [], []
    for o in range(octants):
        part = matmul_rt(upstream, down_ref[o])
        high = part.astype(BF16)
        low = (part - high.astype(F32)).astype(BF16)
        choosers.append(one_hot_columns(codes[o : o + 1, :], table_rows))
        parts.append(jnp.concatenate([high, low], axis=1))
    both = matmul(jnp.concatenate(choosers, axis=1), jnp.concatenate(parts, axis=0))
    total = both[:, :LANES] + both[:, LANES:]
    back_ref[...] = total[:voxels]
    for send, block in zip(sends, to_steps(jnp.split(total[voxels:].astype(BF16), slots), True)):
        send[cap : cap + cap2, :] = block


def half_codes(row, voxels, received):
    half, half_received = voxels // 2, received // 2
    beyond = row - voxels
    outside = beyond >= 0
    near = row - jnp.where(row >= half, half, 0)
    far = half + beyond - jnp.where(beyond >= half_received, half_received, 0)
    code = encode(jnp.where(outside, far, near))
    near_sign = jnp.where(row >= half, -1.0, 1.0)
    far_sign = jnp.where(beyond >= half_received, -1.0, 1.0)
    return code * jnp.where(outside, far_sign, near_sign)


def offset_of(n, middle):
    return n + jnp.where(n >= middle, 1, 0)


def code_column(map_ref, k, voxels, received):
    return column(half_codes(map_ref[pl.ds(k, 1), :], voxels, received).astype(BF16))


def pick_side(col, both):
    return jnp.where(col < jnp.zeros(col.shape, BF16), both[:, LANES:], both[:, :LANES])


def local_kernel(received, features_ref, map_ref, early_ref, table_ref):
    voxels = features_ref.shape[0]
    half = voxels // 2
    table_ref[:, 0:LANES] = features_ref[0:half, :]
    table_ref[:, LANES:] = features_ref[half:, :]
    middle = map_ref.shape[0] // 2
    for n in range(early_ref.shape[1] // LANES):
        col = code_column(map_ref, offset_of(n, middle), voxels, received)
        both = matmul(one_hot_rows(jnp.abs(col), half), table_ref[...]).astype(BF16)
        early_ref[:, n * LANES : (n + 1) * LANES] = pick_side(col, both)


def forward_kernel(slots, *refs):
    received = refs[:slots]
    features_ref, map_ref, weight_ref, child_ref, early_ref = refs[slots : slots + 5]
    hidden_ref, pre_ref, stacked_ref = refs[slots + 5 : slots + 8]
    sends = refs[slots + 8 : 2 * slots + 8]
    table_ref, halo_ref, kernel_ref = refs[2 * slots + 8 :]
    voxels = features_ref.shape[0]
    gathers = map_ref.shape[0] - 1
    middle = gathers // 2
    cap2 = child_ref.shape[1]
    cap = received[0].shape[0] - cap2
    half, half_halo = voxels // 2, slots * cap // 2
    features = features_ref[...]
    table_ref[:, 0:LANES] = features[0:half]
    table_ref[:, LANES:] = features[half:voxels]
    halo_ref[...] = jnp.zeros(halo_ref.shape, BF16)
    for s, block in enumerate(to_slots([r[0:cap, :] for r in received], False)):
        place = (s % (slots // 2)) * cap
        side = (s // (slots // 2)) * LANES
        for n in range(2):
            row, lane = n * half_halo + place, 2 * n * LANES + side
            halo_ref[row : row + cap, lane : lane + LANES] = block
    kernel_ref[0:middle] = weight_ref[0:middle]
    kernel_ref[middle:gathers] = weight_ref[middle + 1 :]
    kernel_ref[gathers] = weight_ref[middle]

    begun = early_ref.shape[1] // (2 * LANES)
    for j in range(middle):
        numbers = (2 * j, 2 * j + 1)
        cols = [code_column(map_ref, offset_of(n, middle), voxels, slots * cap) for n in numbers]
        choosers = [one_hot_rows(jnp.abs(col), half_halo, half) for col in cols]
        far = matmul(jnp.concatenate(choosers, axis=1), halo_ref[...])
        for n in numbers:
            col = cols[n % 2]
            both = far[:, 2 * (n % 2) * LANES : 2 * (n % 2 + 1) * LANES]
            lanes = slice(n * LANES, (n + 1) * LANES)
            if j < begun:
                picked = pick_side(col, both.astype(BF16)) + early_ref[:, lanes]
            else:
                own = matmul(one_hot_rows(jnp.abs(col), half), table_ref[...])
                picked = pick_side(col, (both + own).astype(BF16))
            stacked_ref[:, lanes] = picked

    stacked_ref[:, gathers * LANES :] = features
    pre = matmul(stacked_ref[...], kernel_ref[...].reshape(-1, LANES))
    pre_ref[...] = pre
    hidden = (features.astype(F32) + pre * jax.nn.sigmoid(pre)).astype(BF16)
    hidden_ref[...] = hidden
    leaving = gather_lists(child_ref, hidden).astype(BF16)
    for send, block in zip(sends, to_steps(jnp.split(leaving, slots), False)):
        send[...] = block


def gradient_kernel(slots, *refs):
    received = refs[:slots]
    stacked_ref, pre_ref, child_ref, back_ref = refs[slots : slots + 4]
    hidden_ref, child_map_ref, out_grad_ref = refs[slots + 4 : slots + 7]
    hgrad_ref, pgrad_ref, cgrad_ref, early_ref, upstream_t_ref = refs[slots + 7 :]
    cap2 = child_ref.shape[1]
    cap = received[0].shape[0] - cap2
    kernel_count = cgrad_ref.shape[0] // LANES
    middle = kernel_count // 2
    blocks = to_slots([r[cap : cap + cap2, :] for r in received], True)
    hgrad = add_lists(back_ref[...], child_ref, blocks)
    hgrad_ref[...] = hgrad
    pre = pre_ref[...]
    sig = jax.nn.sigmoid(pre)
    pgrad = hgrad * (sig * (1.0 + pre * (1.0 - sig)))
    pgrad_ref[...] = pgrad.astype(BF16)
    terms = matmul(jnp.transpose(pgrad).astype(BF16), stacked_ref[...])
    order = [k for k in range(kernel_count) if k != middle] + [middle]
    for n, k in enumerate(order):
        block = jnp.transpose(terms[:, n * LANES : (n + 1) * LANES])
        cgrad_ref[k * LANES : (k + 1) * LANES, :] = block.astype(BF16)
    voxels, parents = hidden_ref.shape[0], out_grad_ref.shape[0]
    half = voxels // 2
    hidden = hidden_ref[...]
    table = jnp.concatenate([hidden[0:half], hidden[half:]], axis=1)
    for o in range(child_map_ref.shape[0]):
        col = code_column(child_map_ref, o, voxels, slots * cap2)
        both = matmul(one_hot_rows(jnp.abs(col), half), table).astype(BF16)
        early_ref[:, o * LANES : (o + 1) * LANES] = pick_side(col, both)
    upstream_t_ref[...] = jnp.transpose(out_grad_ref[...].astype(F32)).astype(BF16)


def spread_kernel(slots, pgrad_ref, map_ref, weight_ref, after_ref, back_ref, *sends):
    acc_ref = sends[-1]
    sends = sends[:-1]
    voxels = pgrad_ref.shape[0]
    kernel_count = map_ref.shape[0]
    middle = kernel_count // 2
    cap = sends[0].shape[0]
    half = voxels // 2
    table_rows = half + slots * cap // 2
    pgrad = pgrad_ref[...]
    own = matmul_rt(pgrad, weight_ref[middle])
    acc_ref[0:half, 0:LANES] = own[0:half]
    acc_ref[0:half, LANES:] = own[half:]
    acc_ref[half:, :] = jnp.zeros((table_rows - half, 2 * LANES), F32)

    for j in range(middle):
        numbers = (j, j + middle + 1)
        kernels = jnp.concatenate([weight_ref[k] for k in numbers], axis=0)
        terms = matmul_rt(pgrad, kernels).astype(BF16)
        choosers, sides = [], []
        for n, k in enumerate(numbers):
            codes = half_codes(map_ref[k : k + 1, :], voxels, slots * cap).astype(BF16)
            right = column(codes) < jnp.zeros((voxels, LANES), BF16)
            mine = terms[:, n * LANES : (n + 1) * LANES]
            none = jnp.zeros(mine.shape, BF16)
            pair = [jnp.where(right, none, mine), jnp.where(right, mine, none)]
            sides.append(jnp.concatenate(pair, axis=1))
            choosers.append(one_hot_columns(jnp.abs(codes), table_rows))
        acc_ref[...] += matmul(choosers[0], sides[0]) + matmul(choosers[1], sides[1])

    back_ref[0:half, :] = acc_ref[0:half, 0:LANES]
    back_ref[half:, :] = acc_ref[0:half, LANES:]
    blocks = []
    for s in range(slots):
        first = half + (s % (slots // 2)) * cap
        side = (s // (slots // 2)) * LANES
        blocks.append(acc_ref[first : first + cap, side : side + LANES].astype(BF16))
    for send, block in zip(sends, to_steps(blocks, True)):
        send[...] = block


def my_half(rows):
    core = lax.rem(lax.axis_index("shard"), 2)
    return pl.multiple_of(core * rows, 16), pl.multiple_of((1 - core) * rows, 16)


def down_kernel(slots, voxels, *refs):
    received = refs[:slots]
    (early_ref, map_ref, down_ref, upstream_t_ref, cgrad_ref) = refs[slots : slots + 5]
    coarse_ref, terms_ref, send_ref = refs[slots + 5 :]
    cap2 = received[0].shape[0]
    octants, parents = map_ref.shape
    blocks = to_slots([r[...] for r in received], False)
    halo = jnp.concatenate(blocks, axis=0)
    rows = map_ref[...]
    codes = encode(jnp.where(rows >= voxels, rows - voxels, slots * cap2))
    picked = []
    for o in range(octants):
        chooser = one_hot_rows(column(codes[o : o + 1, :]).astype(BF16), slots * cap2)
        far = matmul(chooser, halo).astype(BF16)
        picked.append(far + early_ref[:, o * LANES : (o + 1) * LANES])
    picked = jnp.concatenate(picked, axis=1)
    row = cgrad_ref.shape[0]
    terms_ref[0:row, :] = cgrad_ref[...]
    terms = matmul(upstream_t_ref[...], picked)
    for o in range(octants):
        for start in range(0, terms.shape[0], LANES):
            block = terms[start : start + LANES, o * LANES : (o + 1) * LANES]
            terms_ref[row : row + LANES, :] = jnp.transpose(block).astype(BF16)
            row += LANES
    total = matmul(picked, down_ref[...].reshape(octants * LANES, down_ref.shape[2]))
    terms_ref[row:, :] = jnp.zeros((terms_ref.shape[0] - row, LANES), BF16)
    coarse_ref[...] = total.astype(BF16)
    send_ref[...] = terms_ref[pl.ds(my_half(send_ref.shape[0])[1], send_ref.shape[0]), :]


def pair_kernel(terms_ref, other_ref, out_ref):
    rows = other_ref.shape[0]
    mine = terms_ref[pl.ds(my_half(rows)[0], rows), :].astype(F32)
    out_ref[...] = (mine + other_ref[...].astype(F32)).astype(BF16)


def sum_kernel(devices, scale, parts_ref, out_ref):
    rows = parts_ref.shape[0] // devices
    for core in range(2):
        total = jnp.zeros((rows, LANES), F32)
        for d in range(core, devices, 2):
            total = total + parts_ref[d * rows : (d + 1) * rows, :].astype(F32)
        out_ref[core * rows : (core + 1) * rows, :] = (total * scale).astype(BF16)


def final_kernel(chips, inner, mine_ref, other_ref, conv_hbm, down_hbm, whole_ref, down_ref, sems):
    half = mine_ref.shape[0]
    rows = half // (2 * chips)
    core = lax.rem(lax.axis_index("shard"), 2)
    outer = chips // inner
    for block_ref, side in ((mine_ref, core), (other_ref, 1 - core)):
        for place in range(chips):
            chip = place % outer * inner + place // outer
            for h in range(2):
                first = (2 * place + h) * rows
                target = pl.multiple_of(h * half + (2 * chip + side) * rows, 8)
                value = block_ref[first : first + rows, :].astype(F32)
                whole_ref[pl.ds(target, rows), :] = value
    row = conv_hbm.shape[0]
    conv_copy = pltpu.make_async_copy(whole_ref.at[pl.ds(0, row)], conv_hbm, sems.at[0])
    conv_copy.start()
    for down in range(0, down_ref.shape[0], LANES):
        for start in range(0, down_ref.shape[1], LANES):
            block = whole_ref[row : row + LANES, :]
            down_ref[down : down + LANES, start : start + LANES] = block
            row += LANES
    down_copy = pltpu.make_async_copy(down_ref, down_hbm, sems.at[1])
    down_copy.start()
    conv_copy.wait()
    down_copy.wait()


def tail_kernel(slots, *refs):
    received = refs[:slots]
    hgrad_ref, back_ref, halo_ref, out_ref = refs[slots:]
    blocks = to_slots([r[...] for r in received], True)
    out_ref[...] = add_lists(hgrad_ref[...] + back_ref[...], halo_ref, blocks)


def call(kernel, operands, outs, scratch=(), limit=32, flops=0, in_hbm=(), out_hbm=False):
    spaces = [pl.ANY if n in in_hbm else pltpu.VMEM for n in range(len(operands))]
    return pl.pallas_call(
        kernel,
        out_shape=[jax.ShapeDtypeStruct(s, d) for s, d in outs],
        in_specs=[pl.BlockSpec(memory_space=space) for space in spaces],
        out_specs=[pl.BlockSpec(memory_space=pl.ANY if out_hbm else pltpu.VMEM) for _ in outs],
        scratch_shapes=list(scratch),
        compiler_params=pltpu.CompilerParams(vmem_limit_bytes=limit * 2**20),
        cost_estimate=pl.CostEstimate(flops=flops, bytes_accessed=4 * 2**20, transcendentals=0),
    )(*operands)


def swap_cores(value, devices):
    return lax.ppermute(value, "shard", [(i, i + 1 - 2 * (i % 2)) for i in range(devices)])


def gather_blocks(value, devices, inner):
    chips = devices // 2
    far = [[2 * c + q for c in range(i, chips, inner)] for i in range(inner) for q in range(2)]
    near = [
        [2 * (o + i) + q for i in range(inner)] for o in range(0, chips, inner) for q in range(2)
    ]
    for groups in (far, near):
        value = lax.all_gather(value, "shard", axis_index_groups=groups, axis=0, tiled=True)
    return value


def exchange(value):
    return lax.all_to_all(value, "shard", 0, 0, tiled=True)


def local(
    features, conv_weight, down_weight, neighbour_map, halo_rows, child_map, child_rows, out_grad
):
    voxels, channels = features.shape
    parents, coarse_channels = out_grad.shape
    kernel_count = conv_weight.shape[0]
    octants = down_weight.shape[0]
    slots, cap = halo_rows.shape
    cap2 = child_rows.shape[1]
    devices = lax.axis_size("shard")
    scale = 1.0 / math.sqrt(voxels * devices)
    giga = 10**9

    first = call(
        head_kernel,
        (features, halo_rows, child_map, out_grad, down_weight),
        [((cap + cap2, channels), BF16)] * slots + [((voxels, channels), F32)],
        scratch=[
            pltpu.VMEM(value.shape, value.dtype)
            for value in (features, halo_rows, child_map, out_grad, down_weight)
        ]
        + [pltpu.SemaphoreType.DMA((5,))],
        limit=60,
        flops=giga,
        in_hbm=range(5),
    )
    back_h = first[-1]
    received = swaps(first[:-1], (2, 3, 1, 0))
    conv_rows = kernel_count * channels
    down_rows = octants * channels * coarse_channels // LANES
    grain = 8 * devices
    half_rows = -(-(conv_rows + down_rows) // (2 * grain)) * grain
    (early,) = call(
        functools.partial(local_kernel, slots * cap),
        (features, neighbour_map),
        [((voxels, 12 * channels), BF16)],
        scratch=[pltpu.VMEM((voxels // 2, 2 * channels), BF16)],
        flops=4 * giga,
    )
    hidden, pre_act, stacked, *leaving = call(
        functools.partial(forward_kernel, slots),
        (*received, features, neighbour_map, conv_weight, child_rows, early),
        [
            ((voxels, channels), BF16),
            ((voxels, channels), F32),
            ((voxels, conv_rows), BF16),
        ]
        + [((cap2, channels), BF16)] * slots,
        scratch=[
            pltpu.VMEM((voxels // 2, 2 * channels), BF16),
            pltpu.VMEM((slots * cap, 4 * channels), BF16),
            pltpu.VMEM(conv_weight.shape, BF16),
        ],
        limit=32,
        flops=12 * giga,
    )
    hidden_grad, pre_grad, conv_terms, early_h, out_grad_t = call(
        functools.partial(gradient_kernel, slots),
        (*received, stacked, pre_act, child_rows, back_h, hidden, child_map, out_grad),
        [
            ((voxels, channels), F32),
            ((voxels, channels), BF16),
            ((conv_rows, channels), BF16),
            ((parents, octants * channels), BF16),
            ((coarse_channels, parents), BF16),
        ],
        flops=3 * giga,
    )
    received_h = swaps(leaving, (1, 3, 2, 0))
    coarse, terms, leaving_terms = call(
        functools.partial(down_kernel, slots, voxels),
        (*received_h, early_h, child_map, down_weight, out_grad_t, conv_terms),
        [
            ((parents, coarse_channels), BF16),
            ((2 * half_rows, LANES), BF16),
            ((half_rows, LANES), BF16),
        ],
        flops=2 * giga,
    )
    (pair_terms,) = call(
        pair_kernel,
        (terms, swap_cores(leaving_terms, devices)),
        [((half_rows, LANES), BF16)],
        flops=10**6,
    )
    parts = exchange(pair_terms)
    spread = call(
        functools.partial(spread_kernel, slots),
        (pre_grad, neighbour_map, conv_weight, pair_terms),
        [((voxels, channels), F32)] + [((cap, channels), BF16)] * slots,
        scratch=[pltpu.VMEM((voxels // 2 + slots * cap // 2, 2 * channels), F32)],
        flops=20 * giga,
        in_hbm=(3,),
    )
    returned = swaps(spread[1:], (0, 1, 2, 3))
    parts, *returned = lax.optimization_barrier((parts, *returned))
    (input_grad,) = call(
        functools.partial(tail_kernel, slots),
        (*returned, hidden_grad, spread[0], halo_rows),
        [((voxels, channels), F32)],
        flops=giga,
    )
    (summed,) = call(
        functools.partial(sum_kernel, devices, scale),
        (parts,),
        [((2 * half_rows // devices, LANES), BF16)],
        flops=10**6,
    )
    inner = 4
    mine = gather_blocks(summed, devices, inner)
    conv_grad, down_grad = call(
        functools.partial(final_kernel, devices // 2, inner),
        (mine, swap_cores(mine, devices)),
        [((conv_rows, LANES), F32), ((octants * channels, coarse_channels), F32)],
        scratch=[
            pltpu.VMEM((2 * half_rows, LANES), F32),
            pltpu.VMEM((octants * channels, coarse_channels), F32),
            pltpu.SemaphoreType.DMA((2,)),
        ],
        flops=10**6,
        out_hbm=True,
    )
    conv_grad = conv_grad.reshape(conv_weight.shape)
    return (coarse, input_grad, conv_grad, down_grad.reshape(down_weight.shape))


def solution(mesh):
    return jax.shard_map(
        local,
        mesh=mesh,
        in_specs=(
            P("shard", None),
            P(),
            P(),
            P(None, "shard"),
            P(None, "shard"),
            P(None, "shard"),
            P(None, "shard"),
            P("shard", None),
        ),
        out_specs=(P("shard", None), P("shard", None), P(), P()),
        check_vma=False,
    )
```

```python
import functools
import math

import jax
import jax.numpy as jnp
from jax import lax
from jax.experimental import pallas as pl
from jax.experimental.pallas import tpu as pltpu
from jax.sharding import PartitionSpec as P

BF16 = jnp.bfloat16
F32 = jnp.float32
LANES = 128


def swaps(by_step, order):
    devices = lax.axis_size("shard")
    moved = {}
    for step in order:
        m, phase = step // 2 + 1, step % 2
        sign = [1 if (i // m) % 2 == phase else -1 for i in range(devices)]
        pairs = [(i, i + m * sign[i]) for i in range(devices) if 0 <= i + m * sign[i] < devices]
        moved[step] = lax.ppermute(by_step[step], "shard", pairs)
    return [moved[step] for step in range(len(by_step))]


def is_even(m):
    return lax.rem(lax.div(lax.axis_index("shard"), m), 2) == 0


def to_steps(slots, back):
    reach = len(slots) // 2
    steps = []
    for m in range(1, reach + 1):
        first, second = slots[reach + m - 1], slots[reach - m]
        if back:
            first, second = second, first
        steps.append(lax.select(is_even(m), first, second))
        steps.append(lax.select(is_even(m), second, first))
    return steps


def to_slots(steps, back):
    reach = len(steps) // 2
    slots = [None] * len(steps)
    for m in range(1, reach + 1):
        first = lax.select(is_even(m), steps[2 * m - 2], steps[2 * m - 1])
        second = lax.select(is_even(m), steps[2 * m - 1], steps[2 * m - 2])
        if back:
            first, second = second, first
        slots[reach - m], slots[reach + m - 1] = first, second
    return slots


def matmul(left, right):
    return jnp.dot(left, right, preferred_element_type=F32)


def matmul_rt(left, right):
    return lax.dot_general(left, right, (((1,), (1,)), ((), ())), preferred_element_type=F32)


def pick_one(mask):
    return jnp.where(mask, jnp.ones(mask.shape, BF16), jnp.zeros(mask.shape, BF16))


def encode(row):
    return jnp.left_shift((row & (LANES - 1)) + LANES, row >> 7).astype(F32)


def column(codes):
    pieces = []
    for start in range(0, codes.shape[1], LANES):
        piece = jnp.broadcast_to(codes[:, start : start + LANES], (LANES, LANES))
        pieces.append(jnp.transpose(piece))
    return pieces[0] if len(pieces) == 1 else jnp.concatenate(pieces, axis=0)


def one_hot_rows(col, width, first=0):
    lane = lax.broadcasted_iota(jnp.int32, (16, LANES), 1)
    blocks = []
    for start in range(first, first + width, LANES):
        pattern = jnp.broadcast_to(encode(lane + start).astype(BF16)[0:1], col.shape)
        blocks.append(pick_one(col == pattern))
    return jnp.concatenate(blocks, axis=1)


def one_hot_columns(codes, height):
    place = lax.broadcasted_iota(jnp.int32, (height, codes.shape[1]), 0)
    pattern = encode(place).astype(BF16)
    return pick_one(jnp.broadcast_to(codes, pattern.shape) == pattern)


def pick_rows(col, table):
    both = matmul(one_hot_rows(jnp.abs(col), table.shape[0]), table).astype(BF16)
    return jnp.where(col < jnp.zeros(col.shape, BF16), both[:, LANES:], both[:, :LANES])


def list_row(lists, first, per_row):
    pieces = [lists[first + n : first + n + 1, :] for n in range(per_row)]
    return pieces[0] if per_row == 1 else jnp.concatenate(pieces, axis=1)


def add_lists(total, lists_ref, blocks):
    slots, cap = lists_ref.shape
    codes = encode(lists_ref[...]).astype(F32)
    per_row = max(1, min(slots, LANES // cap))
    for first in range(0, slots, per_row):
        row = list_row(codes, first, per_row).astype(BF16)
        rows = jnp.concatenate(blocks[first : first + per_row], axis=0)
        total = total + matmul(one_hot_columns(row, total.shape[0]), rows)
    return total


def gather_lists(lists_ref, table):
    slots, cap = lists_ref.shape
    lists = lists_ref[...]
    per_row = max(1, min(slots, LANES // cap))
    parts = []
    for first in range(0, slots, per_row):
        codes = encode(list_row(lists, first, per_row))
        chooser = one_hot_rows(column(codes).astype(BF16), table.shape[0])
        parts.append(matmul(chooser, table))
    return parts[0] if len(parts) == 1 else jnp.concatenate(parts, axis=0)


def head_kernel(features_hbm, halo_hbm, child_map_hbm, out_grad_hbm, down_hbm, *refs):
    sources = (features_hbm, halo_hbm, child_map_hbm, out_grad_hbm, down_hbm)
    buffers, sems = refs[-len(sources) - 1 : -1], refs[-1]
    features_ref, halo_ref, child_map_ref, out_grad_ref, down_ref = buffers
    copies = [
        pltpu.make_async_copy(source, buffer, sems.at[n])
        for n, (source, buffer) in enumerate(zip(sources, buffers))
    ]
    for copy in copies:
        copy.start()
    outs = refs[: -len(sources) - 1]
    sends, back_ref = outs[:-1], outs[-1]
    slots, cap = halo_ref.shape
    voxels = features_ref.shape[0]
    octants = child_map_ref.shape[0]
    cap2 = sends[0].shape[0] - cap
    cap2 //= 1 + octants * out_grad_ref.shape[1] // LANES
    table_rows = voxels + slots * cap2
    copies[0].wait()
    copies[1].wait()
    listed = gather_lists(halo_ref, features_ref[...]).astype(BF16)
    for send, block in zip(sends, to_steps(jnp.split(listed, slots), False)):
        send[0:cap, :] = block
    for copy in copies[2:]:
        copy.wait()
    upstream = out_grad_ref[...]
    codes = encode(child_map_ref[...]).astype(BF16)
    choosers, parts = [], []
    for o in range(octants):
        part = matmul_rt(upstream, down_ref[o])
        high = part.astype(BF16)
        low = (part - high.astype(F32)).astype(BF16)
        choosers.append(one_hot_columns(codes[o : o + 1, :], table_rows))
        parts.append(jnp.concatenate([high, low], axis=1))
    both = matmul(jnp.concatenate(choosers, axis=1), jnp.concatenate(parts, axis=0))
    total = both[:, :LANES] + both[:, LANES:]
    back_ref[...] = total[:voxels]
    for send, block in zip(sends, to_steps(jnp.split(total[voxels:].astype(BF16), slots), True)):
        send[cap : cap + cap2, :] = block
    sums = [matmul(chooser[voxels:], upstream).astype(BF16) for chooser in choosers]
    blocks = []
    for s in range(slots):
        rows = slice(s * cap2, (s + 1) * cap2)
        halves = [
            sums[o][rows, start : start + LANES]
            for o in range(octants)
            for start in range(0, upstream.shape[1], LANES)
        ]
        blocks.append(jnp.concatenate(halves, axis=0))
    for send, block in zip(sends, to_steps(blocks, True)):
        send[cap + cap2 :, :] = block


def half_codes(row, voxels, received):
    half, half_received = voxels // 2, received // 2
    beyond = row - voxels
    outside = beyond >= 0
    near = row - jnp.where(row >= half, half, 0)
    far = half + beyond - jnp.where(beyond >= half_received, half_received, 0)
    code = encode(jnp.where(outside, far, near))
    near_sign = jnp.where(row >= half, -1.0, 1.0)
    far_sign = jnp.where(beyond >= half_received, -1.0, 1.0)
    return code * jnp.where(outside, far_sign, near_sign)


def offset_of(n, middle):
    return n + jnp.where(n >= middle, 1, 0)


def code_column(map_ref, k, voxels, received):
    return column(half_codes(map_ref[pl.ds(k, 1), :], voxels, received).astype(BF16))


def pick_side(col, both):
    return jnp.where(col < jnp.zeros(col.shape, BF16), both[:, LANES:], both[:, :LANES])


def local_kernel(received, features_ref, map_ref, early_ref, table_ref):
    voxels = features_ref.shape[0]
    half = voxels // 2
    table_ref[:, 0:LANES] = features_ref[0:half, :]
    table_ref[:, LANES:] = features_ref[half:, :]
    middle = map_ref.shape[0] // 2
    for n in range(early_ref.shape[1] // LANES):
        col = code_column(map_ref, offset_of(n, middle), voxels, received)
        both = matmul(one_hot_rows(jnp.abs(col), half), table_ref[...]).astype(BF16)
        early_ref[:, n * LANES : (n + 1) * LANES] = pick_side(col, both)


def forward_kernel(slots, cap, *refs):
    received = refs[:slots]
    features_ref, map_ref, weight_ref, child_ref, early_ref = refs[slots : slots + 5]
    hidden_ref, pre_ref, stacked_ref, leaving_ref, halo_ref, kernel_ref = refs[slots + 5 :]
    voxels = features_ref.shape[0]
    gathers = map_ref.shape[0] - 1
    middle = gathers // 2
    half, half_halo = voxels // 2, slots * cap // 2
    features = features_ref[...]
    halo_ref[...] = jnp.zeros(halo_ref.shape, BF16)
    for s, block in enumerate(to_slots([r[0:cap, :] for r in received], False)):
        place = (s % (slots // 2)) * cap
        side = (s // (slots // 2)) * LANES
        for n in range(2):
            row, lane = n * half_halo + place, 2 * n * LANES + side
            halo_ref[row : row + cap, lane : lane + LANES] = block
    kernel_ref[0:middle] = weight_ref[0:middle]
    kernel_ref[middle:gathers] = weight_ref[middle + 1 :]
    kernel_ref[gathers] = weight_ref[middle]

    for j in range(middle):
        numbers = (2 * j, 2 * j + 1)
        cols = [code_column(map_ref, offset_of(n, middle), voxels, slots * cap) for n in numbers]
        choosers = [one_hot_rows(jnp.abs(col), half_halo, half) for col in cols]
        far = matmul(jnp.concatenate(choosers, axis=1), halo_ref[...]).astype(BF16)
        for n in numbers:
            both = far[:, 2 * (n % 2) * LANES : 2 * (n % 2 + 1) * LANES]
            lanes = slice(n * LANES, (n + 1) * LANES)
            stacked_ref[:, lanes] = pick_side(cols[n % 2], both) + early_ref[:, lanes]

    stacked_ref[:, gathers * LANES :] = features
    pre = matmul(stacked_ref[...], kernel_ref[...].reshape(-1, LANES))
    pre_ref[...] = pre
    hidden = (features.astype(F32) + pre * jax.nn.sigmoid(pre)).astype(BF16)
    hidden_ref[...] = hidden
    leaving_ref[...] = gather_lists(child_ref, hidden).astype(BF16)


def gradient_kernel(slots, cap, *refs):
    received = refs[:slots]
    stacked_ref, pre_ref, child_ref, back_ref = refs[slots : slots + 4]
    hidden_ref, leaving_ref, child_map_ref, out_grad_ref = refs[slots + 4 : slots + 8]
    hgrad_ref, pgrad_ref, early_ref, terms_ref, send_ref = refs[slots + 8 :]
    cap2 = child_ref.shape[1]
    kernel_count = stacked_ref.shape[1] // LANES
    middle = kernel_count // 2
    blocks = to_slots([r[cap : cap + cap2, :] for r in received], True)
    hgrad = add_lists(back_ref[...], child_ref, blocks)
    hgrad_ref[...] = hgrad
    pre = pre_ref[...]
    sig = jax.nn.sigmoid(pre)
    pgrad = hgrad * (sig * (1.0 + pre * (1.0 - sig)))
    pgrad_ref[...] = pgrad.astype(BF16)
    terms = matmul(jnp.transpose(pgrad).astype(BF16), stacked_ref[...])
    order = [k for k in range(kernel_count) if k != middle] + [middle]
    for n, k in enumerate(order):
        block = jnp.transpose(terms[:, n * LANES : (n + 1) * LANES])
        terms_ref[k * LANES : (k + 1) * LANES, :] = block.astype(BF16)
    voxels = hidden_ref.shape[0]
    half = voxels // 2
    hidden = hidden_ref[...]
    table = jnp.concatenate([hidden[0:half], hidden[half:]], axis=1)
    octants = child_map_ref.shape[0]
    picked = []
    for o in range(octants):
        col = code_column(child_map_ref, o, voxels, slots * cap2)
        both = matmul(one_hot_rows(jnp.abs(col), half), table).astype(BF16)
        picked.append(pick_side(col, both))
    picked = jnp.concatenate(picked, axis=1)
    early_ref[...] = picked
    upstream_t = jnp.transpose(out_grad_ref[...].astype(F32)).astype(BF16)
    own = matmul(upstream_t, picked)
    blocks = to_slots([r[cap + cap2 :, :] for r in received], True)
    across = upstream_t.shape[0] // LANES
    sums = []
    for n in range(octants * across):
        rows = slice(n * cap2, (n + 1) * cap2)
        sums.append(jnp.concatenate([block[rows, :] for block in blocks], axis=0))
    leaving_t = jnp.transpose(leaving_ref[...].astype(F32)).astype(BF16)
    far = matmul(leaving_t, jnp.concatenate(sums, axis=1))
    row = kernel_count * LANES
    for n in range(octants * across):
        o, side = n // across, n % across
        block = own[side * LANES : (side + 1) * LANES, o * LANES : (o + 1) * LANES]
        value = jnp.transpose(block) + far[:, n * LANES : (n + 1) * LANES]
        terms_ref[row : row + LANES, :] = value.astype(BF16)
        row += LANES
    terms_ref[row:, :] = jnp.zeros((terms_ref.shape[0] - row, LANES), BF16)
    send_ref[...] = terms_ref[pl.ds(my_half(send_ref.shape[0])[1], send_ref.shape[0]), :]


def spread_kernel(
    slots, cap, pgrad_ref, map_ref, weight_ref, leaving_ref, after_ref, back_ref, *sends
):
    acc_ref = sends[-1]
    sends = sends[:-1]
    voxels = pgrad_ref.shape[0]
    kernel_count = map_ref.shape[0]
    middle = kernel_count // 2
    half = voxels // 2
    table_rows = half + slots * cap // 2
    pgrad = pgrad_ref[...]
    own = matmul_rt(pgrad, weight_ref[middle])
    acc_ref[0:half, 0:LANES] = own[0:half]
    acc_ref[0:half, LANES:] = own[half:]
    acc_ref[half:, :] = jnp.zeros((table_rows - half, 2 * LANES), F32)

    def parts(k):
        codes = half_codes(map_ref[pl.ds(k, 1), :], voxels, slots * cap)
        terms = matmul_rt(pgrad, weight_ref[k])
        right = column(codes) < 0.0
        sides = [jnp.where(right, 0.0, terms), jnp.where(right, terms, 0.0)]
        chooser = one_hot_columns(jnp.abs(codes).astype(BF16), table_rows)
        return chooser, jnp.concatenate(sides, axis=1).astype(BF16)

    def step(j, carry):
        near_chooser, near_terms = parts(j)
        far_chooser, far_terms = parts(j + middle + 1)
        acc_ref[...] += matmul(near_chooser, near_terms) + matmul(far_chooser, far_terms)
        return carry

    lax.fori_loop(0, middle, step, 0)
    back_ref[0:half, :] = acc_ref[0:half, 0:LANES]
    back_ref[half:, :] = acc_ref[0:half, LANES:]
    blocks = []
    for s in range(slots):
        first = half + (s % (slots // 2)) * cap
        side = (s // (slots // 2)) * LANES
        blocks.append(acc_ref[first : first + cap, side : side + LANES].astype(BF16))
    for send, block in zip(sends, to_steps(blocks, True)):
        send[0:cap, :] = block
    for send, block in zip(sends, to_steps(jnp.split(leaving_ref[...], slots), False)):
        send[cap:, :] = block


def my_half(rows):
    core = lax.rem(lax.axis_index("shard"), 2)
    return pl.multiple_of(core * rows, 16), pl.multiple_of((1 - core) * rows, 16)


def pair_kernel(terms_ref, other_ref, out_ref):
    rows = other_ref.shape[0]
    mine = terms_ref[pl.ds(my_half(rows)[0], rows), :].astype(F32)
    out_ref[...] = (mine + other_ref[...].astype(F32)).astype(BF16)


def sum_kernel(devices, scale, parts_ref, after_ref, out_ref):
    rows = parts_ref.shape[0] // devices
    for core in range(2):
        mine = range(core, devices, 2)
        total = jnp.zeros((rows, LANES), F32)
        for d in mine:
            total = total + parts_ref[d * rows : (d + 1) * rows, :].astype(F32)
        total = (total * scale).astype(BF16)
        for d in mine:
            out_ref[d * rows : (d + 1) * rows, :] = total


def final_kernel(own, *refs):
    block_ref, conv_hbm, down_hbm = refs[0], *refs[-5:-3]
    conv_ref, down_ref, sems = refs[-3:]
    rows = block_ref.shape[0]
    conv_rows = conv_hbm.shape[0]
    core = lax.rem(lax.axis_index("shard"), 2)
    piece = 4 * LANES
    assert rows <= conv_rows <= 2 * rows and rows % LANES == 0

    def write(half):
        first, last = half * rows, (half + 1) * rows
        copies = []
        for start in range(first, min(last, conv_rows), piece):
            size = min(piece, last - start, conv_rows - start)
            place = pl.ds(start, size)
            value = block_ref[start - first : start - first + size, :]
            conv_ref[place, :] = value.astype(F32)
            sem = sems.at[len(copies)]
            copies.append(pltpu.make_async_copy(conv_ref.at[place], conv_hbm.at[place], sem))
            copies[-1].start()
        across = down_hbm.shape[1] // LANES
        for down in range(0, down_hbm.shape[0], LANES):
            row = conv_rows + down * across
            for side in range(across):
                start = row + side * LANES
                if first <= start < last:
                    value = block_ref[start - first : start - first + LANES, :]
                    lanes = slice(side * LANES, (side + 1) * LANES)
                    down_ref[down : down + LANES, lanes] = value.astype(F32)
            if first <= row < last:
                place = pl.ds(down, LANES)
                sem = sems.at[len(copies)]
                copies.append(pltpu.make_async_copy(down_ref.at[place], down_hbm.at[place], sem))
                copies[-1].start()
        for copy in copies:
            copy.wait()

    for half in range(2):
        pl.when(core == (half if own else 1 - half))(functools.partial(write, half))


def tail_kernel(slots, *refs):
    received = refs[:slots]
    hgrad_ref, back_ref, halo_ref, early_ref, map_ref, down_ref = refs[slots : slots + 6]
    out_ref, coarse_ref = refs[slots + 6 :]
    voxels = hgrad_ref.shape[0]
    cap = halo_ref.shape[1]
    cap2 = received[0].shape[0] - cap
    blocks = to_slots([r[0:cap, :] for r in received], True)
    out_ref[...] = add_lists(hgrad_ref[...] + back_ref[...], halo_ref, blocks)
    halo = jnp.concatenate(to_slots([r[cap:, :] for r in received], False), axis=0)
    octants = map_ref.shape[0]
    rows = map_ref[...]
    codes = encode(jnp.where(rows >= voxels, rows - voxels, slots * cap2))
    picked = []
    for o in range(octants):
        chooser = one_hot_rows(column(codes[o : o + 1, :]).astype(BF16), slots * cap2)
        far = matmul(chooser, halo).astype(BF16)
        picked.append(far + early_ref[:, o * LANES : (o + 1) * LANES])
    kernel = down_ref[...].reshape(octants * LANES, down_ref.shape[2])
    coarse_ref[...] = matmul(jnp.concatenate(picked, axis=1), kernel).astype(BF16)


def call(
    kernel, operands, outs, scratch=(), limit=32, flops=0, in_hbm=(), out_hbm=False, aliases={}
):
    spaces = [pl.ANY if n in in_hbm else pltpu.VMEM for n in range(len(operands))]
    return pl.pallas_call(
        kernel,
        out_shape=[jax.ShapeDtypeStruct(s, d) for s, d in outs],
        in_specs=[pl.BlockSpec(memory_space=space) for space in spaces],
        out_specs=[pl.BlockSpec(memory_space=pl.ANY if out_hbm else pltpu.VMEM) for _ in outs],
        input_output_aliases=aliases,
        scratch_shapes=list(scratch),
        compiler_params=pltpu.CompilerParams(vmem_limit_bytes=limit * 2**20),
        cost_estimate=pl.CostEstimate(flops=flops, bytes_accessed=4 * 2**20, transcendentals=0),
    )(*operands)


def swap_cores(value, devices):
    return lax.ppermute(value, "shard", [(i, i + 1 - 2 * (i % 2)) for i in range(devices)])


def exchange(value):
    return lax.all_to_all(value, "shard", 0, 0, tiled=True)


def local(
    features, conv_weight, down_weight, neighbour_map, halo_rows, child_map, child_rows, out_grad
):
    voxels, channels = features.shape
    parents, coarse_channels = out_grad.shape
    kernel_count = conv_weight.shape[0]
    octants = down_weight.shape[0]
    slots, cap = halo_rows.shape
    cap2 = child_rows.shape[1]
    devices = lax.axis_size("shard")
    scale = 1.0 / math.sqrt(voxels * devices)
    giga = 10**9

    sum_rows = octants * cap2 * coarse_channels // LANES
    conv_rows = kernel_count * channels
    down_rows = octants * channels * coarse_channels // LANES
    grain = 8 * devices
    half_rows = -(-(conv_rows + down_rows) // (2 * grain)) * grain
    first = call(
        head_kernel,
        (features, halo_rows, child_map, out_grad, down_weight),
        [((cap + cap2 + sum_rows, channels), BF16)] * slots + [((voxels, channels), F32)],
        scratch=[
            pltpu.VMEM(value.shape, value.dtype)
            for value in (features, halo_rows, child_map, out_grad, down_weight)
        ]
        + [pltpu.SemaphoreType.DMA((5,))],
        limit=60,
        flops=giga,
        in_hbm=range(5),
    )
    back_h = first[-1]
    received = swaps(first[:-1], (2, 3, 1, 0))
    (early,) = call(
        functools.partial(local_kernel, slots * cap),
        (features, neighbour_map),
        [((voxels, conv_rows - channels), BF16)],
        scratch=[pltpu.VMEM((voxels // 2, 2 * channels), BF16)],
        flops=4 * giga,
    )
    hidden, pre_act, stacked, leaving = call(
        functools.partial(forward_kernel, slots, cap),
        (*received, features, neighbour_map, conv_weight, child_rows, early),
        [
            ((voxels, channels), BF16),
            ((voxels, channels), F32),
            ((voxels, conv_rows), BF16),
            ((slots * cap2, channels), BF16),
        ],
        scratch=[
            pltpu.VMEM((slots * cap, 4 * channels), BF16),
            pltpu.VMEM(conv_weight.shape, BF16),
        ],
        flops=12 * giga,
    )
    hidden_grad, pre_grad, early_h, terms, leaving_terms = call(
        functools.partial(gradient_kernel, slots, cap),
        (
            *received,
            stacked,
            pre_act,
            child_rows,
            back_h,
            hidden,
            leaving,
            child_map,
            out_grad,
        ),
        [
            ((voxels, channels), F32),
            ((voxels, channels), BF16),
            ((parents, octants * channels), BF16),
            ((2 * half_rows, LANES), BF16),
            ((half_rows, LANES), BF16),
        ],
        flops=3 * giga,
    )
    (pair_terms,) = call(
        pair_kernel,
        (terms, swap_cores(leaving_terms, devices)),
        [((half_rows, LANES), BF16)],
        flops=10**6,
    )
    parts = exchange(pair_terms)
    spread = call(
        functools.partial(spread_kernel, slots, cap),
        (pre_grad, neighbour_map, conv_weight, leaving, pair_terms),
        [((voxels, channels), F32)] + [((cap + cap2, channels), BF16)] * slots,
        scratch=[pltpu.VMEM((voxels // 2 + slots * cap // 2, 2 * channels), F32)],
        flops=20 * giga,
        in_hbm=(4,),
    )
    (summed,) = call(
        functools.partial(sum_kernel, devices, scale),
        (parts, spread[1]),
        [((half_rows, LANES), BF16)],
        flops=10**6,
        in_hbm=(1,),
    )
    summed, *returning = lax.optimization_barrier((summed, *spread[1:]))
    returned = swaps(returning, (0, 1, 2, 3))
    input_grad, coarse = call(
        functools.partial(tail_kernel, slots),
        (*returned, hidden_grad, spread[0], halo_rows, early_h, child_map, down_weight),
        [((voxels, channels), F32), ((parents, coarse_channels), BF16)],
        flops=giga,
    )
    mine, input_grad = lax.optimization_barrier((exchange(summed), input_grad))
    other = swap_cores(mine, devices)
    gradients = ()
    for own, block in ((True, mine), (False, other)):
        gradients = call(
            functools.partial(final_kernel, own),
            (block, *gradients),
            [((conv_rows, LANES), F32), ((octants * channels, coarse_channels), F32)],
            scratch=[
                pltpu.VMEM((conv_rows, LANES), F32),
                pltpu.VMEM((octants * channels, coarse_channels), F32),
                pltpu.SemaphoreType.DMA((32,)),
            ],
            flops=10**6,
            in_hbm=(1, 2),
            out_hbm=True,
            aliases={1: 0, 2: 1} if gradients else {},
        )
    conv_grad, down_grad = gradients
    conv_grad = conv_grad.reshape(conv_weight.shape)
    return (coarse, input_grad, conv_grad, down_grad.reshape(down_weight.shape))


def solution(mesh):
    return jax.shard_map(
        local,
        mesh=mesh,
        in_specs=(
            P("shard", None),
            P(),
            P(),
            P(None, "shard"),
            P(None, "shard"),
            P(None, "shard"),
            P(None, "shard"),
            P("shard", None),
        ),
        out_specs=(P("shard", None), P("shard", None), P(), P()),
        check_vma=False,
    )
```

```python
import functools
import math

import jax
import jax.numpy as jnp
from jax import lax
from jax.experimental import pallas as pl
from jax.experimental.pallas import tpu as pltpu
from jax.sharding import PartitionSpec as P

BF16 = jnp.bfloat16
F32 = jnp.float32
LANES = 128


def swaps(by_step, order):
    devices = lax.axis_size("shard")
    moved = {}
    for step in order:
        m, phase = step // 2 + 1, step % 2
        sign = [1 if (i // m) % 2 == phase else -1 for i in range(devices)]
        pairs = [(i, i + m * sign[i]) for i in range(devices) if 0 <= i + m * sign[i] < devices]
        moved[step] = lax.ppermute(by_step[step], "shard", pairs)
    return [moved[step] for step in range(len(by_step))]


def is_even(m):
    return lax.rem(lax.div(lax.axis_index("shard"), m), 2) == 0


def to_steps(slots, back):
    reach = len(slots) // 2
    steps = []
    for m in range(1, reach + 1):
        first, second = slots[reach + m - 1], slots[reach - m]
        if back:
            first, second = second, first
        steps.append(lax.select(is_even(m), first, second))
        steps.append(lax.select(is_even(m), second, first))
    return steps


def to_slots(steps, back):
    reach = len(steps) // 2
    slots = [None] * len(steps)
    for m in range(1, reach + 1):
        first = lax.select(is_even(m), steps[2 * m - 2], steps[2 * m - 1])
        second = lax.select(is_even(m), steps[2 * m - 1], steps[2 * m - 2])
        if back:
            first, second = second, first
        slots[reach - m], slots[reach + m - 1] = first, second
    return slots


def matmul(left, right):
    return jnp.dot(left, right, preferred_element_type=F32)


def matmul_rt(left, right):
    return lax.dot_general(left, right, (((1,), (1,)), ((), ())), preferred_element_type=F32)


def pick_one(mask):
    return jnp.where(mask, jnp.ones(mask.shape, BF16), jnp.zeros(mask.shape, BF16))


def encode(row):
    return jnp.left_shift((row & (LANES - 1)) + LANES, row >> 7).astype(F32)


def column(codes):
    pieces = []
    for start in range(0, codes.shape[1], LANES):
        piece = jnp.broadcast_to(codes[:, start : start + LANES], (LANES, LANES))
        pieces.append(jnp.transpose(piece))
    return pieces[0] if len(pieces) == 1 else jnp.concatenate(pieces, axis=0)


def one_hot_rows(col, width, first=0):
    lane = lax.broadcasted_iota(jnp.int32, (16, LANES), 1)
    blocks = []
    for start in range(first, first + width, LANES):
        pattern = jnp.broadcast_to(encode(lane + start).astype(BF16)[0:1], col.shape)
        blocks.append(pick_one(col == pattern))
    return jnp.concatenate(blocks, axis=1)


def one_hot_columns(codes, height):
    place = lax.broadcasted_iota(jnp.int32, (height, codes.shape[1]), 0)
    pattern = encode(place).astype(BF16)
    return pick_one(jnp.broadcast_to(codes, pattern.shape) == pattern)


def pick_rows(col, table):
    both = matmul(one_hot_rows(jnp.abs(col), table.shape[0]), table).astype(BF16)
    return jnp.where(col < jnp.zeros(col.shape, BF16), both[:, LANES:], both[:, :LANES])


def list_row(lists, first, per_row):
    pieces = [lists[first + n : first + n + 1, :] for n in range(per_row)]
    return pieces[0] if per_row == 1 else jnp.concatenate(pieces, axis=1)


def add_lists(total, lists_ref, blocks):
    slots, cap = lists_ref.shape
    codes = encode(lists_ref[...]).astype(F32)
    per_row = max(1, min(slots, LANES // cap))
    for first in range(0, slots, per_row):
        row = list_row(codes, first, per_row).astype(BF16)
        rows = jnp.concatenate(blocks[first : first + per_row], axis=0)
        total = total + matmul(one_hot_columns(row, total.shape[0]), rows)
    return total


def gather_lists(lists_ref, table):
    slots, cap = lists_ref.shape
    lists = lists_ref[...]
    per_row = max(1, min(slots, LANES // cap))
    parts = []
    for first in range(0, slots, per_row):
        codes = encode(list_row(lists, first, per_row))
        chooser = one_hot_rows(column(codes).astype(BF16), table.shape[0])
        parts.append(matmul(chooser, table))
    return parts[0] if len(parts) == 1 else jnp.concatenate(parts, axis=0)


def head_kernel(features_hbm, halo_hbm, child_map_hbm, out_grad_hbm, down_hbm, *refs):
    sources = (features_hbm, halo_hbm, child_map_hbm, out_grad_hbm, down_hbm)
    buffers, sems = refs[-len(sources) - 1 : -1], refs[-1]
    features_ref, halo_ref, child_map_ref, out_grad_ref, down_ref = buffers
    copies = [
        pltpu.make_async_copy(source, buffer, sems.at[n])
        for n, (source, buffer) in enumerate(zip(sources, buffers))
    ]
    for copy in copies:
        copy.start()
    outs = refs[: -len(sources) - 1]
    sends, back_ref = outs[:-1], outs[-1]
    slots, cap = halo_ref.shape
    voxels = features_ref.shape[0]
    octants = child_map_ref.shape[0]
    cap2 = sends[0].shape[0] - cap
    cap2 //= 1 + octants * out_grad_ref.shape[1] // LANES
    copies[0].wait()
    copies[1].wait()
    listed = gather_lists(halo_ref, features_ref[...]).astype(BF16)
    for send, block in zip(sends, to_steps(jnp.split(listed, slots), False)):
        send[0:cap, :] = block
    for copy in copies[2:]:
        copy.wait()
    upstream = out_grad_ref[...]
    rows = child_map_ref[...]
    codes = half_codes(rows, voxels, slots * cap2)
    half = voxels // 2
    choosers, sides = [], []
    for o in range(octants):
        part = matmul_rt(upstream, down_ref[o]).astype(BF16)
        code = codes[o : o + 1, :].astype(BF16)
        right = column(code) < jnp.zeros(part.shape, BF16)
        none = jnp.zeros(part.shape, BF16)
        pair = [jnp.where(right, none, part), jnp.where(right, part, none)]
        sides.append(jnp.concatenate(pair, axis=1))
        choosers.append(one_hot_columns(jnp.abs(code), half + slots * cap2 // 2))
    both = matmul(jnp.concatenate(choosers, axis=1), jnp.concatenate(sides, axis=0))
    back_ref[0:half, :] = both[0:half, :LANES]
    back_ref[half:, :] = both[0:half, LANES:]
    far = jnp.concatenate([both[half:, :LANES], both[half:, LANES:]], axis=0).astype(BF16)
    for send, block in zip(sends, to_steps(jnp.split(far, slots), True)):
        send[cap : cap + cap2, :] = block
    codes = encode(jnp.where(rows >= voxels, rows - voxels, slots * cap2)).astype(BF16)
    sums = []
    for o in range(octants):
        chooser = one_hot_columns(codes[o : o + 1, :], slots * cap2)
        sums.append(matmul(chooser, upstream).astype(BF16))
    blocks = []
    for s in range(slots):
        rows = slice(s * cap2, (s + 1) * cap2)
        halves = [
            sums[o][rows, start : start + LANES]
            for o in range(octants)
            for start in range(0, upstream.shape[1], LANES)
        ]
        blocks.append(jnp.concatenate(halves, axis=0))
    for send, block in zip(sends, to_steps(blocks, True)):
        send[cap + cap2 :, :] = block


def half_codes(row, voxels, received):
    half, half_received = voxels // 2, received // 2
    beyond = row - voxels
    outside = beyond >= 0
    near = row - jnp.where(row >= half, half, 0)
    far = half + beyond - jnp.where(beyond >= half_received, half_received, 0)
    code = encode(jnp.where(outside, far, near))
    near_sign = jnp.where(row >= half, -1.0, 1.0)
    far_sign = jnp.where(beyond >= half_received, -1.0, 1.0)
    return code * jnp.where(outside, far_sign, near_sign)


def offset_of(n, middle):
    return n + jnp.where(n >= middle, 1, 0)


def code_column(map_ref, k, voxels, received):
    return column(half_codes(map_ref[pl.ds(k, 1), :], voxels, received).astype(BF16))


def pick_side(col, both):
    return jnp.where(col < jnp.zeros(col.shape, BF16), both[:, LANES:], both[:, :LANES])


def local_kernel(received, features_ref, map_ref, early_ref, table_ref):
    voxels = features_ref.shape[0]
    half = voxels // 2
    table_ref[:, 0:LANES] = features_ref[0:half, :]
    table_ref[:, LANES:] = features_ref[half:, :]
    middle = map_ref.shape[0] // 2
    for n in range(early_ref.shape[1] // LANES):
        col = code_column(map_ref, offset_of(n, middle), voxels, received)
        both = matmul(one_hot_rows(jnp.abs(col), half), table_ref[...]).astype(BF16)
        early_ref[:, n * LANES : (n + 1) * LANES] = pick_side(col, both)


def forward_kernel(slots, cap, *refs):
    received = refs[:slots]
    features_ref, map_ref, weight_ref, child_ref, early_ref = refs[slots : slots + 5]
    back_ref, child_map_ref, out_grad_ref = refs[slots + 5 : slots + 8]
    leaving_ref, hgrad_ref, pgrad_ref, early_h_ref, terms_ref, send_ref = refs[slots + 8 : slots + 14]
    stacked_ref, halo_ref, kernel_ref = refs[slots + 14 :]
    cap2 = child_ref.shape[1]
    kernel_count = map_ref.shape[0]
    voxels = features_ref.shape[0]
    gathers = kernel_count - 1
    middle = gathers // 2
    half, half_halo = voxels // 2, slots * cap // 2
    features = features_ref[...]
    halo_ref[...] = jnp.zeros(halo_ref.shape, BF16)
    for s, block in enumerate(to_slots([r[0:cap, :] for r in received], False)):
        place = (s % (slots // 2)) * cap
        side = (s // (slots // 2)) * LANES
        for n in range(2):
            row, lane = n * half_halo + place, 2 * n * LANES + side
            halo_ref[row : row + cap, lane : lane + LANES] = block
    kernel_ref[0:middle] = weight_ref[0:middle]
    kernel_ref[middle:gathers] = weight_ref[middle + 1 :]
    kernel_ref[gathers] = weight_ref[middle]

    for j in range(middle):
        numbers = (2 * j, 2 * j + 1)
        cols = [code_column(map_ref, offset_of(n, middle), voxels, slots * cap) for n in numbers]
        choosers = [one_hot_rows(jnp.abs(col), half_halo, half) for col in cols]
        far = matmul(jnp.concatenate(choosers, axis=1), halo_ref[...]).astype(BF16)
        for n in numbers:
            both = far[:, 2 * (n % 2) * LANES : 2 * (n % 2 + 1) * LANES]
            lanes = slice(n * LANES, (n + 1) * LANES)
            stacked_ref[:, lanes] = pick_side(cols[n % 2], both) + early_ref[:, lanes]

    stacked_ref[:, gathers * LANES :] = features
    pre = matmul(stacked_ref[...], kernel_ref[...].reshape(-1, LANES))
    sig = jax.nn.sigmoid(pre)
    hidden = (features.astype(F32) + pre * sig).astype(BF16)
    leaving = gather_lists(child_ref, hidden).astype(BF16)
    leaving_ref[...] = leaving

    blocks = to_slots([r[cap : cap + cap2, :] for r in received], True)
    hgrad = add_lists(back_ref[...], child_ref, blocks)
    hgrad_ref[...] = hgrad
    pgrad = hgrad * (sig * (1.0 + pre * (1.0 - sig)))
    pgrad_ref[...] = pgrad.astype(BF16)
    terms = matmul(jnp.transpose(pgrad).astype(BF16), stacked_ref[...])
    order = [k for k in range(kernel_count) if k != middle] + [middle]
    for n, k in enumerate(order):
        block = jnp.transpose(terms[:, n * LANES : (n + 1) * LANES])
        terms_ref[k * LANES : (k + 1) * LANES, :] = block.astype(BF16)
    table = jnp.concatenate([hidden[0:half], hidden[half:]], axis=1)
    octants = child_map_ref.shape[0]
    picked = []
    for o in range(octants):
        col = code_column(child_map_ref, o, voxels, slots * cap2)
        both = matmul(one_hot_rows(jnp.abs(col), half), table).astype(BF16)
        picked.append(pick_side(col, both))
    picked = jnp.concatenate(picked, axis=1)
    early_h_ref[...] = picked
    upstream_t = jnp.transpose(out_grad_ref[...].astype(F32)).astype(BF16)
    own = matmul(upstream_t, picked)
    blocks = to_slots([r[cap + cap2 :, :] for r in received], True)
    across = upstream_t.shape[0] // LANES
    sums = []
    for n in range(octants * across):
        rows = slice(n * cap2, (n + 1) * cap2)
        sums.append(jnp.concatenate([block[rows, :] for block in blocks], axis=0))
    leaving_t = jnp.transpose(leaving.astype(F32)).astype(BF16)
    far = matmul(leaving_t, jnp.concatenate(sums, axis=1))
    row = kernel_count * LANES
    for n in range(octants * across):
        o, side = n // across, n % across
        block = own[side * LANES : (side + 1) * LANES, o * LANES : (o + 1) * LANES]
        value = jnp.transpose(block) + far[:, n * LANES : (n + 1) * LANES]
        terms_ref[row : row + LANES, :] = value.astype(BF16)
        row += LANES
    terms_ref[row:, :] = jnp.zeros((terms_ref.shape[0] - row, LANES), BF16)
    send_ref[...] = terms_ref[pl.ds(my_half(send_ref.shape[0])[1], send_ref.shape[0]), :]


def spread_kernel(
    slots, cap, pgrad_ref, map_ref, weight_ref, leaving_ref, after_ref, back_ref, *sends
):
    acc_ref = sends[-1]
    sends = sends[:-1]
    voxels = pgrad_ref.shape[0]
    kernel_count = map_ref.shape[0]
    middle = kernel_count // 2
    half = voxels // 2
    table_rows = half + slots * cap // 2
    pgrad = pgrad_ref[...]
    own = matmul_rt(pgrad, weight_ref[middle])
    acc_ref[0:half, 0:LANES] = own[0:half]
    acc_ref[0:half, LANES:] = own[half:]
    acc_ref[half:, :] = jnp.zeros((table_rows - half, 2 * LANES), F32)

    def parts(k):
        codes = half_codes(map_ref[pl.ds(k, 1), :], voxels, slots * cap)
        terms = matmul_rt(pgrad, weight_ref[k])
        right = column(codes) < 0.0
        sides = [jnp.where(right, 0.0, terms), jnp.where(right, terms, 0.0)]
        chooser = one_hot_columns(jnp.abs(codes).astype(BF16), table_rows)
        return chooser, jnp.concatenate(sides, axis=1).astype(BF16)

    def step(j, carry):
        near_chooser, near_terms = parts(j)
        far_chooser, far_terms = parts(j + middle + 1)
        acc_ref[...] += matmul(near_chooser, near_terms) + matmul(far_chooser, far_terms)
        return carry

    lax.fori_loop(0, middle, step, 0)
    back_ref[0:half, :] = acc_ref[0:half, 0:LANES]
    back_ref[half:, :] = acc_ref[0:half, LANES:]
    blocks = []
    for s in range(slots):
        first = half + (s % (slots // 2)) * cap
        side = (s // (slots // 2)) * LANES
        blocks.append(acc_ref[first : first + cap, side : side + LANES].astype(BF16))
    for send, block in zip(sends, to_steps(blocks, True)):
        send[0:cap, :] = block
    for send, block in zip(sends, to_steps(jnp.split(leaving_ref[...], slots), False)):
        send[cap:, :] = block


def my_half(rows):
    core = lax.rem(lax.axis_index("shard"), 2)
    return pl.multiple_of(core * rows, 16), pl.multiple_of((1 - core) * rows, 16)


def pair_kernel(terms_ref, other_ref, out_ref):
    rows = other_ref.shape[0]
    mine = terms_ref[pl.ds(my_half(rows)[0], rows), :].astype(F32)
    out_ref[...] = (mine + other_ref[...].astype(F32)).astype(BF16)


def sum_kernel(devices, scale, parts_ref, after_ref, out_ref):
    rows = parts_ref.shape[0] // devices
    for core in range(2):
        mine = range(core, devices, 2)
        total = jnp.zeros((rows, LANES), F32)
        for d in mine:
            total = total + parts_ref[d * rows : (d + 1) * rows, :].astype(F32)
        total = (total * scale).astype(BF16)
        for d in mine:
            out_ref[d * rows : (d + 1) * rows, :] = total


def final_kernel(own, *refs):
    block_ref, conv_hbm, down_hbm = refs[0], *refs[-5:-3]
    conv_ref, down_ref, sems = refs[-3:]
    rows = block_ref.shape[0]
    conv_rows = conv_hbm.shape[0]
    core = lax.rem(lax.axis_index("shard"), 2)
    piece = 4 * LANES
    assert rows <= conv_rows <= 2 * rows and rows % LANES == 0

    def write(half):
        first, last = half * rows, (half + 1) * rows
        copies = []
        for start in range(first, min(last, conv_rows), piece):
            size = min(piece, last - start, conv_rows - start)
            place = pl.ds(start, size)
            value = block_ref[start - first : start - first + size, :]
            conv_ref[place, :] = value.astype(F32)
            sem = sems.at[len(copies)]
            copies.append(pltpu.make_async_copy(conv_ref.at[place], conv_hbm.at[place], sem))
            copies[-1].start()
        across = down_hbm.shape[1] // LANES
        for down in range(0, down_hbm.shape[0], LANES):
            row = conv_rows + down * across
            for side in range(across):
                start = row + side * LANES
                if first <= start < last:
                    value = block_ref[start - first : start - first + LANES, :]
                    lanes = slice(side * LANES, (side + 1) * LANES)
                    down_ref[down : down + LANES, lanes] = value.astype(F32)
            if first <= row < last:
                place = pl.ds(down, LANES)
                sem = sems.at[len(copies)]
                copies.append(pltpu.make_async_copy(down_ref.at[place], down_hbm.at[place], sem))
                copies[-1].start()
        for copy in copies:
            copy.wait()

    for half in range(2):
        pl.when(core == (half if own else 1 - half))(functools.partial(write, half))


def tail_kernel(slots, *refs):
    received = refs[:slots]
    hgrad_ref, back_ref, halo_ref, early_ref, map_ref, down_ref = refs[slots : slots + 6]
    out_ref, coarse_ref = refs[slots + 6 :]
    voxels = hgrad_ref.shape[0]
    cap = halo_ref.shape[1]
    cap2 = received[0].shape[0] - cap
    blocks = to_slots([r[0:cap, :] for r in received], True)
    out_ref[...] = add_lists(hgrad_ref[...] + back_ref[...], halo_ref, blocks)
    halo = jnp.concatenate(to_slots([r[cap:, :] for r in received], False), axis=0)
    octants = map_ref.shape[0]
    rows = map_ref[...]
    codes = encode(jnp.where(rows >= voxels, rows - voxels, slots * cap2))
    picked = []
    for o in range(octants):
        chooser = one_hot_rows(column(codes[o : o + 1, :]).astype(BF16), slots * cap2)
        far = matmul(chooser, halo).astype(BF16)
        picked.append(far + early_ref[:, o * LANES : (o + 1) * LANES])
    kernel = down_ref[...].reshape(octants * LANES, down_ref.shape[2])
    coarse_ref[...] = matmul(jnp.concatenate(picked, axis=1), kernel).astype(BF16)


def call(
    kernel, operands, outs, scratch=(), limit=32, flops=0, in_hbm=(), out_hbm=False, aliases={}
):
    spaces = [pl.ANY if n in in_hbm else pltpu.VMEM for n in range(len(operands))]
    return pl.pallas_call(
        kernel,
        out_shape=[jax.ShapeDtypeStruct(s, d) for s, d in outs],
        in_specs=[pl.BlockSpec(memory_space=space) for space in spaces],
        out_specs=[pl.BlockSpec(memory_space=pl.ANY if out_hbm else pltpu.VMEM) for _ in outs],
        input_output_aliases=aliases,
        scratch_shapes=list(scratch),
        compiler_params=pltpu.CompilerParams(vmem_limit_bytes=limit * 2**20),
        cost_estimate=pl.CostEstimate(flops=flops, bytes_accessed=4 * 2**20, transcendentals=0),
    )(*operands)


def swap_cores(value, devices):
    return lax.ppermute(value, "shard", [(i, i + 1 - 2 * (i % 2)) for i in range(devices)])


def exchange(value):
    return lax.all_to_all(value, "shard", 0, 0, tiled=True)


def local(
    features, conv_weight, down_weight, neighbour_map, halo_rows, child_map, child_rows, out_grad
):
    voxels, channels = features.shape
    parents, coarse_channels = out_grad.shape
    kernel_count = conv_weight.shape[0]
    octants = down_weight.shape[0]
    slots, cap = halo_rows.shape
    cap2 = child_rows.shape[1]
    devices = lax.axis_size("shard")
    scale = 1.0 / math.sqrt(voxels * devices)
    giga = 10**9

    sum_rows = octants * cap2 * coarse_channels // LANES
    conv_rows = kernel_count * channels
    down_rows = octants * channels * coarse_channels // LANES
    grain = 8 * devices
    half_rows = -(-(conv_rows + down_rows) // (2 * grain)) * grain
    first = call(
        head_kernel,
        (features, halo_rows, child_map, out_grad, down_weight),
        [((cap + cap2 + sum_rows, channels), BF16)] * slots + [((voxels, channels), F32)],
        scratch=[
            pltpu.VMEM(value.shape, value.dtype)
            for value in (features, halo_rows, child_map, out_grad, down_weight)
        ]
        + [pltpu.SemaphoreType.DMA((5,))],
        limit=60,
        flops=giga,
        in_hbm=range(5),
    )
    back_h = first[-1]
    received = swaps(first[:-1], (2, 3, 1, 0))
    (early,) = call(
        functools.partial(local_kernel, slots * cap),
        (features, neighbour_map),
        [((voxels, conv_rows - channels), BF16)],
        scratch=[pltpu.VMEM((voxels // 2, 2 * channels), BF16)],
        flops=4 * giga,
    )
    leaving, hidden_grad, pre_grad, early_h, terms, leaving_terms = call(
        functools.partial(forward_kernel, slots, cap),
        (
            *received,
            features,
            neighbour_map,
            conv_weight,
            child_rows,
            early,
            back_h,
            child_map,
            out_grad,
        ),
        [
            ((slots * cap2, channels), BF16),
            ((voxels, channels), F32),
            ((voxels, channels), BF16),
            ((parents, octants * channels), BF16),
            ((2 * half_rows, LANES), BF16),
            ((half_rows, LANES), BF16),
        ],
        scratch=[
            pltpu.VMEM((voxels, conv_rows), BF16),
            pltpu.VMEM((slots * cap, 4 * channels), BF16),
            pltpu.VMEM(conv_weight.shape, BF16),
        ],
        flops=15 * giga,
    )
    (pair_terms,) = call(
        pair_kernel,
        (terms, swap_cores(leaving_terms, devices)),
        [((half_rows, LANES), BF16)],
        flops=10**6,
    )
    parts = exchange(pair_terms)
    spread = call(
        functools.partial(spread_kernel, slots, cap),
        (pre_grad, neighbour_map, conv_weight, leaving, pair_terms),
        [((voxels, channels), F32)] + [((cap + cap2, channels), BF16)] * slots,
        scratch=[pltpu.VMEM((voxels // 2 + slots * cap // 2, 2 * channels), F32)],
        flops=20 * giga,
        in_hbm=(4,),
    )
    (summed,) = call(
        functools.partial(sum_kernel, devices, scale),
        (parts, spread[1]),
        [((half_rows, LANES), BF16)],
        flops=10**6,
        in_hbm=(1,),
    )
    summed, *returning = lax.optimization_barrier((summed, *spread[1:]))
    returned = swaps(returning, (0, 1, 2, 3))
    input_grad, coarse = call(
        functools.partial(tail_kernel, slots),
        (*returned, hidden_grad, spread[0], halo_rows, early_h, child_map, down_weight),
        [((voxels, channels), F32), ((parents, coarse_channels), BF16)],
        flops=giga,
    )
    mine, input_grad = lax.optimization_barrier((exchange(summed), input_grad))
    other = swap_cores(mine, devices)
    gradients = ()
    for own, block in ((True, mine), (False, other)):
        gradients = call(
            functools.partial(final_kernel, own),
            (block, *gradients),
            [((conv_rows, LANES), F32), ((octants * channels, coarse_channels), F32)],
            scratch=[
                pltpu.VMEM((conv_rows, LANES), F32),
                pltpu.VMEM((octants * channels, coarse_channels), F32),
                pltpu.SemaphoreType.DMA((32,)),
            ],
            flops=10**6,
            in_hbm=(1, 2),
            out_hbm=True,
            aliases={1: 0, 2: 1} if gradients else {},
        )
    conv_grad, down_grad = gradients
    conv_grad = conv_grad.reshape(conv_weight.shape)
    return (coarse, input_grad, conv_grad, down_grad.reshape(down_weight.shape))


def solution(mesh):
    return jax.shard_map(
        local,
        mesh=mesh,
        in_specs=(
            P("shard", None),
            P(),
            P(),
            P(None, "shard"),
            P(None, "shard"),
            P(None, "shard"),
            P(None, "shard"),
            P("shard", None),
        ),
        out_specs=(P("shard", None), P("shard", None), P(), P()),
        check_vma=False,
    )
```

```python
import functools
import math

import jax
import jax.numpy as jnp
from jax import lax
from jax.experimental import pallas as pl
from jax.experimental.pallas import tpu as pltpu
from jax.sharding import PartitionSpec as P

BF16 = jnp.bfloat16
F32 = jnp.float32
LANES = 128


def swaps(by_step, order):
    devices = lax.axis_size("shard")
    moved = {}
    for step in order:
        m, phase = step // 2 + 1, step % 2
        sign = [1 if (i // m) % 2 == phase else -1 for i in range(devices)]
        pairs = [(i, i + m * sign[i]) for i in range(devices) if 0 <= i + m * sign[i] < devices]
        moved[step] = lax.ppermute(by_step[step], "shard", pairs)
    return [moved[step] for step in range(len(by_step))]


def is_even(m):
    return lax.rem(lax.div(lax.axis_index("shard"), m), 2) == 0


def to_steps(slots, back):
    reach = len(slots) // 2
    steps = []
    for m in range(1, reach + 1):
        first, second = slots[reach + m - 1], slots[reach - m]
        if back:
            first, second = second, first
        steps.append(lax.select(is_even(m), first, second))
        steps.append(lax.select(is_even(m), second, first))
    return steps


def to_slots(steps, back):
    reach = len(steps) // 2
    slots = [None] * len(steps)
    for m in range(1, reach + 1):
        first = lax.select(is_even(m), steps[2 * m - 2], steps[2 * m - 1])
        second = lax.select(is_even(m), steps[2 * m - 1], steps[2 * m - 2])
        if back:
            first, second = second, first
        slots[reach - m], slots[reach + m - 1] = first, second
    return slots


def matmul(left, right):
    return jnp.dot(left, right, preferred_element_type=F32)


def matmul_rt(left, right):
    return lax.dot_general(left, right, (((1,), (1,)), ((), ())), preferred_element_type=F32)


def pick_one(mask):
    return jnp.where(mask, jnp.ones(mask.shape, BF16), jnp.zeros(mask.shape, BF16))


def encode(row):
    return jnp.left_shift((row & (LANES - 1)) + LANES, row >> 7).astype(F32)


def column(codes):
    pieces = []
    for start in range(0, codes.shape[1], LANES):
        piece = jnp.broadcast_to(codes[:, start : start + LANES], (LANES, LANES))
        pieces.append(jnp.transpose(piece))
    return pieces[0] if len(pieces) == 1 else jnp.concatenate(pieces, axis=0)


def one_hot_rows(col, width, first=0):
    lane = lax.broadcasted_iota(jnp.int32, (16, LANES), 1)
    blocks = []
    for start in range(first, first + width, LANES):
        pattern = jnp.broadcast_to(encode(lane + start).astype(BF16)[0:1], col.shape)
        blocks.append(pick_one(col == pattern))
    return jnp.concatenate(blocks, axis=1)


def one_hot_columns(codes, height):
    place = lax.broadcasted_iota(jnp.int32, (height, codes.shape[1]), 0)
    pattern = encode(place).astype(BF16)
    return pick_one(jnp.broadcast_to(codes, pattern.shape) == pattern)


def pick_rows(col, table):
    both = matmul(one_hot_rows(jnp.abs(col), table.shape[0]), table).astype(BF16)
    return jnp.where(col < jnp.zeros(col.shape, BF16), both[:, LANES:], both[:, :LANES])


def list_row(lists, first, per_row):
    pieces = [lists[first + n : first + n + 1, :] for n in range(per_row)]
    return pieces[0] if per_row == 1 else jnp.concatenate(pieces, axis=1)


def add_lists(total, lists_ref, blocks):
    slots, cap = lists_ref.shape
    codes = encode(lists_ref[...]).astype(F32)
    per_row = max(1, min(slots, LANES // cap))
    for first in range(0, slots, per_row):
        row = list_row(codes, first, per_row).astype(BF16)
        rows = jnp.concatenate(blocks[first : first + per_row], axis=0)
        total = total + matmul(one_hot_columns(row, total.shape[0]), rows)
    return total


def gather_lists(lists_ref, table):
    slots, cap = lists_ref.shape
    lists = lists_ref[...]
    per_row = max(1, min(slots, LANES // cap))
    parts = []
    for first in range(0, slots, per_row):
        codes = encode(list_row(lists, first, per_row))
        chooser = one_hot_rows(column(codes).astype(BF16), table.shape[0])
        parts.append(matmul(chooser, table))
    return parts[0] if len(parts) == 1 else jnp.concatenate(parts, axis=0)


def head_kernel(features_hbm, halo_hbm, child_map_hbm, out_grad_hbm, down_hbm, *refs):
    sources = (features_hbm, halo_hbm, child_map_hbm, out_grad_hbm, down_hbm)
    buffers, sems = refs[-len(sources) - 1 : -1], refs[-1]
    features_ref, halo_ref, child_map_ref, out_grad_ref, down_ref = buffers
    copies = [
        pltpu.make_async_copy(source, buffer, sems.at[n])
        for n, (source, buffer) in enumerate(zip(sources, buffers))
    ]
    for copy in copies:
        copy.start()
    outs = refs[: -len(sources) - 1]
    sends, back_ref = outs[:-1], outs[-1]
    slots, cap = halo_ref.shape
    voxels = features_ref.shape[0]
    octants = child_map_ref.shape[0]
    cap2 = sends[0].shape[0] - cap
    cap2 //= 1 + octants * out_grad_ref.shape[1] // LANES
    copies[0].wait()
    copies[1].wait()
    listed = gather_lists(halo_ref, features_ref[...]).astype(BF16)
    for send, block in zip(sends, to_steps(jnp.split(listed, slots), False)):
        send[0:cap, :] = block
    for copy in copies[2:]:
        copy.wait()
    upstream = out_grad_ref[...]
    rows = child_map_ref[...]
    codes = half_codes(rows, voxels, slots * cap2)
    half = voxels // 2
    choosers, sides = [], []
    for o in range(octants):
        part = matmul_rt(upstream, down_ref[o]).astype(BF16)
        code = codes[o : o + 1, :].astype(BF16)
        right = column(code) < jnp.zeros(part.shape, BF16)
        none = jnp.zeros(part.shape, BF16)
        pair = [jnp.where(right, none, part), jnp.where(right, part, none)]
        sides.append(jnp.concatenate(pair, axis=1))
        choosers.append(one_hot_columns(jnp.abs(code), half + slots * cap2 // 2))
    both = matmul(jnp.concatenate(choosers, axis=1), jnp.concatenate(sides, axis=0))
    back_ref[0:half, :] = both[0:half, :LANES]
    back_ref[half:, :] = both[0:half, LANES:]
    far = jnp.concatenate([both[half:, :LANES], both[half:, LANES:]], axis=0).astype(BF16)
    for send, block in zip(sends, to_steps(jnp.split(far, slots), True)):
        send[cap : cap + cap2, :] = block
    codes = encode(jnp.where(rows >= voxels, rows - voxels, slots * cap2)).astype(BF16)
    sums = []
    for o in range(octants):
        chooser = one_hot_columns(codes[o : o + 1, :], slots * cap2)
        sums.append(matmul(chooser, upstream).astype(BF16))
    blocks = []
    for s in range(slots):
        rows = slice(s * cap2, (s + 1) * cap2)
        halves = [
            sums[o][rows, start : start + LANES]
            for o in range(octants)
            for start in range(0, upstream.shape[1], LANES)
        ]
        blocks.append(jnp.concatenate(halves, axis=0))
    for send, block in zip(sends, to_steps(blocks, True)):
        send[cap + cap2 :, :] = block


def half_codes(row, voxels, received):
    half, half_received = voxels // 2, received // 2
    beyond = row - voxels
    outside = beyond >= 0
    near = row - jnp.where(row >= half, half, 0)
    far = half + beyond - jnp.where(beyond >= half_received, half_received, 0)
    code = encode(jnp.where(outside, far, near))
    near_sign = jnp.where(row >= half, -1.0, 1.0)
    far_sign = jnp.where(beyond >= half_received, -1.0, 1.0)
    return code * jnp.where(outside, far_sign, near_sign)


def offset_of(n, middle):
    return n + jnp.where(n >= middle, 1, 0)


def code_column(map_ref, k, voxels, received):
    return column(half_codes(map_ref[pl.ds(k, 1), :], voxels, received).astype(BF16))


def pick_side(col, both):
    return jnp.where(col < jnp.zeros(col.shape, BF16), both[:, LANES:], both[:, :LANES])


def local_kernel(received, features_ref, map_ref, early_ref, table_ref):
    voxels = features_ref.shape[0]
    half = voxels // 2
    table_ref[:, 0:LANES] = features_ref[0:half, :]
    table_ref[:, LANES:] = features_ref[half:, :]
    middle = map_ref.shape[0] // 2
    for n in range(early_ref.shape[1] // LANES):
        col = code_column(map_ref, offset_of(n, middle), voxels, received)
        both = matmul(one_hot_rows(jnp.abs(col), half), table_ref[...]).astype(BF16)
        early_ref[:, n * LANES : (n + 1) * LANES] = pick_side(col, both)


def forward_kernel(slots, cap, *refs):
    received = refs[:slots]
    features_ref, map_ref, weight_ref, child_ref, early_ref = refs[slots : slots + 5]
    hidden_ref, pre_ref, stacked_ref, leaving_ref, halo_ref, kernel_ref = refs[slots + 5 :]
    voxels = features_ref.shape[0]
    gathers = map_ref.shape[0] - 1
    middle = gathers // 2
    half, half_halo = voxels // 2, slots * cap // 2
    features = features_ref[...]
    halo_ref[...] = jnp.zeros(halo_ref.shape, BF16)
    for s, block in enumerate(to_slots([r[0:cap, :] for r in received], False)):
        place = (s % (slots // 2)) * cap
        side = (s // (slots // 2)) * LANES
        for n in range(2):
            row, lane = n * half_halo + place, 2 * n * LANES + side
            halo_ref[row : row + cap, lane : lane + LANES] = block
    kernel_ref[0:middle] = weight_ref[0:middle]
    kernel_ref[middle:gathers] = weight_ref[middle + 1 :]
    kernel_ref[gathers] = weight_ref[middle]

    for j in range(middle):
        numbers = (2 * j, 2 * j + 1)
        cols = [code_column(map_ref, offset_of(n, middle), voxels, slots * cap) for n in numbers]
        choosers = [one_hot_rows(jnp.abs(col), half_halo, half) for col in cols]
        far = matmul(jnp.concatenate(choosers, axis=1), halo_ref[...]).astype(BF16)
        for n in numbers:
            both = far[:, 2 * (n % 2) * LANES : 2 * (n % 2 + 1) * LANES]
            lanes = slice(n * LANES, (n + 1) * LANES)
            stacked_ref[:, lanes] = pick_side(cols[n % 2], both) + early_ref[:, lanes]

    stacked_ref[:, gathers * LANES :] = features
    pre = matmul(stacked_ref[...], kernel_ref[...].reshape(-1, LANES))
    pre_ref[...] = pre
    hidden = (features.astype(F32) + pre * jax.nn.sigmoid(pre)).astype(BF16)
    hidden_ref[...] = hidden
    leaving_ref[...] = gather_lists(child_ref, hidden).astype(BF16)


def gradient_kernel(slots, cap, *refs):
    received = refs[:slots]
    stacked_ref, pre_ref, child_ref, back_ref = refs[slots : slots + 4]
    hidden_ref, leaving_ref, child_map_ref, out_grad_ref = refs[slots + 4 : slots + 8]
    hgrad_ref, pgrad_ref, early_ref, terms_ref, send_ref = refs[slots + 8 :]
    cap2 = child_ref.shape[1]
    kernel_count = stacked_ref.shape[1] // LANES
    middle = kernel_count // 2
    blocks = to_slots([r[cap : cap + cap2, :] for r in received], True)
    hgrad = add_lists(back_ref[...], child_ref, blocks)
    hgrad_ref[...] = hgrad
    pre = pre_ref[...]
    sig = jax.nn.sigmoid(pre)
    pgrad = hgrad * (sig * (1.0 + pre * (1.0 - sig)))
    pgrad_ref[...] = pgrad.astype(BF16)
    terms = matmul(jnp.transpose(pgrad).astype(BF16), stacked_ref[...])
    order = [k for k in range(kernel_count) if k != middle] + [middle]
    for n, k in enumerate(order):
        block = jnp.transpose(terms[:, n * LANES : (n + 1) * LANES])
        terms_ref[k * LANES : (k + 1) * LANES, :] = block.astype(BF16)
    voxels = hidden_ref.shape[0]
    half = voxels // 2
    hidden = hidden_ref[...]
    table = jnp.concatenate([hidden[0:half], hidden[half:]], axis=1)
    octants = child_map_ref.shape[0]
    picked = []
    for o in range(octants):
        col = code_column(child_map_ref, o, voxels, slots * cap2)
        both = matmul(one_hot_rows(jnp.abs(col), half), table).astype(BF16)
        picked.append(pick_side(col, both))
    picked = jnp.concatenate(picked, axis=1)
    early_ref[...] = picked
    upstream_t = jnp.transpose(out_grad_ref[...].astype(F32)).astype(BF16)
    own = matmul(upstream_t, picked)
    blocks = to_slots([r[cap + cap2 :, :] for r in received], True)
    across = upstream_t.shape[0] // LANES
    sums = []
    for n in range(octants * across):
        rows = slice(n * cap2, (n + 1) * cap2)
        sums.append(jnp.concatenate([block[rows, :] for block in blocks], axis=0))
    leaving_t = jnp.transpose(leaving_ref[...].astype(F32)).astype(BF16)
    far = matmul(leaving_t, jnp.concatenate(sums, axis=1))
    row = kernel_count * LANES
    for n in range(octants * across):
        o, side = n // across, n % across
        block = own[side * LANES : (side + 1) * LANES, o * LANES : (o + 1) * LANES]
        value = jnp.transpose(block) + far[:, n * LANES : (n + 1) * LANES]
        terms_ref[row : row + LANES, :] = value.astype(BF16)
        row += LANES
    terms_ref[row:, :] = jnp.zeros((terms_ref.shape[0] - row, LANES), BF16)
    send_ref[...] = terms_ref[pl.ds(my_half(send_ref.shape[0])[1], send_ref.shape[0]), :]


def spread_kernel(
    slots, cap, pgrad_ref, map_ref, weight_ref, leaving_ref, after_ref, back_ref, *sends
):
    acc_ref = sends[-1]
    sends = sends[:-1]
    voxels = pgrad_ref.shape[0]
    kernel_count = map_ref.shape[0]
    middle = kernel_count // 2
    half = voxels // 2
    table_rows = half + slots * cap // 2
    pgrad = pgrad_ref[...]
    own = matmul_rt(pgrad, weight_ref[middle])
    acc_ref[0:half, 0:LANES] = own[0:half]
    acc_ref[0:half, LANES:] = own[half:]
    acc_ref[half:, :] = jnp.zeros((table_rows - half, 2 * LANES), F32)

    def parts(k):
        codes = half_codes(map_ref[pl.ds(k, 1), :], voxels, slots * cap)
        terms = matmul_rt(pgrad, weight_ref[k])
        right = column(codes) < 0.0
        sides = [jnp.where(right, 0.0, terms), jnp.where(right, terms, 0.0)]
        chooser = one_hot_columns(jnp.abs(codes).astype(BF16), table_rows)
        return chooser, jnp.concatenate(sides, axis=1).astype(BF16)

    def step(j, carry):
        near_chooser, near_terms = parts(j)
        far_chooser, far_terms = parts(j + middle + 1)
        acc_ref[...] += matmul(near_chooser, near_terms) + matmul(far_chooser, far_terms)
        return carry

    lax.fori_loop(0, middle, step, 0)
    back_ref[0:half, :] = acc_ref[0:half, 0:LANES]
    back_ref[half:, :] = acc_ref[0:half, LANES:]
    blocks = []
    for s in range(slots):
        first = half + (s % (slots // 2)) * cap
        side = (s // (slots // 2)) * LANES
        blocks.append(acc_ref[first : first + cap, side : side + LANES].astype(BF16))
    for send, block in zip(sends, to_steps(blocks, True)):
        send[0:cap, :] = block
    for send, block in zip(sends, to_steps(jnp.split(leaving_ref[...], slots), False)):
        send[cap:, :] = block


def my_half(rows):
    core = lax.rem(lax.axis_index("shard"), 2)
    return pl.multiple_of(core * rows, 16), pl.multiple_of((1 - core) * rows, 16)


def pair_kernel(terms_ref, other_ref, out_ref):
    rows = other_ref.shape[0]
    mine = terms_ref[pl.ds(my_half(rows)[0], rows), :].astype(F32)
    out_ref[...] = (mine + other_ref[...].astype(F32)).astype(BF16)


def sum_kernel(order, scale, parts_ref, after_ref, out_ref):
    rows = parts_ref.shape[0] // len(order)
    for core in range(2):
        mine = [n for n in range(len(order)) if order[n] % 2 == core]
        total = jnp.zeros((rows, LANES), F32)
        for n in mine:
            total = total + parts_ref[n * rows : (n + 1) * rows, :].astype(F32)
        total = (total * scale).astype(BF16)
        for n in mine:
            out_ref[n * rows : (n + 1) * rows, :] = total


def final_kernel(own, *refs):
    block_ref, conv_hbm, down_hbm = refs[0], *refs[-5:-3]
    conv_ref, down_ref, sems = refs[-3:]
    rows = block_ref.shape[0]
    conv_rows = conv_hbm.shape[0]
    core = lax.rem(lax.axis_index("shard"), 2)
    piece = 4 * LANES
    assert rows <= conv_rows <= 2 * rows and rows % LANES == 0

    def write(half):
        first, last = half * rows, (half + 1) * rows
        copies = []
        for start in range(first, min(last, conv_rows), piece):
            size = min(piece, last - start, conv_rows - start)
            place = pl.ds(start, size)
            value = block_ref[start - first : start - first + size, :]
            conv_ref[place, :] = value.astype(F32)
            sem = sems.at[len(copies)]
            copies.append(pltpu.make_async_copy(conv_ref.at[place], conv_hbm.at[place], sem))
            copies[-1].start()
        across = down_hbm.shape[1] // LANES
        for down in range(0, down_hbm.shape[0], LANES):
            row = conv_rows + down * across
            for side in range(across):
                start = row + side * LANES
                if first <= start < last:
                    value = block_ref[start - first : start - first + LANES, :]
                    lanes = slice(side * LANES, (side + 1) * LANES)
                    down_ref[down : down + LANES, lanes] = value.astype(F32)
            if first <= row < last:
                place = pl.ds(down, LANES)
                sem = sems.at[len(copies)]
                copies.append(pltpu.make_async_copy(down_ref.at[place], down_hbm.at[place], sem))
                copies[-1].start()
        for copy in copies:
            copy.wait()

    for half in range(2):
        pl.when(core == (half if own else 1 - half))(functools.partial(write, half))


def tail_kernel(slots, *refs):
    received = refs[:slots]
    hgrad_ref, back_ref, halo_ref, early_ref, map_ref, down_ref = refs[slots : slots + 6]
    out_ref, coarse_ref = refs[slots + 6 :]
    voxels = hgrad_ref.shape[0]
    cap = halo_ref.shape[1]
    cap2 = received[0].shape[0] - cap
    blocks = to_slots([r[0:cap, :] for r in received], True)
    out_ref[...] = add_lists(hgrad_ref[...] + back_ref[...], halo_ref, blocks)
    halo = jnp.concatenate(to_slots([r[cap:, :] for r in received], False), axis=0)
    octants = map_ref.shape[0]
    rows = map_ref[...]
    codes = encode(jnp.where(rows >= voxels, rows - voxels, slots * cap2))
    picked = []
    for o in range(octants):
        chooser = one_hot_rows(column(codes[o : o + 1, :]).astype(BF16), slots * cap2)
        far = matmul(chooser, halo).astype(BF16)
        picked.append(far + early_ref[:, o * LANES : (o + 1) * LANES])
    kernel = down_ref[...].reshape(octants * LANES, down_ref.shape[2])
    coarse_ref[...] = matmul(jnp.concatenate(picked, axis=1), kernel).astype(BF16)


def call(
    kernel, operands, outs, scratch=(), limit=32, flops=0, in_hbm=(), out_hbm=False, aliases={}
):
    spaces = [pl.ANY if n in in_hbm else pltpu.VMEM for n in range(len(operands))]
    return pl.pallas_call(
        kernel,
        out_shape=[jax.ShapeDtypeStruct(s, d) for s, d in outs],
        in_specs=[pl.BlockSpec(memory_space=space) for space in spaces],
        out_specs=[pl.BlockSpec(memory_space=pl.ANY if out_hbm else pltpu.VMEM) for _ in outs],
        input_output_aliases=aliases,
        scratch_shapes=list(scratch),
        compiler_params=pltpu.CompilerParams(vmem_limit_bytes=limit * 2**20),
        cost_estimate=pl.CostEstimate(flops=flops, bytes_accessed=4 * 2**20, transcendentals=0),
    )(*operands)


def swap_cores(value, devices):
    return lax.ppermute(value, "shard", [(i, i + 1 - 2 * (i % 2)) for i in range(devices)])


def far_order(devices):
    order = [0]
    while len(order) < devices:
        order = [2 * n for n in order] + [2 * n + 1 for n in order]
    return order if len(order) == devices else list(range(devices))


def exchange(value, order):
    return lax.all_to_all(value, "shard", 0, 0, axis_index_groups=[order], tiled=True)


def local(
    features, conv_weight, down_weight, neighbour_map, halo_rows, child_map, child_rows, out_grad
):
    voxels, channels = features.shape
    parents, coarse_channels = out_grad.shape
    kernel_count = conv_weight.shape[0]
    octants = down_weight.shape[0]
    slots, cap = halo_rows.shape
    cap2 = child_rows.shape[1]
    devices = lax.axis_size("shard")
    scale = 1.0 / math.sqrt(voxels * devices)
    giga = 10**9

    sum_rows = octants * cap2 * coarse_channels // LANES
    conv_rows = kernel_count * channels
    down_rows = octants * channels * coarse_channels // LANES
    grain = 8 * devices
    half_rows = -(-(conv_rows + down_rows) // (2 * grain)) * grain
    first = call(
        head_kernel,
        (features, halo_rows, child_map, out_grad, down_weight),
        [((cap + cap2 + sum_rows, channels), BF16)] * slots + [((voxels, channels), F32)],
        scratch=[
            pltpu.VMEM(value.shape, value.dtype)
            for value in (features, halo_rows, child_map, out_grad, down_weight)
        ]
        + [pltpu.SemaphoreType.DMA((5,))],
        limit=60,
        flops=giga,
        in_hbm=range(5),
    )
    back_h = first[-1]
    received = swaps(first[:-1], (2, 3, 1, 0))
    (early,) = call(
        functools.partial(local_kernel, slots * cap),
        (features, neighbour_map),
        [((voxels, conv_rows - channels), BF16)],
        scratch=[pltpu.VMEM((voxels // 2, 2 * channels), BF16)],
        flops=4 * giga,
    )
    hidden, pre_act, stacked, leaving = call(
        functools.partial(forward_kernel, slots, cap),
        (*received, features, neighbour_map, conv_weight, child_rows, early),
        [
            ((voxels, channels), BF16),
            ((voxels, channels), F32),
            ((voxels, conv_rows), BF16),
            ((slots * cap2, channels), BF16),
        ],
        scratch=[
            pltpu.VMEM((slots * cap, 4 * channels), BF16),
            pltpu.VMEM(conv_weight.shape, BF16),
        ],
        flops=12 * giga,
    )
    hidden_grad, pre_grad, early_h, terms, leaving_terms = call(
        functools.partial(gradient_kernel, slots, cap),
        (
            *received,
            stacked,
            pre_act,
            child_rows,
            back_h,
            hidden,
            leaving,
            child_map,
            out_grad,
        ),
        [
            ((voxels, channels), F32),
            ((voxels, channels), BF16),
            ((parents, octants * channels), BF16),
            ((2 * half_rows, LANES), BF16),
            ((half_rows, LANES), BF16),
        ],
        flops=3 * giga,
    )
    (pair_terms,) = call(
        pair_kernel,
        (terms, swap_cores(leaving_terms, devices)),
        [((half_rows, LANES), BF16)],
        flops=10**6,
    )
    order = far_order(devices)
    parts = exchange(pair_terms, order)
    spread = call(
        functools.partial(spread_kernel, slots, cap),
        (pre_grad, neighbour_map, conv_weight, leaving, pair_terms),
        [((voxels, channels), F32)] + [((cap + cap2, channels), BF16)] * slots,
        scratch=[pltpu.VMEM((voxels // 2 + slots * cap // 2, 2 * channels), F32)],
        flops=20 * giga,
        in_hbm=(4,),
    )
    (summed,) = call(
        functools.partial(sum_kernel, order, scale),
        (parts, spread[1]),
        [((half_rows, LANES), BF16)],
        flops=10**6,
        in_hbm=(1,),
    )
    summed, *returning = lax.optimization_barrier((summed, *spread[1:]))
    returned = swaps(returning, (0, 1, 2, 3))
    input_grad, coarse = call(
        functools.partial(tail_kernel, slots),
        (*returned, hidden_grad, spread[0], halo_rows, early_h, child_map, down_weight),
        [((voxels, channels), F32), ((parents, coarse_channels), BF16)],
        flops=giga,
    )
    mine, input_grad = lax.optimization_barrier((exchange(summed, order), input_grad))
    other = swap_cores(mine, devices)
    gradients = ()
    for own, block in ((True, mine), (False, other)):
        gradients = call(
            functools.partial(final_kernel, own),
            (block, *gradients),
            [((conv_rows, LANES), F32), ((octants * channels, coarse_channels), F32)],
            scratch=[
                pltpu.VMEM((conv_rows, LANES), F32),
                pltpu.VMEM((octants * channels, coarse_channels), F32),
                pltpu.SemaphoreType.DMA((32,)),
            ],
            flops=10**6,
            in_hbm=(1, 2),
            out_hbm=True,
            aliases={1: 0, 2: 1} if gradients else {},
        )
    conv_grad, down_grad = gradients
    conv_grad = conv_grad.reshape(conv_weight.shape)
    return (coarse, input_grad, conv_grad, down_grad.reshape(down_weight.shape))


def solution(mesh):
    return jax.shard_map(
        local,
        mesh=mesh,
        in_specs=(
            P("shard", None),
            P(),
            P(),
            P(None, "shard"),
            P(None, "shard"),
            P(None, "shard"),
            P(None, "shard"),
            P("shard", None),
        ),
        out_specs=(P("shard", None), P("shard", None), P(), P()),
        check_vma=False,
    )
```

```python
import functools
import math

import jax
import jax.numpy as jnp
from jax import lax
from jax.experimental import pallas as pl
from jax.experimental.pallas import tpu as pltpu
from jax.sharding import PartitionSpec as P

BF16 = jnp.bfloat16
F32 = jnp.float32
LANES = 128


def swaps(by_step, order):
    devices = lax.axis_size("shard")
    moved = {}
    for step in order:
        m, phase = step // 2 + 1, step % 2
        sign = [1 if (i // m) % 2 == phase else -1 for i in range(devices)]
        pairs = [(i, i + m * sign[i]) for i in range(devices) if 0 <= i + m * sign[i] < devices]
        moved[step] = lax.ppermute(by_step[step], "shard", pairs)
    return [moved[step] for step in range(len(by_step))]


def is_even(m):
    return lax.rem(lax.div(lax.axis_index("shard"), m), 2) == 0


def to_steps(slots, back):
    reach = len(slots) // 2
    steps = []
    for m in range(1, reach + 1):
        first, second = slots[reach + m - 1], slots[reach - m]
        if back:
            first, second = second, first
        steps.append(lax.select(is_even(m), first, second))
        steps.append(lax.select(is_even(m), second, first))
    return steps


def to_slots(steps, back):
    reach = len(steps) // 2
    slots = [None] * len(steps)
    for m in range(1, reach + 1):
        first = lax.select(is_even(m), steps[2 * m - 2], steps[2 * m - 1])
        second = lax.select(is_even(m), steps[2 * m - 1], steps[2 * m - 2])
        if back:
            first, second = second, first
        slots[reach - m], slots[reach + m - 1] = first, second
    return slots


def matmul(left, right):
    return jnp.dot(left, right, preferred_element_type=F32)


def matmul_rt(left, right):
    return lax.dot_general(left, right, (((1,), (1,)), ((), ())), preferred_element_type=F32)


def pick_one(mask):
    return jnp.where(mask, jnp.ones(mask.shape, BF16), jnp.zeros(mask.shape, BF16))


def encode(row):
    return jnp.left_shift((row & (LANES - 1)) + LANES, row >> 7).astype(F32)


def column(codes):
    pieces = []
    for start in range(0, codes.shape[1], LANES):
        piece = jnp.broadcast_to(codes[:, start : start + LANES], (LANES, LANES))
        pieces.append(jnp.transpose(piece))
    return pieces[0] if len(pieces) == 1 else jnp.concatenate(pieces, axis=0)


def one_hot_rows(col, width, first=0):
    lane = lax.broadcasted_iota(jnp.int32, (16, LANES), 1)
    blocks = []
    for start in range(first, first + width, LANES):
        pattern = jnp.broadcast_to(encode(lane + start).astype(BF16)[0:1], col.shape)
        blocks.append(pick_one(col == pattern))
    return jnp.concatenate(blocks, axis=1)


def one_hot_columns(codes, height):
    place = lax.broadcasted_iota(jnp.int32, (height, codes.shape[1]), 0)
    pattern = encode(place).astype(BF16)
    return pick_one(jnp.broadcast_to(codes, pattern.shape) == pattern)


def pick_rows(col, table):
    both = matmul(one_hot_rows(jnp.abs(col), table.shape[0]), table).astype(BF16)
    return jnp.where(col < jnp.zeros(col.shape, BF16), both[:, LANES:], both[:, :LANES])


def list_row(lists, first, per_row):
    pieces = [lists[first + n : first + n + 1, :] for n in range(per_row)]
    return pieces[0] if per_row == 1 else jnp.concatenate(pieces, axis=1)


def add_lists(total, lists_ref, blocks):
    slots, cap = lists_ref.shape
    codes = encode(lists_ref[...]).astype(F32)
    per_row = max(1, min(slots, LANES // cap))
    for first in range(0, slots, per_row):
        row = list_row(codes, first, per_row).astype(BF16)
        rows = jnp.concatenate(blocks[first : first + per_row], axis=0)
        total = total + matmul(one_hot_columns(row, total.shape[0]), rows)
    return total


def gather_lists(lists_ref, table):
    slots, cap = lists_ref.shape
    lists = lists_ref[...]
    per_row = max(1, min(slots, LANES // cap))
    parts = []
    for first in range(0, slots, per_row):
        codes = encode(list_row(lists, first, per_row))
        chooser = one_hot_rows(column(codes).astype(BF16), table.shape[0])
        parts.append(matmul(chooser, table))
    return parts[0] if len(parts) == 1 else jnp.concatenate(parts, axis=0)


def head_kernel(features_hbm, halo_hbm, child_map_hbm, out_grad_hbm, down_hbm, *refs):
    sources = (features_hbm, halo_hbm, child_map_hbm, out_grad_hbm, down_hbm)
    buffers, sems = refs[-len(sources) - 2 : -2], refs[-2]
    back_sems = refs[-1]
    features_ref, halo_ref, child_map_ref, out_grad_ref, down_ref = buffers
    copies = [
        pltpu.make_async_copy(source, buffer, sems.at[n])
        for n, (source, buffer) in enumerate(zip(sources, buffers))
    ]
    for copy in copies:
        copy.start()
    slots, cap = halo_ref.shape
    send_hbms, back_hbm = refs[:slots], refs[slots]
    sends, back_ref = refs[slots + 1 : 2 * slots + 1], refs[2 * slots + 1]
    voxels = features_ref.shape[0]
    octants = child_map_ref.shape[0]
    cap2 = sends[0].shape[0] - cap
    cap2 //= 1 + octants * out_grad_ref.shape[1] // LANES
    written = []

    def write(first, last):
        for send, send_hbm in zip(sends, send_hbms):
            place = pl.ds(first, last - first)
            sem = sems.at[len(copies) + len(written)]
            written.append(pltpu.make_async_copy(send.at[place], send_hbm.at[place], sem))
            written[-1].start()

    copies[0].wait()
    copies[1].wait()
    listed = gather_lists(halo_ref, features_ref[...]).astype(BF16)
    for send, block in zip(sends, to_steps(jnp.split(listed, slots), False)):
        send[0:cap, :] = block
    for copy in copies[2:]:
        copy.wait()
    upstream = out_grad_ref[...]
    rows = child_map_ref[...]
    codes = encode(jnp.where(rows >= voxels, rows - voxels, slots * cap2)).astype(BF16)
    sums = []
    for o in range(octants):
        chooser = one_hot_columns(codes[o : o + 1, :], slots * cap2)
        sums.append(matmul(chooser, upstream).astype(BF16))
    blocks = []
    for s in range(slots):
        listed_rows = slice(s * cap2, (s + 1) * cap2)
        halves = [
            sums[o][listed_rows, start : start + LANES]
            for o in range(octants)
            for start in range(0, upstream.shape[1], LANES)
        ]
        blocks.append(jnp.concatenate(halves, axis=0))
    for send, block in zip(sends, to_steps(blocks, True)):
        send[cap + cap2 :, :] = block
    write(cap + cap2, sends[0].shape[0])
    codes = half_codes(rows, voxels, slots * cap2)
    half = voxels // 2
    choosers, sides = [], []
    for o in range(octants):
        part = matmul_rt(upstream, down_ref[o]).astype(BF16)
        code = codes[o : o + 1, :].astype(BF16)
        right = column(code) < jnp.zeros(part.shape, BF16)
        none = jnp.zeros(part.shape, BF16)
        pair = [jnp.where(right, none, part), jnp.where(right, part, none)]
        sides.append(jnp.concatenate(pair, axis=1))
        choosers.append(one_hot_columns(jnp.abs(code), half + slots * cap2 // 2))
    both = matmul(jnp.concatenate(choosers, axis=1), jnp.concatenate(sides, axis=0))
    back_ref[0:half, :] = both[0:half, :LANES]
    back_ref[half:, :] = both[0:half, LANES:]
    far = jnp.concatenate([both[half:, :LANES], both[half:, LANES:]], axis=0).astype(BF16)
    for send, block in zip(sends, to_steps(jnp.split(far, slots), True)):
        send[cap : cap + cap2, :] = block
    write(0, cap + cap2)
    written += write_pieces(back_ref, back_hbm, back_sems)
    for copy in written:
        copy.wait()


def half_codes(row, voxels, received):
    half, half_received = voxels // 2, received // 2
    beyond = row - voxels
    outside = beyond >= 0
    near = row - jnp.where(row >= half, half, 0)
    far = half + beyond - jnp.where(beyond >= half_received, half_received, 0)
    code = encode(jnp.where(outside, far, near))
    near_sign = jnp.where(row >= half, -1.0, 1.0)
    far_sign = jnp.where(beyond >= half_received, -1.0, 1.0)
    return code * jnp.where(outside, far_sign, near_sign)


def offset_of(n, middle):
    return n + jnp.where(n >= middle, 1, 0)


def code_column(map_ref, k, voxels, received):
    return column(half_codes(map_ref[pl.ds(k, 1), :], voxels, received).astype(BF16))


def pick_side(col, both):
    return jnp.where(col < jnp.zeros(col.shape, BF16), both[:, LANES:], both[:, :LANES])


def local_kernel(received, features_ref, map_ref, early_ref, table_ref):
    voxels = features_ref.shape[0]
    half = voxels // 2
    table_ref[:, 0:LANES] = features_ref[0:half, :]
    table_ref[:, LANES:] = features_ref[half:, :]
    middle = map_ref.shape[0] // 2
    for n in range(early_ref.shape[1] // LANES):
        col = code_column(map_ref, offset_of(n, middle), voxels, received)
        both = matmul(one_hot_rows(jnp.abs(col), half), table_ref[...]).astype(BF16)
        early_ref[:, n * LANES : (n + 1) * LANES] = pick_side(col, both)


def forward_kernel(slots, cap, *refs):
    received = refs[:slots]
    features_ref, map_ref, weight_ref, child_ref, early_ref = refs[slots : slots + 5]
    hidden_ref, pre_ref, stacked_ref, leaving_ref, halo_ref, kernel_ref = refs[slots + 5 :]
    voxels = features_ref.shape[0]
    gathers = map_ref.shape[0] - 1
    middle = gathers // 2
    half, half_halo = voxels // 2, slots * cap // 2
    features = features_ref[...]
    halo_ref[...] = jnp.zeros(halo_ref.shape, BF16)
    for s, block in enumerate(to_slots([r[0:cap, :] for r in received], False)):
        place = (s % (slots // 2)) * cap
        side = (s // (slots // 2)) * LANES
        for n in range(2):
            row, lane = n * half_halo + place, 2 * n * LANES + side
            halo_ref[row : row + cap, lane : lane + LANES] = block
    kernel_ref[0:middle] = weight_ref[0:middle]
    kernel_ref[middle:gathers] = weight_ref[middle + 1 :]
    kernel_ref[gathers] = weight_ref[middle]

    for j in range(middle):
        numbers = (2 * j, 2 * j + 1)
        cols = [code_column(map_ref, offset_of(n, middle), voxels, slots * cap) for n in numbers]
        choosers = [one_hot_rows(jnp.abs(col), half_halo, half) for col in cols]
        far = matmul(jnp.concatenate(choosers, axis=1), halo_ref[...]).astype(BF16)
        for n in numbers:
            both = far[:, 2 * (n % 2) * LANES : 2 * (n % 2 + 1) * LANES]
            lanes = slice(n * LANES, (n + 1) * LANES)
            stacked_ref[:, lanes] = pick_side(cols[n % 2], both) + early_ref[:, lanes]

    stacked_ref[:, gathers * LANES :] = features
    pre = matmul(stacked_ref[...], kernel_ref[...].reshape(-1, LANES))
    pre_ref[...] = pre
    hidden = (features.astype(F32) + pre * jax.nn.sigmoid(pre)).astype(BF16)
    hidden_ref[...] = hidden
    leaving_ref[...] = gather_lists(child_ref, hidden).astype(BF16)


def gradient_kernel(slots, cap, *refs):
    received = refs[:slots]
    stacked_ref, pre_ref, child_ref, back_ref = refs[slots : slots + 4]
    hidden_ref, leaving_ref, child_map_ref, out_grad_ref = refs[slots + 4 : slots + 8]
    hgrad_ref, pgrad_ref, early_ref, terms_ref, send_ref = refs[slots + 8 :]
    cap2 = child_ref.shape[1]
    kernel_count = stacked_ref.shape[1] // LANES
    middle = kernel_count // 2
    blocks = to_slots([r[cap : cap + cap2, :] for r in received], True)
    hgrad = add_lists(back_ref[...], child_ref, blocks)
    hgrad_ref[...] = hgrad
    pre = pre_ref[...]
    sig = jax.nn.sigmoid(pre)
    pgrad = hgrad * (sig * (1.0 + pre * (1.0 - sig)))
    pgrad_ref[...] = pgrad.astype(BF16)
    terms = matmul(jnp.transpose(pgrad).astype(BF16), stacked_ref[...])
    order = [k for k in range(kernel_count) if k != middle] + [middle]
    for n, k in enumerate(order):
        block = jnp.transpose(terms[:, n * LANES : (n + 1) * LANES])
        terms_ref[k * LANES : (k + 1) * LANES, :] = block.astype(BF16)
    voxels = hidden_ref.shape[0]
    half = voxels // 2
    hidden = hidden_ref[...]
    table = jnp.concatenate([hidden[0:half], hidden[half:]], axis=1)
    octants = child_map_ref.shape[0]
    picked = []
    for o in range(octants):
        col = code_column(child_map_ref, o, voxels, slots * cap2)
        both = matmul(one_hot_rows(jnp.abs(col), half), table).astype(BF16)
        picked.append(pick_side(col, both))
    picked = jnp.concatenate(picked, axis=1)
    early_ref[...] = picked
    upstream_t = jnp.transpose(out_grad_ref[...].astype(F32)).astype(BF16)
    own = matmul(upstream_t, picked)
    blocks = to_slots([r[cap + cap2 :, :] for r in received], True)
    across = upstream_t.shape[0] // LANES
    sums = []
    for n in range(octants * across):
        rows = slice(n * cap2, (n + 1) * cap2)
        sums.append(jnp.concatenate([block[rows, :] for block in blocks], axis=0))
    leaving_t = jnp.transpose(leaving_ref[...].astype(F32)).astype(BF16)
    far = matmul(leaving_t, jnp.concatenate(sums, axis=1))
    row = kernel_count * LANES
    for n in range(octants * across):
        o, side = n // across, n % across
        block = own[side * LANES : (side + 1) * LANES, o * LANES : (o + 1) * LANES]
        value = jnp.transpose(block) + far[:, n * LANES : (n + 1) * LANES]
        terms_ref[row : row + LANES, :] = value.astype(BF16)
        row += LANES
    terms_ref[row:, :] = jnp.zeros((terms_ref.shape[0] - row, LANES), BF16)
    send_ref[...] = terms_ref[pl.ds(my_half(send_ref.shape[0])[1], send_ref.shape[0]), :]


def spread_kernel(
    slots, cap, pgrad_ref, map_ref, weight_ref, leaving_ref, after_ref, back_ref, *sends
):
    acc_ref = sends[-1]
    sends = sends[:-1]
    voxels = pgrad_ref.shape[0]
    kernel_count = map_ref.shape[0]
    middle = kernel_count // 2
    half = voxels // 2
    table_rows = half + slots * cap // 2
    pgrad = pgrad_ref[...]
    own = matmul_rt(pgrad, weight_ref[middle])
    acc_ref[0:half, 0:LANES] = own[0:half]
    acc_ref[0:half, LANES:] = own[half:]
    acc_ref[half:, :] = jnp.zeros((table_rows - half, 2 * LANES), F32)

    def parts(k):
        codes = half_codes(map_ref[pl.ds(k, 1), :], voxels, slots * cap)
        terms = matmul_rt(pgrad, weight_ref[k])
        right = column(codes) < 0.0
        sides = [jnp.where(right, 0.0, terms), jnp.where(right, terms, 0.0)]
        chooser = one_hot_columns(jnp.abs(codes).astype(BF16), table_rows)
        return chooser, jnp.concatenate(sides, axis=1).astype(BF16)

    def step(j, carry):
        near_chooser, near_terms = parts(j)
        far_chooser, far_terms = parts(j + middle + 1)
        acc_ref[...] += matmul(near_chooser, near_terms) + matmul(far_chooser, far_terms)
        return carry

    lax.fori_loop(0, middle, step, 0)
    back_ref[0:half, :] = acc_ref[0:half, 0:LANES]
    back_ref[half:, :] = acc_ref[0:half, LANES:]
    blocks = []
    for s in range(slots):
        first = half + (s % (slots // 2)) * cap
        side = (s // (slots // 2)) * LANES
        blocks.append(acc_ref[first : first + cap, side : side + LANES].astype(BF16))
    for send, block in zip(sends, to_steps(blocks, True)):
        send[0:cap, :] = block
    for send, block in zip(sends, to_steps(jnp.split(leaving_ref[...], slots), False)):
        send[cap:, :] = block


def my_half(rows):
    core = lax.rem(lax.axis_index("shard"), 2)
    return pl.multiple_of(core * rows, 16), pl.multiple_of((1 - core) * rows, 16)


def write_pieces(stage_ref, out_hbm, sems, first=0, last=None):
    pieces = sems.shape[0]
    rows = stage_ref.shape[0] // pieces
    copies = []
    for n in range(first, pieces if last is None else last):
        place = pl.ds(n * rows, rows)
        copies.append(pltpu.make_async_copy(stage_ref.at[place], out_hbm.at[place], sems.at[n]))
        copies[-1].start()
    return copies


def pair_kernel(terms_ref, other_ref, out_hbm, stage_ref, sems):
    pieces = sems.shape[0]
    rows = stage_ref.shape[0] // pieces
    first = my_half(stage_ref.shape[0])[0]
    copies = []
    for n in range(pieces):
        place = pl.ds(pl.multiple_of(first + n * rows, 16), rows)
        other = other_ref[n * rows : (n + 1) * rows, :].astype(F32)
        value = terms_ref[place, :].astype(F32) + other
        stage_ref[n * rows : (n + 1) * rows, :] = value.astype(BF16)
        copies += write_pieces(stage_ref, out_hbm, sems, n, n + 1)
    for copy in copies:
        copy.wait()


def sum_kernel(devices, scale, parts_ref, after_ref, out_hbm, stage_ref, sems):
    rows = parts_ref.shape[0] // devices
    sums = []
    for core in range(2):
        total = jnp.zeros((rows, LANES), F32)
        for d in range(core, devices, 2):
            total = total + parts_ref[d * rows : (d + 1) * rows, :].astype(F32)
        sums.append((total * scale).astype(BF16))
    pieces = sems.shape[0]
    copies = []
    for d in range(devices):
        stage_ref[d * rows : (d + 1) * rows, :] = sums[d % 2]
        if (d + 1) % (devices // pieces) == 0:
            piece = d // (devices // pieces)
            copies += write_pieces(stage_ref, out_hbm, sems, piece, piece + 1)
    for copy in copies:
        copy.wait()


def final_kernel(own, *refs):
    block_ref, conv_hbm, down_hbm = refs[0], *refs[-5:-3]
    conv_ref, down_ref, sems = refs[-3:]
    rows = block_ref.shape[0]
    conv_rows = conv_hbm.shape[0]
    core = lax.rem(lax.axis_index("shard"), 2)
    piece = 4 * LANES
    assert rows <= conv_rows <= 2 * rows and rows % LANES == 0

    def write(half):
        first, last = half * rows, (half + 1) * rows
        copies = []
        for start in range(first, min(last, conv_rows), piece):
            size = min(piece, last - start, conv_rows - start)
            place = pl.ds(start, size)
            value = block_ref[start - first : start - first + size, :]
            conv_ref[place, :] = value.astype(F32)
            sem = sems.at[len(copies)]
            copies.append(pltpu.make_async_copy(conv_ref.at[place], conv_hbm.at[place], sem))
            copies[-1].start()
        across = down_hbm.shape[1] // LANES
        for down in range(0, down_hbm.shape[0], LANES):
            row = conv_rows + down * across
            for side in range(across):
                start = row + side * LANES
                if first <= start < last:
                    value = block_ref[start - first : start - first + LANES, :]
                    lanes = slice(side * LANES, (side + 1) * LANES)
                    down_ref[down : down + LANES, lanes] = value.astype(F32)
            if first <= row < last:
                place = pl.ds(down, LANES)
                sem = sems.at[len(copies)]
                copies.append(pltpu.make_async_copy(down_ref.at[place], down_hbm.at[place], sem))
                copies[-1].start()
        for copy in copies:
            copy.wait()

    for half in range(2):
        pl.when(core == (half if own else 1 - half))(functools.partial(write, half))


def tail_kernel(slots, *refs):
    received = refs[:slots]
    hgrad_ref, back_ref, halo_ref, early_ref, map_ref, down_ref = refs[slots : slots + 6]
    out_ref, coarse_ref = refs[slots + 6 :]
    voxels = hgrad_ref.shape[0]
    cap = halo_ref.shape[1]
    cap2 = received[0].shape[0] - cap
    blocks = to_slots([r[0:cap, :] for r in received], True)
    out_ref[...] = add_lists(hgrad_ref[...] + back_ref[...], halo_ref, blocks)
    halo = jnp.concatenate(to_slots([r[cap:, :] for r in received], False), axis=0)
    octants = map_ref.shape[0]
    rows = map_ref[...]
    codes = encode(jnp.where(rows >= voxels, rows - voxels, slots * cap2))
    picked = []
    for o in range(octants):
        chooser = one_hot_rows(column(codes[o : o + 1, :]).astype(BF16), slots * cap2)
        far = matmul(chooser, halo).astype(BF16)
        picked.append(far + early_ref[:, o * LANES : (o + 1) * LANES])
    kernel = down_ref[...].reshape(octants * LANES, down_ref.shape[2])
    coarse_ref[...] = matmul(jnp.concatenate(picked, axis=1), kernel).astype(BF16)


def call(
    kernel, operands, outs, scratch=(), limit=32, flops=0, in_hbm=(), out_hbm=False, aliases={}
):
    spaces = [pl.ANY if n in in_hbm else pltpu.VMEM for n in range(len(operands))]
    return pl.pallas_call(
        kernel,
        out_shape=[jax.ShapeDtypeStruct(s, d) for s, d in outs],
        in_specs=[pl.BlockSpec(memory_space=space) for space in spaces],
        out_specs=[pl.BlockSpec(memory_space=pl.ANY if out_hbm else pltpu.VMEM) for _ in outs],
        input_output_aliases=aliases,
        scratch_shapes=list(scratch),
        compiler_params=pltpu.CompilerParams(vmem_limit_bytes=limit * 2**20),
        cost_estimate=pl.CostEstimate(flops=flops, bytes_accessed=4 * 2**20, transcendentals=0),
    )(*operands)


def swap_cores(value, devices):
    return lax.ppermute(value, "shard", [(i, i + 1 - 2 * (i % 2)) for i in range(devices)])


def exchange(value):
    return lax.all_to_all(value, "shard", 0, 0, tiled=True)


def local(
    features, conv_weight, down_weight, neighbour_map, halo_rows, child_map, child_rows, out_grad
):
    voxels, channels = features.shape
    parents, coarse_channels = out_grad.shape
    kernel_count = conv_weight.shape[0]
    octants = down_weight.shape[0]
    slots, cap = halo_rows.shape
    cap2 = child_rows.shape[1]
    devices = lax.axis_size("shard")
    scale = 1.0 / math.sqrt(voxels * devices)
    giga = 10**9

    sum_rows = octants * cap2 * coarse_channels // LANES
    conv_rows = kernel_count * channels
    down_rows = octants * channels * coarse_channels // LANES
    grain = 8 * devices
    half_rows = -(-(conv_rows + down_rows) // (2 * grain)) * grain
    first = call(
        head_kernel,
        (features, halo_rows, child_map, out_grad, down_weight),
        [((cap + cap2 + sum_rows, channels), BF16)] * slots + [((voxels, channels), F32)],
        scratch=[pltpu.VMEM((cap + cap2 + sum_rows, channels), BF16)] * slots
        + [pltpu.VMEM((voxels, channels), F32)]
        + [
            pltpu.VMEM(value.shape, value.dtype)
            for value in (features, halo_rows, child_map, out_grad, down_weight)
        ]
        + [pltpu.SemaphoreType.DMA((5 + 2 * slots,)), pltpu.SemaphoreType.DMA((4,))],
        limit=60,
        flops=giga,
        in_hbm=range(5),
        out_hbm=True,
    )
    back_h = first[-1]
    received = swaps(first[:-1], (2, 3, 1, 0))
    (early,) = call(
        functools.partial(local_kernel, slots * cap),
        (features, neighbour_map),
        [((voxels, conv_rows - channels), BF16)],
        scratch=[pltpu.VMEM((voxels // 2, 2 * channels), BF16)],
        flops=4 * giga,
    )
    hidden, pre_act, stacked, leaving = call(
        functools.partial(forward_kernel, slots, cap),
        (*received, features, neighbour_map, conv_weight, child_rows, early),
        [
            ((voxels, channels), BF16),
            ((voxels, channels), F32),
            ((voxels, conv_rows), BF16),
            ((slots * cap2, channels), BF16),
        ],
        scratch=[
            pltpu.VMEM((slots * cap, 4 * channels), BF16),
            pltpu.VMEM(conv_weight.shape, BF16),
        ],
        flops=12 * giga,
    )
    hidden_grad, pre_grad, early_h, terms, leaving_terms = call(
        functools.partial(gradient_kernel, slots, cap),
        (
            *received,
            stacked,
            pre_act,
            child_rows,
            back_h,
            hidden,
            leaving,
            child_map,
            out_grad,
        ),
        [
            ((voxels, channels), F32),
            ((voxels, channels), BF16),
            ((parents, octants * channels), BF16),
            ((2 * half_rows, LANES), BF16),
            ((half_rows, LANES), BF16),
        ],
        flops=3 * giga,
    )
    (pair_terms,) = call(
        pair_kernel,
        (terms, swap_cores(leaving_terms, devices)),
        [((half_rows, LANES), BF16)],
        scratch=[pltpu.VMEM((half_rows, LANES), BF16), pltpu.SemaphoreType.DMA((8,))],
        flops=10**6,
        out_hbm=True,
    )
    parts = exchange(pair_terms)
    spread = call(
        functools.partial(spread_kernel, slots, cap),
        (pre_grad, neighbour_map, conv_weight, leaving, pair_terms),
        [((voxels, channels), F32)] + [((cap + cap2, channels), BF16)] * slots,
        scratch=[pltpu.VMEM((voxels // 2 + slots * cap // 2, 2 * channels), F32)],
        flops=20 * giga,
        in_hbm=(4,),
    )
    (summed,) = call(
        functools.partial(sum_kernel, devices, scale),
        (parts, spread[1]),
        [((half_rows, LANES), BF16)],
        scratch=[pltpu.VMEM((half_rows, LANES), BF16), pltpu.SemaphoreType.DMA((8,))],
        flops=10**6,
        in_hbm=(1,),
        out_hbm=True,
    )
    summed, *returning = lax.optimization_barrier((summed, *spread[1:]))
    returned = swaps(returning, (0, 1, 2, 3))
    input_grad, coarse = call(
        functools.partial(tail_kernel, slots),
        (*returned, hidden_grad, spread[0], halo_rows, early_h, child_map, down_weight),
        [((voxels, channels), F32), ((parents, coarse_channels), BF16)],
        flops=giga,
    )
    mine, input_grad = lax.optimization_barrier((exchange(summed), input_grad))
    other = swap_cores(mine, devices)
    gradients = ()
    for own, block in ((True, mine), (False, other)):
        gradients = call(
            functools.partial(final_kernel, own),
            (block, *gradients),
            [((conv_rows, LANES), F32), ((octants * channels, coarse_channels), F32)],
            scratch=[
                pltpu.VMEM((conv_rows, LANES), F32),
                pltpu.VMEM((octants * channels, coarse_channels), F32),
                pltpu.SemaphoreType.DMA((32,)),
            ],
            flops=10**6,
            in_hbm=(1, 2),
            out_hbm=True,
            aliases={1: 0, 2: 1} if gradients else {},
        )
    conv_grad, down_grad = gradients
    conv_grad = conv_grad.reshape(conv_weight.shape)
    return (coarse, input_grad, conv_grad, down_grad.reshape(down_weight.shape))


def solution(mesh):
    return jax.shard_map(
        local,
        mesh=mesh,
        in_specs=(
            P("shard", None),
            P(),
            P(),
            P(None, "shard"),
            P(None, "shard"),
            P(None, "shard"),
            P(None, "shard"),
            P("shard", None),
        ),
        out_specs=(P("shard", None), P("shard", None), P(), P()),
        check_vma=False,
    )
```

```python
import functools
import math

import jax
import jax.numpy as jnp
from jax import lax
from jax.experimental import pallas as pl
from jax.experimental.pallas import tpu as pltpu
from jax.sharding import PartitionSpec as P

BF16 = jnp.bfloat16
F32 = jnp.float32
LANES = 128


def swaps(by_step, order):
    devices = lax.axis_size("shard")
    moved = {}
    for step in order:
        m, phase = step // 2 + 1, step % 2
        sign = [1 if (i // m) % 2 == phase else -1 for i in range(devices)]
        pairs = [(i, i + m * sign[i]) for i in range(devices) if 0 <= i + m * sign[i] < devices]
        moved[step] = lax.ppermute(by_step[step], "shard", pairs)
    return [moved[step] for step in range(len(by_step))]


def is_even(m):
    return lax.rem(lax.div(lax.axis_index("shard"), m), 2) == 0


def to_steps(slots, back):
    reach = len(slots) // 2
    steps = []
    for m in range(1, reach + 1):
        first, second = slots[reach + m - 1], slots[reach - m]
        if back:
            first, second = second, first
        steps.append(lax.select(is_even(m), first, second))
        steps.append(lax.select(is_even(m), second, first))
    return steps


def to_slots(steps, back):
    reach = len(steps) // 2
    slots = [None] * len(steps)
    for m in range(1, reach + 1):
        first = lax.select(is_even(m), steps[2 * m - 2], steps[2 * m - 1])
        second = lax.select(is_even(m), steps[2 * m - 1], steps[2 * m - 2])
        if back:
            first, second = second, first
        slots[reach - m], slots[reach + m - 1] = first, second
    return slots


def matmul(left, right):
    return jnp.dot(left, right, preferred_element_type=F32)


def matmul_rt(left, right):
    return lax.dot_general(left, right, (((1,), (1,)), ((), ())), preferred_element_type=F32)


def pick_one(mask):
    return jnp.where(mask, jnp.ones(mask.shape, BF16), jnp.zeros(mask.shape, BF16))


def encode(row):
    return jnp.left_shift((row & (LANES - 1)) + LANES, row >> 7).astype(F32)


def column(codes):
    pieces = []
    for start in range(0, codes.shape[1], LANES):
        piece = jnp.broadcast_to(codes[:, start : start + LANES], (LANES, LANES))
        pieces.append(jnp.transpose(piece))
    return pieces[0] if len(pieces) == 1 else jnp.concatenate(pieces, axis=0)


def one_hot_rows(col, width, first=0):
    lane = lax.broadcasted_iota(jnp.int32, (16, LANES), 1)
    blocks = []
    for start in range(first, first + width, LANES):
        pattern = jnp.broadcast_to(encode(lane + start).astype(BF16)[0:1], col.shape)
        blocks.append(pick_one(col == pattern))
    return jnp.concatenate(blocks, axis=1)


def one_hot_columns(codes, height):
    place = lax.broadcasted_iota(jnp.int32, (height, codes.shape[1]), 0)
    pattern = encode(place).astype(BF16)
    return pick_one(jnp.broadcast_to(codes, pattern.shape) == pattern)


def pick_rows(col, table):
    both = matmul(one_hot_rows(jnp.abs(col), table.shape[0]), table).astype(BF16)
    return jnp.where(col < jnp.zeros(col.shape, BF16), both[:, LANES:], both[:, :LANES])


def list_row(lists, first, per_row):
    pieces = [lists[first + n : first + n + 1, :] for n in range(per_row)]
    return pieces[0] if per_row == 1 else jnp.concatenate(pieces, axis=1)


def add_lists(total, lists_ref, blocks):
    slots, cap = lists_ref.shape
    codes = encode(lists_ref[...]).astype(F32)
    per_row = max(1, min(slots, LANES // cap))
    for first in range(0, slots, per_row):
        row = list_row(codes, first, per_row).astype(BF16)
        rows = jnp.concatenate(blocks[first : first + per_row], axis=0)
        total = total + matmul(one_hot_columns(row, total.shape[0]), rows)
    return total


def gather_lists(lists_ref, table):
    slots, cap = lists_ref.shape
    lists = lists_ref[...]
    per_row = max(1, min(slots, LANES // cap))
    parts = []
    for first in range(0, slots, per_row):
        codes = encode(list_row(lists, first, per_row))
        chooser = one_hot_rows(column(codes).astype(BF16), table.shape[0])
        parts.append(matmul(chooser, table))
    return parts[0] if len(parts) == 1 else jnp.concatenate(parts, axis=0)


def head_kernel(features_hbm, halo_hbm, child_map_hbm, out_grad_hbm, down_hbm, *refs):
    sources = (features_hbm, halo_hbm, child_map_hbm, out_grad_hbm, down_hbm)
    buffers, sems = refs[-len(sources) - 2 : -2], refs[-2]
    back_sems = refs[-1]
    features_ref, halo_ref, child_map_ref, out_grad_ref, down_ref = buffers
    copies = [
        pltpu.make_async_copy(source, buffer, sems.at[n])
        for n, (source, buffer) in enumerate(zip(sources, buffers))
    ]
    for copy in copies:
        copy.start()
    slots, cap = halo_ref.shape
    send_hbms, back_hbm = refs[:slots], refs[slots]
    sends, back_ref = refs[slots + 1 : 2 * slots + 1], refs[2 * slots + 1]
    voxels = features_ref.shape[0]
    octants = child_map_ref.shape[0]
    cap2 = sends[0].shape[0] - cap
    cap2 //= 1 + octants * out_grad_ref.shape[1] // LANES
    written = []

    def write(first, last):
        for send, send_hbm in zip(sends, send_hbms):
            place = pl.ds(first, last - first)
            sem = sems.at[len(copies) + len(written)]
            written.append(pltpu.make_async_copy(send.at[place], send_hbm.at[place], sem))
            written[-1].start()

    copies[0].wait()
    copies[1].wait()
    listed = gather_lists(halo_ref, features_ref[...]).astype(BF16)
    for send, block in zip(sends, to_steps(jnp.split(listed, slots), False)):
        send[0:cap, :] = block
    for copy in copies[2:]:
        copy.wait()
    upstream = out_grad_ref[...]
    rows = child_map_ref[...]
    codes = encode(jnp.where(rows >= voxels, rows - voxels, slots * cap2)).astype(BF16)
    sums = []
    for o in range(octants):
        chooser = one_hot_columns(codes[o : o + 1, :], slots * cap2)
        sums.append(matmul(chooser, upstream).astype(BF16))
    blocks = []
    for s in range(slots):
        listed_rows = slice(s * cap2, (s + 1) * cap2)
        halves = [
            sums[o][listed_rows, start : start + LANES]
            for o in range(octants)
            for start in range(0, upstream.shape[1], LANES)
        ]
        blocks.append(jnp.concatenate(halves, axis=0))
    for send, block in zip(sends, to_steps(blocks, True)):
        send[cap + cap2 :, :] = block
    write(cap + cap2, sends[0].shape[0])
    codes = half_codes(rows, voxels, slots * cap2)
    half = voxels // 2
    choosers, sides = [], []
    for o in range(octants):
        part = matmul_rt(upstream, down_ref[o]).astype(BF16)
        code = codes[o : o + 1, :].astype(BF16)
        right = column(code) < jnp.zeros(part.shape, BF16)
        none = jnp.zeros(part.shape, BF16)
        pair = [jnp.where(right, none, part), jnp.where(right, part, none)]
        sides.append(jnp.concatenate(pair, axis=1))
        choosers.append(one_hot_columns(jnp.abs(code), half + slots * cap2 // 2))
    both = matmul(jnp.concatenate(choosers, axis=1), jnp.concatenate(sides, axis=0))
    back_ref[0:half, :] = both[0:half, :LANES]
    back_ref[half:, :] = both[0:half, LANES:]
    far = jnp.concatenate([both[half:, :LANES], both[half:, LANES:]], axis=0).astype(BF16)
    for send, block in zip(sends, to_steps(jnp.split(far, slots), True)):
        send[cap : cap + cap2, :] = block
    write(0, cap + cap2)
    written += write_pieces(back_ref, back_hbm, back_sems)
    for copy in written:
        copy.wait()


def half_codes(row, voxels, received):
    half, half_received = voxels // 2, received // 2
    beyond = row - voxels
    outside = beyond >= 0
    near = row - jnp.where(row >= half, half, 0)
    far = half + beyond - jnp.where(beyond >= half_received, half_received, 0)
    code = encode(jnp.where(outside, far, near))
    near_sign = jnp.where(row >= half, -1.0, 1.0)
    far_sign = jnp.where(beyond >= half_received, -1.0, 1.0)
    return code * jnp.where(outside, far_sign, near_sign)


def outer_offsets(kernel_count):
    return [k for k in range(kernel_count) if k != kernel_count // 2]


def code_column(map_ref, k, voxels, received):
    return column(half_codes(map_ref[pl.ds(k, 1), :], voxels, received).astype(BF16))


def pick_side(col, both):
    return jnp.where(col < jnp.zeros(col.shape, BF16), both[:, LANES:], both[:, :LANES])


def local_kernel(received, features_ref, map_ref, early_ref, col_ref, table_ref):
    voxels = features_ref.shape[0]
    kernel_count = map_ref.shape[0]
    half, middle = voxels // 2, kernel_count // 2
    table_ref[:, 0:LANES] = features_ref[0:half, :]
    table_ref[:, LANES:] = features_ref[half:, :]
    early_ref[:, middle * LANES : (middle + 1) * LANES] = features_ref[...]
    for k in outer_offsets(kernel_count):
        lanes = slice(k * LANES, (k + 1) * LANES)
        col = code_column(map_ref, k, voxels, received)
        col_ref[:, lanes] = col
        both = matmul(one_hot_rows(jnp.abs(col), half), table_ref[...]).astype(BF16)
        early_ref[:, lanes] = pick_side(col, both)


def forward_kernel(slots, cap, *refs):
    received = refs[:slots]
    features_ref, weight_ref, child_ref, early_ref, col_ref = refs[slots : slots + 5]
    hidden_ref, pre_ref, stacked_ref, leaving_ref, halo_ref = refs[slots + 5 :]
    voxels = features_ref.shape[0]
    kernel_count = weight_ref.shape[0]
    middle = kernel_count // 2
    half, half_halo = voxels // 2, slots * cap // 2
    features = features_ref[...]
    halo_ref[...] = jnp.zeros(halo_ref.shape, BF16)
    for s, block in enumerate(to_slots([r[0:cap, :] for r in received], False)):
        place = (s % (slots // 2)) * cap
        side = (s // (slots // 2)) * LANES
        for n in range(2):
            row, lane = n * half_halo + place, 2 * n * LANES + side
            halo_ref[row : row + cap, lane : lane + LANES] = block
    outer = outer_offsets(kernel_count)
    for first in range(0, len(outer), 2):
        places = [slice(k * LANES, (k + 1) * LANES) for k in outer[first : first + 2]]
        cols = [col_ref[:, lanes] for lanes in places]
        choosers = [one_hot_rows(jnp.abs(col), half_halo, half) for col in cols]
        far = matmul(jnp.concatenate(choosers, axis=1), halo_ref[...]).astype(BF16)
        for n, lanes in enumerate(places):
            both = far[:, 2 * n * LANES : 2 * (n + 1) * LANES]
            stacked_ref[:, lanes] = pick_side(cols[n], both) + early_ref[:, lanes]
    lanes = slice(middle * LANES, (middle + 1) * LANES)
    stacked_ref[:, lanes] = early_ref[:, lanes]
    pre = matmul(stacked_ref[...], weight_ref[...].reshape(-1, LANES))
    pre_ref[...] = pre
    hidden = (features.astype(F32) + pre * jax.nn.sigmoid(pre)).astype(BF16)
    hidden_ref[...] = hidden
    leaving_ref[...] = gather_lists(child_ref, hidden).astype(BF16)


def gradient_kernel(slots, cap, *refs):
    received = refs[:slots]
    stacked_ref, pre_ref, child_ref, back_ref = refs[slots : slots + 4]
    hidden_ref, leaving_ref, child_map_ref, out_grad_ref = refs[slots + 4 : slots + 8]
    hgrad_ref, pgrad_ref, early_ref, terms_ref, send_ref = refs[slots + 8 :]
    cap2 = child_ref.shape[1]
    kernel_count = stacked_ref.shape[1] // LANES
    blocks = to_slots([r[cap : cap + cap2, :] for r in received], True)
    hgrad = add_lists(back_ref[...], child_ref, blocks)
    hgrad_ref[...] = hgrad
    pre = pre_ref[...]
    sig = jax.nn.sigmoid(pre)
    pgrad = hgrad * (sig * (1.0 + pre * (1.0 - sig)))
    pgrad_ref[...] = pgrad.astype(BF16)
    terms = matmul(jnp.transpose(pgrad).astype(BF16), stacked_ref[...])
    for k in range(kernel_count):
        block = jnp.transpose(terms[:, k * LANES : (k + 1) * LANES])
        terms_ref[k * LANES : (k + 1) * LANES, :] = block.astype(BF16)
    voxels = hidden_ref.shape[0]
    half = voxels // 2
    hidden = hidden_ref[...]
    table = jnp.concatenate([hidden[0:half], hidden[half:]], axis=1)
    octants = child_map_ref.shape[0]
    picked = []
    for o in range(octants):
        col = code_column(child_map_ref, o, voxels, slots * cap2)
        both = matmul(one_hot_rows(jnp.abs(col), half), table).astype(BF16)
        picked.append(pick_side(col, both))
    picked = jnp.concatenate(picked, axis=1)
    early_ref[...] = picked
    upstream_t = jnp.transpose(out_grad_ref[...].astype(F32)).astype(BF16)
    own = matmul(upstream_t, picked)
    blocks = to_slots([r[cap + cap2 :, :] for r in received], True)
    across = upstream_t.shape[0] // LANES
    sums = []
    for n in range(octants * across):
        rows = slice(n * cap2, (n + 1) * cap2)
        sums.append(jnp.concatenate([block[rows, :] for block in blocks], axis=0))
    leaving_t = jnp.transpose(leaving_ref[...].astype(F32)).astype(BF16)
    far = matmul(leaving_t, jnp.concatenate(sums, axis=1))
    row = kernel_count * LANES
    for n in range(octants * across):
        o, side = n // across, n % across
        block = own[side * LANES : (side + 1) * LANES, o * LANES : (o + 1) * LANES]
        value = jnp.transpose(block) + far[:, n * LANES : (n + 1) * LANES]
        terms_ref[row : row + LANES, :] = value.astype(BF16)
        row += LANES
    terms_ref[row:, :] = jnp.zeros((terms_ref.shape[0] - row, LANES), BF16)
    send_ref[...] = terms_ref[pl.ds(my_half(send_ref.shape[0])[1], send_ref.shape[0]), :]


def spread_kernel(
    slots, cap, pgrad_ref, map_ref, weight_ref, leaving_ref, after_ref, back_ref, *sends
):
    acc_ref = sends[-1]
    sends = sends[:-1]
    voxels = pgrad_ref.shape[0]
    kernel_count = map_ref.shape[0]
    middle = kernel_count // 2
    half = voxels // 2
    table_rows = half + slots * cap // 2
    pgrad = pgrad_ref[...]
    own = matmul_rt(pgrad, weight_ref[middle])
    acc_ref[0:half, 0:LANES] = own[0:half]
    acc_ref[0:half, LANES:] = own[half:]
    acc_ref[half:, :] = jnp.zeros((table_rows - half, 2 * LANES), F32)

    def parts(k):
        codes = half_codes(map_ref[pl.ds(k, 1), :], voxels, slots * cap)
        terms = matmul_rt(pgrad, weight_ref[k])
        right = column(codes) < 0.0
        sides = [jnp.where(right, 0.0, terms), jnp.where(right, terms, 0.0)]
        chooser = one_hot_columns(jnp.abs(codes).astype(BF16), table_rows)
        return chooser, jnp.concatenate(sides, axis=1).astype(BF16)

    def step(j, carry):
        near_chooser, near_terms = parts(j)
        far_chooser, far_terms = parts(j + middle + 1)
        acc_ref[...] += matmul(near_chooser, near_terms) + matmul(far_chooser, far_terms)
        return carry

    lax.fori_loop(0, middle, step, 0)
    back_ref[0:half, :] = acc_ref[0:half, 0:LANES]
    back_ref[half:, :] = acc_ref[0:half, LANES:]
    blocks = []
    for s in range(slots):
        first = half + (s % (slots // 2)) * cap
        side = (s // (slots // 2)) * LANES
        blocks.append(acc_ref[first : first + cap, side : side + LANES].astype(BF16))
    for send, block in zip(sends, to_steps(blocks, True)):
        send[0:cap, :] = block
    for send, block in zip(sends, to_steps(jnp.split(leaving_ref[...], slots), False)):
        send[cap:, :] = block


def my_half(rows):
    core = lax.rem(lax.axis_index("shard"), 2)
    return pl.multiple_of(core * rows, 16), pl.multiple_of((1 - core) * rows, 16)


def write_pieces(stage_ref, out_hbm, sems, first=0, last=None):
    pieces = sems.shape[0]
    rows = stage_ref.shape[0] // pieces
    copies = []
    for n in range(first, pieces if last is None else last):
        place = pl.ds(n * rows, rows)
        copies.append(pltpu.make_async_copy(stage_ref.at[place], out_hbm.at[place], sems.at[n]))
        copies[-1].start()
    return copies


def pair_kernel(terms_ref, other_ref, out_hbm, stage_ref, sems):
    pieces = sems.shape[0]
    rows = stage_ref.shape[0] // pieces
    first = my_half(stage_ref.shape[0])[0]
    copies = []
    for n in range(pieces):
        place = pl.ds(pl.multiple_of(first + n * rows, 16), rows)
        other = other_ref[n * rows : (n + 1) * rows, :].astype(F32)
        value = terms_ref[place, :].astype(F32) + other
        stage_ref[n * rows : (n + 1) * rows, :] = value.astype(BF16)
        copies += write_pieces(stage_ref, out_hbm, sems, n, n + 1)
    for copy in copies:
        copy.wait()


def sum_kernel(devices, scale, parts_ref, after_ref, out_hbm, stage_ref, sems):
    rows = parts_ref.shape[0] // devices
    sums = []
    for core in range(2):
        total = jnp.zeros((rows, LANES), F32)
        for d in range(core, devices, 2):
            total = total + parts_ref[d * rows : (d + 1) * rows, :].astype(F32)
        sums.append((total * scale).astype(BF16))
    pieces = sems.shape[0]
    copies = []
    for d in range(devices):
        stage_ref[d * rows : (d + 1) * rows, :] = sums[d % 2]
        if (d + 1) % (devices // pieces) == 0:
            piece = d // (devices // pieces)
            copies += write_pieces(stage_ref, out_hbm, sems, piece, piece + 1)
    for copy in copies:
        copy.wait()


def final_kernel(own, *refs):
    block_ref, conv_hbm, down_hbm = refs[0], *refs[-5:-3]
    conv_ref, down_ref, sems = refs[-3:]
    rows = block_ref.shape[0]
    conv_rows = conv_hbm.shape[0]
    core = lax.rem(lax.axis_index("shard"), 2)
    piece = 4 * LANES
    assert rows <= conv_rows <= 2 * rows and rows % LANES == 0

    def write(half):
        first, last = half * rows, (half + 1) * rows
        copies = []
        for start in range(first, min(last, conv_rows), piece):
            size = min(piece, last - start, conv_rows - start)
            place = pl.ds(start, size)
            value = block_ref[start - first : start - first + size, :]
            conv_ref[place, :] = value.astype(F32)
            sem = sems.at[len(copies)]
            copies.append(pltpu.make_async_copy(conv_ref.at[place], conv_hbm.at[place], sem))
            copies[-1].start()
        across = down_hbm.shape[1] // LANES
        for down in range(0, down_hbm.shape[0], LANES):
            row = conv_rows + down * across
            for side in range(across):
                start = row + side * LANES
                if first <= start < last:
                    value = block_ref[start - first : start - first + LANES, :]
                    lanes = slice(side * LANES, (side + 1) * LANES)
                    down_ref[down : down + LANES, lanes] = value.astype(F32)
            if first <= row < last:
                place = pl.ds(down, LANES)
                sem = sems.at[len(copies)]
                copies.append(pltpu.make_async_copy(down_ref.at[place], down_hbm.at[place], sem))
                copies[-1].start()
        for copy in copies:
            copy.wait()

    for half in range(2):
        pl.when(core == (half if own else 1 - half))(functools.partial(write, half))


def tail_kernel(slots, *refs):
    received = refs[:slots]
    hgrad_ref, back_ref, halo_ref, early_ref, map_ref, down_ref = refs[slots : slots + 6]
    out_ref, coarse_ref = refs[slots + 6 :]
    voxels = hgrad_ref.shape[0]
    cap = halo_ref.shape[1]
    cap2 = received[0].shape[0] - cap
    blocks = to_slots([r[0:cap, :] for r in received], True)
    out_ref[...] = add_lists(hgrad_ref[...] + back_ref[...], halo_ref, blocks)
    halo = jnp.concatenate(to_slots([r[cap:, :] for r in received], False), axis=0)
    octants = map_ref.shape[0]
    rows = map_ref[...]
    codes = encode(jnp.where(rows >= voxels, rows - voxels, slots * cap2))
    picked = []
    for o in range(octants):
        chooser = one_hot_rows(column(codes[o : o + 1, :]).astype(BF16), slots * cap2)
        far = matmul(chooser, halo).astype(BF16)
        picked.append(far + early_ref[:, o * LANES : (o + 1) * LANES])
    kernel = down_ref[...].reshape(octants * LANES, down_ref.shape[2])
    coarse_ref[...] = matmul(jnp.concatenate(picked, axis=1), kernel).astype(BF16)


def call(
    kernel, operands, outs, scratch=(), limit=32, flops=0, in_hbm=(), out_hbm=False, aliases={}
):
    spaces = [pl.ANY if n in in_hbm else pltpu.VMEM for n in range(len(operands))]
    return pl.pallas_call(
        kernel,
        out_shape=[jax.ShapeDtypeStruct(s, d) for s, d in outs],
        in_specs=[pl.BlockSpec(memory_space=space) for space in spaces],
        out_specs=[pl.BlockSpec(memory_space=pl.ANY if out_hbm else pltpu.VMEM) for _ in outs],
        input_output_aliases=aliases,
        scratch_shapes=list(scratch),
        compiler_params=pltpu.CompilerParams(vmem_limit_bytes=limit * 2**20),
        cost_estimate=pl.CostEstimate(flops=flops, bytes_accessed=4 * 2**20, transcendentals=0),
    )(*operands)


def swap_cores(value, devices):
    return lax.ppermute(value, "shard", [(i, i + 1 - 2 * (i % 2)) for i in range(devices)])


def exchange(value):
    return lax.all_to_all(value, "shard", 0, 0, tiled=True)


def local(
    features, conv_weight, down_weight, neighbour_map, halo_rows, child_map, child_rows, out_grad
):
    voxels, channels = features.shape
    parents, coarse_channels = out_grad.shape
    kernel_count = conv_weight.shape[0]
    octants = down_weight.shape[0]
    slots, cap = halo_rows.shape
    cap2 = child_rows.shape[1]
    devices = lax.axis_size("shard")
    scale = 1.0 / math.sqrt(voxels * devices)
    giga = 10**9

    sum_rows = octants * cap2 * coarse_channels // LANES
    conv_rows = kernel_count * channels
    down_rows = octants * channels * coarse_channels // LANES
    grain = 8 * devices
    half_rows = -(-(conv_rows + down_rows) // (2 * grain)) * grain
    first = call(
        head_kernel,
        (features, halo_rows, child_map, out_grad, down_weight),
        [((cap + cap2 + sum_rows, channels), BF16)] * slots + [((voxels, channels), F32)],
        scratch=[pltpu.VMEM((cap + cap2 + sum_rows, channels), BF16)] * slots
        + [pltpu.VMEM((voxels, channels), F32)]
        + [
            pltpu.VMEM(value.shape, value.dtype)
            for value in (features, halo_rows, child_map, out_grad, down_weight)
        ]
        + [pltpu.SemaphoreType.DMA((5 + 2 * slots,)), pltpu.SemaphoreType.DMA((4,))],
        limit=60,
        flops=giga,
        in_hbm=range(5),
        out_hbm=True,
    )
    back_h = first[-1]
    received = swaps(first[:-1], (2, 3, 1, 0))
    early, cols = call(
        functools.partial(local_kernel, slots * cap),
        (features, neighbour_map),
        [((voxels, conv_rows), BF16)] * 2,
        scratch=[pltpu.VMEM((voxels // 2, 2 * channels), BF16)],
        flops=4 * giga,
    )
    hidden, pre_act, stacked, leaving = call(
        functools.partial(forward_kernel, slots, cap),
        (*received, features, conv_weight, child_rows, early, cols),
        [
            ((voxels, channels), BF16),
            ((voxels, channels), F32),
            ((voxels, conv_rows), BF16),
            ((slots * cap2, channels), BF16),
        ],
        scratch=[pltpu.VMEM((slots * cap, 4 * channels), BF16)],
        flops=12 * giga,
    )
    hidden_grad, pre_grad, early_h, terms, leaving_terms = call(
        functools.partial(gradient_kernel, slots, cap),
        (
            *received,
            stacked,
            pre_act,
            child_rows,
            back_h,
            hidden,
            leaving,
            child_map,
            out_grad,
        ),
        [
            ((voxels, channels), F32),
            ((voxels, channels), BF16),
            ((parents, octants * channels), BF16),
            ((2 * half_rows, LANES), BF16),
            ((half_rows, LANES), BF16),
        ],
        flops=3 * giga,
    )
    (pair_terms,) = call(
        pair_kernel,
        (terms, swap_cores(leaving_terms, devices)),
        [((half_rows, LANES), BF16)],
        scratch=[pltpu.VMEM((half_rows, LANES), BF16), pltpu.SemaphoreType.DMA((8,))],
        flops=10**6,
        out_hbm=True,
    )
    parts = exchange(pair_terms)
    spread = call(
        functools.partial(spread_kernel, slots, cap),
        (pre_grad, neighbour_map, conv_weight, leaving, pair_terms),
        [((voxels, channels), F32)] + [((cap + cap2, channels), BF16)] * slots,
        scratch=[pltpu.VMEM((voxels // 2 + slots * cap // 2, 2 * channels), F32)],
        flops=20 * giga,
        in_hbm=(4,),
    )
    (summed,) = call(
        functools.partial(sum_kernel, devices, scale),
        (parts, spread[1]),
        [((half_rows, LANES), BF16)],
        scratch=[pltpu.VMEM((half_rows, LANES), BF16), pltpu.SemaphoreType.DMA((8,))],
        flops=10**6,
        in_hbm=(1,),
        out_hbm=True,
    )
    summed, *returning = lax.optimization_barrier((summed, *spread[1:]))
    returned = swaps(returning, (0, 1, 2, 3))
    input_grad, coarse = call(
        functools.partial(tail_kernel, slots),
        (*returned, hidden_grad, spread[0], halo_rows, early_h, child_map, down_weight),
        [((voxels, channels), F32), ((parents, coarse_channels), BF16)],
        flops=giga,
    )
    mine, input_grad = lax.optimization_barrier((exchange(summed), input_grad))
    other = swap_cores(mine, devices)
    gradients = ()
    for own, block in ((True, mine), (False, other)):
        gradients = call(
            functools.partial(final_kernel, own),
            (block, *gradients),
            [((conv_rows, LANES), F32), ((octants * channels, coarse_channels), F32)],
            scratch=[
                pltpu.VMEM((conv_rows, LANES), F32),
                pltpu.VMEM((octants * channels, coarse_channels), F32),
                pltpu.SemaphoreType.DMA((32,)),
            ],
            flops=10**6,
            in_hbm=(1, 2),
            out_hbm=True,
            aliases={1: 0, 2: 1} if gradients else {},
        )
    conv_grad, down_grad = gradients
    conv_grad = conv_grad.reshape(conv_weight.shape)
    return (coarse, input_grad, conv_grad, down_grad.reshape(down_weight.shape))


def solution(mesh):
    return jax.shard_map(
        local,
        mesh=mesh,
        in_specs=(
            P("shard", None),
            P(),
            P(),
            P(None, "shard"),
            P(None, "shard"),
            P(None, "shard"),
            P(None, "shard"),
            P("shard", None),
        ),
        out_specs=(P("shard", None), P("shard", None), P(), P()),
        check_vma=False,
    )
```

```python
import functools
import math

import jax
import jax.numpy as jnp
from jax import lax
from jax.experimental import pallas as pl
from jax.experimental.pallas import tpu as pltpu
from jax.sharding import PartitionSpec as P

BF16 = jnp.bfloat16
F32 = jnp.float32
LANES = 128


def swaps(by_step, order):
    devices = lax.axis_size("shard")
    moved = {}
    for step in order:
        m, phase = step // 2 + 1, step % 2
        sign = [1 if (i // m) % 2 == phase else -1 for i in range(devices)]
        pairs = [(i, i + m * sign[i]) for i in range(devices) if 0 <= i + m * sign[i] < devices]
        moved[step] = lax.ppermute(by_step[step], "shard", pairs)
    return [moved[step] for step in range(len(by_step))]


def is_even(m):
    return lax.rem(lax.div(lax.axis_index("shard"), m), 2) == 0


def to_steps(slots, back):
    reach = len(slots) // 2
    steps = []
    for m in range(1, reach + 1):
        first, second = slots[reach + m - 1], slots[reach - m]
        if back:
            first, second = second, first
        steps.append(lax.select(is_even(m), first, second))
        steps.append(lax.select(is_even(m), second, first))
    return steps


def to_slots(steps, back):
    reach = len(steps) // 2
    slots = [None] * len(steps)
    for m in range(1, reach + 1):
        first = lax.select(is_even(m), steps[2 * m - 2], steps[2 * m - 1])
        second = lax.select(is_even(m), steps[2 * m - 1], steps[2 * m - 2])
        if back:
            first, second = second, first
        slots[reach - m], slots[reach + m - 1] = first, second
    return slots


def matmul(left, right):
    return jnp.dot(left, right, preferred_element_type=F32)


def matmul_rt(left, right):
    return lax.dot_general(left, right, (((1,), (1,)), ((), ())), preferred_element_type=F32)


def pick_one(mask):
    return jnp.where(mask, jnp.ones(mask.shape, BF16), jnp.zeros(mask.shape, BF16))


def encode(row):
    return jnp.left_shift((row & (LANES - 1)) + LANES, row >> 7).astype(F32)


def column(codes):
    pieces = []
    for start in range(0, codes.shape[1], LANES):
        piece = jnp.broadcast_to(codes[:, start : start + LANES], (LANES, LANES))
        pieces.append(jnp.transpose(piece))
    return pieces[0] if len(pieces) == 1 else jnp.concatenate(pieces, axis=0)


def one_hot_rows(col, width, first=0):
    lane = lax.broadcasted_iota(jnp.int32, (16, LANES), 1)
    blocks = []
    for start in range(first, first + width, LANES):
        pattern = jnp.broadcast_to(encode(lane + start).astype(BF16)[0:1], col.shape)
        blocks.append(pick_one(col == pattern))
    return jnp.concatenate(blocks, axis=1)


def one_hot_columns(codes, height):
    place = lax.broadcasted_iota(jnp.int32, (height, codes.shape[1]), 0)
    pattern = encode(place).astype(BF16)
    return pick_one(jnp.broadcast_to(codes, pattern.shape) == pattern)


def pick_rows(col, table):
    both = matmul(one_hot_rows(jnp.abs(col), table.shape[0]), table).astype(BF16)
    return jnp.where(col < jnp.zeros(col.shape, BF16), both[:, LANES:], both[:, :LANES])


def list_row(lists, first, per_row):
    pieces = [lists[first + n : first + n + 1, :] for n in range(per_row)]
    return pieces[0] if per_row == 1 else jnp.concatenate(pieces, axis=1)


def add_lists(total, lists_ref, blocks):
    slots, cap = lists_ref.shape
    codes = encode(lists_ref[...]).astype(F32)
    per_row = max(1, min(slots, LANES // cap))
    for first in range(0, slots, per_row):
        row = list_row(codes, first, per_row).astype(BF16)
        rows = jnp.concatenate(blocks[first : first + per_row], axis=0)
        total = total + matmul(one_hot_columns(row, total.shape[0]), rows)
    return total


def gather_lists(lists_ref, table):
    slots, cap = lists_ref.shape
    lists = lists_ref[...]
    per_row = max(1, min(slots, LANES // cap))
    parts = []
    for first in range(0, slots, per_row):
        codes = encode(list_row(lists, first, per_row))
        chooser = one_hot_rows(column(codes).astype(BF16), table.shape[0])
        parts.append(matmul(chooser, table))
    return parts[0] if len(parts) == 1 else jnp.concatenate(parts, axis=0)


def head_kernel(features_hbm, halo_hbm, child_map_hbm, out_grad_hbm, down_hbm, *refs):
    sources = (features_hbm, halo_hbm, child_map_hbm, out_grad_hbm, down_hbm)
    buffers, sems = refs[-len(sources) - 2 : -2], refs[-2]
    back_sems = refs[-1]
    features_ref, halo_ref, child_map_ref, out_grad_ref, down_ref = buffers
    copies = [
        pltpu.make_async_copy(source, buffer, sems.at[n])
        for n, (source, buffer) in enumerate(zip(sources, buffers))
    ]
    for copy in copies:
        copy.start()
    slots, cap = halo_ref.shape
    send_hbms, back_hbm = refs[:slots], refs[slots]
    sends, back_ref = refs[slots + 1 : 2 * slots + 1], refs[2 * slots + 1]
    voxels = features_ref.shape[0]
    octants = child_map_ref.shape[0]
    cap2 = sends[0].shape[0] - cap
    cap2 //= 1 + octants * out_grad_ref.shape[1] // LANES
    written = []

    def write(first, last):
        for send, send_hbm in zip(sends, send_hbms):
            place = pl.ds(first, last - first)
            sem = sems.at[len(copies) + len(written)]
            written.append(pltpu.make_async_copy(send.at[place], send_hbm.at[place], sem))
            written[-1].start()

    copies[0].wait()
    copies[1].wait()
    listed = gather_lists(halo_ref, features_ref[...]).astype(BF16)
    for send, block in zip(sends, to_steps(jnp.split(listed, slots), False)):
        send[0:cap, :] = block
    for copy in copies[2:]:
        copy.wait()
    upstream = out_grad_ref[...]
    rows = child_map_ref[...]
    codes = encode(jnp.where(rows >= voxels, rows - voxels, slots * cap2)).astype(BF16)
    sums = []
    for o in range(octants):
        chooser = one_hot_columns(codes[o : o + 1, :], slots * cap2)
        sums.append(matmul(chooser, upstream).astype(BF16))
    blocks = []
    for s in range(slots):
        listed_rows = slice(s * cap2, (s + 1) * cap2)
        halves = [
            sums[o][listed_rows, start : start + LANES]
            for o in range(octants)
            for start in range(0, upstream.shape[1], LANES)
        ]
        blocks.append(jnp.concatenate(halves, axis=0))
    for send, block in zip(sends, to_steps(blocks, True)):
        send[cap + cap2 :, :] = block
    write(cap + cap2, sends[0].shape[0])
    codes = half_codes(rows, voxels, slots * cap2)
    half = voxels // 2
    choosers, sides = [], []
    for o in range(octants):
        part = matmul_rt(upstream, down_ref[o]).astype(BF16)
        code = codes[o : o + 1, :].astype(BF16)
        right = column(code) < jnp.zeros(part.shape, BF16)
        none = jnp.zeros(part.shape, BF16)
        pair = [jnp.where(right, none, part), jnp.where(right, part, none)]
        sides.append(jnp.concatenate(pair, axis=1))
        choosers.append(one_hot_columns(jnp.abs(code), half + slots * cap2 // 2))
    both = matmul(jnp.concatenate(choosers, axis=1), jnp.concatenate(sides, axis=0))
    back_ref[0:half, :] = both[0:half, :LANES]
    back_ref[half:, :] = both[0:half, LANES:]
    far = jnp.concatenate([both[half:, :LANES], both[half:, LANES:]], axis=0).astype(BF16)
    for send, block in zip(sends, to_steps(jnp.split(far, slots), True)):
        send[cap : cap + cap2, :] = block
    write(0, cap + cap2)
    written += write_pieces(back_ref, back_hbm, back_sems)
    for copy in written:
        copy.wait()


def half_codes(row, voxels, received):
    half, half_received = voxels // 2, received // 2
    beyond = row - voxels
    outside = beyond >= 0
    near = row - jnp.where(row >= half, half, 0)
    far = half + beyond - jnp.where(beyond >= half_received, half_received, 0)
    code = encode(jnp.where(outside, far, near))
    near_sign = jnp.where(row >= half, -1.0, 1.0)
    far_sign = jnp.where(beyond >= half_received, -1.0, 1.0)
    return code * jnp.where(outside, far_sign, near_sign)


def offset_of(n, middle):
    return n + jnp.where(n >= middle, 1, 0)


def code_column(map_ref, k, voxels, received):
    return column(half_codes(map_ref[pl.ds(k, 1), :], voxels, received).astype(BF16))


def pick_side(col, both):
    return jnp.where(col < jnp.zeros(col.shape, BF16), both[:, LANES:], both[:, :LANES])


def local_kernel(received, features_ref, map_ref, early_ref, table_ref):
    voxels = features_ref.shape[0]
    half = voxels // 2
    table_ref[:, 0:LANES] = features_ref[0:half, :]
    table_ref[:, LANES:] = features_ref[half:, :]
    middle = map_ref.shape[0] // 2
    for n in range(early_ref.shape[1] // LANES):
        col = code_column(map_ref, offset_of(n, middle), voxels, received)
        both = matmul(one_hot_rows(jnp.abs(col), half), table_ref[...]).astype(BF16)
        early_ref[:, n * LANES : (n + 1) * LANES] = pick_side(col, both)


def forward_kernel(slots, cap, *refs):
    received = refs[:slots]
    features_ref, map_ref, weight_ref, child_ref, early_ref = refs[slots : slots + 5]
    hidden_ref, pre_ref, stacked_ref, leaving_ref, halo_ref, kernel_ref = refs[slots + 5 :]
    done = 0
    voxels = features_ref.shape[0]
    gathers = map_ref.shape[0] - 1
    middle = gathers // 2
    half, half_halo = voxels // 2, slots * cap // 2
    features = features_ref[...]
    halo_ref[...] = jnp.zeros(halo_ref.shape, BF16)
    for s, block in enumerate(to_slots([r[0:cap, :] for r in received], False)):
        place = (s % (slots // 2)) * cap
        side = (s // (slots // 2)) * LANES
        for n in range(2):
            row, lane = n * half_halo + place, 2 * n * LANES + side
            halo_ref[row : row + cap, lane : lane + LANES] = block
    kernel_ref[0:middle] = weight_ref[0:middle]
    kernel_ref[middle:gathers] = weight_ref[middle + 1 :]
    kernel_ref[gathers] = weight_ref[middle]

    for j in range(middle):
        numbers = (2 * j, 2 * j + 1)
        cols = [code_column(map_ref, offset_of(n, middle), voxels, slots * cap) for n in numbers]
        choosers = [one_hot_rows(jnp.abs(col), half_halo, half) for col in cols]
        far = matmul(jnp.concatenate(choosers, axis=1), halo_ref[...]).astype(BF16)
        for n in numbers:
            both = far[:, 2 * (n % 2) * LANES : 2 * (n % 2 + 1) * LANES]
            lanes = slice(n * LANES, (n + 1) * LANES)
            stacked_ref[:, lanes] = pick_side(cols[n % 2], both) + early_ref[:, lanes]
        last = 2 * j + 2
        if last == gathers:
            stacked_ref[:, gathers * LANES :] = features
            last = gathers + 1
        if last - done > 2:
            columns = stacked_ref[:, done * LANES : last * LANES]
            term = matmul(columns, kernel_ref[done:last].reshape(-1, LANES))
            pre_ref[...] = term if done == 0 else pre_ref[...] + term
            done = last

    pre = pre_ref[...]
    hidden = (features.astype(F32) + pre * jax.nn.sigmoid(pre)).astype(BF16)
    hidden_ref[...] = hidden
    leaving_ref[...] = gather_lists(child_ref, hidden).astype(BF16)


def gradient_kernel(slots, cap, *refs):
    received = refs[:slots]
    stacked_ref, pre_ref, child_ref, back_ref = refs[slots : slots + 4]
    hidden_ref, leaving_ref, child_map_ref, out_grad_ref = refs[slots + 4 : slots + 8]
    hgrad_ref, pgrad_ref, early_ref, terms_ref, send_ref = refs[slots + 8 :]
    cap2 = child_ref.shape[1]
    kernel_count = stacked_ref.shape[1] // LANES
    middle = kernel_count // 2
    blocks = to_slots([r[cap : cap + cap2, :] for r in received], True)
    hgrad = add_lists(back_ref[...], child_ref, blocks)
    hgrad_ref[...] = hgrad
    pre = pre_ref[...]
    sig = jax.nn.sigmoid(pre)
    pgrad = hgrad * (sig * (1.0 + pre * (1.0 - sig)))
    pgrad_ref[...] = pgrad.astype(BF16)
    terms = matmul(jnp.transpose(pgrad).astype(BF16), stacked_ref[...])
    order = [k for k in range(kernel_count) if k != middle] + [middle]
    for n, k in enumerate(order):
        block = jnp.transpose(terms[:, n * LANES : (n + 1) * LANES])
        terms_ref[k * LANES : (k + 1) * LANES, :] = block.astype(BF16)
    voxels = hidden_ref.shape[0]
    half = voxels // 2
    hidden = hidden_ref[...]
    table = jnp.concatenate([hidden[0:half], hidden[half:]], axis=1)
    octants = child_map_ref.shape[0]
    picked = []
    for o in range(octants):
        col = code_column(child_map_ref, o, voxels, slots * cap2)
        both = matmul(one_hot_rows(jnp.abs(col), half), table).astype(BF16)
        picked.append(pick_side(col, both))
    picked = jnp.concatenate(picked, axis=1)
    early_ref[...] = picked
    upstream_t = jnp.transpose(out_grad_ref[...].astype(F32)).astype(BF16)
    own = matmul(upstream_t, picked)
    blocks = to_slots([r[cap + cap2 :, :] for r in received], True)
    across = upstream_t.shape[0] // LANES
    sums = []
    for n in range(octants * across):
        rows = slice(n * cap2, (n + 1) * cap2)
        sums.append(jnp.concatenate([block[rows, :] for block in blocks], axis=0))
    leaving_t = jnp.transpose(leaving_ref[...].astype(F32)).astype(BF16)
    far = matmul(leaving_t, jnp.concatenate(sums, axis=1))
    row = kernel_count * LANES
    for n in range(octants * across):
        o, side = n // across, n % across
        block = own[side * LANES : (side + 1) * LANES, o * LANES : (o + 1) * LANES]
        value = jnp.transpose(block) + far[:, n * LANES : (n + 1) * LANES]
        terms_ref[row : row + LANES, :] = value.astype(BF16)
        row += LANES
    terms_ref[row:, :] = jnp.zeros((terms_ref.shape[0] - row, LANES), BF16)
    send_ref[...] = terms_ref[pl.ds(my_half(send_ref.shape[0])[1], send_ref.shape[0]), :]


def spread_kernel(
    slots, cap, pgrad_ref, map_ref, weight_ref, leaving_ref, after_ref, back_ref, *sends
):
    acc_ref = sends[-1]
    sends = sends[:-1]
    voxels = pgrad_ref.shape[0]
    kernel_count = map_ref.shape[0]
    middle = kernel_count // 2
    half = voxels // 2
    table_rows = half + slots * cap // 2
    pgrad = pgrad_ref[...]
    own = matmul_rt(pgrad, weight_ref[middle])
    acc_ref[0:half, 0:LANES] = own[0:half]
    acc_ref[0:half, LANES:] = own[half:]
    acc_ref[half:, :] = jnp.zeros((table_rows - half, 2 * LANES), F32)

    def parts(k):
        codes = half_codes(map_ref[pl.ds(k, 1), :], voxels, slots * cap)
        terms = matmul_rt(pgrad, weight_ref[k])
        right = column(codes) < 0.0
        sides = [jnp.where(right, 0.0, terms), jnp.where(right, terms, 0.0)]
        chooser = one_hot_columns(jnp.abs(codes).astype(BF16), table_rows)
        return chooser, jnp.concatenate(sides, axis=1).astype(BF16)

    def step(j, carry):
        near_chooser, near_terms = parts(j)
        far_chooser, far_terms = parts(j + middle + 1)
        acc_ref[...] += matmul(near_chooser, near_terms) + matmul(far_chooser, far_terms)
        return carry

    lax.fori_loop(0, middle, step, 0)
    back_ref[0:half, :] = acc_ref[0:half, 0:LANES]
    back_ref[half:, :] = acc_ref[0:half, LANES:]
    blocks = []
    for s in range(slots):
        first = half + (s % (slots // 2)) * cap
        side = (s // (slots // 2)) * LANES
        blocks.append(acc_ref[first : first + cap, side : side + LANES].astype(BF16))
    for send, block in zip(sends, to_steps(blocks, True)):
        send[0:cap, :] = block
    for send, block in zip(sends, to_steps(jnp.split(leaving_ref[...], slots), False)):
        send[cap:, :] = block


def my_half(rows):
    core = lax.rem(lax.axis_index("shard"), 2)
    return pl.multiple_of(core * rows, 16), pl.multiple_of((1 - core) * rows, 16)


def write_pieces(stage_ref, out_hbm, sems, first=0, last=None):
    pieces = sems.shape[0]
    rows = stage_ref.shape[0] // pieces
    copies = []
    for n in range(first, pieces if last is None else last):
        place = pl.ds(n * rows, rows)
        copies.append(pltpu.make_async_copy(stage_ref.at[place], out_hbm.at[place], sems.at[n]))
        copies[-1].start()
    return copies


def pair_kernel(terms_ref, other_ref, out_hbm, stage_ref, sems):
    pieces = sems.shape[0]
    rows = stage_ref.shape[0] // pieces
    first = my_half(stage_ref.shape[0])[0]
    copies = []
    for n in range(pieces):
        place = pl.ds(pl.multiple_of(first + n * rows, 16), rows)
        other = other_ref[n * rows : (n + 1) * rows, :].astype(F32)
        value = terms_ref[place, :].astype(F32) + other
        stage_ref[n * rows : (n + 1) * rows, :] = value.astype(BF16)
        copies += write_pieces(stage_ref, out_hbm, sems, n, n + 1)
    for copy in copies:
        copy.wait()


def sum_kernel(devices, scale, parts_ref, after_ref, out_hbm, stage_ref, sems):
    rows = parts_ref.shape[0] // devices
    sums = []
    for core in range(2):
        total = jnp.zeros((rows, LANES), F32)
        for d in range(core, devices, 2):
            total = total + parts_ref[d * rows : (d + 1) * rows, :].astype(F32)
        sums.append((total * scale).astype(BF16))
    pieces = sems.shape[0]
    copies = []
    for d in range(devices):
        stage_ref[d * rows : (d + 1) * rows, :] = sums[d % 2]
        if (d + 1) % (devices // pieces) == 0:
            piece = d // (devices // pieces)
            copies += write_pieces(stage_ref, out_hbm, sems, piece, piece + 1)
    for copy in copies:
        copy.wait()


def final_kernel(own, *refs):
    block_ref, conv_hbm, down_hbm = refs[0], *refs[-5:-3]
    conv_ref, down_ref, sems = refs[-3:]
    rows = block_ref.shape[0]
    conv_rows = conv_hbm.shape[0]
    core = lax.rem(lax.axis_index("shard"), 2)
    piece = 4 * LANES
    assert rows <= conv_rows <= 2 * rows and rows % LANES == 0

    def write(half):
        first, last = half * rows, (half + 1) * rows
        copies = []
        for start in range(first, min(last, conv_rows), piece):
            size = min(piece, last - start, conv_rows - start)
            place = pl.ds(start, size)
            value = block_ref[start - first : start - first + size, :]
            conv_ref[place, :] = value.astype(F32)
            sem = sems.at[len(copies)]
            copies.append(pltpu.make_async_copy(conv_ref.at[place], conv_hbm.at[place], sem))
            copies[-1].start()
        across = down_hbm.shape[1] // LANES
        for down in range(0, down_hbm.shape[0], LANES):
            row = conv_rows + down * across
            for side in range(across):
                start = row + side * LANES
                if first <= start < last:
                    value = block_ref[start - first : start - first + LANES, :]
                    lanes = slice(side * LANES, (side + 1) * LANES)
                    down_ref[down : down + LANES, lanes] = value.astype(F32)
            if first <= row < last:
                place = pl.ds(down, LANES)
                sem = sems.at[len(copies)]
                copies.append(pltpu.make_async_copy(down_ref.at[place], down_hbm.at[place], sem))
                copies[-1].start()
        for copy in copies:
            copy.wait()

    for half in range(2):
        pl.when(core == (half if own else 1 - half))(functools.partial(write, half))


def tail_kernel(slots, *refs):
    received = refs[:slots]
    hgrad_ref, back_ref, halo_ref, early_ref, map_ref, down_ref = refs[slots : slots + 6]
    out_ref, coarse_ref = refs[slots + 6 :]
    voxels = hgrad_ref.shape[0]
    cap = halo_ref.shape[1]
    cap2 = received[0].shape[0] - cap
    blocks = to_slots([r[0:cap, :] for r in received], True)
    out_ref[...] = add_lists(hgrad_ref[...] + back_ref[...], halo_ref, blocks)
    halo = jnp.concatenate(to_slots([r[cap:, :] for r in received], False), axis=0)
    octants = map_ref.shape[0]
    rows = map_ref[...]
    codes = encode(jnp.where(rows >= voxels, rows - voxels, slots * cap2))
    picked = []
    for o in range(octants):
        chooser = one_hot_rows(column(codes[o : o + 1, :]).astype(BF16), slots * cap2)
        far = matmul(chooser, halo).astype(BF16)
        picked.append(far + early_ref[:, o * LANES : (o + 1) * LANES])
    kernel = down_ref[...].reshape(octants * LANES, down_ref.shape[2])
    coarse_ref[...] = matmul(jnp.concatenate(picked, axis=1), kernel).astype(BF16)


def call(
    kernel, operands, outs, scratch=(), limit=32, flops=0, in_hbm=(), out_hbm=False, aliases={}
):
    spaces = [pl.ANY if n in in_hbm else pltpu.VMEM for n in range(len(operands))]
    return pl.pallas_call(
        kernel,
        out_shape=[jax.ShapeDtypeStruct(s, d) for s, d in outs],
        in_specs=[pl.BlockSpec(memory_space=space) for space in spaces],
        out_specs=[pl.BlockSpec(memory_space=pl.ANY if out_hbm else pltpu.VMEM) for _ in outs],
        input_output_aliases=aliases,
        scratch_shapes=list(scratch),
        compiler_params=pltpu.CompilerParams(vmem_limit_bytes=limit * 2**20),
        cost_estimate=pl.CostEstimate(flops=flops, bytes_accessed=4 * 2**20, transcendentals=0),
    )(*operands)


def swap_cores(value, devices):
    return lax.ppermute(value, "shard", [(i, i + 1 - 2 * (i % 2)) for i in range(devices)])


def exchange(value):
    return lax.all_to_all(value, "shard", 0, 0, tiled=True)


def local(
    features, conv_weight, down_weight, neighbour_map, halo_rows, child_map, child_rows, out_grad
):
    voxels, channels = features.shape
    parents, coarse_channels = out_grad.shape
    kernel_count = conv_weight.shape[0]
    octants = down_weight.shape[0]
    slots, cap = halo_rows.shape
    cap2 = child_rows.shape[1]
    devices = lax.axis_size("shard")
    scale = 1.0 / math.sqrt(voxels * devices)
    giga = 10**9

    sum_rows = octants * cap2 * coarse_channels // LANES
    conv_rows = kernel_count * channels
    down_rows = octants * channels * coarse_channels // LANES
    grain = 8 * devices
    half_rows = -(-(conv_rows + down_rows) // (2 * grain)) * grain
    first = call(
        head_kernel,
        (features, halo_rows, child_map, out_grad, down_weight),
        [((cap + cap2 + sum_rows, channels), BF16)] * slots + [((voxels, channels), F32)],
        scratch=[pltpu.VMEM((cap + cap2 + sum_rows, channels), BF16)] * slots
        + [pltpu.VMEM((voxels, channels), F32)]
        + [
            pltpu.VMEM(value.shape, value.dtype)
            for value in (features, halo_rows, child_map, out_grad, down_weight)
        ]
        + [pltpu.SemaphoreType.DMA((5 + 2 * slots,)), pltpu.SemaphoreType.DMA((4,))],
        limit=60,
        flops=giga,
        in_hbm=range(5),
        out_hbm=True,
    )
    back_h = first[-1]
    received = swaps(first[:-1], (2, 3, 1, 0))
    (early,) = call(
        functools.partial(local_kernel, slots * cap),
        (features, neighbour_map),
        [((voxels, conv_rows - channels), BF16)],
        scratch=[pltpu.VMEM((voxels // 2, 2 * channels), BF16)],
        flops=4 * giga,
    )
    hidden, pre_act, stacked, leaving = call(
        functools.partial(forward_kernel, slots, cap),
        (*received, features, neighbour_map, conv_weight, child_rows, early),
        [
            ((voxels, channels), BF16),
            ((voxels, channels), F32),
            ((voxels, conv_rows), BF16),
            ((slots * cap2, channels), BF16),
        ],
        scratch=[
            pltpu.VMEM((slots * cap, 4 * channels), BF16),
            pltpu.VMEM(conv_weight.shape, BF16),
        ],
        flops=12 * giga,
    )
    hidden_grad, pre_grad, early_h, terms, leaving_terms = call(
        functools.partial(gradient_kernel, slots, cap),
        (
            *received,
            stacked,
            pre_act,
            child_rows,
            back_h,
            hidden,
            leaving,
            child_map,
            out_grad,
        ),
        [
            ((voxels, channels), F32),
            ((voxels, channels), BF16),
            ((parents, octants * channels), BF16),
            ((2 * half_rows, LANES), BF16),
            ((half_rows, LANES), BF16),
        ],
        flops=3 * giga,
    )
    (pair_terms,) = call(
        pair_kernel,
        (terms, swap_cores(leaving_terms, devices)),
        [((half_rows, LANES), BF16)],
        scratch=[pltpu.VMEM((half_rows, LANES), BF16), pltpu.SemaphoreType.DMA((8,))],
        flops=10**6,
        out_hbm=True,
    )
    parts = exchange(pair_terms)
    spread = call(
        functools.partial(spread_kernel, slots, cap),
        (pre_grad, neighbour_map, conv_weight, leaving, pair_terms),
        [((voxels, channels), F32)] + [((cap + cap2, channels), BF16)] * slots,
        scratch=[pltpu.VMEM((voxels // 2 + slots * cap // 2, 2 * channels), F32)],
        flops=20 * giga,
        in_hbm=(4,),
    )
    (summed,) = call(
        functools.partial(sum_kernel, devices, scale),
        (parts, spread[1]),
        [((half_rows, LANES), BF16)],
        scratch=[pltpu.VMEM((half_rows, LANES), BF16), pltpu.SemaphoreType.DMA((8,))],
        flops=10**6,
        in_hbm=(1,),
        out_hbm=True,
    )
    summed, *returning = lax.optimization_barrier((summed, *spread[1:]))
    returned = swaps(returning, (0, 1, 2, 3))
    input_grad, coarse = call(
        functools.partial(tail_kernel, slots),
        (*returned, hidden_grad, spread[0], halo_rows, early_h, child_map, down_weight),
        [((voxels, channels), F32), ((parents, coarse_channels), BF16)],
        flops=giga,
    )
    mine, input_grad = lax.optimization_barrier((exchange(summed), input_grad))
    other = swap_cores(mine, devices)
    gradients = ()
    for own, block in ((True, mine), (False, other)):
        gradients = call(
            functools.partial(final_kernel, own),
            (block, *gradients),
            [((conv_rows, LANES), F32), ((octants * channels, coarse_channels), F32)],
            scratch=[
                pltpu.VMEM((conv_rows, LANES), F32),
                pltpu.VMEM((octants * channels, coarse_channels), F32),
                pltpu.SemaphoreType.DMA((32,)),
            ],
            flops=10**6,
            in_hbm=(1, 2),
            out_hbm=True,
            aliases={1: 0, 2: 1} if gradients else {},
        )
    conv_grad, down_grad = gradients
    conv_grad = conv_grad.reshape(conv_weight.shape)
    return (coarse, input_grad, conv_grad, down_grad.reshape(down_weight.shape))


def solution(mesh):
    return jax.shard_map(
        local,
        mesh=mesh,
        in_specs=(
            P("shard", None),
            P(),
            P(),
            P(None, "shard"),
            P(None, "shard"),
            P(None, "shard"),
            P(None, "shard"),
            P("shard", None),
        ),
        out_specs=(P("shard", None), P("shard", None), P(), P()),
        check_vma=False,
    )
```

```python
import functools
import math

import jax
import jax.numpy as jnp
from jax import lax
from jax.experimental import pallas as pl
from jax.experimental.pallas import tpu as pltpu
from jax.sharding import PartitionSpec as P

BF16 = jnp.bfloat16
F32 = jnp.float32
LANES = 128


def swaps(by_step, order):
    devices = lax.axis_size("shard")
    moved = {}
    for step in order:
        m, phase = step // 2 + 1, step % 2
        sign = [1 if (i // m) % 2 == phase else -1 for i in range(devices)]
        pairs = [(i, i + m * sign[i]) for i in range(devices) if 0 <= i + m * sign[i] < devices]
        moved[step] = lax.ppermute(by_step[step], "shard", pairs)
    return [moved[step] for step in range(len(by_step))]


def is_even(m):
    return lax.rem(lax.div(lax.axis_index("shard"), m), 2) == 0


def to_steps(slots, back):
    reach = len(slots) // 2
    steps = []
    for m in range(1, reach + 1):
        first, second = slots[reach + m - 1], slots[reach - m]
        if back:
            first, second = second, first
        steps.append(lax.select(is_even(m), first, second))
        steps.append(lax.select(is_even(m), second, first))
    return steps


def to_slots(steps, back):
    reach = len(steps) // 2
    slots = [None] * len(steps)
    for m in range(1, reach + 1):
        first = lax.select(is_even(m), steps[2 * m - 2], steps[2 * m - 1])
        second = lax.select(is_even(m), steps[2 * m - 1], steps[2 * m - 2])
        if back:
            first, second = second, first
        slots[reach - m], slots[reach + m - 1] = first, second
    return slots


def matmul(left, right):
    return jnp.dot(left, right, preferred_element_type=F32)


def matmul_rt(left, right):
    return lax.dot_general(left, right, (((1,), (1,)), ((), ())), preferred_element_type=F32)


def pick_one(mask):
    return jnp.where(mask, jnp.ones(mask.shape, BF16), jnp.zeros(mask.shape, BF16))


def encode(row):
    return jnp.left_shift((row & (LANES - 1)) + LANES, row >> 7).astype(F32)


def column(codes):
    pieces = []
    for start in range(0, codes.shape[1], LANES):
        piece = jnp.broadcast_to(codes[:, start : start + LANES], (LANES, LANES))
        pieces.append(jnp.transpose(piece))
    return pieces[0] if len(pieces) == 1 else jnp.concatenate(pieces, axis=0)


def one_hot_rows(col, width, first=0):
    lane = lax.broadcasted_iota(jnp.int32, (16, LANES), 1)
    blocks = []
    for start in range(first, first + width, LANES):
        pattern = jnp.broadcast_to(encode(lane + start).astype(BF16)[0:1], col.shape)
        blocks.append(pick_one(col == pattern))
    return jnp.concatenate(blocks, axis=1)


def one_hot_columns(codes, height):
    place = lax.broadcasted_iota(jnp.int32, (height, codes.shape[1]), 0)
    pattern = encode(place).astype(BF16)
    return pick_one(jnp.broadcast_to(codes, pattern.shape) == pattern)


def pick_rows(col, table):
    both = matmul(one_hot_rows(jnp.abs(col), table.shape[0]), table).astype(BF16)
    return jnp.where(col < jnp.zeros(col.shape, BF16), both[:, LANES:], both[:, :LANES])


def list_row(lists, first, per_row):
    pieces = [lists[first + n : first + n + 1, :] for n in range(per_row)]
    return pieces[0] if per_row == 1 else jnp.concatenate(pieces, axis=1)


def add_lists(total, lists_ref, blocks):
    slots, cap = lists_ref.shape
    codes = encode(lists_ref[...]).astype(F32)
    per_row = max(1, min(slots, LANES // cap))
    for first in range(0, slots, per_row):
        row = list_row(codes, first, per_row).astype(BF16)
        rows = jnp.concatenate(blocks[first : first + per_row], axis=0)
        total = total + matmul(one_hot_columns(row, total.shape[0]), rows)
    return total


def gather_lists(lists_ref, table):
    slots, cap = lists_ref.shape
    lists = lists_ref[...]
    per_row = max(1, min(slots, LANES // cap))
    parts = []
    for first in range(0, slots, per_row):
        codes = encode(list_row(lists, first, per_row))
        chooser = one_hot_rows(column(codes).astype(BF16), table.shape[0])
        parts.append(matmul(chooser, table))
    return parts[0] if len(parts) == 1 else jnp.concatenate(parts, axis=0)


def head_kernel(features_hbm, halo_hbm, child_map_hbm, out_grad_hbm, down_hbm, *refs):
    sources = (features_hbm, halo_hbm, child_map_hbm, out_grad_hbm, down_hbm)
    buffers, sems = refs[-len(sources) - 2 : -2], refs[-2]
    back_sems = refs[-1]
    features_ref, halo_ref, child_map_ref, out_grad_ref, down_ref = buffers
    copies = [
        pltpu.make_async_copy(source, buffer, sems.at[n])
        for n, (source, buffer) in enumerate(zip(sources, buffers))
    ]
    for copy in copies:
        copy.start()
    slots, cap = halo_ref.shape
    send_hbms, back_hbm = refs[:slots], refs[slots]
    sends, back_ref = refs[slots + 1 : 2 * slots + 1], refs[2 * slots + 1]
    voxels = features_ref.shape[0]
    octants = child_map_ref.shape[0]
    cap2 = sends[0].shape[0] - cap
    cap2 //= 1 + octants * out_grad_ref.shape[1] // LANES
    written = []

    def write(first, last):
        for send, send_hbm in zip(sends, send_hbms):
            place = pl.ds(first, last - first)
            sem = sems.at[len(copies) + len(written)]
            written.append(pltpu.make_async_copy(send.at[place], send_hbm.at[place], sem))
            written[-1].start()

    copies[0].wait()
    copies[1].wait()
    listed = gather_lists(halo_ref, features_ref[...]).astype(BF16)
    for send, block in zip(sends, to_steps(jnp.split(listed, slots), False)):
        send[0:cap, :] = block
    for copy in copies[2:]:
        copy.wait()
    upstream = out_grad_ref[...]
    rows = child_map_ref[...]
    codes = encode(jnp.where(rows >= voxels, rows - voxels, slots * cap2)).astype(BF16)
    sums = []
    for o in range(octants):
        chooser = one_hot_columns(codes[o : o + 1, :], slots * cap2)
        sums.append(matmul(chooser, upstream).astype(BF16))
    blocks = []
    for s in range(slots):
        listed_rows = slice(s * cap2, (s + 1) * cap2)
        halves = [
            sums[o][listed_rows, start : start + LANES]
            for o in range(octants)
            for start in range(0, upstream.shape[1], LANES)
        ]
        blocks.append(jnp.concatenate(halves, axis=0))
    for send, block in zip(sends, to_steps(blocks, True)):
        send[cap + cap2 :, :] = block
    write(cap + cap2, sends[0].shape[0])
    codes = half_codes(rows, voxels, slots * cap2)
    half = voxels // 2
    choosers, sides = [], []
    for o in range(octants):
        part = matmul_rt(upstream, down_ref[o]).astype(BF16)
        code = codes[o : o + 1, :].astype(BF16)
        right = column(code) < jnp.zeros(part.shape, BF16)
        none = jnp.zeros(part.shape, BF16)
        pair = [jnp.where(right, none, part), jnp.where(right, part, none)]
        sides.append(jnp.concatenate(pair, axis=1))
        choosers.append(one_hot_columns(jnp.abs(code), half + slots * cap2 // 2))
    both = matmul(jnp.concatenate(choosers, axis=1), jnp.concatenate(sides, axis=0))
    back_ref[0:half, :] = both[0:half, :LANES]
    back_ref[half:, :] = both[0:half, LANES:]
    far = jnp.concatenate([both[half:, :LANES], both[half:, LANES:]], axis=0).astype(BF16)
    for send, block in zip(sends, to_steps(jnp.split(far, slots), True)):
        send[cap : cap + cap2, :] = block
    write(0, cap + cap2)
    written += write_pieces(back_ref, back_hbm, back_sems)
    for copy in written:
        copy.wait()


def half_codes(row, voxels, received):
    half, half_received = voxels // 2, received // 2
    beyond = row - voxels
    outside = beyond >= 0
    near = row - jnp.where(row >= half, half, 0)
    far = half + beyond - jnp.where(beyond >= half_received, half_received, 0)
    code = encode(jnp.where(outside, far, near))
    near_sign = jnp.where(row >= half, -1.0, 1.0)
    far_sign = jnp.where(beyond >= half_received, -1.0, 1.0)
    return code * jnp.where(outside, far_sign, near_sign)


def offset_of(n, middle):
    return n + jnp.where(n >= middle, 1, 0)


def code_column(map_ref, k, voxels, received):
    return column(half_codes(map_ref[pl.ds(k, 1), :], voxels, received).astype(BF16))


def pick_side(col, both):
    return jnp.where(col < jnp.zeros(col.shape, BF16), both[:, LANES:], both[:, :LANES])


def local_kernel(received, features_ref, map_ref, early_ref, table_ref):
    voxels = features_ref.shape[0]
    half = voxels // 2
    table_ref[:, 0:LANES] = features_ref[0:half, :]
    table_ref[:, LANES:] = features_ref[half:, :]
    middle = map_ref.shape[0] // 2
    for n in range(early_ref.shape[1] // LANES):
        col = code_column(map_ref, offset_of(n, middle), voxels, received)
        both = matmul(one_hot_rows(jnp.abs(col), half), table_ref[...]).astype(BF16)
        early_ref[:, n * LANES : (n + 1) * LANES] = pick_side(col, both)


def forward_kernel(slots, cap, *refs):
    received = refs[:slots]
    features_ref, map_ref, weight_ref, child_ref, early_ref = refs[slots : slots + 5]
    hidden_ref, pre_ref, stacked_ref, leaving_ref, kernel_ref = refs[slots + 5 :]
    done = 0
    voxels = features_ref.shape[0]
    gathers = map_ref.shape[0] - 1
    middle = gathers // 2
    features = features_ref[...]
    halo = jnp.concatenate(to_slots([r[0:cap, :] for r in received], False), axis=0)
    kernel_ref[0:middle] = weight_ref[0:middle]
    kernel_ref[middle:gathers] = weight_ref[middle + 1 :]
    kernel_ref[gathers] = weight_ref[middle]

    for j in range(middle):
        numbers = (2 * j, 2 * j + 1)
        for n in numbers:
            rows = map_ref[pl.ds(offset_of(n, middle), 1), :]
            codes = encode(jnp.where(rows >= voxels, rows - voxels, slots * cap)).astype(BF16)
            far = matmul(one_hot_rows(column(codes), slots * cap), halo).astype(BF16)
            lanes = slice(n * LANES, (n + 1) * LANES)
            stacked_ref[:, lanes] = far + early_ref[:, lanes]
        last = 2 * j + 2
        if last == gathers:
            stacked_ref[:, gathers * LANES :] = features
            last = gathers + 1
        if last - done > 2:
            columns = stacked_ref[:, done * LANES : last * LANES]
            term = matmul(columns, kernel_ref[done:last].reshape(-1, LANES))
            pre_ref[...] = term if done == 0 else pre_ref[...] + term
            done = last

    pre = pre_ref[...]
    hidden = (features.astype(F32) + pre * jax.nn.sigmoid(pre)).astype(BF16)
    hidden_ref[...] = hidden
    leaving_ref[...] = gather_lists(child_ref, hidden).astype(BF16)


def gradient_kernel(slots, cap, *refs):
    received = refs[:slots]
    stacked_ref, pre_ref, child_ref, back_ref = refs[slots : slots + 4]
    hidden_ref, leaving_ref, child_map_ref, out_grad_ref = refs[slots + 4 : slots + 8]
    hgrad_ref, pgrad_ref, early_ref, terms_ref, send_ref = refs[slots + 8 :]
    cap2 = child_ref.shape[1]
    kernel_count = stacked_ref.shape[1] // LANES
    middle = kernel_count // 2
    blocks = to_slots([r[cap : cap + cap2, :] for r in received], True)
    hgrad = add_lists(back_ref[...], child_ref, blocks)
    hgrad_ref[...] = hgrad
    pre = pre_ref[...]
    sig = jax.nn.sigmoid(pre)
    pgrad = hgrad * (sig * (1.0 + pre * (1.0 - sig)))
    pgrad_ref[...] = pgrad.astype(BF16)
    terms = matmul(jnp.transpose(pgrad).astype(BF16), stacked_ref[...])
    order = [k for k in range(kernel_count) if k != middle] + [middle]
    for n, k in enumerate(order):
        block = jnp.transpose(terms[:, n * LANES : (n + 1) * LANES])
        terms_ref[k * LANES : (k + 1) * LANES, :] = block.astype(BF16)
    voxels = hidden_ref.shape[0]
    half = voxels // 2
    hidden = hidden_ref[...]
    table = jnp.concatenate([hidden[0:half], hidden[half:]], axis=1)
    octants = child_map_ref.shape[0]
    picked = []
    for o in range(octants):
        col = code_column(child_map_ref, o, voxels, slots * cap2)
        both = matmul(one_hot_rows(jnp.abs(col), half), table).astype(BF16)
        picked.append(pick_side(col, both))
    picked = jnp.concatenate(picked, axis=1)
    early_ref[...] = picked
    upstream_t = jnp.transpose(out_grad_ref[...].astype(F32)).astype(BF16)
    own = matmul(upstream_t, picked)
    blocks = to_slots([r[cap + cap2 :, :] for r in received], True)
    across = upstream_t.shape[0] // LANES
    sums = []
    for n in range(octants * across):
        rows = slice(n * cap2, (n + 1) * cap2)
        sums.append(jnp.concatenate([block[rows, :] for block in blocks], axis=0))
    leaving_t = jnp.transpose(leaving_ref[...].astype(F32)).astype(BF16)
    far = matmul(leaving_t, jnp.concatenate(sums, axis=1))
    row = kernel_count * LANES
    for n in range(octants * across):
        o, side = n // across, n % across
        block = own[side * LANES : (side + 1) * LANES, o * LANES : (o + 1) * LANES]
        value = jnp.transpose(block) + far[:, n * LANES : (n + 1) * LANES]
        terms_ref[row : row + LANES, :] = value.astype(BF16)
        row += LANES
    terms_ref[row:, :] = jnp.zeros((terms_ref.shape[0] - row, LANES), BF16)
    send_ref[...] = terms_ref[pl.ds(my_half(send_ref.shape[0])[1], send_ref.shape[0]), :]


def spread_kernel(
    slots, cap, pgrad_ref, map_ref, weight_ref, leaving_ref, after_ref, back_ref, *sends
):
    acc_ref = sends[-1]
    sends = sends[:-1]
    voxels = pgrad_ref.shape[0]
    kernel_count = map_ref.shape[0]
    middle = kernel_count // 2
    half = voxels // 2
    table_rows = half + slots * cap // 2
    pgrad = pgrad_ref[...]
    own = matmul_rt(pgrad, weight_ref[middle])
    acc_ref[0:half, 0:LANES] = own[0:half]
    acc_ref[0:half, LANES:] = own[half:]
    acc_ref[half:, :] = jnp.zeros((table_rows - half, 2 * LANES), F32)

    def parts(k):
        codes = half_codes(map_ref[pl.ds(k, 1), :], voxels, slots * cap)
        terms = matmul_rt(pgrad, weight_ref[k])
        right = column(codes) < 0.0
        sides = [jnp.where(right, 0.0, terms), jnp.where(right, terms, 0.0)]
        chooser = one_hot_columns(jnp.abs(codes).astype(BF16), table_rows)
        return chooser, jnp.concatenate(sides, axis=1).astype(BF16)

    def step(j, carry):
        near_chooser, near_terms = parts(j)
        far_chooser, far_terms = parts(j + middle + 1)
        acc_ref[...] += matmul(near_chooser, near_terms) + matmul(far_chooser, far_terms)
        return carry

    lax.fori_loop(0, middle, step, 0)
    back_ref[0:half, :] = acc_ref[0:half, 0:LANES]
    back_ref[half:, :] = acc_ref[0:half, LANES:]
    blocks = []
    for s in range(slots):
        first = half + (s % (slots // 2)) * cap
        side = (s // (slots // 2)) * LANES
        blocks.append(acc_ref[first : first + cap, side : side + LANES].astype(BF16))
    for send, block in zip(sends, to_steps(blocks, True)):
        send[0:cap, :] = block
    for send, block in zip(sends, to_steps(jnp.split(leaving_ref[...], slots), False)):
        send[cap:, :] = block


def my_half(rows):
    core = lax.rem(lax.axis_index("shard"), 2)
    return pl.multiple_of(core * rows, 16), pl.multiple_of((1 - core) * rows, 16)


def write_pieces(stage_ref, out_hbm, sems, first=0, last=None):
    pieces = sems.shape[0]
    rows = stage_ref.shape[0] // pieces
    copies = []
    for n in range(first, pieces if last is None else last):
        place = pl.ds(n * rows, rows)
        copies.append(pltpu.make_async_copy(stage_ref.at[place], out_hbm.at[place], sems.at[n]))
        copies[-1].start()
    return copies


def pair_kernel(terms_ref, other_ref, out_hbm, stage_ref, sems):
    pieces = sems.shape[0]
    rows = stage_ref.shape[0] // pieces
    first = my_half(stage_ref.shape[0])[0]
    copies = []
    for n in range(pieces):
        place = pl.ds(pl.multiple_of(first + n * rows, 16), rows)
        other = other_ref[n * rows : (n + 1) * rows, :].astype(F32)
        value = terms_ref[place, :].astype(F32) + other
        stage_ref[n * rows : (n + 1) * rows, :] = value.astype(BF16)
        copies += write_pieces(stage_ref, out_hbm, sems, n, n + 1)
    for copy in copies:
        copy.wait()


def sum_kernel(devices, scale, parts_ref, after_ref, out_hbm, stage_ref, sems):
    rows = parts_ref.shape[0] // devices
    sums = []
    for core in range(2):
        total = jnp.zeros((rows, LANES), F32)
        for d in range(core, devices, 2):
            total = total + parts_ref[d * rows : (d + 1) * rows, :].astype(F32)
        sums.append((total * scale).astype(BF16))
    pieces = sems.shape[0]
    copies = []
    for d in range(devices):
        stage_ref[d * rows : (d + 1) * rows, :] = sums[d % 2]
        if (d + 1) % (devices // pieces) == 0:
            piece = d // (devices // pieces)
            copies += write_pieces(stage_ref, out_hbm, sems, piece, piece + 1)
    for copy in copies:
        copy.wait()


def final_kernel(own, *refs):
    block_ref, conv_hbm, down_hbm = refs[0], *refs[-5:-3]
    conv_ref, down_ref, sems = refs[-3:]
    rows = block_ref.shape[0]
    conv_rows = conv_hbm.shape[0]
    core = lax.rem(lax.axis_index("shard"), 2)
    piece = 4 * LANES
    assert rows <= conv_rows <= 2 * rows and rows % LANES == 0

    def write(half):
        first, last = half * rows, (half + 1) * rows
        copies = []
        for start in range(first, min(last, conv_rows), piece):
            size = min(piece, last - start, conv_rows - start)
            place = pl.ds(start, size)
            value = block_ref[start - first : start - first + size, :]
            conv_ref[place, :] = value.astype(F32)
            sem = sems.at[len(copies)]
            copies.append(pltpu.make_async_copy(conv_ref.at[place], conv_hbm.at[place], sem))
            copies[-1].start()
        across = down_hbm.shape[1] // LANES
        for down in range(0, down_hbm.shape[0], LANES):
            row = conv_rows + down * across
            for side in range(across):
                start = row + side * LANES
                if first <= start < last:
                    value = block_ref[start - first : start - first + LANES, :]
                    lanes = slice(side * LANES, (side + 1) * LANES)
                    down_ref[down : down + LANES, lanes] = value.astype(F32)
            if first <= row < last:
                place = pl.ds(down, LANES)
                sem = sems.at[len(copies)]
                copies.append(pltpu.make_async_copy(down_ref.at[place], down_hbm.at[place], sem))
                copies[-1].start()
        for copy in copies:
            copy.wait()

    for half in range(2):
        pl.when(core == (half if own else 1 - half))(functools.partial(write, half))


def tail_kernel(slots, *refs):
    received = refs[:slots]
    hgrad_ref, back_ref, halo_ref, early_ref, map_ref, down_ref = refs[slots : slots + 6]
    out_ref, coarse_ref = refs[slots + 6 :]
    voxels = hgrad_ref.shape[0]
    cap = halo_ref.shape[1]
    cap2 = received[0].shape[0] - cap
    blocks = to_slots([r[0:cap, :] for r in received], True)
    out_ref[...] = add_lists(hgrad_ref[...] + back_ref[...], halo_ref, blocks)
    halo = jnp.concatenate(to_slots([r[cap:, :] for r in received], False), axis=0)
    octants = map_ref.shape[0]
    rows = map_ref[...]
    codes = encode(jnp.where(rows >= voxels, rows - voxels, slots * cap2))
    picked = []
    for o in range(octants):
        chooser = one_hot_rows(column(codes[o : o + 1, :]).astype(BF16), slots * cap2)
        far = matmul(chooser, halo).astype(BF16)
        picked.append(far + early_ref[:, o * LANES : (o + 1) * LANES])
    kernel = down_ref[...].reshape(octants * LANES, down_ref.shape[2])
    coarse_ref[...] = matmul(jnp.concatenate(picked, axis=1), kernel).astype(BF16)


def call(
    kernel, operands, outs, scratch=(), limit=32, flops=0, in_hbm=(), out_hbm=False, aliases={}
):
    spaces = [pl.ANY if n in in_hbm else pltpu.VMEM for n in range(len(operands))]
    return pl.pallas_call(
        kernel,
        out_shape=[jax.ShapeDtypeStruct(s, d) for s, d in outs],
        in_specs=[pl.BlockSpec(memory_space=space) for space in spaces],
        out_specs=[pl.BlockSpec(memory_space=pl.ANY if out_hbm else pltpu.VMEM) for _ in outs],
        input_output_aliases=aliases,
        scratch_shapes=list(scratch),
        compiler_params=pltpu.CompilerParams(vmem_limit_bytes=limit * 2**20),
        cost_estimate=pl.CostEstimate(flops=flops, bytes_accessed=4 * 2**20, transcendentals=0),
    )(*operands)


def swap_cores(value, devices):
    return lax.ppermute(value, "shard", [(i, i + 1 - 2 * (i % 2)) for i in range(devices)])


def exchange(value):
    return lax.all_to_all(value, "shard", 0, 0, tiled=True)


def local(
    features, conv_weight, down_weight, neighbour_map, halo_rows, child_map, child_rows, out_grad
):
    voxels, channels = features.shape
    parents, coarse_channels = out_grad.shape
    kernel_count = conv_weight.shape[0]
    octants = down_weight.shape[0]
    slots, cap = halo_rows.shape
    cap2 = child_rows.shape[1]
    devices = lax.axis_size("shard")
    scale = 1.0 / math.sqrt(voxels * devices)
    giga = 10**9

    sum_rows = octants * cap2 * coarse_channels // LANES
    conv_rows = kernel_count * channels
    down_rows = octants * channels * coarse_channels // LANES
    grain = 8 * devices
    half_rows = -(-(conv_rows + down_rows) // (2 * grain)) * grain
    first = call(
        head_kernel,
        (features, halo_rows, child_map, out_grad, down_weight),
        [((cap + cap2 + sum_rows, channels), BF16)] * slots + [((voxels, channels), F32)],
        scratch=[pltpu.VMEM((cap + cap2 + sum_rows, channels), BF16)] * slots
        + [pltpu.VMEM((voxels, channels), F32)]
        + [
            pltpu.VMEM(value.shape, value.dtype)
            for value in (features, halo_rows, child_map, out_grad, down_weight)
        ]
        + [pltpu.SemaphoreType.DMA((5 + 2 * slots,)), pltpu.SemaphoreType.DMA((4,))],
        limit=60,
        flops=giga,
        in_hbm=range(5),
        out_hbm=True,
    )
    back_h = first[-1]
    received = swaps(first[:-1], (2, 3, 1, 0))
    (early,) = call(
        functools.partial(local_kernel, slots * cap),
        (features, neighbour_map),
        [((voxels, conv_rows - channels), BF16)],
        scratch=[pltpu.VMEM((voxels // 2, 2 * channels), BF16)],
        flops=4 * giga,
    )
    hidden, pre_act, stacked, leaving = call(
        functools.partial(forward_kernel, slots, cap),
        (*received, features, neighbour_map, conv_weight, child_rows, early),
        [
            ((voxels, channels), BF16),
            ((voxels, channels), F32),
            ((voxels, conv_rows), BF16),
            ((slots * cap2, channels), BF16),
        ],
        scratch=[pltpu.VMEM(conv_weight.shape, BF16)],
        flops=12 * giga,
    )
    hidden_grad, pre_grad, early_h, terms, leaving_terms = call(
        functools.partial(gradient_kernel, slots, cap),
        (
            *received,
            stacked,
            pre_act,
            child_rows,
            back_h,
            hidden,
            leaving,
            child_map,
            out_grad,
        ),
        [
            ((voxels, channels), F32),
            ((voxels, channels), BF16),
            ((parents, octants * channels), BF16),
            ((2 * half_rows, LANES), BF16),
            ((half_rows, LANES), BF16),
        ],
        flops=3 * giga,
    )
    (pair_terms,) = call(
        pair_kernel,
        (terms, swap_cores(leaving_terms, devices)),
        [((half_rows, LANES), BF16)],
        scratch=[pltpu.VMEM((half_rows, LANES), BF16), pltpu.SemaphoreType.DMA((8,))],
        flops=10**6,
        out_hbm=True,
    )
    parts = exchange(pair_terms)
    spread = call(
        functools.partial(spread_kernel, slots, cap),
        (pre_grad, neighbour_map, conv_weight, leaving, pair_terms),
        [((voxels, channels), F32)] + [((cap + cap2, channels), BF16)] * slots,
        scratch=[pltpu.VMEM((voxels // 2 + slots * cap // 2, 2 * channels), F32)],
        flops=20 * giga,
        in_hbm=(4,),
    )
    (summed,) = call(
        functools.partial(sum_kernel, devices, scale),
        (parts, spread[1]),
        [((half_rows, LANES), BF16)],
        scratch=[pltpu.VMEM((half_rows, LANES), BF16), pltpu.SemaphoreType.DMA((8,))],
        flops=10**6,
        in_hbm=(1,),
        out_hbm=True,
    )
    summed, *returning = lax.optimization_barrier((summed, *spread[1:]))
    returned = swaps(returning, (0, 1, 2, 3))
    input_grad, coarse = call(
        functools.partial(tail_kernel, slots),
        (*returned, hidden_grad, spread[0], halo_rows, early_h, child_map, down_weight),
        [((voxels, channels), F32), ((parents, coarse_channels), BF16)],
        flops=giga,
    )
    mine, input_grad = lax.optimization_barrier((exchange(summed), input_grad))
    other = swap_cores(mine, devices)
    gradients = ()
    for own, block in ((True, mine), (False, other)):
        gradients = call(
            functools.partial(final_kernel, own),
            (block, *gradients),
            [((conv_rows, LANES), F32), ((octants * channels, coarse_channels), F32)],
            scratch=[
                pltpu.VMEM((conv_rows, LANES), F32),
                pltpu.VMEM((octants * channels, coarse_channels), F32),
                pltpu.SemaphoreType.DMA((32,)),
            ],
            flops=10**6,
            in_hbm=(1, 2),
            out_hbm=True,
            aliases={1: 0, 2: 1} if gradients else {},
        )
    conv_grad, down_grad = gradients
    conv_grad = conv_grad.reshape(conv_weight.shape)
    return (coarse, input_grad, conv_grad, down_grad.reshape(down_weight.shape))


def solution(mesh):
    return jax.shard_map(
        local,
        mesh=mesh,
        in_specs=(
            P("shard", None),
            P(),
            P(),
            P(None, "shard"),
            P(None, "shard"),
            P(None, "shard"),
            P(None, "shard"),
            P("shard", None),
        ),
        out_specs=(P("shard", None), P("shard", None), P(), P()),
        check_vma=False,
    )
```

```python
import functools
import math

import jax
import jax.numpy as jnp
from jax import lax
from jax.experimental import pallas as pl
from jax.experimental.pallas import tpu as pltpu
from jax.sharding import PartitionSpec as P

BF16 = jnp.bfloat16
F32 = jnp.float32
LANES = 128


def swaps(by_step, order):
    devices = lax.axis_size("shard")
    moved = {}
    for step in order:
        m, phase = step // 2 + 1, step % 2
        sign = [1 if (i // m) % 2 == phase else -1 for i in range(devices)]
        pairs = [(i, i + m * sign[i]) for i in range(devices) if 0 <= i + m * sign[i] < devices]
        moved[step] = lax.ppermute(by_step[step], "shard", pairs)
    return [moved[step] for step in range(len(by_step))]


def is_even(m):
    return lax.rem(lax.div(lax.axis_index("shard"), m), 2) == 0


def to_steps(slots, back):
    reach = len(slots) // 2
    steps = []
    for m in range(1, reach + 1):
        first, second = slots[reach + m - 1], slots[reach - m]
        if back:
            first, second = second, first
        steps.append(lax.select(is_even(m), first, second))
        steps.append(lax.select(is_even(m), second, first))
    return steps


def to_slots(steps, back):
    reach = len(steps) // 2
    slots = [None] * len(steps)
    for m in range(1, reach + 1):
        first = lax.select(is_even(m), steps[2 * m - 2], steps[2 * m - 1])
        second = lax.select(is_even(m), steps[2 * m - 1], steps[2 * m - 2])
        if back:
            first, second = second, first
        slots[reach - m], slots[reach + m - 1] = first, second
    return slots


def matmul(left, right):
    return jnp.dot(left, right, preferred_element_type=F32)


def matmul_rt(left, right):
    return lax.dot_general(left, right, (((1,), (1,)), ((), ())), preferred_element_type=F32)


def pick_one(mask):
    return jnp.where(mask, jnp.ones(mask.shape, BF16), jnp.zeros(mask.shape, BF16))


def encode(row):
    return jnp.left_shift((row & (LANES - 1)) + LANES, row >> 7).astype(F32)


def column(codes):
    pieces = []
    for start in range(0, codes.shape[1], LANES):
        piece = jnp.broadcast_to(codes[:, start : start + LANES], (LANES, LANES))
        pieces.append(jnp.transpose(piece))
    return pieces[0] if len(pieces) == 1 else jnp.concatenate(pieces, axis=0)


def one_hot_rows(col, width, first=0):
    lane = lax.broadcasted_iota(jnp.int32, (16, LANES), 1)
    blocks = []
    for start in range(first, first + width, LANES):
        pattern = jnp.broadcast_to(encode(lane + start).astype(BF16)[0:1], col.shape)
        blocks.append(pick_one(col == pattern))
    return jnp.concatenate(blocks, axis=1)


def one_hot_columns(codes, height):
    place = lax.broadcasted_iota(jnp.int32, (height, codes.shape[1]), 0)
    pattern = encode(place).astype(BF16)
    return pick_one(jnp.broadcast_to(codes, pattern.shape) == pattern)


def pick_rows(col, table):
    both = matmul(one_hot_rows(jnp.abs(col), table.shape[0]), table).astype(BF16)
    return jnp.where(col < jnp.zeros(col.shape, BF16), both[:, LANES:], both[:, :LANES])


def turn(value):
    blocks = [jnp.transpose(value[n : n + LANES, :]) for n in range(0, value.shape[0], LANES)]
    return jnp.concatenate(blocks, axis=1)


def list_row(lists, first, per_row):
    pieces = [lists[first + n : first + n + 1, :] for n in range(per_row)]
    return pieces[0] if per_row == 1 else jnp.concatenate(pieces, axis=1)


def add_lists(total, lists_ref, blocks):
    slots, cap = lists_ref.shape
    codes = encode(lists_ref[...]).astype(F32)
    per_row = max(1, min(slots, LANES // cap))
    for first in range(0, slots, per_row):
        row = list_row(codes, first, per_row).astype(BF16)
        rows = jnp.concatenate(blocks[first : first + per_row], axis=0)
        total = total + matmul(one_hot_columns(row, total.shape[0]), rows)
    return total


def gather_lists(lists_ref, table):
    slots, cap = lists_ref.shape
    lists = lists_ref[...]
    per_row = max(1, min(slots, LANES // cap))
    parts = []
    for first in range(0, slots, per_row):
        codes = encode(list_row(lists, first, per_row))
        chooser = one_hot_rows(column(codes).astype(BF16), table.shape[0])
        parts.append(matmul(chooser, table))
    return parts[0] if len(parts) == 1 else jnp.concatenate(parts, axis=0)


def head_kernel(features_hbm, halo_hbm, child_map_hbm, out_grad_hbm, down_hbm, *refs):
    sources = (features_hbm, halo_hbm, child_map_hbm, out_grad_hbm, down_hbm)
    buffers, sems = refs[-len(sources) - 2 : -2], refs[-2]
    back_sems = refs[-1]
    features_ref, halo_ref, child_map_ref, out_grad_ref, down_ref = buffers
    copies = [
        pltpu.make_async_copy(source, buffer, sems.at[n])
        for n, (source, buffer) in enumerate(zip(sources, buffers))
    ]
    for copy in copies:
        copy.start()
    slots, cap = halo_ref.shape
    send_hbms, back_hbm = refs[:slots], refs[slots]
    sends, back_ref = refs[slots + 1 : 2 * slots + 1], refs[2 * slots + 1]
    voxels = features_ref.shape[0]
    octants = child_map_ref.shape[0]
    cap2 = sends[0].shape[0] - cap
    cap2 //= 1 + octants * out_grad_ref.shape[1] // LANES
    written = []

    def write(first, last):
        for send, send_hbm in zip(sends, send_hbms):
            place = pl.ds(first, last - first)
            sem = sems.at[len(copies) + len(written)]
            written.append(pltpu.make_async_copy(send.at[place], send_hbm.at[place], sem))
            written[-1].start()

    copies[0].wait()
    copies[1].wait()
    listed = gather_lists(halo_ref, features_ref[...]).astype(BF16)
    for send, block in zip(sends, to_steps(jnp.split(listed, slots), False)):
        send[0:cap, :] = block
    for copy in copies[2:]:
        copy.wait()
    upstream = out_grad_ref[...]
    rows = child_map_ref[...]
    codes = encode(jnp.where(rows >= voxels, rows - voxels, slots * cap2)).astype(BF16)
    sums = []
    for o in range(octants):
        chooser = one_hot_columns(codes[o : o + 1, :], slots * cap2)
        sums.append(matmul(chooser, upstream).astype(BF16))
    blocks = []
    for s in range(slots):
        listed_rows = slice(s * cap2, (s + 1) * cap2)
        halves = [
            sums[o][listed_rows, start : start + LANES]
            for o in range(octants)
            for start in range(0, upstream.shape[1], LANES)
        ]
        blocks.append(jnp.concatenate(halves, axis=0))
    for send, block in zip(sends, to_steps(blocks, True)):
        send[cap + cap2 :, :] = block
    write(cap + cap2, sends[0].shape[0])
    codes = half_codes(rows, voxels, slots * cap2)
    half = voxels // 2
    choosers, sides = [], []
    for o in range(octants):
        part = matmul_rt(upstream, down_ref[o]).astype(BF16)
        code = codes[o : o + 1, :].astype(BF16)
        right = column(code) < jnp.zeros(part.shape, BF16)
        none = jnp.zeros(part.shape, BF16)
        pair = [jnp.where(right, none, part), jnp.where(right, part, none)]
        sides.append(jnp.concatenate(pair, axis=1))
        choosers.append(one_hot_columns(jnp.abs(code), half + slots * cap2 // 2))
    both = matmul(jnp.concatenate(choosers, axis=1), jnp.concatenate(sides, axis=0))
    back_ref[0:half, :] = both[0:half, :LANES]
    back_ref[half:, :] = both[0:half, LANES:]
    far = jnp.concatenate([both[half:, :LANES], both[half:, LANES:]], axis=0).astype(BF16)
    for send, block in zip(sends, to_steps(jnp.split(far, slots), True)):
        send[cap : cap + cap2, :] = block
    write(0, cap + cap2)
    written += write_pieces(back_ref, back_hbm, back_sems)
    for copy in written:
        copy.wait()


def half_codes(row, voxels, received):
    half, half_received = voxels // 2, received // 2
    beyond = row - voxels
    outside = beyond >= 0
    near = row - jnp.where(row >= half, half, 0)
    far = half + beyond - jnp.where(beyond >= half_received, half_received, 0)
    code = encode(jnp.where(outside, far, near))
    near_sign = jnp.where(row >= half, -1.0, 1.0)
    far_sign = jnp.where(beyond >= half_received, -1.0, 1.0)
    return code * jnp.where(outside, far_sign, near_sign)


def offset_of(n, middle):
    return n + jnp.where(n >= middle, 1, 0)


def code_column(map_ref, k, voxels, received):
    return column(half_codes(map_ref[pl.ds(k, 1), :], voxels, received).astype(BF16))


def pick_side(col, both):
    return jnp.where(col < jnp.zeros(col.shape, BF16), both[:, LANES:], both[:, :LANES])


def local_kernel(received, features_ref, map_ref, early_ref, table_ref):
    voxels = features_ref.shape[0]
    half = voxels // 2
    table_ref[:, 0:LANES] = features_ref[0:half, :]
    table_ref[:, LANES:] = features_ref[half:, :]
    middle = map_ref.shape[0] // 2
    for n in range(early_ref.shape[1] // LANES):
        col = code_column(map_ref, offset_of(n, middle), voxels, received)
        both = matmul(one_hot_rows(jnp.abs(col), half), table_ref[...]).astype(BF16)
        early_ref[:, n * LANES : (n + 1) * LANES] = pick_side(col, both)


def forward_kernel(slots, cap, *refs):
    received = refs[:slots]
    features_ref, map_ref, weight_ref, child_ref, early_ref = refs[slots : slots + 5]
    hidden_ref, pre_ref, stacked_ref, leaving_ref, kernel_ref = refs[slots + 5 :]
    done = 0
    voxels = features_ref.shape[0]
    gathers = map_ref.shape[0] - 1
    middle = gathers // 2
    features = features_ref[...]
    halo = jnp.concatenate(to_slots([r[0:cap, :] for r in received], False), axis=0)
    kernel_ref[0:middle] = weight_ref[0:middle]
    kernel_ref[middle:gathers] = weight_ref[middle + 1 :]
    kernel_ref[gathers] = weight_ref[middle]

    for j in range(middle):
        numbers = (2 * j, 2 * j + 1)
        for n in numbers:
            rows = map_ref[pl.ds(offset_of(n, middle), 1), :]
            codes = encode(jnp.where(rows >= voxels, rows - voxels, slots * cap)).astype(BF16)
            far = matmul(one_hot_rows(column(codes), slots * cap), halo).astype(BF16)
            lanes = slice(n * LANES, (n + 1) * LANES)
            stacked_ref[:, lanes] = far + early_ref[:, lanes]
        last = 2 * j + 2
        if last == gathers:
            stacked_ref[:, gathers * LANES :] = features
            last = gathers + 1
        if last - done > 2:
            columns = stacked_ref[:, done * LANES : last * LANES]
            term = matmul(columns, kernel_ref[done:last].reshape(-1, LANES))
            pre_ref[...] = term if done == 0 else pre_ref[...] + term
            done = last

    pre = pre_ref[...]
    hidden = (features.astype(F32) + pre * jax.nn.sigmoid(pre)).astype(BF16)
    hidden_ref[...] = hidden
    leaving_ref[...] = gather_lists(child_ref, hidden).astype(BF16)


def gradient_kernel(slots, cap, *refs):
    received = refs[:slots]
    stacked_ref, pre_ref, child_ref, back_ref = refs[slots : slots + 4]
    hidden_ref, leaving_ref, child_map_ref, out_grad_ref = refs[slots + 4 : slots + 8]
    hgrad_ref, pgrad_ref, early_ref, terms_ref, send_ref = refs[slots + 8 :]
    cap2 = child_ref.shape[1]
    kernel_count = stacked_ref.shape[1] // LANES
    middle = kernel_count // 2
    blocks = to_slots([r[cap : cap + cap2, :] for r in received], True)
    hgrad = add_lists(back_ref[...], child_ref, blocks)
    hgrad_ref[...] = hgrad
    pre = pre_ref[...]
    sig = jax.nn.sigmoid(pre)
    pgrad = (hgrad * (sig * (1.0 + pre * (1.0 - sig)))).astype(BF16)
    pgrad_ref[...] = pgrad
    terms = matmul(turn(pgrad), stacked_ref[...]).astype(BF16)
    order = [k for k in range(kernel_count) if k != middle] + [middle]
    for n, k in enumerate(order):
        block = jnp.transpose(terms[:, n * LANES : (n + 1) * LANES])
        terms_ref[k * LANES : (k + 1) * LANES, :] = block
    voxels = hidden_ref.shape[0]
    half = voxels // 2
    hidden = hidden_ref[...]
    table = jnp.concatenate([hidden[0:half], hidden[half:]], axis=1)
    octants = child_map_ref.shape[0]
    picked = []
    for o in range(octants):
        col = code_column(child_map_ref, o, voxels, slots * cap2)
        both = matmul(one_hot_rows(jnp.abs(col), half), table).astype(BF16)
        picked.append(pick_side(col, both))
    picked = jnp.concatenate(picked, axis=1)
    early_ref[...] = picked
    upstream_t = jnp.transpose(out_grad_ref[...].astype(F32)).astype(BF16)
    own = matmul(upstream_t, picked)
    blocks = to_slots([r[cap + cap2 :, :] for r in received], True)
    across = upstream_t.shape[0] // LANES
    sums = []
    for n in range(octants * across):
        rows = slice(n * cap2, (n + 1) * cap2)
        sums.append(jnp.concatenate([block[rows, :] for block in blocks], axis=0))
    leaving_t = turn(leaving_ref[...])
    far = matmul(leaving_t, jnp.concatenate(sums, axis=1))
    row = kernel_count * LANES
    for n in range(octants * across):
        o, side = n // across, n % across
        block = own[side * LANES : (side + 1) * LANES, o * LANES : (o + 1) * LANES]
        value = jnp.transpose(block) + far[:, n * LANES : (n + 1) * LANES]
        terms_ref[row : row + LANES, :] = value.astype(BF16)
        row += LANES
    terms_ref[row:, :] = jnp.zeros((terms_ref.shape[0] - row, LANES), BF16)
    send_ref[...] = terms_ref[pl.ds(my_half(send_ref.shape[0])[1], send_ref.shape[0]), :]


def spread_kernel(
    slots, cap, pgrad_ref, map_ref, weight_ref, leaving_ref, after_ref, back_ref, *sends
):
    acc_ref = sends[-1]
    sends = sends[:-1]
    voxels = pgrad_ref.shape[0]
    kernel_count = map_ref.shape[0]
    middle = kernel_count // 2
    half = voxels // 2
    table_rows = half + slots * cap // 2
    pgrad = pgrad_ref[...]
    own = matmul_rt(pgrad, weight_ref[middle])
    acc_ref[0:half, 0:LANES] = own[0:half]
    acc_ref[0:half, LANES:] = own[half:]
    acc_ref[half:, :] = jnp.zeros((table_rows - half, 2 * LANES), F32)

    def parts(k):
        codes = half_codes(map_ref[pl.ds(k, 1), :], voxels, slots * cap)
        terms = matmul_rt(pgrad, weight_ref[k])
        right = column(codes) < 0.0
        sides = [jnp.where(right, 0.0, terms), jnp.where(right, terms, 0.0)]
        chooser = one_hot_columns(jnp.abs(codes).astype(BF16), table_rows)
        return chooser, jnp.concatenate(sides, axis=1).astype(BF16)

    def step(j, carry):
        near_chooser, near_terms = parts(j)
        far_chooser, far_terms = parts(j + middle + 1)
        acc_ref[...] += matmul(near_chooser, near_terms) + matmul(far_chooser, far_terms)
        return carry

    lax.fori_loop(0, middle, step, 0)
    back_ref[0:half, :] = acc_ref[0:half, 0:LANES]
    back_ref[half:, :] = acc_ref[0:half, LANES:]
    blocks = []
    for s in range(slots):
        first = half + (s % (slots // 2)) * cap
        side = (s // (slots // 2)) * LANES
        blocks.append(acc_ref[first : first + cap, side : side + LANES].astype(BF16))
    for send, block in zip(sends, to_steps(blocks, True)):
        send[0:cap, :] = block
    for send, block in zip(sends, to_steps(jnp.split(leaving_ref[...], slots), False)):
        send[cap:, :] = block


def my_half(rows):
    core = lax.rem(lax.axis_index("shard"), 2)
    return pl.multiple_of(core * rows, 16), pl.multiple_of((1 - core) * rows, 16)


def write_pieces(stage_ref, out_hbm, sems, first=0, last=None):
    pieces = sems.shape[0]
    rows = stage_ref.shape[0] // pieces
    copies = []
    for n in range(first, pieces if last is None else last):
        place = pl.ds(n * rows, rows)
        copies.append(pltpu.make_async_copy(stage_ref.at[place], out_hbm.at[place], sems.at[n]))
        copies[-1].start()
    return copies


def pair_kernel(terms_ref, other_ref, out_hbm, stage_ref, sems):
    pieces = sems.shape[0]
    rows = stage_ref.shape[0] // pieces
    first = my_half(stage_ref.shape[0])[0]
    copies = []
    for n in range(pieces):
        place = pl.ds(pl.multiple_of(first + n * rows, 16), rows)
        other = other_ref[n * rows : (n + 1) * rows, :].astype(F32)
        value = terms_ref[place, :].astype(F32) + other
        stage_ref[n * rows : (n + 1) * rows, :] = value.astype(BF16)
        copies += write_pieces(stage_ref, out_hbm, sems, n, n + 1)
    for copy in copies:
        copy.wait()


def sum_kernel(devices, scale, parts_ref, after_ref, out_hbm, stage_ref, sems):
    rows = parts_ref.shape[0] // devices
    sums = []
    for core in range(2):
        total = jnp.zeros((rows, LANES), F32)
        for d in range(core, devices, 2):
            total = total + parts_ref[d * rows : (d + 1) * rows, :].astype(F32)
        sums.append((total * scale).astype(BF16))
    pieces = sems.shape[0]
    copies = []
    for d in range(devices):
        stage_ref[d * rows : (d + 1) * rows, :] = sums[d % 2]
        if (d + 1) % (devices // pieces) == 0:
            piece = d // (devices // pieces)
            copies += write_pieces(stage_ref, out_hbm, sems, piece, piece + 1)
    for copy in copies:
        copy.wait()


def final_kernel(own, *refs):
    block_ref, conv_hbm, down_hbm = refs[0], *refs[-5:-3]
    conv_ref, down_ref, sems = refs[-3:]
    rows = block_ref.shape[0]
    conv_rows = conv_hbm.shape[0]
    core = lax.rem(lax.axis_index("shard"), 2)
    piece = 2 * LANES
    assert rows <= conv_rows <= 2 * rows and rows % LANES == 0

    def write(half):
        first, last = half * rows, (half + 1) * rows
        copies = []
        for start in range(first, min(last, conv_rows), piece):
            size = min(piece, last - start, conv_rows - start)
            place = pl.ds(start, size)
            value = block_ref[start - first : start - first + size, :]
            conv_ref[place, :] = value.astype(F32)
            sem = sems.at[len(copies)]
            copies.append(pltpu.make_async_copy(conv_ref.at[place], conv_hbm.at[place], sem))
            copies[-1].start()
        across = down_hbm.shape[1] // LANES
        for down in range(0, down_hbm.shape[0], LANES):
            row = conv_rows + down * across
            for side in range(across):
                start = row + side * LANES
                if first <= start < last:
                    value = block_ref[start - first : start - first + LANES, :]
                    lanes = slice(side * LANES, (side + 1) * LANES)
                    down_ref[down : down + LANES, lanes] = value.astype(F32)
            if first <= row < last:
                place = pl.ds(down, LANES)
                sem = sems.at[len(copies)]
                copies.append(pltpu.make_async_copy(down_ref.at[place], down_hbm.at[place], sem))
                copies[-1].start()
        for copy in copies:
            copy.wait()

    for half in range(2):
        pl.when(core == (half if own else 1 - half))(functools.partial(write, half))


def tail_kernel(slots, *refs):
    received = refs[:slots]
    hgrad_ref, back_ref, halo_ref, early_ref, map_ref, down_ref = refs[slots : slots + 6]
    out_ref, coarse_ref = refs[slots + 6 :]
    voxels = hgrad_ref.shape[0]
    cap = halo_ref.shape[1]
    cap2 = received[0].shape[0] - cap
    blocks = to_slots([r[0:cap, :] for r in received], True)
    out_ref[...] = add_lists(hgrad_ref[...] + back_ref[...], halo_ref, blocks)
    halo = jnp.concatenate(to_slots([r[cap:, :] for r in received], False), axis=0)
    octants = map_ref.shape[0]
    rows = map_ref[...]
    codes = encode(jnp.where(rows >= voxels, rows - voxels, slots * cap2))
    picked = []
    for o in range(octants):
        chooser = one_hot_rows(column(codes[o : o + 1, :]).astype(BF16), slots * cap2)
        far = matmul(chooser, halo).astype(BF16)
        picked.append(far + early_ref[:, o * LANES : (o + 1) * LANES])
    kernel = down_ref[...].reshape(octants * LANES, down_ref.shape[2])
    coarse_ref[...] = matmul(jnp.concatenate(picked, axis=1), kernel).astype(BF16)


def call(
    kernel, operands, outs, scratch=(), limit=32, flops=0, in_hbm=(), out_hbm=False, aliases={}
):
    spaces = [pl.ANY if n in in_hbm else pltpu.VMEM for n in range(len(operands))]
    return pl.pallas_call(
        kernel,
        out_shape=[jax.ShapeDtypeStruct(s, d) for s, d in outs],
        in_specs=[pl.BlockSpec(memory_space=space) for space in spaces],
        out_specs=[pl.BlockSpec(memory_space=pl.ANY if out_hbm else pltpu.VMEM) for _ in outs],
        input_output_aliases=aliases,
        scratch_shapes=list(scratch),
        compiler_params=pltpu.CompilerParams(vmem_limit_bytes=limit * 2**20),
        cost_estimate=pl.CostEstimate(flops=flops, bytes_accessed=4 * 2**20, transcendentals=0),
    )(*operands)


def swap_cores(value, devices):
    return lax.ppermute(value, "shard", [(i, i + 1 - 2 * (i % 2)) for i in range(devices)])


def exchange(value):
    return lax.all_to_all(value, "shard", 0, 0, tiled=True)


def local(
    features, conv_weight, down_weight, neighbour_map, halo_rows, child_map, child_rows, out_grad
):
    voxels, channels = features.shape
    parents, coarse_channels = out_grad.shape
    kernel_count = conv_weight.shape[0]
    octants = down_weight.shape[0]
    slots, cap = halo_rows.shape
    cap2 = child_rows.shape[1]
    devices = lax.axis_size("shard")
    scale = 1.0 / math.sqrt(voxels * devices)
    giga = 10**9

    sum_rows = octants * cap2 * coarse_channels // LANES
    conv_rows = kernel_count * channels
    down_rows = octants * channels * coarse_channels // LANES
    grain = 8 * devices
    half_rows = -(-(conv_rows + down_rows) // (2 * grain)) * grain
    first = call(
        head_kernel,
        (features, halo_rows, child_map, out_grad, down_weight),
        [((cap + cap2 + sum_rows, channels), BF16)] * slots + [((voxels, channels), F32)],
        scratch=[pltpu.VMEM((cap + cap2 + sum_rows, channels), BF16)] * slots
        + [pltpu.VMEM((voxels, channels), F32)]
        + [
            pltpu.VMEM(value.shape, value.dtype)
            for value in (features, halo_rows, child_map, out_grad, down_weight)
        ]
        + [pltpu.SemaphoreType.DMA((5 + 2 * slots,)), pltpu.SemaphoreType.DMA((4,))],
        limit=60,
        flops=giga,
        in_hbm=range(5),
        out_hbm=True,
    )
    back_h = first[-1]
    received = swaps(first[:-1], (2, 3, 1, 0))
    (early,) = call(
        functools.partial(local_kernel, slots * cap),
        (features, neighbour_map),
        [((voxels, conv_rows - channels), BF16)],
        scratch=[pltpu.VMEM((voxels // 2, 2 * channels), BF16)],
        flops=4 * giga,
    )
    hidden, pre_act, stacked, leaving = call(
        functools.partial(forward_kernel, slots, cap),
        (*received, features, neighbour_map, conv_weight, child_rows, early),
        [
            ((voxels, channels), BF16),
            ((voxels, channels), F32),
            ((voxels, conv_rows), BF16),
            ((slots * cap2, channels), BF16),
        ],
        scratch=[pltpu.VMEM(conv_weight.shape, BF16)],
        flops=12 * giga,
    )
    hidden_grad, pre_grad, early_h, terms, leaving_terms = call(
        functools.partial(gradient_kernel, slots, cap),
        (
            *received,
            stacked,
            pre_act,
            child_rows,
            back_h,
            hidden,
            leaving,
            child_map,
            out_grad,
        ),
        [
            ((voxels, channels), F32),
            ((voxels, channels), BF16),
            ((parents, octants * channels), BF16),
            ((2 * half_rows, LANES), BF16),
            ((half_rows, LANES), BF16),
        ],
        flops=3 * giga,
    )
    (pair_terms,) = call(
        pair_kernel,
        (terms, swap_cores(leaving_terms, devices)),
        [((half_rows, LANES), BF16)],
        scratch=[pltpu.VMEM((half_rows, LANES), BF16), pltpu.SemaphoreType.DMA((8,))],
        flops=10**6,
        out_hbm=True,
    )
    parts = exchange(pair_terms)
    spread = call(
        functools.partial(spread_kernel, slots, cap),
        (pre_grad, neighbour_map, conv_weight, leaving, pair_terms),
        [((voxels, channels), F32)] + [((cap + cap2, channels), BF16)] * slots,
        scratch=[pltpu.VMEM((voxels // 2 + slots * cap // 2, 2 * channels), F32)],
        flops=20 * giga,
        in_hbm=(4,),
    )
    (summed,) = call(
        functools.partial(sum_kernel, devices, scale),
        (parts, spread[1]),
        [((half_rows, LANES), BF16)],
        scratch=[pltpu.VMEM((half_rows, LANES), BF16), pltpu.SemaphoreType.DMA((8,))],
        flops=10**6,
        in_hbm=(1,),
        out_hbm=True,
    )
    summed, *returning = lax.optimization_barrier((summed, *spread[1:]))
    returned = swaps(returning, (0, 1, 2, 3))
    input_grad, coarse = call(
        functools.partial(tail_kernel, slots),
        (*returned, hidden_grad, spread[0], halo_rows, early_h, child_map, down_weight),
        [((voxels, channels), F32), ((parents, coarse_channels), BF16)],
        flops=giga,
    )
    mine, input_grad = lax.optimization_barrier((exchange(summed), input_grad))
    other = swap_cores(mine, devices)
    gradients = ()
    for own, block in ((True, mine), (False, other)):
        gradients = call(
            functools.partial(final_kernel, own),
            (block, *gradients),
            [((conv_rows, LANES), F32), ((octants * channels, coarse_channels), F32)],
            scratch=[
                pltpu.VMEM((conv_rows, LANES), F32),
                pltpu.VMEM((octants * channels, coarse_channels), F32),
                pltpu.SemaphoreType.DMA((32,)),
            ],
            flops=10**6,
            in_hbm=(1, 2),
            out_hbm=True,
            aliases={1: 0, 2: 1} if gradients else {},
        )
    conv_grad, down_grad = gradients
    conv_grad = conv_grad.reshape(conv_weight.shape)
    return (coarse, input_grad, conv_grad, down_grad.reshape(down_weight.shape))


def solution(mesh):
    return jax.shard_map(
        local,
        mesh=mesh,
        in_specs=(
            P("shard", None),
            P(),
            P(),
            P(None, "shard"),
            P(None, "shard"),
            P(None, "shard"),
            P(None, "shard"),
            P("shard", None),
        ),
        out_specs=(P("shard", None), P("shard", None), P(), P()),
        check_vma=False,
    )
```
